32 devices in a mesh: atoms: 32 (over z, y, x, core).
Axes of the slice: x: 2, y: 2, z: 4, core: 2. Of those that a mesh axis runs over, the one named last changes fastest.
Arguments:
- positions: float32 [3, 2048], P(None, 'atoms'), as said below
- species: int32 [2048], P('atoms'), may hold values from 0 to 59
- neighbours: int32 [53248], P('atoms'), may hold values from 0 to 2047, as said below
- counts: int32 [2048], P('atoms'), may hold values from 10 to 26, as said below
- species_scale: float32 [60], replicated, may hold values from 0.5 to 2
- species_shift: float32 [60], replicated, may hold values from -4 to 4
- energy_cot: float32 [2048], P('atoms'), may hold values from -5 to 5
- blocks: float32 [512, 64, 128], P('atoms')
- left: float32 [512, 64, 64], P('atoms')
- right: float32 [512, 128, 128], P('atoms')
- left_root: float32 [512, 64, 64], P('atoms')
- right_root: float32 [512, 128, 128], P('atoms')
- late_blocks: float32 [256, 64, 128], P('atoms')
- late_left: float32 [256, 64, 64], P('atoms')
- late_right: float32 [256, 128, 128], P('atoms')
- late_left_root: float32 [256, 64, 64], P('atoms')
- late_right_root: float32 [256, 128, 128], P('atoms')
- out_vector: float32 [128], replicated, may hold values from -0.5 to 0.5
- vector_state: float32 [128], replicated, may hold values from 0.5 to 2
Outputs:
- energies: float32 [2048], P('atoms')
- forces: float32 [3, 2048], P(None, 'atoms')
- block_grads: float32 [512, 64, 128], P('atoms')
- new_left: float32 [512, 64, 64], P('atoms')
- new_right: float32 [512, 128, 128], P('atoms')
- new_blocks: float32 [512, 64, 128], P('atoms')
- late_grads: float32 [256, 64, 128], P('atoms')
- new_late_left: float32 [256, 64, 64], P('atoms')
- new_late_right: float32 [256, 128, 128], P('atoms')
- new_late_blocks: float32 [256, 64, 128], P('atoms')
- vector_grad: float32 [128], replicated
- new_vector_state: float32 [128], replicated
- new_vector: float32 [128], replicated
The draws below stay inside these ranges and needn't reach their ends.
Inputs may be any that keep to these rules, and one draw needn't show every extreme that they name: `positions`: atom g sits at 1.6 times its lattice coordinates plus a displacement of at most 0.3 per coordinate. The 26 slots of an atom name its 26 distinct lattice neighbours (steps of -1, 0 or 1 along each coordinate, periodically, not all 0), in an order of its own. `counts`: in every aligned block of 64 atoms some atom has 26 live edges.
All inputs are finite; a program needn't handle non-finite values.
Results may differ from the reference program's by a relative error of at most 0.019.
The reference program's roundings to bfloat16 on the way count: a program that leaves them out, or rounds other values in their place, can miss the bound.
Values may be sent and summed in bfloat16 or wider, within the bound.
A program may use at most 256 MiB of HBM per device.

```python
import math
import jax
import jax.numpy as jnp
import numpy as np
from jax import lax

SIDE = 8
SLOTS = 26
SPECIES = 60
BESSEL = 8
CHANNELS = 64
LATENT = 1024
FINAL = 128
BLOCK_ROWS = 64
BLOCK_COLS = 128
ATOM_DEV = 64
ATOMS = 2048
FIRST_BLOCKS = 512
SECOND_BLOCKS = 256
N_ATOMS = 32


def offset_table():
    rows_list = []
    for step_x in (-1, 0, 1):
        for step_y in (-1, 0, 1):
            for step_z in (-1, 0, 1):
                if step_x != 0 or step_y != 0 or step_z != 0:
                    rows_list.append([step_x, step_y, step_z])
    return jnp.array(rows_list, dtype=jnp.int32)


def lattice_coords(total):
    atom_ids = jnp.arange(total, dtype=jnp.int32)
    plane = SIDE * SIDE
    return (atom_ids // plane, atom_ids % plane // SIDE, atom_ids % SIDE)


def to_blocks_drawn(matrix):
    rows_count, cols_count = matrix.shape
    shaped = matrix.reshape(rows_count // BLOCK_ROWS, BLOCK_ROWS, cols_count // BLOCK_COLS, BLOCK_COLS)
    return shaped.transpose(0, 2, 1, 3).reshape(-1, BLOCK_ROWS, BLOCK_COLS)


def matrix_blocks(key, specs):
    pieces = []
    for position, spec in enumerate(specs):
        rows_count, cols_count, spread = spec
        matrix = jax.random.normal(jax.random.fold_in(key, position), (rows_count, cols_count), jnp.float32) * spread
        pieces.append(to_blocks_drawn(matrix))
    return jnp.concatenate(pieces, axis=0)


def diagonal_draw(key, amount, width, lower, upper):
    values = jnp.exp(jax.random.uniform(key, (amount, width), jnp.float32, math.log(lower), math.log(upper)))
    return values[:, :, None] * jnp.eye(width, dtype=jnp.float32)[None, :, :]


def root_draw(key, amount, width):
    key_diag, key_off = jax.random.split(key)
    values = jnp.exp(jax.random.uniform(key_diag, (amount, width), jnp.float32, math.log(0.5), math.log(2.0)))
    raw = jax.random.normal(key_off, (amount, width, width), jnp.float32)
    symmetric = (raw + jnp.swapaxes(raw, 1, 2)) * (0.22 / math.sqrt(2.0 * width))
    return symmetric + values[:, :, None] * jnp.eye(width, dtype=jnp.float32)[None, :, :]


def draw_positions(key, part):
    key = jax.random.fold_in(key, 1)
    coord_x, coord_y, coord_z = lattice_coords(ATOMS)
    base = jnp.stack([coord_x, coord_y, coord_z], axis=0).astype(jnp.float32) * 1.6
    return base + jax.random.uniform(key, (3, ATOMS), jnp.float32, -0.3, 0.3)


def draw_neighbours(key, part):
    key = jax.random.fold_in(key, 2)
    scores = jax.random.randint(key, (ATOMS, SLOTS), 0, 1 << 20) * 32 + jnp.arange(SLOTS, dtype=jnp.int32)[None, :]
    order = jnp.argsort(scores, axis=1)
    chosen = offset_table()[order]
    coord_x, coord_y, coord_z = lattice_coords(ATOMS)
    planes = ATOMS // (SIDE * SIDE)
    near_x = (coord_x[:, None] + chosen[:, :, 0]) % planes
    near_y = (coord_y[:, None] + chosen[:, :, 1]) % SIDE
    near_z = (coord_z[:, None] + chosen[:, :, 2]) % SIDE
    return (near_x * SIDE * SIDE + near_y * SIDE + near_z).reshape(ATOMS * SLOTS).astype(jnp.int32)


def draw_counts(key, part):
    key = jax.random.fold_in(key, 3)
    key_base, key_pick = jax.random.split(key)
    base = jax.random.randint(key_base, (ATOMS,), 10, SLOTS + 1)
    pick = jax.random.randint(key_pick, (ATOMS // ATOM_DEV, 1), 0, ATOM_DEV)
    full = (jnp.arange(ATOM_DEV, dtype=jnp.int32)[None, :] == pick).reshape(ATOMS)
    return jnp.where(full, SLOTS, base).astype(jnp.int32)


def draw_blocks(key, part):
    key = jax.random.fold_in(key, 5)
    drawn = 1.0 / math.sqrt(LATENT)
    scalars = 2.0 / math.sqrt(3 * CHANNELS)
    specs = [(BESSEL + 2 * SPECIES, LATENT, 0.6), (LATENT, LATENT, drawn), (LATENT, 2 * CHANNELS, drawn), (LATENT, 2 * CHANNELS, drawn), (LATENT, LATENT, drawn), (3 * CHANNELS, LATENT, scalars), (LATENT, LATENT, drawn), (LATENT, 2 * CHANNELS, drawn), (3 * CHANNELS, LATENT, scalars), (LATENT, FINAL, drawn)]
    return matrix_blocks(key, specs)


def draw_late_blocks(key, part):
    key = jax.random.fold_in(key, 6)
    drawn = 1.0 / math.sqrt(LATENT)
    return matrix_blocks(key, [(LATENT, LATENT, drawn), (LATENT, LATENT, drawn)])


def draw_left(key, part):
    key = jax.random.fold_in(key, 7)
    return diagonal_draw(key, FIRST_BLOCKS, BLOCK_ROWS, 0.5 * BLOCK_COLS, 2.0 * BLOCK_COLS)


def draw_right(key, part):
    key = jax.random.fold_in(key, 8)
    return diagonal_draw(key, FIRST_BLOCKS, BLOCK_COLS, 0.5 * BLOCK_ROWS, 2.0 * BLOCK_ROWS)


def draw_left_root(key, part):
    key = jax.random.fold_in(key, 9)
    return root_draw(key, FIRST_BLOCKS, BLOCK_ROWS)


def draw_right_root(key, part):
    key = jax.random.fold_in(key, 10)
    return root_draw(key, FIRST_BLOCKS, BLOCK_COLS)


def draw_late_left(key, part):
    key = jax.random.fold_in(key, 11)
    return diagonal_draw(key, SECOND_BLOCKS, BLOCK_ROWS, 0.5 * BLOCK_COLS, 2.0 * BLOCK_COLS)


def draw_late_right(key, part):
    key = jax.random.fold_in(key, 12)
    return diagonal_draw(key, SECOND_BLOCKS, BLOCK_COLS, 0.5 * BLOCK_ROWS, 2.0 * BLOCK_ROWS)


def draw_late_left_root(key, part):
    key = jax.random.fold_in(key, 13)
    return root_draw(key, SECOND_BLOCKS, BLOCK_ROWS)


def draw_late_right_root(key, part):
    key = jax.random.fold_in(key, 14)
    return root_draw(key, SECOND_BLOCKS, BLOCK_COLS)


def set_ends(values, rng, smallest, largest):
    place = [jax.random.randint(jax.random.fold_in(rng, axis), (), 0, length) for axis, length in enumerate(values.shape)]
    widest = values.shape.index(max(values.shape))
    beside = place[:widest] + [(place[widest] + 1) % values.shape[widest]] + place[widest + 1:]
    return values.at[tuple(place)].set(smallest).at[tuple(beside)].set(largest)


def steps_of(key, dims, cuts, smallest, high):
    gain = 1.0
    for axis_at, blocks in cuts:
        heights = jax.random.uniform(jax.random.fold_in(jax.random.fold_in(key, 6), axis_at), (blocks,), jnp.float32, smallest / len(cuts), high / len(cuts))
        gain = gain * jnp.repeat(jnp.exp(heights), dims[axis_at] // blocks).reshape((-1,) + (1,) * (len(dims) - 1 - axis_at))
    return gain


def rank_bounds(count, slope):
    portions = [(1 << 20) // math.isqrt(standing ** slope) + 1 for standing in range(1, count + 1)]
    deviation = 1 + sum(portions) // (1 << 30)
    return np.cumsum(np.array([max(1, weight // deviation) for weight in portions]))


def skewed_ids(own_key, shape, number_of, slope):
    table = rank_bounds(number_of, slope)
    ticket = jax.random.randint(jax.random.fold_in(own_key, 1), shape, 0, int(table[number_of - 1]))
    rank = jnp.searchsorted(jnp.asarray(table, jnp.int32), ticket, side="right")
    return jax.random.permutation(jax.random.fold_in(own_key, 2), number_of)[rank].astype(jnp.int32)


def centred(stream_key, dims, scale, bound, cuts=(), kind=jnp.bfloat16):
    drawn = scale * jax.random.normal(stream_key, dims, jnp.float32)
    if cuts:
        drawn = drawn * steps_of(stream_key, dims, cuts, -0.22, 0.18)
    return jnp.clip(drawn, -bound, bound).astype(kind)


def setup_inputs(seed: int = 0) -> dict:
    arg_keys = jax.random.split(jax.random.key(seed), 20)
    return {
        "positions": draw_positions(jax.random.fold_in(arg_keys[19], 71), 0),
        "species": set_ends(skewed_ids(arg_keys[1], (ATOMS,), SPECIES, 2), jax.random.fold_in(arg_keys[1], 3), 0, SPECIES - 1).astype(jnp.int32),
        "neighbours": draw_neighbours(jax.random.fold_in(arg_keys[19], 71), 0),
        "counts": draw_counts(jax.random.fold_in(arg_keys[19], 71), 0),
        "species_scale": jnp.clip(jnp.exp(jax.random.uniform(arg_keys[4], (SPECIES,), jnp.float32, math.log(0.5), math.log(2.0))), 0.5, 2.0),
        "species_shift": centred(arg_keys[5], (SPECIES,), 1.0, 4.0, (), jnp.float32),
        "energy_cot": centred(arg_keys[6], (ATOMS,), 1.0, 5.0, ((0, 32),), jnp.float32),
        "blocks": draw_blocks(jax.random.fold_in(arg_keys[19], 71), 0),
        "left": draw_left(jax.random.fold_in(arg_keys[19], 71), 0),
        "right": draw_right(jax.random.fold_in(arg_keys[19], 71), 0),
        "left_root": draw_left_root(jax.random.fold_in(arg_keys[19], 71), 0),
        "right_root": draw_right_root(jax.random.fold_in(arg_keys[19], 71), 0),
        "late_blocks": draw_late_blocks(jax.random.fold_in(arg_keys[19], 71), 0),
        "late_left": draw_late_left(jax.random.fold_in(arg_keys[19], 71), 0),
        "late_right": draw_late_right(jax.random.fold_in(arg_keys[19], 71), 0),
        "late_left_root": draw_late_left_root(jax.random.fold_in(arg_keys[19], 71), 0),
        "late_right_root": draw_late_right_root(jax.random.fold_in(arg_keys[19], 71), 0),
        "out_vector": centred(arg_keys[17], (FINAL,), FINAL ** -0.5, 0.5, (), jnp.float32),
        "vector_state": jnp.clip(jnp.exp(jax.random.uniform(arg_keys[18], (FINAL,), jnp.float32, math.log(0.5), math.log(2.0))), 0.5, 2.0),
    }


highest = lax.Precision.HIGHEST
spacing = 1.6
cutoff_radius = 4.0
env_scale = 0.25
half_root = 0.7071067811865476
decay_rate = 0.5
learn_rate = 0.02
vector_rate = 0.03
epsilon = 1e-06

@jax.custom_vjp
def low(v):
    return lax.optimization_barrier(v.astype(jnp.bfloat16)).astype(jnp.float32)

@jax.custom_vjp
def low_back(v):
    return v

def low_keep(v):
    return (low(v), None)

def low_pass(kept, grad):
    return (grad,)

def back_keep(v):
    return (v, None)

def back_low(kept, grad):
    return (low(grad),)
low.defvjp(low_keep, low_pass)
low_back.defvjp(back_keep, back_low)

def first_shapes():
    width_in = BESSEL + 2 * SPECIES
    return [(width_in, LATENT), (LATENT, LATENT), (LATENT, 2 * CHANNELS), (LATENT, 2 * CHANNELS), (LATENT, LATENT), (3 * CHANNELS, LATENT), (LATENT, LATENT), (LATENT, 2 * CHANNELS), (3 * CHANNELS, LATENT), (LATENT, FINAL)]

def second_shapes():
    return [(LATENT, LATENT), (LATENT, LATENT)]

def unblock(flat, shapes):
    matrices = []
    start = 0
    for rows_count, cols_count in shapes:
        amount = rows_count // BLOCK_ROWS * (cols_count // BLOCK_COLS)
        piece = flat[start:start + amount]
        piece = piece.reshape(rows_count // BLOCK_ROWS, cols_count // BLOCK_COLS, BLOCK_ROWS, BLOCK_COLS)
        matrices.append(piece.transpose(0, 2, 1, 3).reshape(rows_count, cols_count))
        start = start + amount
    return matrices

def to_blocks(matrix):
    rows_count, cols_count = matrix.shape
    shaped = matrix.reshape(rows_count // BLOCK_ROWS, BLOCK_ROWS, cols_count // BLOCK_COLS, BLOCK_COLS)
    return shaped.transpose(0, 2, 1, 3).reshape(-1, BLOCK_ROWS, BLOCK_COLS)

def harmonics(direction):
    axis_x = direction[:, 0]
    axis_y = direction[:, 1]
    axis_z = direction[:, 2]
    root_three = math.sqrt(3.0)
    root_fifteen = math.sqrt(15.0)
    root_five = math.sqrt(5.0)
    return jnp.stack([jnp.ones_like(axis_x), root_three * axis_x, root_three * axis_y, root_three * axis_z, root_fifteen * axis_x * axis_y, root_fifteen * axis_y * axis_z, 0.5 * root_five * (3.0 * axis_z * axis_z - 1.0), root_fifteen * axis_x * axis_z, 0.5 * root_fifteen * (axis_x * axis_x - axis_y * axis_y)], axis=1)

def geometry(displace):
    length = jnp.sqrt(lax.optimization_barrier(jnp.sum(displace * displace, axis=1)))
    direction = displace / length[:, None]
    scaled = length / cutoff_radius
    envelope = 1.0 - 28.0 * scaled ** 6 + 48.0 * scaled ** 7 - 21.0 * scaled ** 8
    orders = jnp.arange(1, BESSEL + 1).astype(jnp.float32)
    bessel = math.sqrt(2.0 / cutoff_radius) * jnp.sin(orders[None, :] * (math.pi / cutoff_radius) * length[:, None]) / length[:, None]
    return (bessel, envelope, harmonics(direction))

def image_shift(centre, other, total):
    plane = SIDE * SIDE
    periods = (total // plane, SIDE, SIDE)
    centre_coords = (centre // plane, centre % plane // SIDE, centre % SIDE)
    other_coords = (other // plane, other % plane // SIDE, other % SIDE)
    columns = []
    for position in range(3):
        step = (other_coords[position] - centre_coords[position] + 1) % periods[position] - 1
        columns.append((centre_coords[position] + step - other_coords[position]).astype(jnp.float32))
    return jnp.stack(columns, axis=1) * spacing

def embed(weights_out, harm):
    scalar_part = weights_out[:, None, :CHANNELS] * harm[:, 0:1, None]
    higher_part = weights_out[:, None, CHANNELS:] * harm[:, 1:, None]
    return jnp.concatenate([scalar_part, higher_part], axis=1)

def environment(env_weights, harm, edge_mask):
    edges = env_weights.shape[0]
    scalar_part = env_weights[:, None, :CHANNELS]
    higher_part = jnp.broadcast_to(env_weights[:, None, CHANNELS:], (edges, 8, CHANNELS))
    terms = jnp.concatenate([scalar_part, higher_part], axis=1) * (harm * edge_mask[:, None])[:, :, None]
    summed = env_scale * lax.optimization_barrier(jnp.sum(terms.reshape(-1, SLOTS, 9, CHANNELS), axis=1))
    return jnp.repeat(summed, SLOTS, axis=0)

def invariants(feat, env):
    first = feat[:, 0] * env[:, 0]
    second = lax.optimization_barrier(jnp.sum(feat[:, 1:4] * env[:, 1:4], axis=1))
    third = lax.optimization_barrier(jnp.sum(feat[:, 4:] * env[:, 4:], axis=1))
    return jnp.concatenate([first, second, third], axis=1)

def update(feat, env):
    feat_scalar = feat[:, 0:1]
    env_scalar = env[:, 0:1]
    feat_vector = feat[:, 1:4]
    env_vector = env[:, 1:4]
    crossed = jnp.cross(feat_vector, env_vector, axis=1)
    return jnp.concatenate([feat_scalar * env_scalar, feat_vector * env_scalar + feat_scalar * env_vector + crossed, feat[:, 4:] * env_scalar + feat_scalar * env[:, 4:]], axis=1)

def matmul(left_side, right_side):
    return jnp.dot(left_side, right_side, precision=highest)

def shampoo(grads, left, right, left_root, right_root, master):
    mean_square = lax.optimization_barrier(jnp.mean(grads * grads, axis=(1, 2), keepdims=True))
    normed = grads * lax.rsqrt(mean_square + epsilon)
    new_left = decay_rate * left + (1.0 - decay_rate) * jnp.einsum('bij,bkj->bik', normed, normed, precision=highest)
    new_right = decay_rate * right + (1.0 - decay_rate) * jnp.einsum('bji,bjk->bik', normed, normed, precision=highest)
    direction = jnp.einsum('bij,bjk->bik', left_root, normed, precision=highest)
    direction = jnp.einsum('bij,bjk->bik', direction, right_root, precision=highest)
    step_square = lax.optimization_barrier(jnp.mean(direction * direction, axis=(1, 2), keepdims=True))
    return (new_left, new_right, master - learn_rate * direction * lax.rsqrt(step_square + epsilon))

def diagonal_rule(grads, state, vector):
    normed = grads * lax.rsqrt(jnp.mean(grads * grads) + epsilon)
    new_state = decay_rate * state + (1.0 - decay_rate) * normed * normed
    return (new_state, vector - vector_rate * normed * lax.rsqrt(new_state + epsilon))

def block_energy(block_index, neighbour_rows, count_rows, positions, species, species_scale, species_shift, first, second, vector):
    w_input, w_two_body, w_embed, w_env_one, w_lat_one, w_scal_one, w_out_one, w_env_two, w_scal_two, w_final = first
    w_lat_two, w_out_two = second
    atom_ids = block_index * ATOM_DEV + jnp.arange(ATOM_DEV, dtype=jnp.int32)
    centre = jnp.repeat(atom_ids, SLOTS)
    centre_pos = jnp.take(positions, centre, axis=1).T
    near_pos = jnp.take(positions, neighbour_rows, axis=1).T
    bessel, envelope, harm = geometry(near_pos - centre_pos + image_shift(centre, neighbour_rows, ATOMS))
    kinds = jnp.arange(SPECIES, dtype=jnp.int32)
    centre_kind = (jnp.take(species, centre)[:, None] == kinds[None, :]).astype(jnp.float32)
    other_kind = (jnp.take(species, neighbour_rows)[:, None] == kinds[None, :]).astype(jnp.float32)
    edge_mask = (jnp.arange(SLOTS, dtype=jnp.int32)[None, :] < count_rows[:, None]).astype(jnp.float32).reshape(-1)
    inputs = low(jnp.concatenate([bessel, centre_kind, other_kind], axis=1))
    pre_input = low_back(matmul(inputs, w_input))
    hidden = low(jax.nn.silu(pre_input))
    two_body = low_back(matmul(hidden, w_two_body))
    latent_zero = two_body * envelope[:, None]
    low_zero = low(latent_zero)
    feat_zero = embed(low_back(matmul(low_zero, w_embed)), harm)
    env_one = environment(low_back(matmul(low_zero, w_env_one)), harm, edge_mask)
    scal_one = low(invariants(feat_zero, env_one))
    pre_one = low_back(matmul(low_zero, w_lat_one) + matmul(scal_one, w_scal_one))
    act_one = low(jax.nn.silu(pre_one))
    latent_one = (latent_zero + low_back(matmul(act_one, w_out_one))) * half_root
    feat_one = update(feat_zero, env_one)
    low_one = low(latent_one)
    env_two = environment(low_back(matmul(low_one, w_env_two)), harm, edge_mask)
    scal_two = low(invariants(feat_one, env_two))
    pre_two = low_back(matmul(low_one, w_lat_two) + matmul(scal_two, w_scal_two))
    act_two = low(jax.nn.silu(pre_two))
    latent_two = (latent_one + low_back(matmul(act_two, w_out_two))) * half_root
    final_act = jax.nn.silu(low_back(matmul(low(latent_two), w_final)))
    edge_energy = edge_mask * envelope * matmul(final_act, vector)
    atom_sum = lax.optimization_barrier(jnp.sum(edge_energy.reshape(ATOM_DEV, SLOTS), axis=1))
    atom_kind = jnp.take(species, atom_ids)
    return jnp.take(species_scale, atom_kind) * atom_sum + jnp.take(species_shift, atom_kind)

def reference(positions, species, neighbours, counts, species_scale, species_shift, energy_cot, blocks, left, right, left_root, right_root, late_blocks, late_left, late_right, late_left_root, late_right_root, out_vector, vector_state):
    first = tuple(unblock(low(blocks), first_shapes()))
    second = tuple(unblock(low(late_blocks), second_shapes()))

    def energies_of(pos, first_mats, second_mats, vector):

        def one_block(items):
            return block_energy(items[0], items[1], items[2], pos, species, species_scale, species_shift, first_mats, second_mats, vector)
        per_block = lax.map(jax.checkpoint(one_block), (jnp.arange(N_ATOMS, dtype=jnp.int32), neighbours.reshape(N_ATOMS, ATOM_DEV * SLOTS), counts.reshape(N_ATOMS, ATOM_DEV)))
        return per_block.reshape(ATOMS)
    energies, pullback = jax.vjp(energies_of, positions, first, second, out_vector)
    grad_pos, grad_first, grad_second, grad_vector = pullback(energy_cot)
    block_grads = jnp.concatenate([to_blocks(item) for item in grad_first], axis=0)
    late_grads = jnp.concatenate([to_blocks(item) for item in grad_second], axis=0)
    new_left, new_right, new_blocks = shampoo(block_grads, left, right, left_root, right_root, blocks)
    new_late_left, new_late_right, new_late_blocks = shampoo(late_grads, late_left, late_right, late_left_root, late_right_root, late_blocks)
    new_state, new_vector = diagonal_rule(grad_vector, vector_state, out_vector)
    return (energies, -grad_pos, block_grads, new_left, new_right, new_blocks, late_grads, new_late_left, new_late_right, new_late_blocks, grad_vector, new_state, new_vector)
```

```python
import functools
import math

import jax
import jax.numpy as jnp
from jax import lax
from jax.experimental import pallas as pl
from jax.experimental.pallas import tpu as pltpu
from jax.sharding import PartitionSpec as P

SIDE = 8
SLOTS = 26
SPECIES = 60
BESSEL = 8
CHANNELS = 64
LATENT = 1024
FINAL = 128
BLOCK_ROWS = 64
BLOCK_COLS = 128
PLANE = SIDE * SIDE

f32 = jnp.float32
bf16 = jnp.bfloat16
highest = lax.Precision.HIGHEST
spacing = 1.6
cutoff_radius = 4.0
env_scale = 0.25
half_root = 0.7071067811865476
decay_rate = 0.5
learn_rate = 0.02
vector_rate = 0.03
epsilon = 1e-06

LANES = 128
ROWS = SLOTS * PLANE
TILES = ROWS // LANES
KINDS = 64

W_INPUT = (0, 2, 8)
W_TWO = (16, 16, 8)
W_EMBED = (144, 16, 1)
W_ENV_ONE = (160, 16, 1)
W_LAT_ONE = (176, 16, 8)
W_SCAL_ONE = (304, 3, 8)
W_OUT_ONE = (328, 16, 8)
W_ENV_TWO = (456, 16, 1)
W_SCAL_TWO = (472, 3, 8)
W_FINAL = (496, 16, 1)
W_LAT_TWO = (0, 16, 8)
W_OUT_TWO = (128, 16, 8)


def nn(a, b, precision=None):
    return lax.dot_general(
        a, b, (((1,), (0,)), ((), ())), preferred_element_type=f32, precision=precision
    )


def nt(a, b, precision=None):
    return lax.dot_general(
        a, b, (((1,), (1,)), ((), ())), preferred_element_type=f32, precision=precision
    )


def tn(a, b):
    return lax.dot_general(a, b, (((0,), (0,)), ((), ())), preferred_element_type=f32)


def cols_panel(ref, where, n, width=2):
    start, up, across = where
    cols = []
    for b in range(width):
        cols.append(
            jnp.concatenate([ref[start + a * across + n * width + b] for a in range(up)], axis=0)
        )
    return cols[0] if width == 1 else jnp.concatenate(cols, axis=1)


def rows_panel(ref, where, n, height=4):
    start, _, across = where
    rows = []
    for a in range(height):
        base = start + (n * height + a) * across
        row = [ref[base + b] for b in range(across)]
        rows.append(row[0] if across == 1 else jnp.concatenate(row, axis=1))
    return jnp.concatenate(rows, axis=0)


def sigmoid(x):
    return 1.0 / (1.0 + jnp.exp(-x))


def halves(x):
    return x + pltpu.roll(x, PLANE, 1)


def lanes(t):
    return pl.ds(pl.multiple_of(t * LANES, LANES), LANES)


def panel(n, width=256):
    return pl.ds(pl.multiple_of(n * width, width), width)


CHUNKS = 2
CHUNK = ROWS // CHUNKS


def loop_panels(body):
    def step(n):
        for c in range(CHUNKS):
            body(n, slice(c * CHUNK, (c + 1) * CHUNK))

    loop(4, step)


def loop(count, body):
    def step(i, carry):
        body(i)
        return carry

    lax.fori_loop(0, count, step, 0)


def parts(x):
    a = x.astype(bf16)
    rest = x - a.astype(f32)
    b = rest.astype(bf16)
    c = (rest - b.astype(f32)).astype(bf16)
    return a, b, c


def network(
    idx_ref,
    ext_ref,
    own_ref,
    tab_ref,
    vec_ref,
    first_ref,
    late_ref,
    energy_ref,
    centre_ref,
    spread_ref,
    vector_ref,
    first_out,
    late_out,
    hot,
    z_t,
    z_r,
    geo,
    yrow,
    env_b,
    edge_b,
    wee_t,
    we2_t,
    ee_t,
    en2_t,
    s1_t,
    s2_t,
    gam,
    dlt,
    coef,
    ds_t,
    de_t,
    dy,
    dg,
    dw_t,
    dw_r,
    dpf,
    den,
    lat,
    hid,
    low0,
    act1,
    sl1,
    low1,
    act2,
    sl2,
    low2,
    stage,
    sem,
):
    s_r = dw_r
    fact = den

    idx = idx_ref[...]
    hot[...] = (lax.broadcasted_iota(jnp.int32, (3 * PLANE, ROWS), 0) == idx).astype(f32).astype(bf16)
    ga, gb, gc = parts(ext_ref[...])
    got = nn(ga, hot[...]) + nn(gb, hot[...]) + nn(gc, hot[...])
    own = own_ref[...]
    mine = jnp.concatenate([own] * TILES, axis=1)
    lane = lax.broadcasted_iota(jnp.int32, (1, ROWS), 1)
    slot = lane >> 6
    atom = lane & (PLANE - 1)

    def wrapped(step):
        return jnp.where(step > 1.5, -8.0, jnp.where(step < -1.5, 8.0, 0.0)) * spacing

    disp = [
        got[0:1] - mine[0:1],
        got[1:2] - mine[1:2] + wrapped(got[4:5] - (atom >> 3).astype(f32)),
        got[2:3] - mine[2:3] + wrapped(got[5:6] - (atom & (SIDE - 1)).astype(f32)),
    ]
    length = jnp.sqrt(disp[0] * disp[0] + disp[1] * disp[1] + disp[2] * disp[2])
    inverse = 1.0 / length
    unit = [disp[0] * inverse, disp[1] * inverse, disp[2] * inverse]
    angle = length * (math.pi / cutoff_radius)
    sin_k = [jnp.sin(angle)]
    cos_k = [jnp.cos(angle)]
    sin_k.append(2.0 * cos_k[0] * sin_k[0])
    cos_k.append(2.0 * cos_k[0] * cos_k[0] - 1.0)
    for k in range(2, BESSEL):
        sin_k.append(2.0 * cos_k[0] * sin_k[k - 1] - sin_k[k - 2])
        cos_k.append(2.0 * cos_k[0] * cos_k[k - 1] - cos_k[k - 2])
    sines = jnp.concatenate(sin_k, axis=0)
    cosines = jnp.concatenate(cos_k, axis=0)
    bessel = (math.sqrt(2.0 / cutoff_radius) * inverse) * sines
    scaled = length * (1.0 / cutoff_radius)
    t2 = scaled * scaled
    t4 = t2 * t2
    t5 = t4 * scaled
    t6 = t4 * t2
    envelope = 1.0 - 28.0 * t6 + 48.0 * (t6 * scaled) - 21.0 * (t4 * t4)
    denvelope = (-168.0 * t5 + 336.0 * t6 - 168.0 * (t6 * scaled)) * (1.0 / cutoff_radius)
    live = jnp.where(slot.astype(f32) < mine[4:5], 1.0, 0.0)

    kind = lax.broadcasted_iota(jnp.int32, (KINDS, LANES), 0).astype(f32)
    is_kind = kind == own[3:4]
    scale = jnp.sum(jnp.where(is_kind, tab_ref[:, 0:1], 0.0), axis=0, keepdims=True)
    shift = jnp.sum(jnp.where(is_kind, tab_ref[:, 1:2], 0.0), axis=0, keepdims=True)
    cot = jnp.concatenate([own[5:6] * scale] * TILES, axis=1) * live
    weight = cot * envelope

    root3 = math.sqrt(3.0)
    root15 = math.sqrt(15.0)
    root5 = math.sqrt(5.0)
    ux, uy, uz = unit
    yrow[0:8] = jnp.concatenate(
        [
            root3 * ux,
            root3 * uy,
            root3 * uz,
            root15 * ux * uy,
            root15 * uy * uz,
            0.5 * root5 * (3.0 * uz * uz - 1.0),
            root15 * ux * uz,
            0.5 * root15 * (ux * ux - uy * uy),
        ],
        axis=0,
    )
    yrow[8:16] = yrow[0:8] * (live * env_scale)
    yrow[16:17] = live * env_scale
    geo[0:8] = jnp.concatenate([ux, uy, uz, inverse, envelope, denvelope, live, cot], axis=0)
    geo[8:16] = math.sqrt(2.0 / cutoff_radius) * (
        (math.pi / cutoff_radius)
        * lax.broadcasted_iota(jnp.int32, (BESSEL, ROWS), 0).astype(f32)
        * cosines
        + (math.pi / cutoff_radius) * cosines
        - sines * inverse
    ) * inverse

    def one_hots(t):
        row = lax.broadcasted_iota(jnp.int32, (LANES, LANES), 0).astype(f32)
        here = jnp.where(row == own[3:4] + float(BESSEL), 1.0, 0.0)
        there = jnp.where(row == kinds_near[t] + float(BESSEL + SPECIES), 1.0, 0.0)
        return here + there

    kinds_near = [got[3:4, t * LANES : (t + 1) * LANES] for t in range(TILES)]
    for t in range(TILES):
        at = slice(t * LANES, (t + 1) * LANES)
        column = jnp.concatenate([bessel[:, at], one_hots(t)[BESSEL:]], axis=0)
        z_t[:, at] = column.astype(bf16)
        z_r[at, :] = column.T.astype(bf16)
        env_b[at, :] = jnp.broadcast_to(envelope[:, at], (LANES, LANES)).T
        edge_b[at, :] = jnp.broadcast_to(weight[:, at], (LANES, LANES)).T

    wee_t[0:128, :] = cols_panel(first_ref, W_EMBED, 0, 1).T
    wee_t[128:256, :] = cols_panel(first_ref, W_ENV_ONE, 0, 1).T
    we2_t[...] = cols_panel(first_ref, W_ENV_TWO, 0, 1).T

    def twice(x):
        return jnp.concatenate([x, x], axis=1)

    def in_body(n, r):
        pre = nn(z_r[r], cols_panel(first_ref, W_INPUT, n))
        hid[r, panel(n)] = (pre * sigmoid(pre)).astype(bf16)

    loop_panels(in_body)

    def two_body(n, r):
        zero = nn(hid[r], cols_panel(first_ref, W_TWO, n)) * twice(env_b[r])
        lat[r, panel(n)] = zero
        low0[r, panel(n)] = zero.astype(bf16)

    loop_panels(two_body)

    def transposed_product(out, weights, right, width=256):
        at = 0
        while at < ROWS:
            end = min(at + width, ROWS)
            out[:, at:end] = nt(weights, right[at:end, :])
            at = end

    transposed_product(ee_t, wee_t[...], low0)

    def environment(out, v0_ref, v0_at, v1_at):
        v0 = v0_ref[v0_at : v0_at + CHANNELS, :]
        v1 = v0_ref[v1_at : v1_at + CHANNELS, :]
        for m in range(9):
            total = None
            for t in range(TILES):
                at = slice(t * LANES, (t + 1) * LANES)
                if m == 0:
                    term = v0[:, at] * yrow[16:17, at]
                else:
                    term = v1[:, at] * yrow[7 + m : 8 + m, at]
                total = term if total is None else total + term
            out[m] = halves(total)

    def put_scalars(t, s_t, rows):
        s_t[:, lanes(t)] = jnp.concatenate(rows, axis=0).astype(bf16)
        filled = jnp.concatenate(rows + [jnp.zeros_like(rows[0])], axis=0)
        flipped = filled.T.astype(bf16)
        s_r[lanes(t), :] = flipped

    def weighted(y, first, count, source, offset):
        total = None
        for m in range(count):
            term = y[first + m : first + m + 1] * source[offset + m]
            total = term if total is None else total + term
        return total

    environment(gam, ee_t, 128, 192)

    def scalars_one(t):
        e0 = ee_t[0:64, lanes(t)]
        e1 = ee_t[64:128, lanes(t)]
        y = yrow[0:8, lanes(t)]
        put_scalars(
            t,
            s1_t,
            [e0 * gam[0], e1 * weighted(y, 0, 3, gam, 1), e1 * weighted(y, 3, 5, gam, 4)],
        )

    loop(TILES, scalars_one)

    def pre_one(n, r):
        pre = nn(low0[r], cols_panel(first_ref, W_LAT_ONE, n)) + nn(
            s_r[r, : 3 * CHANNELS], cols_panel(first_ref, W_SCAL_ONE, n)
        )
        sig = sigmoid(pre)
        act = pre * sig
        act1[r, panel(n)] = act.astype(bf16)
        sl1[r, panel(n)] = (sig + act * (1.0 - sig)).astype(bf16)

    loop_panels(pre_one)

    def out_one(n, r):
        new = (lat[r, panel(n)] + nn(act1[r], cols_panel(first_ref, W_OUT_ONE, n))) * half_root
        lat[r, panel(n)] = new
        low1[r, panel(n)] = new.astype(bf16)

    loop_panels(out_one)
    transposed_product(en2_t, we2_t[...], low1)
    environment(dlt, en2_t, 0, 64)

    g0 = gam[0]
    coef[0] = g0 * dlt[0]
    for m in range(3):
        a, b = 1 + (m + 1) % 3, 1 + (m + 2) % 3
        coef[1 + m] = g0 * dlt[1 + m] + (gam[a] * dlt[b] - gam[b] * dlt[a])
    coef[9] = gam[1] * dlt[1] + gam[2] * dlt[2] + gam[3] * dlt[3]
    second = None
    for m in range(4, 9):
        coef[m] = g0 * dlt[m]
        term = gam[m] * dlt[m]
        second = term if second is None else second + term
    coef[10] = second

    def scalars_two(t):
        e0 = ee_t[0:64, lanes(t)]
        e1 = ee_t[64:128, lanes(t)]
        y = yrow[0:8, lanes(t)]
        put_scalars(
            t,
            s2_t,
            [
                e0 * coef[0],
                e1 * weighted(y, 0, 3, coef, 1) + e0 * coef[9],
                e1 * weighted(y, 3, 5, coef, 4) + e0 * coef[10],
            ],
        )

    loop(TILES, scalars_two)

    def pre_two(n, r):
        pre = nn(low1[r], cols_panel(late_ref, W_LAT_TWO, n)) + nn(
            s_r[r, : 3 * CHANNELS], cols_panel(first_ref, W_SCAL_TWO, n)
        )
        sig = sigmoid(pre)
        act = pre * sig
        act2[r, panel(n)] = act.astype(bf16)
        sl2[r, panel(n)] = (sig + act * (1.0 - sig)).astype(bf16)

    loop_panels(pre_two)

    def out_two(n, r):
        new = (lat[r, panel(n)] + nn(act2[r], cols_panel(late_ref, W_OUT_TWO, n))) * half_root
        low2[r, panel(n)] = new.astype(bf16)

    loop_panels(out_two)

    pre = nn(low2[...], cols_panel(first_ref, W_FINAL, 0, 1))
    sig = sigmoid(pre)
    final_act = pre * sig
    fact[...] = final_act
    vec = vec_ref[...]
    dpf[...] = (edge_b[...] * vec[0:1] * (sig + final_act * (1.0 - sig))).astype(bf16)
    value = nt(vec, fact[...], highest)[0:1]
    geo_live = geo[6:7]
    geo_env = geo[4:5]
    geo_cot = geo[7:8]
    edge_energy = geo_live * geo_env * value
    summed = None
    for t in range(TILES):
        term = edge_energy[:, t * LANES : (t + 1) * LANES]
        summed = term if summed is None else summed + term
    energy_ref[...] = scale * halves(summed) + shift
    all_weights = jnp.broadcast_to(geo_cot * geo_env, (8, ROWS))
    vector_ref[...] = nn(all_weights, fact[...], highest)
    geo[16:17] = geo_cot * value

    def put(out, where, count, sem_at):
        copy = pltpu.make_async_copy(
            stage.at[sem_at, pl.ds(0, count)], out.at[pl.ds(where, count)], sem.at[sem_at]
        )
        copy.start()
        return copy

    def store_blocks(slot_at, grad, up, across):
        for a in range(up):
            for b in range(across):
                stage[slot_at, a * across + b] = grad[
                    a * BLOCK_ROWS : (a + 1) * BLOCK_ROWS, b * BLOCK_COLS : (b + 1) * BLOCK_COLS
                ].astype(bf16)

    def big_grad(out, where, left, right):
        def body(i):
            grad = tn(left[:, panel(i)], right[...])
            store_blocks(0, grad, 4, 8)
            put(out, where[0] + i * 32, 32, 0).wait()

        loop(4, body)

    def wide_grad(out, where, left, right):
        grad = nn(left[...], right[...])
        store_blocks(0, grad, where[1], where[2])
        put(out, where[0], where[1] * where[2], 0).wait()

    def narrow_grad(out, where, left, right):
        grad = nn(left, right[...]).T
        store_blocks(0, grad, where[1], 1)
        put(out, where[0], where[1], 0).wait()

    narrow_grad(first_out, W_FINAL, dpf[...].T, low2)

    def back_final(n, r):
        grad = nt(dpf[r], rows_panel(first_ref, W_FINAL, n)) * half_root
        lat[r, panel(n)] = grad
        low2[r, panel(n)] = grad.astype(bf16)

    loop_panels(back_final)
    big_grad(late_out, W_OUT_TWO, act2, low2)

    def back_out_two(n, r):
        grad = nt(low2[r], rows_panel(late_ref, W_OUT_TWO, n))
        sl2[r, panel(n)] = (grad * sl2[r, panel(n)].astype(f32)).astype(bf16)

    loop_panels(back_out_two)
    transposed_product(ds_t, rows_panel(first_ref, W_SCAL_TWO, 0, 3), sl2)
    wide_grad(first_out, W_SCAL_TWO, s2_t, sl2)
    big_grad(late_out, W_LAT_TWO, low1, sl2)

    dg[...] = jnp.zeros_like(dg)

    def tensors_two(t):
        e0 = ee_t[0:64, lanes(t)]
        e1 = ee_t[64:128, lanes(t)]
        y = yrow[0:8, lanes(t)]
        r0 = ds_t[0:64, lanes(t)]
        r1 = ds_t[64:128, lanes(t)]
        r2 = ds_t[128:192, lanes(t)]
        de_t[0:64, lanes(t)] = r0 * coef[0] + r1 * coef[9] + r2 * coef[10]
        de_t[64:128, lanes(t)] = r1 * weighted(y, 0, 3, coef, 1) + r2 * weighted(y, 3, 5, coef, 4)
        p1 = r1 * e1
        p2 = r2 * e1
        rows = []
        for m in range(8):
            p = p1 if m < 3 else p2
            rows.append(jnp.sum(p * coef[1 + m], axis=0, keepdims=True))
            dg[1 + m] += p * y[m : m + 1]
        dy[:, lanes(t)] = jnp.concatenate(rows, axis=0)
        dg[0] += r0 * e0
        dg[9] += r1 * e0
        dg[10] += r2 * e0

    loop(TILES, tensors_two)
    total = [halves(dg[m]) for m in range(11)]
    g0 = gam[0]
    d0 = dlt[0]
    new_g0 = total[0] * d0
    for m in range(1, 9):
        new_g0 = new_g0 + total[m] * dlt[m]
    dlt_grads = [total[0] * g0]
    gam_grads = [new_g0]
    for m in range(3):
        a, b = 1 + (m + 1) % 3, 1 + (m + 2) % 3
        dlt_grads.append(
            total[1 + m] * g0 + total[9] * gam[1 + m] + (total[a] * gam[b] - total[b] * gam[a])
        )
        gam_grads.append(total[9] * dlt[1 + m] + (dlt[a] * total[b] - dlt[b] * total[a]))
    for m in range(4, 9):
        dlt_grads.append(total[m] * g0 + total[10] * gam[m])
        gam_grads.append(total[10] * dlt[m])
    for m in range(9):
        dlt[m] = dlt_grads[m]
        dg[m] = gam_grads[m]

    def environment_back(t, grads, source, v1_at, at):
        y4 = yrow[8:16, lanes(t)]
        l4 = yrow[16:17, lanes(t)]
        v1 = source[v1_at : v1_at + 64, lanes(t)]
        low = l4 * grads[0]
        high = weighted(y4, 0, 8, grads, 1)
        both = jnp.concatenate([low, high], axis=0)
        dw_t[at : at + 128, lanes(t)] = both.astype(bf16)
        dw_r[lanes(t), at : at + 128] = both.T.astype(bf16)
        v1 = v1 * l4
        rows = [jnp.sum(v1 * grads[1 + m], axis=0, keepdims=True) for m in range(8)]
        dy[:, lanes(t)] += jnp.concatenate(rows, axis=0)

    loop(TILES, lambda t: environment_back(t, dlt, en2_t, 64, 128))
    narrow_grad(first_out, W_ENV_TWO, dw_t[128:256, :], low1)

    def back_lat_two(n, r):
        grad = (
            lat[r, panel(n)]
            + nt(sl2[r], rows_panel(late_ref, W_LAT_TWO, n))
            + nt(dw_r[r, 128:256], rows_panel(first_ref, W_ENV_TWO, n))
        ) * half_root
        lat[r, panel(n)] = grad
        act2[r, panel(n)] = grad.astype(bf16)

    loop_panels(back_lat_two)
    big_grad(first_out, W_OUT_ONE, act1, act2)

    def back_out_one(n, r):
        grad = nt(act2[r], rows_panel(first_ref, W_OUT_ONE, n))
        sl1[r, panel(n)] = (grad * sl1[r, panel(n)].astype(f32)).astype(bf16)

    loop_panels(back_out_one)
    transposed_product(ds_t, rows_panel(first_ref, W_SCAL_ONE, 0, 3), sl1)
    wide_grad(first_out, W_SCAL_ONE, s1_t, sl1)
    big_grad(first_out, W_LAT_ONE, low0, sl1)

    def tensors_one(t):
        e0 = ee_t[0:64, lanes(t)]
        e1 = ee_t[64:128, lanes(t)]
        y = yrow[0:8, lanes(t)]
        r0 = ds_t[0:64, lanes(t)]
        r1 = ds_t[64:128, lanes(t)]
        r2 = ds_t[128:192, lanes(t)]
        low = de_t[0:64, lanes(t)] + r0 * gam[0]
        high = (
            de_t[64:128, lanes(t)]
            + r1 * weighted(y, 0, 3, gam, 1)
            + r2 * weighted(y, 3, 5, gam, 4)
        )
        both = jnp.concatenate([low, high], axis=0)
        dw_t[0:128, lanes(t)] = both.astype(bf16)
        dw_r[lanes(t), 0:128] = both.T.astype(bf16)
        p1 = r1 * e1
        p2 = r2 * e1
        rows = []
        for m in range(8):
            p = p1 if m < 3 else p2
            rows.append(jnp.sum(p * gam[1 + m], axis=0, keepdims=True))
            coef[1 + m] += p * y[m : m + 1]
        dy[:, lanes(t)] += jnp.concatenate(rows, axis=0)
        coef[0] += r0 * e0

    for m in range(9):
        coef[m] = jnp.zeros((CHANNELS, LANES), f32)
    loop(TILES, tensors_one)
    for m in range(9):
        dg[m] = dg[m] + halves(coef[m])
    loop(TILES, lambda t: environment_back(t, dg, ee_t, 192, 128))
    narrow_grad(first_out, W_EMBED, dw_t[0:128, :], low0)
    narrow_grad(first_out, W_ENV_ONE, dw_t[128:256, :], low0)

    den[...] = jnp.zeros_like(den)

    def back_lat_one(n, r):
        both = jnp.concatenate(
            [rows_panel(first_ref, W_EMBED, n), rows_panel(first_ref, W_ENV_ONE, n)], axis=1
        )
        grad = (
            lat[r, panel(n)]
            + nt(sl1[r], rows_panel(first_ref, W_LAT_ONE, n))
            + nt(dw_r[r], both)
        )
        low1[r, panel(n)] = (grad * twice(env_b[r])).astype(bf16)
        part = grad * low0[r, panel(n)].astype(f32)
        den[r] += part[:, :LANES] + part[:, LANES:]

    loop_panels(back_lat_one)
    big_grad(first_out, W_TWO, hid, low1)

    def back_two(n, r):
        grad = nt(low1[r], rows_panel(first_ref, W_TWO, n))
        pre = nn(z_r[r], cols_panel(first_ref, W_INPUT, n))
        sig = sigmoid(pre)
        act1[r, panel(n)] = (grad * (sig + pre * sig * (1.0 - sig))).astype(bf16)

    loop_panels(back_two)
    wide_grad(first_out, W_INPUT, z_t, act1)

    transposed_product(ds_t.at[0:64], rows_panel(first_ref, W_INPUT, 0, 1), act1)
    dbessel = ds_t[0:8, :]
    through = nt(jnp.ones((8, LANES), f32), den[...], highest)[0:1]
    ux, uy, uz = geo[0:1], geo[1:2], geo[2:3]
    inverse = geo[3:4]
    envelope = geo[4:5]
    denv = geo[16:17] + through / envelope
    dlength = jnp.sum(dbessel * geo[8:16], axis=0, keepdims=True) + denv * geo[5:6]
    g = [dy[m : m + 1, :] for m in range(8)]
    dux = root3 * g[0] + root15 * (uy * g[3] + uz * g[6] + ux * g[7])
    duy = root3 * g[1] + root15 * (ux * g[3] + uz * g[4] - uy * g[7])
    duz = root3 * g[2] + root15 * (uy * g[4] + ux * g[6]) + (3.0 * root5) * uz * g[5]
    along = dlength - (ux * dux + uy * duy + uz * duz) * inverse
    near = jnp.concatenate(
        [
            dux * inverse + ux * along,
            duy * inverse + uy * along,
            duz * inverse + uz * along,
            jnp.zeros((5, ROWS), f32),
        ],
        axis=0,
    )
    summed = None
    for t in range(TILES):
        term = near[:, t * LANES : (t + 1) * LANES]
        summed = term if summed is None else summed + term
    centre_ref[...] = halves(summed)
    na, nb, nc = parts(near)
    spread_ref[...] = nt(na, hot[...]) + nt(nb, hot[...]) + nt(nc, hot[...])


def run_network(idx, ext, own, tab, vec, first, late):
    S = jax.ShapeDtypeStruct
    wide = pltpu.VMEM((ROWS, LATENT), bf16)
    scratch = [
        pltpu.VMEM((3 * PLANE, ROWS), bf16),
        pltpu.VMEM((LANES, ROWS), bf16),
        pltpu.VMEM((ROWS, LANES), bf16),
        pltpu.VMEM((24, ROWS), f32),
        pltpu.VMEM((24, ROWS), f32),
        pltpu.VMEM((ROWS, LANES), f32),
        pltpu.VMEM((ROWS, LANES), f32),
        pltpu.VMEM((256, LATENT), bf16),
        pltpu.VMEM((128, LATENT), bf16),
        pltpu.VMEM((256, ROWS), f32),
        pltpu.VMEM((128, ROWS), f32),
        pltpu.VMEM((192, ROWS), bf16),
        pltpu.VMEM((192, ROWS), bf16),
        pltpu.VMEM((9, CHANNELS, LANES), f32),
        pltpu.VMEM((9, CHANNELS, LANES), f32),
        pltpu.VMEM((11, CHANNELS, LANES), f32),
        pltpu.VMEM((192, ROWS), f32),
        pltpu.VMEM((128, ROWS), f32),
        pltpu.VMEM((8, ROWS), f32),
        pltpu.VMEM((11, CHANNELS, LANES), f32),
        pltpu.VMEM((256, ROWS), bf16),
        pltpu.VMEM((ROWS, 256), bf16),
        pltpu.VMEM((ROWS, LANES), bf16),
        pltpu.VMEM((ROWS, LANES), f32),
        pltpu.VMEM((ROWS, LATENT), f32),
        wide,
        wide,
        wide,
        wide,
        wide,
        wide,
        wide,
        wide,
        pltpu.VMEM((1, 32, BLOCK_ROWS, BLOCK_COLS), bf16),
        pltpu.SemaphoreType.DMA((1,)),
    ]
    vmem = pl.BlockSpec(memory_space=pltpu.VMEM)
    hbm = pl.BlockSpec(memory_space=pl.ANY)
    return pl.pallas_call(
        network,
        out_shape=[
            S((1, LANES), f32),
            S((8, LANES), f32),
            S((8, 3 * PLANE), f32),
            S((8, LANES), f32),
            S(first.shape, bf16),
            S(late.shape, bf16),
        ],
        in_specs=[vmem] * 7,
        out_specs=[vmem] * 4 + [hbm] * 2,
        scratch_shapes=scratch,
        compiler_params=pltpu.CompilerParams(vmem_limit_bytes=63 << 20),
        name="network",
    )(idx, ext, own, tab, vec, first, late)


def shampoo(grads, left, right, left_root, right_root, master):
    mean_square = jnp.mean(grads * grads, axis=(1, 2), keepdims=True)
    normed = grads * lax.rsqrt(mean_square + epsilon)
    new_left = decay_rate * left + (1.0 - decay_rate) * jnp.einsum(
        "bij,bkj->bik", normed, normed, precision=highest
    )
    new_right = decay_rate * right + (1.0 - decay_rate) * jnp.einsum(
        "bji,bjk->bik", normed, normed, precision=highest
    )
    direction = jnp.einsum("bij,bjk->bik", left_root, normed, precision=highest)
    direction = jnp.einsum("bij,bjk->bik", direction, right_root, precision=highest)
    step_square = jnp.mean(direction * direction, axis=(1, 2), keepdims=True)
    return (new_left, new_right, master - learn_rate * direction * lax.rsqrt(step_square + epsilon))


def diagonal_rule(grads, state, vector):
    normed = grads * lax.rsqrt(jnp.mean(grads * grads) + epsilon)
    new_state = decay_rate * state + (1.0 - decay_rate) * normed * normed
    return (new_state, vector - vector_rate * normed * lax.rsqrt(new_state + epsilon))


def shifted(block, axis, distance):
    devices = range(lax.axis_size(axis))
    route = [((i - distance) % len(devices), i) for i in devices]
    return lax.ppermute(block, axis, route)


def local(
    positions,
    species,
    neighbours,
    counts,
    species_scale,
    species_shift,
    energy_cot,
    blocks,
    left,
    right,
    left_root,
    right_root,
    late_blocks,
    late_left,
    late_right,
    late_left_root,
    late_right_root,
    out_vector,
    vector_state,
):
    devices = lax.axis_size("atoms")
    me = lax.axis_index("atoms")
    total_atoms = PLANE * devices
    first_atom = me * PLANE
    whole_first = lax.all_gather(blocks.astype(bf16), "atoms", axis=0, tiled=True)
    whole_late = lax.all_gather(late_blocks.astype(bf16), "atoms", axis=0, tiled=True)

    own = jnp.concatenate(
        [
            positions,
            species.astype(f32)[None],
            counts.astype(f32)[None],
            energy_cot[None],
            jnp.zeros((2, PLANE), f32),
        ],
        axis=0,
    )
    before = shifted(own, "atoms", 1)
    after = shifted(own, "atoms", -1)
    edge = spacing * devices
    before = before.at[0].add(jnp.where(me == 0, -edge, 0.0))
    after = after.at[0].add(jnp.where(me == devices - 1, edge, 0.0))
    ids = jnp.arange(3 * PLANE, dtype=jnp.int32) % PLANE
    ext = jnp.concatenate([before, own, after], axis=1)
    ext = jnp.concatenate(
        [
            ext[:4],
            (ids // SIDE).astype(f32)[None],
            (ids % SIDE).astype(f32)[None],
            jnp.zeros((2, 3 * PLANE), f32),
        ],
        axis=0,
    )
    idx = (neighbours - first_atom + PLANE) % total_atoms
    idx = idx.reshape(PLANE, SLOTS).T.reshape(1, ROWS)
    own_twice = jnp.concatenate([own, own], axis=1)
    tab = jnp.pad(jnp.stack([species_scale, species_shift], axis=1), ((0, KINDS - SPECIES), (0, 126)))
    vec = jnp.broadcast_to(out_vector[None], (8, FINAL))
    energy, centre, spread, vector_part, first_grads, late_grads = run_network(
        idx, ext, own_twice, tab, vec, whole_first, whole_late
    )
    energies = energy[0, :PLANE]
    from_next = shifted(spread[:3, :PLANE], "atoms", -1)
    from_prev = shifted(spread[:3, 2 * PLANE :], "atoms", 1)
    forces = centre[:3, :PLANE] - spread[:3, PLANE : 2 * PLANE] - from_next - from_prev
    first_reduced = lax.psum_scatter(first_grads, "atoms", scatter_dimension=0, tiled=True).astype(f32)
    late_reduced = lax.psum_scatter(late_grads, "atoms", scatter_dimension=0, tiled=True).astype(f32)
    vector_grad = lax.psum(vector_part[0], "atoms")
    new_left, new_right, new_blocks = shampoo(
        first_reduced, left, right, left_root, right_root, blocks
    )
    new_late_left, new_late_right, new_late_blocks = shampoo(
        late_reduced, late_left, late_right, late_left_root, late_right_root, late_blocks
    )
    new_state, new_vector = diagonal_rule(vector_grad, vector_state, out_vector)
    return (
        energies,
        forces,
        first_reduced,
        new_left,
        new_right,
        new_blocks,
        late_reduced,
        new_late_left,
        new_late_right,
        new_late_blocks,
        vector_grad,
        new_state,
        new_vector,
    )


def solution(mesh):
    row = P("atoms")
    block = P("atoms", None, None)
    placed = (
        (P(None, "atoms"), row, row, row, P(), P(), row)
        + (block,) * 10
        + (P(), P())
    )
    return jax.shard_map(
        local,
        mesh=mesh,
        in_specs=placed,
        out_specs=(row, P(None, "atoms")) + (block,) * 8 + (P(), P(), P()),
        check_vma=False,
    )
```

```python
import functools
import math

import jax
import jax.numpy as jnp
from jax import lax
from jax.experimental import pallas as pl
from jax.experimental.pallas import tpu as pltpu
from jax.sharding import PartitionSpec as P

SIDE = 8
SLOTS = 26
SPECIES = 60
BESSEL = 8
CHANNELS = 64
LATENT = 1024
FINAL = 128
BLOCK_ROWS = 64
BLOCK_COLS = 128
PLANE = SIDE * SIDE

f32 = jnp.float32
bf16 = jnp.bfloat16
highest = lax.Precision.HIGHEST
spacing = 1.6
cutoff_radius = 4.0
env_scale = 0.25
half_root = 0.7071067811865476
decay_rate = 0.5
learn_rate = 0.02
vector_rate = 0.03
epsilon = 1e-06

LANES = 128
ROWS = SLOTS * PLANE
TILES = ROWS // LANES
KINDS = 64

PANEL = 8
WIDE = PANEL * BLOCK_COLS
W_INPUT = (0, 128)
W_TWO = (128, 1024)
W_EMBED = (1152, 128)
W_ENV_ONE = (1280, 128)
W_LAT_ONE = (1408, 1024)
W_SCAL_ONE = (2432, 192)
W_OUT_ONE = (2624, 1024)
W_ENV_TWO = (3648, 128)
W_SCAL_TWO = (3776, 192)
W_FINAL = (3968, 128)
W_LAT_TWO = (0, 1024)
W_OUT_TWO = (1024, 1024)

MESH = pl.DeviceIdType.MESH


def nn(a, b, precision=None):
    return lax.dot_general(
        a, b, (((1,), (0,)), ((), ())), preferred_element_type=f32, precision=precision
    )


def nt(a, b, precision=None):
    return lax.dot_general(
        a, b, (((1,), (1,)), ((), ())), preferred_element_type=f32, precision=precision
    )


def tn(a, b):
    return lax.dot_general(a, b, (((0,), (0,)), ((), ())), preferred_element_type=f32)


def cols_panel(ref, where, n):
    return ref[where[0] : where[0] + where[1], panel(n)]


def rows_panel(ref, where, n):
    return ref[pl.ds(pl.multiple_of(where[0] + n * 256, 64), 256), :]


def narrow(ref, where):
    pieces = []
    for j in range(LATENT // BLOCK_ROWS):
        row = where[0] + j // PANEL * BLOCK_ROWS
        col = j % PANEL * BLOCK_COLS
        pieces.append(ref[row : row + BLOCK_ROWS, col : col + BLOCK_COLS])
    return jnp.concatenate(pieces, axis=0)


def narrow_panel(ref, where, n):
    row = pl.multiple_of(where[0] + n // 2 * BLOCK_ROWS, BLOCK_ROWS)
    col = pl.multiple_of(n % 2 * 512, 512)
    part = ref[pl.ds(row, BLOCK_ROWS), pl.ds(col, 512)]
    return jnp.concatenate([part[:, b * 128 : (b + 1) * 128] for b in range(4)], axis=0)


def sigmoid(x):
    return 1.0 / (1.0 + jnp.exp(-x))


def halves(x):
    return x + pltpu.roll(x, PLANE, 1)


def lanes(t):
    return pl.ds(pl.multiple_of(t * LANES, LANES), LANES)


def panel(n, width=256):
    return pl.ds(pl.multiple_of(n * width, width), width)


CHUNKS = 2
CHUNK = ROWS // CHUNKS


def loop_panels(body):
    def step(n):
        for c in range(CHUNKS):
            body(n, slice(c * CHUNK, (c + 1) * CHUNK))

    loop(4, step)


def loop(count, body):
    def step(i, carry):
        body(i)
        return carry

    lax.fori_loop(0, count, step, 0)


def parts(x):
    a = x.astype(bf16)
    rest = x - a.astype(f32)
    b = rest.astype(bf16)
    c = (rest - b.astype(f32)).astype(bf16)
    return a, b, c


class Place:
    def __init__(self, devices):
        side = math.isqrt(devices // 8)
        self.devices = devices
        self.sizes = (4, side, side)
        me = lax.axis_index("atoms")
        core = me % 2
        chip = me // 2
        last = chip % side
        middle = chip // side % side
        self.me = me
        self.core = core
        self.pos = (
            chip // (side * side),
            last + core * (middle - last),
            middle + core * (last - middle),
        )
        self.half = (side * side, 1 + core * (side - 1), side + core * (1 - side))
        self.step = tuple(2 * h for h in self.half)
        self.sibling = me + 1 - 2 * core

    def owner(self, q):
        return q[0] * self.step[0] + q[1] * self.step[1] + q[2] * self.step[2] + self.core

    def near(self, dim, up):
        return self.me + self.step[dim] if up else self.me - self.step[dim]

    def has(self, dim, up):
        return self.pos[dim] < self.sizes[dim] - 1 if up else self.pos[dim] > 0


class Units:
    def __init__(self, ref, rows, cols):
        self.ref, self.rows, self.cols = ref, rows, cols
        self.per = WIDE // cols

    def window(self, s):
        if self.per == 1:
            row, col = s * self.rows, 0
            return (pl.ds(pl.multiple_of(row, self.rows), self.rows), slice(None))
        row, col = s // self.per * self.rows, s % self.per * self.cols
        return (
            pl.ds(pl.multiple_of(row, self.rows), self.rows),
            pl.ds(pl.multiple_of(col, self.cols), self.cols),
        )

    def at(self, s):
        return self.ref.at[self.window(s)]

    def get(self, s):
        return self.ref[self.window(s)]

    def put(self, s, value):
        self.ref[self.window(s)] = value


def remote(src, dst, send, recv, device):
    return pltpu.make_async_remote_copy(
        src_ref=src,
        dst_ref=dst,
        send_sem=send,
        recv_sem=recv,
        device_id=(device,),
        device_id_type=MESH,
    )


def others(place, dim, first=False):
    n, p = place.sizes[dim], place.pos[dim]
    if n == 2:
        return [(1 - p, None)]
    found = []
    for distance in range(1, n):
        found.append((p - distance, p >= distance))
        found.append((p + distance, p < n - distance))
    return found


def gated(cond, body):
    if cond is None:
        body()
    else:
        pl.when(cond)(body)


def both(a, b):
    return b if a is None else (a if b is None else a & b)


class Gather:
    def __init__(self, place, units, recv, send):
        self.place, self.units, self.recv, self.send = place, units, recv, send
        n0, na, nb = place.sizes
        self.waits = []
        self.base = []
        at = 0
        for dim in range(3):
            length = n0 * (1, na, na * nb)[dim]
            self.base.append((at, at + length))
            at += 2 * length
        self.core_base = at

    @staticmethod
    def sems(devices):
        side = math.isqrt(devices // 8)
        return 8 + 8 * side + 12 * side * side

    def linear(self, q, dim):
        _, na, nb = self.place.sizes
        return (q[0], q[0] * na + q[1], (q[0] * na + q[1]) * nb + q[2])[dim]

    def emit(self, cond, q, sem, device):
        owner = self.place.owner(q)

        def copy():
            piece = self.units.at(owner)
            return remote(piece, piece, self.send.at[sem], self.recv.at[owner], device)

        gated(cond, lambda: copy().start())
        self.waits.append(lambda: gated(cond, lambda: copy().wait_send()))

    def forward(self, cond, q, via, arrived):
        place = self.place
        for dim in (0, 2, 1):
            if dim < via or (arrived and dim == via and place.sizes[dim] == 2):
                continue
            for up in (True, False):
                open_end = place.has(dim, up)
                if arrived and dim == via:
                    p = place.pos[dim]
                    open_end = open_end & ((q[dim] < p) if up else (q[dim] > p))
                self.emit(
                    both(cond, open_end),
                    q,
                    self.base[dim][0 if up else 1] + self.linear(q, dim),
                    place.near(dim, up),
                )
        self.emit(cond, q, self.core_base + self.linear(q, 2), place.sibling)

    def wait(self, cond, owner):
        piece = self.units.at(owner)
        gated(
            cond,
            lambda: remote(
                piece, piece, self.send.at[0], self.recv.at[owner], self.place.sibling
            ).wait_recv(),
        )

    def own(self, lo, hi):
        p = self.place.pos
        cond = None if hi - lo == self.place.sizes[0] else (p[0] >= lo) & (p[0] < hi)
        self.forward(cond, p, 0, False)

    def take(self, cond, q, via):
        self.wait(cond, self.place.owner(q))
        self.forward(cond, q, via, True)

    def line(self, lo, hi):
        p = self.place.pos
        for q0, there in others(self.place, 0):
            cond = both(there, (q0 >= lo) & (q0 < hi))
            self.take(cond, (q0, p[1], p[2]), 0)

    def second(self, lo, hi):
        for q0 in range(lo, hi):
            for qa, there in others(self.place, 1):
                self.take(there, (q0, qa, self.place.pos[2]), 1)

    def third(self, lo, hi):
        for qb, there in others(self.place, 2):
            for q0 in range(lo, hi):
                for qa in range(self.place.sizes[1]):
                    self.take(there, (q0, qa, qb), 2)

    def across(self, lo, hi):
        place = self.place
        per = place.sizes[1] * place.sizes[2]

        def body(j):
            self.wait(None, 2 * (lo * per + j) + 1 - place.core)

        loop((hi - lo) * per, body)

    def finish(self):
        for wait in self.waits:
            wait()
        self.waits = []


def landing(n):
    return 1 if n == 2 else n + 1


class Reduce:
    def __init__(self, place, units, lo, hi, land_one, land_two, sems, ready):
        self.place, self.units, self.lo, self.hi = place, units, lo, hi
        n0, na, nb = place.sizes
        self.count = (hi - lo) * na * nb
        land_one = Units(land_one, units.rows, units.cols)
        land_two = Units(land_two, units.rows, units.cols)
        self.lands = (land_one, land_two, land_two)
        self.land_core = land_one
        lines = ((1, n0), (hi - lo, na), ((hi - lo) * na, nb))
        self.land_at = (self.count, lines[2][0] * landing(nb), 0)
        self.sems, self.ready = sems, ready
        at = 2 * self.count
        self.recv_at, self.up_at, self.down_at = [], [], []
        for units_here, n in lines:
            self.recv_at.append(at)
            at += units_here * landing(n)
            self.up_at.append(at)
            at += units_here * n
            self.down_at.append(at)
            at += units_here * n
        self.waits = []

    @staticmethod
    def amount(devices, share):
        side = math.isqrt(devices // 8)
        count = share * side * side
        total = 2 * count
        for units_here, n in ((1, 4), (share, side), (share * side, side)):
            total += units_here * (landing(n) + 2 * n)
        return total

    def unit(self, dim, q):
        na = self.place.sizes[1]
        return (0, q[0] - self.lo, (q[0] - self.lo) * na + q[1])[dim]

    def add(self, owner, land, slot):
        self.units.put(owner, self.units.get(owner) + land.get(slot))

    def start(self):
        place = self.place
        pl.semaphore_signal(
            self.ready.at[0], inc=1, device_id=(place.sibling,), device_id_type=MESH
        )
        for dim in range(3):
            for up in (True, False):

                def signal(dim=dim, up=up):
                    pl.semaphore_signal(
                        self.ready.at[1 + 2 * dim + (1 if up else 0)],
                        inc=1,
                        device_id=(place.near(dim, up),),
                        device_id_type=MESH,
                    )

                pl.when(place.has(dim, up))(signal)
        pl.semaphore_wait(self.ready.at[0], 1)
        per = place.sizes[1] * place.sizes[2]

        def copy(j):
            owner = 2 * (self.lo * per + j) + 1 - place.core
            return remote(
                self.units.at(owner),
                self.land_core.at(j),
                self.sems.at[j],
                self.sems.at[self.count + j],
                place.sibling,
            )

        loop(self.count, lambda j: copy(j).start())
        self.waits.append(lambda: loop(self.count, lambda j: copy(j).wait_send()))

    def allow(self, dim):
        for up in (True, False):
            pl.when(self.place.has(dim, up))(
                lambda up=up: pl.semaphore_wait(self.ready.at[1 + 2 * dim + (0 if up else 1)], 1)
            )

    def push(self, cond, dim, q, up, slot):
        place = self.place
        n = place.sizes[dim]
        u = self.unit(dim, q)
        owner = place.owner(q)
        sem = (self.up_at if up else self.down_at)[dim] + u * n + q[dim]
        device = place.near(dim, up)
        land = self.lands[dim]
        target = u * landing(n) + slot

        def copy():
            return remote(
                self.units.at(owner),
                land.at(self.land_at[dim] + target),
                self.sems.at[sem],
                self.sems.at[self.recv_at[dim] + target],
                device,
            )

        gated(cond, lambda: copy().start())
        self.waits.append(lambda: gated(cond, lambda: copy().wait_send()))

    def pull(self, dim, q, slot):
        place = self.place
        target = self.unit(dim, q) * landing(place.sizes[dim]) + slot
        owner = place.owner(q)
        land = self.lands[dim]
        piece = land.at(self.land_at[dim] + target)
        remote(
            piece,
            piece,
            self.sems.at[0],
            self.sems.at[self.recv_at[dim] + target],
            place.sibling,
        ).wait_recv()
        self.add(owner, land, self.land_at[dim] + target)

    def first(self, dim, q):
        place = self.place
        n, p = place.sizes[dim], place.pos[dim]
        for up in (True, False):
            end = 0 if up else n - 1
            away = (q[dim] > p) if up else (q[dim] < p)
            self.push((p == end) & away, dim, q, up, self.slot_up(q[dim], 0) if up else self.slot_down(n, q[dim], n - 1))

    @staticmethod
    def slot_up(q, p):
        return q - (p + 1)

    @staticmethod
    def slot_down(n, q, p):
        to = p - 1
        return q + (n - to if to > 0 else 0)

    def pairs(self):
        place = self.place
        na, nb = place.sizes[1:]
        self.allow(2)
        last = [q for q, _ in others(place, 2)] if nb == 2 else list(range(nb))
        second = [q for q, _ in others(place, 1)] + [place.pos[1]] if na == 2 else list(range(na))
        if nb == 2:
            last.append(place.pos[2])
        for qb in last:
            for qa in second:
                for q0 in range(self.lo, self.hi):
                    q = (q0, qa, qb)
                    j = (q0 - self.lo) * place.half[0] + qa * place.half[1] + qb * place.half[2]
                    piece = self.land_core.at(j)
                    remote(
                        piece,
                        piece,
                        self.sems.at[0],
                        self.sems.at[self.count + j],
                        place.sibling,
                    ).wait_recv()
                    self.add(place.owner(q), self.land_core, j)
                    if qb is not place.pos[2]:
                        self.first(2, q)

    def along(self, dim):
        place = self.place
        n, p = place.sizes[dim], place.pos[dim]
        self.allow(dim - 1)
        if dim == 2:
            second = (
                [q for q, _ in others(place, 1)] + [place.pos[1]]
                if place.sizes[1] == 2
                else list(range(place.sizes[1]))
            )
            rows = [(q0, qa) for qa in second for q0 in range(self.lo, self.hi)]
        else:
            rows = [(q0,) for q0 in range(self.lo, self.hi)]

        def whole(row, at):
            return row + (at,) + place.pos[dim + 1 :]

        if n == 2:
            for row in rows:
                self.pull(dim, whole(row, p), 0)
                if row[dim - 1] is not place.pos[dim - 1]:
                    self.first(dim - 1, whole(row, p))
        else:
            for k in range(1, n):
                self.hop(dim, k, [whole(row, None) for row in rows])
            for row in rows:
                self.first(dim - 1, whole(row, p))

    def hop(self, dim, k, rows):
        place = self.place
        n, p = place.sizes[dim], place.pos[dim]
        lo, hi = (self.lo, self.hi) if dim == 0 else (0, n)
        for up in (True, False):
            here = k if up else n - 1 - k
            cond = p == here
            span = range(max(lo, here), hi) if up else range(lo, min(hi, here + 1))

            def receive(up=up, here=here, span=span):
                for row in rows:
                    for at in span:
                        slot = at - here if up else at + (n - here if here > 0 else 0)
                        self.pull(dim, row[:dim] + (at,) + row[dim + 1 :], slot)
                        if at != here:
                            q = row[:dim] + (at,) + row[dim + 1 :]
                            self.push_now(dim, q, up, here)

            pl.when(cond)(receive)
            for row in rows:
                for at in span:
                    if at != here:
                        q = row[:dim] + (at,) + row[dim + 1 :]
                        self.waits.append(
                            lambda cond=cond, q=q, up=up, here=here: pl.when(cond)(
                                lambda: self.hop_copy(dim, q, up, here).wait_send()
                            )
                        )

    def hop_copy(self, dim, q, up, here):
        place = self.place
        n = place.sizes[dim]
        u = self.unit(dim, q)
        slot = self.slot_up(q[dim], here) if up else self.slot_down(n, q[dim], here)
        target = u * landing(n) + slot
        return remote(
            self.units.at(place.owner(q)),
            self.lands[dim].at(self.land_at[dim] + target),
            self.sems.at[(self.up_at if up else self.down_at)[dim] + u * n + q[dim]],
            self.sems.at[self.recv_at[dim] + target],
            place.near(dim, up),
        )

    def push_now(self, dim, q, up, here):
        self.hop_copy(dim, q, up, here).start()

    def last(self, k):
        self.hop(0, k, [(None,) + self.place.pos[1:]])

    def finish(self):
        for wait in self.waits:
            wait()
        self.waits = []


class Ring:
    def __init__(self, me, devices, land, sems):
        self.after = (me + 1) % devices
        self.before = (me + devices - 1) % devices
        self.land, self.sems = land, sems

    def copies(self, to_before, to_after):
        return (
            remote(to_before, self.land.at[1], self.sems.at[0], self.sems.at[1], self.before),
            remote(to_after, self.land.at[0], self.sems.at[2], self.sems.at[3], self.after),
        )

    def start(self, to_before, to_after):
        for copy in self.copies(to_before, to_after):
            copy.start()

    def wait(self, to_before, to_after):
        for copy in self.copies(to_before, to_after):
            copy.wait_recv()

    def finish(self, to_before, to_after):
        for copy in self.copies(to_before, to_after):
            copy.wait_send()


def unit_shape(amount):
    across = min(amount, PANEL)
    return amount // across * BLOCK_ROWS, across * BLOCK_COLS


def own_unit(units, me, blocks):
    across = units.cols // BLOCK_COLS
    rows = []
    for a in range(units.rows // BLOCK_ROWS):
        row = [blocks[a * across + b].astype(bf16) for b in range(across)]
        rows.append(jnp.concatenate(row, axis=1))
    units.put(me, jnp.concatenate(rows, axis=0))


def network(
    idx_ref,
    own_ref,
    tab_ref,
    vec_ref,
    state_ref,
    blocks_ref,
    late_in,
    energy_ref,
    forces_ref,
    vector_ref,
    first_out,
    late_out,
    first_w,
    late_w,
    hot,
    z_t,
    z_r,
    geo,
    yrow,
    env_b,
    edge_b,
    ee_t,
    en2_t,
    s1_t,
    s2_t,
    gam,
    dlt,
    coef,
    ds_t,
    de_t,
    dy,
    dg,
    dw_t,
    dw_r,
    dpf,
    den,
    lat,
    hid,
    low0,
    act1,
    sl1,
    low1,
    act2,
    sl2,
    low2,
    stage,
    halo,
    force_in,
    sides,
    vector_in,
    gather_sems,
    send_sems,
    late_sems,
    high_sems,
    low_sems,
    ring_sems,
    vector_sems,
    ready,
):
    s_r = dw_r
    fact = den

    wee_t = dw_t.at[:, 0:LATENT]
    we2_t = dw_t.at[0:128, 0:LATENT]
    devices = lax.axis_size("atoms")
    me = lax.axis_index("atoms")
    place = Place(devices)
    first_units = Units(first_w, *unit_shape(blocks_ref.shape[0]))
    late_units = Units(late_w, *unit_shape(late_in.shape[0]))
    gather_first = Gather(place, first_units, gather_sems.at[0], send_sems.at[0])
    gather_late = Gather(place, late_units, gather_sems.at[1], send_sems.at[1])
    middle = place.sizes[0] // 2
    top = place.sizes[0]
    sum_late = Reduce(place, late_units, 0, top, low2, sl2, late_sems, ready.at[0])
    sum_high = Reduce(place, first_units, middle, top, act2, sl1, high_sems, ready.at[1])
    sum_low = Reduce(place, first_units, 0, middle, low0, hid, low_sems, ready.at[2])
    link_halo = Ring(me, devices, halo, ring_sems.at[0])
    link_force = Ring(me, devices, force_in, ring_sems.at[1])

    barrier = pltpu.get_barrier_semaphore()

    def greet(j):
        pl.semaphore_signal(
            barrier, inc=1, device_id=((me + j + 1) % devices,), device_id_type=MESH
        )

    loop(devices - 1, greet)
    own_unit(first_units, me, blocks_ref)
    own_unit(late_units, me, late_in)
    pl.semaphore_wait(barrier, devices - 1)
    link_halo.start(own_ref, own_ref)
    gather_first.own(0, top)

    ids = lax.broadcasted_iota(jnp.int32, (3 * PLANE, LANES), 0)

    def find(t):
        hot[:, lanes(t)] = jnp.where(ids == idx_ref[:, lanes(t)], 1.0, 0.0).astype(bf16)

    loop(TILES, find)
    link_halo.wait(own_ref, own_ref)
    own = own_ref[...]
    lane = lax.broadcasted_iota(jnp.int32, (8, LANES), 1)
    row = lax.broadcasted_iota(jnp.int32, (8, LANES), 0)
    edge = spacing * devices
    x_row = row == 0
    before = halo[0] - jnp.where(x_row, jnp.where(me == 0, edge, 0.0), 0.0)
    after = halo[1] + jnp.where(x_row, jnp.where(me == devices - 1, edge, 0.0), 0.0)
    rank_y = ((lane & (PLANE - 1)) >> 3).astype(f32)
    rank_z = (lane & (SIDE - 1)).astype(f32)
    table = jnp.concatenate([jnp.where(lane < PLANE, before, own), after], axis=1)
    ranks = jnp.where(row == 4, rank_y, rank_z)
    table = jnp.where(
        jnp.concatenate([row, row], axis=1) < 4, table, jnp.concatenate([ranks, ranks], axis=1)
    )[:, : 3 * PLANE]
    ga, gb, gc = parts(table)
    got = nn(ga, hot[...]) + nn(gb, hot[...]) + nn(gc, hot[...])
    mine = jnp.concatenate([own] * TILES, axis=1)
    lane = lax.broadcasted_iota(jnp.int32, (1, ROWS), 1)
    slot = lane >> 6
    atom = lane & (PLANE - 1)

    def wrapped(step):
        return jnp.where(step > 1.5, -8.0, jnp.where(step < -1.5, 8.0, 0.0)) * spacing

    disp = [
        got[0:1] - mine[0:1],
        got[1:2] - mine[1:2] + wrapped(got[4:5] - (atom >> 3).astype(f32)),
        got[2:3] - mine[2:3] + wrapped(got[5:6] - (atom & (SIDE - 1)).astype(f32)),
    ]
    length = jnp.sqrt(disp[0] * disp[0] + disp[1] * disp[1] + disp[2] * disp[2])
    inverse = 1.0 / length
    unit = [disp[0] * inverse, disp[1] * inverse, disp[2] * inverse]
    angle = length * (math.pi / cutoff_radius)
    sin_k = [jnp.sin(angle)]
    cos_k = [jnp.cos(angle)]
    sin_k.append(2.0 * cos_k[0] * sin_k[0])
    cos_k.append(2.0 * cos_k[0] * cos_k[0] - 1.0)
    for k in range(2, BESSEL):
        sin_k.append(2.0 * cos_k[0] * sin_k[k - 1] - sin_k[k - 2])
        cos_k.append(2.0 * cos_k[0] * cos_k[k - 1] - cos_k[k - 2])
    sines = jnp.concatenate(sin_k, axis=0)
    cosines = jnp.concatenate(cos_k, axis=0)
    bessel = (math.sqrt(2.0 / cutoff_radius) * inverse) * sines
    scaled = length * (1.0 / cutoff_radius)
    t2 = scaled * scaled
    t4 = t2 * t2
    t5 = t4 * scaled
    t6 = t4 * t2
    envelope = 1.0 - 28.0 * t6 + 48.0 * (t6 * scaled) - 21.0 * (t4 * t4)
    denvelope = (-168.0 * t5 + 336.0 * t6 - 168.0 * (t6 * scaled)) * (1.0 / cutoff_radius)
    live = jnp.where(slot.astype(f32) < mine[4:5], 1.0, 0.0)

    kind = lax.broadcasted_iota(jnp.int32, (KINDS, LANES), 0).astype(f32)
    is_kind = kind == own[3:4]
    scale = jnp.sum(jnp.where(is_kind, tab_ref[:, 0:1], 0.0), axis=0, keepdims=True)
    shift = jnp.sum(jnp.where(is_kind, tab_ref[:, 1:2], 0.0), axis=0, keepdims=True)
    cot = jnp.concatenate([own[5:6] * scale] * TILES, axis=1) * live
    weight = cot * envelope

    root3 = math.sqrt(3.0)
    root15 = math.sqrt(15.0)
    root5 = math.sqrt(5.0)
    ux, uy, uz = unit
    yrow[0:8] = jnp.concatenate(
        [
            root3 * ux,
            root3 * uy,
            root3 * uz,
            root15 * ux * uy,
            root15 * uy * uz,
            0.5 * root5 * (3.0 * uz * uz - 1.0),
            root15 * ux * uz,
            0.5 * root15 * (ux * ux - uy * uy),
        ],
        axis=0,
    )
    yrow[8:16] = yrow[0:8] * (live * env_scale)
    yrow[16:17] = live * env_scale
    geo[0:8] = jnp.concatenate([ux, uy, uz, inverse, envelope, denvelope, live, cot], axis=0)
    geo[8:16] = math.sqrt(2.0 / cutoff_radius) * (
        (math.pi / cutoff_radius)
        * lax.broadcasted_iota(jnp.int32, (BESSEL, ROWS), 0).astype(f32)
        * cosines
        + (math.pi / cutoff_radius) * cosines
        - sines * inverse
    ) * inverse

    def one_hots(t):
        row = lax.broadcasted_iota(jnp.int32, (LANES, LANES), 0).astype(f32)
        here = jnp.where(row == own[3:4] + float(BESSEL), 1.0, 0.0)
        there = jnp.where(row == kinds_near[t] + float(BESSEL + SPECIES), 1.0, 0.0)
        return here + there

    kinds_near = [got[3:4, t * LANES : (t + 1) * LANES] for t in range(TILES)]
    for t in range(TILES):
        at = slice(t * LANES, (t + 1) * LANES)
        column = jnp.concatenate([bessel[:, at], one_hots(t)[BESSEL:]], axis=0)
        z_t[:, at] = column.astype(bf16)
        z_r[at, :] = column.T.astype(bf16)
        env_b[at, :] = jnp.broadcast_to(envelope[:, at], (LANES, LANES)).T
        edge_b[at, :] = jnp.broadcast_to(weight[:, at], (LANES, LANES)).T

    gather_first.line(0, top)
    gather_first.second(0, middle)
    gather_first.third(0, middle)
    gather_first.second(middle, top)
    gather_late.own(0, top)
    gather_first.across(0, middle)

    def twice(x):
        return jnp.concatenate([x, x], axis=1)

    def in_body(n, r):
        pre = nn(z_r[r], cols_panel(first_w, W_INPUT, n))
        hid[r, panel(n)] = (pre * sigmoid(pre)).astype(bf16)

    loop_panels(in_body)

    def two_body(n, r):
        zero = nn(hid[r], cols_panel(first_w, W_TWO, n)) * twice(env_b[r])
        lat[r, panel(n)] = zero
        low0[r, panel(n)] = zero.astype(bf16)

    loop_panels(two_body)

    def transposed_product(out, weights, right, width=256):
        at = 0
        while at < ROWS:
            end = min(at + width, ROWS)
            out[:, at:end] = nt(weights, right[at:end, :])
            at = end

    gather_first.third(middle, top)
    gather_late.line(0, top)
    wee_t[0:128, :] = narrow(first_w, W_EMBED).T
    wee_t[128:256, :] = narrow(first_w, W_ENV_ONE).T
    transposed_product(ee_t, wee_t[...], low0)

    def environment(out, v0_ref, v0_at, v1_at):
        for m in range(9):
            total = None
            begin = v0_at if m == 0 else v1_at
            y = yrow[16:17, :] if m == 0 else yrow[7 + m : 8 + m, :]
            for t in range(TILES):
                at = slice(t * LANES, (t + 1) * LANES)
                term = v0_ref[begin : begin + CHANNELS, at] * y[:, at]
                total = term if total is None else total + term
            out[m] = halves(total)

    def put_scalars(t, s_t, rows):
        s_t[:, lanes(t)] = jnp.concatenate(rows, axis=0).astype(bf16)
        filled = jnp.concatenate(rows + [jnp.zeros_like(rows[0])], axis=0)
        flipped = filled.T.astype(bf16)
        s_r[lanes(t), :] = flipped

    def weighted(y, first, count, source, offset):
        total = None
        for m in range(count):
            term = y[first + m : first + m + 1] * source[offset + m]
            total = term if total is None else total + term
        return total

    environment(gam, ee_t, 128, 192)

    def scalars_one(t):
        e0 = ee_t[0:64, lanes(t)]
        e1 = ee_t[64:128, lanes(t)]
        y = yrow[0:8, lanes(t)]
        put_scalars(
            t,
            s1_t,
            [e0 * gam[0], e1 * weighted(y, 0, 3, gam, 1), e1 * weighted(y, 3, 5, gam, 4)],
        )

    loop(TILES, scalars_one)

    gather_first.across(middle, top)
    gather_late.second(0, top)
    def pre_one(n, r):
        pre = nn(low0[r], cols_panel(first_w, W_LAT_ONE, n)) + nn(
            s_r[r, : 3 * CHANNELS], cols_panel(first_w, W_SCAL_ONE, n)
        )
        sig = sigmoid(pre)
        act = pre * sig
        act1[r, panel(n)] = act.astype(bf16)
        sl1[r, panel(n)] = (sig + act * (1.0 - sig)).astype(bf16)

    loop_panels(pre_one)
    gather_late.third(0, top)

    def out_one(n, r):
        new = (lat[r, panel(n)] + nn(act1[r], cols_panel(first_w, W_OUT_ONE, n))) * half_root
        lat[r, panel(n)] = new
        low1[r, panel(n)] = new.astype(bf16)

    loop_panels(out_one)
    we2_t[...] = narrow(first_w, W_ENV_TWO).T
    transposed_product(en2_t, we2_t[...], low1)
    environment(dlt, en2_t, 0, 64)

    g0 = gam[0]
    coef[0] = g0 * dlt[0]
    for m in range(3):
        a, b = 1 + (m + 1) % 3, 1 + (m + 2) % 3
        coef[1 + m] = g0 * dlt[1 + m] + (gam[a] * dlt[b] - gam[b] * dlt[a])
    coef[9] = gam[1] * dlt[1] + gam[2] * dlt[2] + gam[3] * dlt[3]
    second = None
    for m in range(4, 9):
        coef[m] = g0 * dlt[m]
        term = gam[m] * dlt[m]
        second = term if second is None else second + term
    coef[10] = second

    def scalars_two(t):
        e0 = ee_t[0:64, lanes(t)]
        e1 = ee_t[64:128, lanes(t)]
        y = yrow[0:8, lanes(t)]
        put_scalars(
            t,
            s2_t,
            [
                e0 * coef[0],
                e1 * weighted(y, 0, 3, coef, 1) + e0 * coef[9],
                e1 * weighted(y, 3, 5, coef, 4) + e0 * coef[10],
            ],
        )

    loop(TILES, scalars_two)

    gather_late.across(0, top)
    gather_first.finish()
    gather_late.finish()
    def pre_two(n, r):
        pre = nn(low1[r], cols_panel(late_w, W_LAT_TWO, n)) + nn(
            s_r[r, : 3 * CHANNELS], cols_panel(first_w, W_SCAL_TWO, n)
        )
        sig = sigmoid(pre)
        act = pre * sig
        act2[r, panel(n)] = act.astype(bf16)
        sl2[r, panel(n)] = (sig + act * (1.0 - sig)).astype(bf16)

    loop_panels(pre_two)

    def out_two(n, r):
        new = (lat[r, panel(n)] + nn(act2[r], cols_panel(late_w, W_OUT_TWO, n))) * half_root
        low2[r, panel(n)] = new.astype(bf16)

    loop_panels(out_two)

    vec = vec_ref[...]
    stage[...] = narrow(first_w, W_FINAL)

    def read_out(i):
        r = pl.ds(pl.multiple_of(i * 416, 16), 416)
        pre = nn(low2[r, :], stage[...])
        sig = sigmoid(pre)
        final_act = pre * sig
        fact[r, :] = final_act
        dpf[r, :] = (edge_b[r, :] * vec[0:1] * (sig + final_act * (1.0 - sig))).astype(bf16)

    loop(4, read_out)
    value = nt(vec, fact[...], highest)[0:1]
    geo_live = geo[6:7]
    geo_env = geo[4:5]
    geo_cot = geo[7:8]
    edge_energy = geo_live * geo_env * value
    summed = None
    for t in range(TILES):
        term = edge_energy[:, t * LANES : (t + 1) * LANES]
        summed = term if summed is None else summed + term
    energy_ref[...] = scale * halves(summed) + shift
    all_weights = jnp.broadcast_to(geo_cot * geo_env, (8, ROWS))
    vector_in[me] = nn(all_weights, fact[...], highest)

    def vector_copy(j, source):
        return remote(
            vector_in.at[me],
            vector_in.at[source],
            vector_sems.at[j],
            vector_sems.at[devices + source],
            (me + j) % devices,
        )

    loop(devices - 1, lambda i: vector_copy(i + 1, me).start())
    vector_waits = [
        lambda: loop(
            devices - 1,
            lambda i: vector_copy(i + 1, (me + devices - 1 - i) % devices).wait(),
        )
    ]
    geo[16:17] = geo_cot * value

    def big_grad(out, where, left, right):
        def step(i):
            grad = tn(left[:, panel(i)], right[...])
            out[pl.ds(pl.multiple_of(where[0] + i * 256, 64), 256), :] = grad.astype(bf16)

        loop(4, step)

    def wide_grad(out, where, left, right):
        def step(n):
            out[where[0] : where[0] + where[1], panel(n)] = nn(
                left[...], right[:, panel(n)]
            ).astype(bf16)

        loop(4, step)

    def narrow_grad(left, right, put):
        def step(n):
            put(n, nn(left, right[:, panel(n)]).T.astype(bf16))

        loop(4, step)

    def put_narrow(where, n, grad):
        row = pl.multiple_of(where[0] + n // 2 * BLOCK_ROWS, BLOCK_ROWS)
        col = pl.multiple_of(n % 2 * 512, 512)
        first_w[pl.ds(row, BLOCK_ROWS), pl.ds(col, 512)] = jnp.concatenate(
            [grad[b * BLOCK_ROWS : (b + 1) * BLOCK_ROWS] for b in range(4)], axis=1
        )

    def put_stage(n, grad):
        stage[panel(n), :] = grad

    narrow_grad(dpf[...].T, low2, put_stage)

    def back_final(n, r):
        grad = nt(dpf[r], narrow_panel(first_w, W_FINAL, n)) * half_root
        lat[r, panel(n)] = grad
        low2[r, panel(n)] = grad.astype(bf16)

    loop_panels(back_final)
    loop(4, lambda n: put_narrow(W_FINAL, n, stage[panel(n), :]))

    def back_out_two(n, r):
        grad = nt(low2[r], rows_panel(late_w, W_OUT_TWO, n))
        sl2[r, panel(n)] = (grad * sl2[r, panel(n)].astype(f32)).astype(bf16)

    loop_panels(back_out_two)
    transposed_product(ds_t, first_w[W_SCAL_TWO[0] : W_SCAL_TWO[0] + W_SCAL_TWO[1], :], sl2)
    wide_grad(first_w, W_SCAL_TWO, s2_t, sl2)
    big_grad(late_w, W_OUT_TWO, act2, low2)

    dg[...] = jnp.zeros_like(dg)

    def tensors_two(t):
        e0 = ee_t[0:64, lanes(t)]
        e1 = ee_t[64:128, lanes(t)]
        y = yrow[0:8, lanes(t)]
        r0 = ds_t[0:64, lanes(t)]
        r1 = ds_t[64:128, lanes(t)]
        r2 = ds_t[128:192, lanes(t)]
        de_t[0:64, lanes(t)] = r0 * coef[0] + r1 * coef[9] + r2 * coef[10]
        de_t[64:128, lanes(t)] = r1 * weighted(y, 0, 3, coef, 1) + r2 * weighted(y, 3, 5, coef, 4)
        p1 = r1 * e1
        p2 = r2 * e1
        rows = []
        for m in range(8):
            p = p1 if m < 3 else p2
            rows.append(jnp.sum(p * coef[1 + m], axis=0, keepdims=True))
            dg[1 + m] += p * y[m : m + 1]
        dy[:, lanes(t)] = jnp.concatenate(rows, axis=0)
        dg[0] += r0 * e0
        dg[9] += r1 * e0
        dg[10] += r2 * e0

    loop(TILES, tensors_two)
    total = [halves(dg[m]) for m in range(11)]
    g0 = gam[0]
    d0 = dlt[0]
    new_g0 = total[0] * d0
    for m in range(1, 9):
        new_g0 = new_g0 + total[m] * dlt[m]
    dlt_grads = [total[0] * g0]
    gam_grads = [new_g0]
    for m in range(3):
        a, b = 1 + (m + 1) % 3, 1 + (m + 2) % 3
        dlt_grads.append(
            total[1 + m] * g0 + total[9] * gam[1 + m] + (total[a] * gam[b] - total[b] * gam[a])
        )
        gam_grads.append(total[9] * dlt[1 + m] + (dlt[a] * total[b] - dlt[b] * total[a]))
    for m in range(4, 9):
        dlt_grads.append(total[m] * g0 + total[10] * gam[m])
        gam_grads.append(total[10] * dlt[m])
    for m in range(9):
        dlt[m] = dlt_grads[m]
        dg[m] = gam_grads[m]

    def environment_back(t, grads, source, v1_at, at):
        y4 = yrow[8:16, lanes(t)]
        l4 = yrow[16:17, lanes(t)]
        v1 = source[v1_at : v1_at + 64, lanes(t)]
        low = l4 * grads[0]
        high = weighted(y4, 0, 8, grads, 1)
        both = jnp.concatenate([low, high], axis=0)
        dw_t[at : at + 128, lanes(t)] = both.astype(bf16)
        dw_r[lanes(t), at : at + 128] = both.T.astype(bf16)
        v1 = v1 * l4
        rows = [jnp.sum(v1 * grads[1 + m], axis=0, keepdims=True) for m in range(8)]
        dy[:, lanes(t)] += jnp.concatenate(rows, axis=0)

    loop(TILES, lambda t: environment_back(t, dlt, en2_t, 64, 128))

    def back_lat_two(n, r):
        grad = (
            lat[r, panel(n)]
            + nt(sl2[r], rows_panel(late_w, W_LAT_TWO, n))
            + nt(dw_r[r, 128:256], narrow_panel(first_w, W_ENV_TWO, n))
        ) * half_root
        lat[r, panel(n)] = grad
        act2[r, panel(n)] = grad.astype(bf16)

    loop_panels(back_lat_two)
    big_grad(late_w, W_LAT_TWO, low1, sl2)
    narrow_grad(dw_t[128:256, :], low1, functools.partial(put_narrow, W_ENV_TWO))
    sum_late.start()

    def back_out_one(n, r):
        grad = nt(act2[r], rows_panel(first_w, W_OUT_ONE, n))
        sl1[r, panel(n)] = (grad * sl1[r, panel(n)].astype(f32)).astype(bf16)

    loop_panels(back_out_one)
    sum_late.pairs()
    big_grad(first_w, W_OUT_ONE, act1, act2)
    sum_late.along(2)
    transposed_product(ds_t, first_w[W_SCAL_ONE[0] : W_SCAL_ONE[0] + W_SCAL_ONE[1], :], sl1)
    wide_grad(first_w, W_SCAL_ONE, s1_t, sl1)
    sum_late.along(1)

    def tensors_one(t):
        e0 = ee_t[0:64, lanes(t)]
        e1 = ee_t[64:128, lanes(t)]
        y = yrow[0:8, lanes(t)]
        r0 = ds_t[0:64, lanes(t)]
        r1 = ds_t[64:128, lanes(t)]
        r2 = ds_t[128:192, lanes(t)]
        low = de_t[0:64, lanes(t)] + r0 * gam[0]
        high = (
            de_t[64:128, lanes(t)]
            + r1 * weighted(y, 0, 3, gam, 1)
            + r2 * weighted(y, 3, 5, gam, 4)
        )
        both = jnp.concatenate([low, high], axis=0)
        dw_t[0:128, lanes(t)] = both.astype(bf16)
        dw_r[lanes(t), 0:128] = both.T.astype(bf16)
        p1 = r1 * e1
        p2 = r2 * e1
        rows = []
        for m in range(8):
            p = p1 if m < 3 else p2
            rows.append(jnp.sum(p * gam[1 + m], axis=0, keepdims=True))
            coef[1 + m] += p * y[m : m + 1]
        dy[:, lanes(t)] += jnp.concatenate(rows, axis=0)
        coef[0] += r0 * e0

    for m in range(9):
        coef[m] = jnp.zeros((CHANNELS, LANES), f32)
    loop(TILES, tensors_one)
    for m in range(9):
        dg[m] = dg[m] + halves(coef[m])
    loop(TILES, lambda t: environment_back(t, dg, ee_t, 192, 128))
    sum_late.last(1)

    den[...] = jnp.zeros_like(den)

    def back_lat_one(n, r):
        both = jnp.concatenate(
            [narrow_panel(first_w, W_EMBED, n), narrow_panel(first_w, W_ENV_ONE, n)], axis=1
        )
        grad = (
            lat[r, panel(n)]
            + nt(sl1[r], rows_panel(first_w, W_LAT_ONE, n))
            + nt(dw_r[r], both)
        )
        low1[r, panel(n)] = (grad * twice(env_b[r])).astype(bf16)
        part = grad * low0[r, panel(n)].astype(f32)
        den[r] += part[:, :LANES] + part[:, LANES:]

    loop_panels(back_lat_one)
    sum_late.last(2)
    big_grad(first_w, W_LAT_ONE, low0, sl1)
    sum_late.last(3)
    sum_high.start()
    narrow_grad(dw_t[0:128, :], low0, functools.partial(put_narrow, W_EMBED))
    narrow_grad(dw_t[128:256, :], low0, functools.partial(put_narrow, W_ENV_ONE))

    def back_two(n, r):
        grad = nt(low1[r], rows_panel(first_w, W_TWO, n))
        pre = nn(z_r[r], cols_panel(first_w, W_INPUT, n))
        sig = sigmoid(pre)
        act1[r, panel(n)] = (grad * (sig + pre * sig * (1.0 - sig))).astype(bf16)

    loop_panels(back_two)
    sum_high.pairs()

    transposed_product(ds_t.at[0:64], first_w[0:64, :], act1)
    dbessel = ds_t[0:8, :]
    through = nt(jnp.ones((8, LANES), f32), den[...], highest)[0:1]
    ux, uy, uz = geo[0:1], geo[1:2], geo[2:3]
    inverse = geo[3:4]
    envelope = geo[4:5]
    denv = geo[16:17] + through / envelope
    dlength = jnp.sum(dbessel * geo[8:16], axis=0, keepdims=True) + denv * geo[5:6]
    g = [dy[m : m + 1, :] for m in range(8)]
    dux = root3 * g[0] + root15 * (uy * g[3] + uz * g[6] + ux * g[7])
    duy = root3 * g[1] + root15 * (ux * g[3] + uz * g[4] - uy * g[7])
    duz = root3 * g[2] + root15 * (uy * g[4] + ux * g[6]) + (3.0 * root5) * uz * g[5]
    along = dlength - (ux * dux + uy * duy + uz * duz) * inverse
    near = jnp.concatenate(
        [
            dux * inverse + ux * along,
            duy * inverse + uy * along,
            duz * inverse + uz * along,
            jnp.zeros((5, ROWS), f32),
        ],
        axis=0,
    )
    wide_grad(first_w, W_INPUT, z_t, act1)
    sum_high.along(2)
    summed = None
    for t in range(TILES):
        term = near[:, t * LANES : (t + 1) * LANES]
        summed = term if summed is None else summed + term
    centre = halves(summed)
    na, nb, nc = parts(near)
    spread = nt(na, hot[...]) + nt(nb, hot[...]) + nt(nc, hot[...])
    sides[0] = spread[:, :LANES]
    sides[1, :, 0:PLANE] = spread[:, LANES:]
    link_force.start(sides.at[0], sides.at[1])
    big_grad(first_w, W_TWO, hid, low1)
    sum_low.start()
    sum_high.along(1)
    sum_high.last(1)
    sum_low.pairs()
    sum_high.last(2)
    sum_low.along(2)
    sum_high.last(3)
    sum_low.along(1)
    link_force.wait(sides.at[0], sides.at[1])
    forces_ref[...] = (
        centre - pltpu.roll(sides[0], PLANE, 1) - force_in[1] - force_in[0]
    )
    for wait in vector_waits:
        wait()
    total = jnp.sum(vector_in[...], axis=0)
    normed = total * lax.rsqrt(jnp.sum(total[0:1] * total[0:1]) * (1.0 / FINAL) + epsilon)
    state = decay_rate * state_ref[...] + (1.0 - decay_rate) * normed * normed
    vector_ref[0:1] = total[0:1]
    vector_ref[1:2] = state[0:1]
    vector_ref[2:3] = (vec_ref[...] - vector_rate * normed * lax.rsqrt(state + epsilon))[0:1]
    for k in range(1, 4):
        sum_low.last(k)

    def results(units, out):
        mine = units.get(me)
        per = units.cols // BLOCK_COLS
        for b in range(out.shape[0]):
            row, col = b // per * BLOCK_ROWS, b % per * BLOCK_COLS
            out[b] = mine[row : row + BLOCK_ROWS, col : col + BLOCK_COLS].astype(f32)

    results(late_units, late_out)
    results(first_units, first_out)
    for group in (sum_late, sum_high, sum_low):
        group.finish()
    link_halo.finish(own_ref, own_ref)
    link_force.finish(sides.at[0], sides.at[1])


def run_network(devices, idx, own, tab, vec, state, blocks, late):
    S = jax.ShapeDtypeStruct
    wide = pltpu.VMEM((ROWS, LATENT), bf16)
    slab = pltpu.VMEM((ROWS, LANES), f32)
    panels = lambda amount: pltpu.VMEM((amount * devices // PANEL * BLOCK_ROWS, WIDE), bf16)
    scratch = [
        panels(blocks.shape[0]),
        panels(late.shape[0]),
        pltpu.VMEM((3 * PLANE, ROWS), bf16),
        pltpu.VMEM((LANES, ROWS), bf16),
        pltpu.VMEM((ROWS, LANES), bf16),
        pltpu.VMEM((24, ROWS), f32),
        pltpu.VMEM((24, ROWS), f32),
        slab,
        slab,
        pltpu.VMEM((256, ROWS), f32),
        pltpu.VMEM((128, ROWS), f32),
        pltpu.VMEM((192, ROWS), bf16),
        pltpu.VMEM((192, ROWS), bf16),
        pltpu.VMEM((9, CHANNELS, LANES), f32),
        pltpu.VMEM((9, CHANNELS, LANES), f32),
        pltpu.VMEM((11, CHANNELS, LANES), f32),
        pltpu.VMEM((192, ROWS), f32),
        pltpu.VMEM((128, ROWS), f32),
        pltpu.VMEM((8, ROWS), f32),
        pltpu.VMEM((11, CHANNELS, LANES), f32),
        pltpu.VMEM((256, ROWS), bf16),
        pltpu.VMEM((ROWS, 256), bf16),
        pltpu.VMEM((ROWS, LANES), bf16),
        slab,
        pltpu.VMEM((ROWS, LATENT), f32),
    ] + [wide] * 8 + [
        pltpu.VMEM((LATENT, LANES), bf16),
        pltpu.VMEM((2, 8, LANES), f32),
        pltpu.VMEM((2, 8, LANES), f32),
        pltpu.VMEM((2, 8, LANES), f32),
        pltpu.VMEM((devices, 8, LANES), f32),
        pltpu.SemaphoreType.DMA((2, devices)),
        pltpu.SemaphoreType.DMA((2, Gather.sems(devices))),
        pltpu.SemaphoreType.DMA((Reduce.amount(devices, 4),)),
        pltpu.SemaphoreType.DMA((Reduce.amount(devices, 2),)),
        pltpu.SemaphoreType.DMA((Reduce.amount(devices, 2),)),
        pltpu.SemaphoreType.DMA((2, 4)),
        pltpu.SemaphoreType.DMA((2 * devices,)),
        pltpu.SemaphoreType.REGULAR((3, 7)),
    ]
    vmem = pl.BlockSpec(memory_space=pltpu.VMEM)
    return pl.pallas_call(
        network,
        out_shape=[
            S((1, LANES), f32),
            S((8, LANES), f32),
            S((8, LANES), f32),
            S(blocks.shape, f32),
            S(late.shape, f32),
        ],
        in_specs=[vmem] * 7,
        out_specs=[vmem] * 5,
        scratch_shapes=scratch,
        compiler_params=pltpu.CompilerParams(
            vmem_limit_bytes=63 << 20, collective_id=0, has_side_effects=True
        ),
        name="network",
    )(idx, own, tab, vec, state, blocks, late)


def shampoo(grads, left, right, left_root, right_root, master):
    mean_square = jnp.mean(grads * grads, axis=(1, 2), keepdims=True)
    normed = grads * lax.rsqrt(mean_square + epsilon)
    new_left = decay_rate * left + (1.0 - decay_rate) * jnp.einsum(
        "bij,bkj->bik", normed, normed, precision=highest
    )
    new_right = decay_rate * right + (1.0 - decay_rate) * jnp.einsum(
        "bji,bjk->bik", normed, normed, precision=highest
    )
    direction = jnp.einsum("bij,bjk->bik", left_root, normed, precision=highest)
    direction = jnp.einsum("bij,bjk->bik", direction, right_root, precision=highest)
    step_square = jnp.mean(direction * direction, axis=(1, 2), keepdims=True)
    return (new_left, new_right, master - learn_rate * direction * lax.rsqrt(step_square + epsilon))


def local(
    positions,
    species,
    neighbours,
    counts,
    species_scale,
    species_shift,
    energy_cot,
    blocks,
    left,
    right,
    left_root,
    right_root,
    late_blocks,
    late_left,
    late_right,
    late_left_root,
    late_right_root,
    out_vector,
    vector_state,
):
    devices = lax.axis_size("atoms")
    me = lax.axis_index("atoms")
    total_atoms = PLANE * devices
    first_atom = me * PLANE
    own = jnp.concatenate(
        [
            positions,
            species.astype(f32)[None],
            counts.astype(f32)[None],
            energy_cot[None],
            jnp.zeros((2, PLANE), f32),
        ],
        axis=0,
    )
    idx = (neighbours - first_atom + PLANE) % total_atoms
    idx = idx.reshape(PLANE, SLOTS).T.reshape(1, ROWS)
    own_twice = jnp.concatenate([own, own], axis=1)
    tab = jnp.pad(jnp.stack([species_scale, species_shift], axis=1), ((0, KINDS - SPECIES), (0, 126)))
    vec = jnp.broadcast_to(out_vector[None], (8, FINAL))
    state = jnp.broadcast_to(vector_state[None], (8, FINAL))
    energy, force, vectors, first_reduced, late_reduced = run_network(
        devices, idx, own_twice, tab, vec, state, blocks, late_blocks
    )
    energies = energy[0, :PLANE]
    forces = force[:3, :PLANE]
    vector_grad, new_state, new_vector = vectors[0], vectors[1], vectors[2]
    new_left, new_right, new_blocks = shampoo(
        first_reduced, left, right, left_root, right_root, blocks
    )
    new_late_left, new_late_right, new_late_blocks = shampoo(
        late_reduced, late_left, late_right, late_left_root, late_right_root, late_blocks
    )
    return (
        energies,
        forces,
        first_reduced,
        new_left,
        new_right,
        new_blocks,
        late_reduced,
        new_late_left,
        new_late_right,
        new_late_blocks,
        vector_grad,
        new_state,
        new_vector,
    )


def solution(mesh):
    row = P("atoms")
    block = P("atoms", None, None)
    placed = (
        (P(None, "atoms"), row, row, row, P(), P(), row)
        + (block,) * 10
        + (P(), P())
    )
    return jax.shard_map(
        local,
        mesh=mesh,
        in_specs=placed,
        out_specs=(row, P(None, "atoms")) + (block,) * 8 + (P(), P(), P()),
        check_vma=False,
    )
```

```python
import functools
import math

import jax
import jax.numpy as jnp
from jax import lax
from jax.experimental import pallas as pl
from jax.experimental.pallas import tpu as pltpu
from jax.sharding import PartitionSpec as P

SIDE = 8
SLOTS = 26
SPECIES = 60
BESSEL = 8
CHANNELS = 64
LATENT = 1024
FINAL = 128
BLOCK_ROWS = 64
BLOCK_COLS = 128
PLANE = SIDE * SIDE

f32 = jnp.float32
bf16 = jnp.bfloat16
highest = lax.Precision.HIGHEST
spacing = 1.6
cutoff_radius = 4.0
env_scale = 0.25
half_root = 0.7071067811865476
decay_rate = 0.5
learn_rate = 0.02
vector_rate = 0.03
epsilon = 1e-06

LANES = 128
ROWS = SLOTS * PLANE
TILES = ROWS // LANES
KINDS = 64

PANEL = 8
WIDE = PANEL * BLOCK_COLS
W_INPUT = (0, 128)
W_TWO = (128, 1024)
W_EMBED = (1152, 128)
W_ENV_ONE = (1280, 128)
W_LAT_ONE = (1408, 1024)
W_SCAL_ONE = (2432, 192)
W_OUT_ONE = (2624, 1024)
W_ENV_TWO = (3648, 128)
W_SCAL_TWO = (3776, 192)
W_FINAL = (3968, 128)
W_LAT_TWO = (0, 1024)
W_OUT_TWO = (1024, 1024)

MESH = pl.DeviceIdType.MESH


def nn(a, b, precision=None):
    return lax.dot_general(
        a, b, (((1,), (0,)), ((), ())), preferred_element_type=f32, precision=precision
    )


def nt(a, b, precision=None):
    return lax.dot_general(
        a, b, (((1,), (1,)), ((), ())), preferred_element_type=f32, precision=precision
    )


def tn(a, b):
    return lax.dot_general(a, b, (((0,), (0,)), ((), ())), preferred_element_type=f32)


def cols_panel(ref, where, n):
    return ref[where[0] : where[0] + where[1], panel(n, STRIP)]


def rows_panel(ref, where, n):
    return ref[pl.ds(pl.multiple_of(where[0] + n * STRIP, 64), STRIP), :]


def narrow(ref, where):
    pieces = []
    for j in range(LATENT // BLOCK_ROWS):
        row = where[0] + j // PANEL * BLOCK_ROWS
        col = j % PANEL * BLOCK_COLS
        pieces.append(ref[row : row + BLOCK_ROWS, col : col + BLOCK_COLS])
    return jnp.concatenate(pieces, axis=0)


def narrow_panel(ref, where, n):
    part = ref[pl.ds(pl.multiple_of(where[0] + n * BLOCK_ROWS, BLOCK_ROWS), BLOCK_ROWS), :]
    return jnp.concatenate([part[:, b * 128 : (b + 1) * 128] for b in range(PANEL)], axis=0)


def sigmoid(x):
    return 0.5 * jnp.tanh(0.5 * x) + 0.5


def halves(x):
    return x + pltpu.roll(x, PLANE, 1)


def lanes(t):
    return pl.ds(pl.multiple_of(t * LANES, LANES), LANES)


def panel(n, width=256):
    return pl.ds(pl.multiple_of(n * width, width), width)


STRIP = 512
CHUNKS = 2
CHUNK = ROWS // CHUNKS


def loop_panels(body):
    def step(n):
        for c in range(CHUNKS):
            body(n, slice(c * CHUNK, (c + 1) * CHUNK))

    loop(LATENT // STRIP, step)


def loop(count, body):
    def step(i, carry):
        body(i)
        return carry

    lax.fori_loop(0, count, step, 0)


def parts(x):
    a = x.astype(bf16)
    rest = x - a.astype(f32)
    b = rest.astype(bf16)
    c = (rest - b.astype(f32)).astype(bf16)
    return a, b, c


class Place:
    def __init__(self, devices):
        side = math.isqrt(devices // 8)
        self.devices = devices
        self.sizes = (4, side, side)
        me = lax.axis_index("atoms")
        core = me % 2
        chip = me // 2
        last = chip % side
        middle = chip // side % side
        self.me = me
        self.core = core
        self.pos = (
            chip // (side * side),
            last + core * (middle - last),
            middle + core * (last - middle),
        )
        self.half = (side * side, 1 + core * (side - 1), side + core * (1 - side))
        self.step = tuple(2 * h for h in self.half)
        self.sibling = me + 1 - 2 * core

    def owner(self, q):
        return q[0] * self.step[0] + q[1] * self.step[1] + q[2] * self.step[2] + self.core

    def near(self, dim, up):
        return self.me + self.step[dim] if up else self.me - self.step[dim]

    def has(self, dim, up):
        return self.pos[dim] < self.sizes[dim] - 1 if up else self.pos[dim] > 0


class Units:
    def __init__(self, ref, rows, cols):
        self.ref, self.rows, self.cols = ref, rows, cols
        self.per = WIDE // cols

    def window(self, s):
        if self.per == 1:
            row, col = s * self.rows, 0
            return (pl.ds(pl.multiple_of(row, self.rows), self.rows), slice(None))
        row, col = s // self.per * self.rows, s % self.per * self.cols
        return (
            pl.ds(pl.multiple_of(row, self.rows), self.rows),
            pl.ds(pl.multiple_of(col, self.cols), self.cols),
        )

    def at(self, s):
        return self.ref.at[self.window(s)]

    def get(self, s):
        return self.ref[self.window(s)]

    def put(self, s, value):
        self.ref[self.window(s)] = value


def remote(src, dst, send, recv, device):
    return pltpu.make_async_remote_copy(
        src_ref=src,
        dst_ref=dst,
        send_sem=send,
        recv_sem=recv,
        device_id=(device,),
        device_id_type=MESH,
    )


def others(place, dim, first=False):
    n, p = place.sizes[dim], place.pos[dim]
    if n == 2:
        return [(1 - p, None)]
    found = []
    for distance in range(1, n):
        found.append((p - distance, p >= distance))
        found.append((p + distance, p < n - distance))
    return found


def gated(cond, body):
    if cond is None:
        body()
    else:
        pl.when(cond)(body)


def both(a, b):
    return b if a is None else (a if b is None else a & b)


class Gather:
    def __init__(self, place, units, recv, send):
        self.place, self.units, self.recv, self.send = place, units, recv, send
        n0, na, nb = place.sizes
        self.waits = []
        self.base = []
        at = 0
        for dim in range(3):
            length = n0 * (1, na, na * nb)[dim]
            self.base.append((at, at + length))
            at += 2 * length
        self.core_base = at

    @staticmethod
    def sems(devices):
        side = math.isqrt(devices // 8)
        return 8 + 8 * side + 12 * side * side

    def linear(self, q, dim):
        _, na, nb = self.place.sizes
        return (q[0], q[0] * na + q[1], (q[0] * na + q[1]) * nb + q[2])[dim]

    def emit(self, cond, q, sem, device):
        owner = self.place.owner(q)

        def copy():
            piece = self.units.at(owner)
            return remote(piece, piece, self.send.at[sem], self.recv.at[owner], device)

        gated(cond, lambda: copy().start())
        self.waits.append(lambda: gated(cond, lambda: copy().wait_send()))

    def forward(self, cond, q, via, arrived, dims=(0, 2, 1), core=True):
        place = self.place
        for dim in dims:
            if dim < via or (arrived and dim == via and place.sizes[dim] == 2):
                continue
            for up in (True, False):
                open_end = place.has(dim, up)
                if arrived and dim == via:
                    p = place.pos[dim]
                    open_end = open_end & ((q[dim] < p) if up else (q[dim] > p))
                self.emit(
                    both(cond, open_end),
                    q,
                    self.base[dim][0 if up else 1] + self.linear(q, dim),
                    place.near(dim, up),
                )
        if core:
            self.emit(cond, q, self.core_base + self.linear(q, 2), place.sibling)

    def wait(self, cond, owner):
        piece = self.units.at(owner)
        gated(
            cond,
            lambda: remote(
                piece, piece, self.send.at[0], self.recv.at[owner], self.place.sibling
            ).wait_recv(),
        )

    def own(self, lo, hi, **how):
        p = self.place.pos
        cond = None if hi - lo == self.place.sizes[0] else (p[0] >= lo) & (p[0] < hi)
        self.forward(cond, p, 0, False, **how)

    def take(self, cond, q, via):
        self.wait(cond, self.place.owner(q))
        self.forward(cond, q, via, True)

    def line(self, lo, hi, distances=(1, 2, 3), wait=True, **how):
        p = self.place.pos
        for distance in distances:
            for q0, there in ((p[0] - distance, p[0] >= distance), (p[0] + distance, p[0] < 4 - distance)):
                cond = there & (q0 >= lo) & (q0 < hi)
                q = (q0, p[1], p[2])
                if wait:
                    self.wait(cond, self.place.owner(q))
                self.forward(cond, q, 0, True, **how)

    def second(self, lo, hi):
        for q0 in range(lo, hi):
            for qa, there in others(self.place, 1):
                self.take(there, (q0, qa, self.place.pos[2]), 1)

    def third(self, lo, hi):
        for qb, there in others(self.place, 2):
            for q0 in range(lo, hi):
                for qa in range(self.place.sizes[1]):
                    self.take(there, (q0, qa, qb), 2)

    def across(self, lo, hi):
        place = self.place
        per = place.sizes[1] * place.sizes[2]

        def body(j):
            self.wait(None, 2 * (lo * per + j) + 1 - place.core)

        loop((hi - lo) * per, body)

    def finish(self):
        for wait in self.waits:
            wait()
        self.waits = []


def landing(n):
    return 1 if n == 2 else n + 1


class Reduce:
    def __init__(self, place, units, lo, hi, land_one, land_two, sems, ready):
        self.place, self.units, self.lo, self.hi = place, units, lo, hi
        n0, na, nb = place.sizes
        self.count = (hi - lo) * na * nb
        land_one = Units(land_one, units.rows, units.cols)
        land_two = Units(land_two, units.rows, units.cols)
        self.lands = (land_one, land_two, land_two)
        self.land_core = land_one
        lines = ((1, n0), (hi - lo, na), ((hi - lo) * na, nb))
        self.land_at = (self.count, lines[2][0] * landing(nb), 0)
        self.sems, self.ready = sems, ready
        at = 2 * self.count
        self.recv_at, self.up_at, self.down_at = [], [], []
        for units_here, n in lines:
            self.recv_at.append(at)
            at += units_here * landing(n)
            self.up_at.append(at)
            at += units_here * n
            self.down_at.append(at)
            at += units_here * n
        self.waits = []

    @staticmethod
    def amount(devices, share):
        side = math.isqrt(devices // 8)
        count = share * side * side
        total = 2 * count
        for units_here, n in ((1, 4), (share, side), (share * side, side)):
            total += units_here * (landing(n) + 2 * n)
        return total

    def unit(self, dim, q):
        na = self.place.sizes[1]
        return (0, q[0] - self.lo, (q[0] - self.lo) * na + q[1])[dim]

    def add(self, owner, land, slot):
        self.units.put(owner, self.units.get(owner) + land.get(slot))

    def start(self):
        place = self.place
        pl.semaphore_signal(
            self.ready.at[0], inc=1, device_id=(place.sibling,), device_id_type=MESH
        )
        for dim in range(3):
            for up in (True, False):

                def signal(dim=dim, up=up):
                    pl.semaphore_signal(
                        self.ready.at[1 + 2 * dim + (1 if up else 0)],
                        inc=1,
                        device_id=(place.near(dim, up),),
                        device_id_type=MESH,
                    )

                pl.when(place.has(dim, up))(signal)
        pl.semaphore_wait(self.ready.at[0], 1)
        per = place.sizes[1] * place.sizes[2]

        def copy(j):
            owner = 2 * (self.lo * per + j) + 1 - place.core
            return remote(
                self.units.at(owner),
                self.land_core.at(j),
                self.sems.at[j],
                self.sems.at[self.count + j],
                place.sibling,
            )

        loop(self.count, lambda j: copy(j).start())
        self.waits.append(lambda: loop(self.count, lambda j: copy(j).wait_send()))

    def allow(self, dim):
        for up in (True, False):
            pl.when(self.place.has(dim, up))(
                lambda up=up: pl.semaphore_wait(self.ready.at[1 + 2 * dim + (0 if up else 1)], 1)
            )

    def push(self, cond, dim, q, up, slot):
        place = self.place
        n = place.sizes[dim]
        u = self.unit(dim, q)
        owner = place.owner(q)
        sem = (self.up_at if up else self.down_at)[dim] + u * n + q[dim]
        device = place.near(dim, up)
        land = self.lands[dim]
        target = u * landing(n) + slot

        def copy():
            return remote(
                self.units.at(owner),
                land.at(self.land_at[dim] + target),
                self.sems.at[sem],
                self.sems.at[self.recv_at[dim] + target],
                device,
            )

        gated(cond, lambda: copy().start())
        self.waits.append(lambda: gated(cond, lambda: copy().wait_send()))

    def pull(self, dim, q, slot):
        place = self.place
        target = self.unit(dim, q) * landing(place.sizes[dim]) + slot
        owner = place.owner(q)
        land = self.lands[dim]
        piece = land.at(self.land_at[dim] + target)
        remote(
            piece,
            piece,
            self.sems.at[0],
            self.sems.at[self.recv_at[dim] + target],
            place.sibling,
        ).wait_recv()
        self.add(owner, land, self.land_at[dim] + target)

    def first(self, dim, q):
        place = self.place
        n, p = place.sizes[dim], place.pos[dim]
        for up in (True, False):
            end = 0 if up else n - 1
            away = (q[dim] > p) if up else (q[dim] < p)
            self.push((p == end) & away, dim, q, up, self.slot_up(q[dim], 0) if up else self.slot_down(n, q[dim], n - 1))

    @staticmethod
    def slot_up(q, p):
        return q - (p + 1)

    @staticmethod
    def slot_down(n, q, p):
        to = p - 1
        return q + (n - to if to > 0 else 0)

    def pairs(self):
        place = self.place
        na, nb = place.sizes[1:]
        self.allow(2)
        last = [q for q, _ in others(place, 2)] if nb == 2 else list(range(nb))
        second = [q for q, _ in others(place, 1)] + [place.pos[1]] if na == 2 else list(range(na))
        if nb == 2:
            last.append(place.pos[2])
        for qb in last:
            for qa in second:
                for q0 in range(self.lo, self.hi):
                    q = (q0, qa, qb)
                    j = (q0 - self.lo) * place.half[0] + qa * place.half[1] + qb * place.half[2]
                    piece = self.land_core.at(j)
                    remote(
                        piece,
                        piece,
                        self.sems.at[0],
                        self.sems.at[self.count + j],
                        place.sibling,
                    ).wait_recv()
                    self.add(place.owner(q), self.land_core, j)
                    if qb is not place.pos[2]:
                        self.first(2, q)

    def along(self, dim):
        place = self.place
        n, p = place.sizes[dim], place.pos[dim]
        self.allow(dim - 1)
        if dim == 2:
            second = (
                [q for q, _ in others(place, 1)] + [place.pos[1]]
                if place.sizes[1] == 2
                else list(range(place.sizes[1]))
            )
            rows = [(q0, qa) for qa in second for q0 in range(self.lo, self.hi)]
        else:
            rows = [(q0,) for q0 in range(self.lo, self.hi)]

        def whole(row, at):
            return row + (at,) + place.pos[dim + 1 :]

        if n == 2:
            for row in rows:
                self.pull(dim, whole(row, p), 0)
                if row[dim - 1] is not place.pos[dim - 1]:
                    self.first(dim - 1, whole(row, p))
        else:
            for k in range(1, n):
                self.hop(dim, k, [whole(row, None) for row in rows])
            for row in rows:
                self.first(dim - 1, whole(row, p))

    def hop(self, dim, k, rows):
        place = self.place
        n, p = place.sizes[dim], place.pos[dim]
        lo, hi = (self.lo, self.hi) if dim == 0 else (0, n)
        for up in (True, False):
            here = k if up else n - 1 - k
            cond = p == here
            span = range(max(lo, here), hi) if up else range(lo, min(hi, here + 1))

            def receive(up=up, here=here, span=span):
                for row in rows:
                    for at in span:
                        slot = at - here if up else at + (n - here if here > 0 else 0)
                        self.pull(dim, row[:dim] + (at,) + row[dim + 1 :], slot)
                        if at != here:
                            q = row[:dim] + (at,) + row[dim + 1 :]
                            self.push_now(dim, q, up, here)

            pl.when(cond)(receive)
            for row in rows:
                for at in span:
                    if at != here:
                        q = row[:dim] + (at,) + row[dim + 1 :]
                        self.waits.append(
                            lambda cond=cond, q=q, up=up, here=here: pl.when(cond)(
                                lambda: self.hop_copy(dim, q, up, here).wait_send()
                            )
                        )

    def hop_copy(self, dim, q, up, here):
        place = self.place
        n = place.sizes[dim]
        u = self.unit(dim, q)
        slot = self.slot_up(q[dim], here) if up else self.slot_down(n, q[dim], here)
        target = u * landing(n) + slot
        return remote(
            self.units.at(place.owner(q)),
            self.lands[dim].at(self.land_at[dim] + target),
            self.sems.at[(self.up_at if up else self.down_at)[dim] + u * n + q[dim]],
            self.sems.at[self.recv_at[dim] + target],
            place.near(dim, up),
        )

    def push_now(self, dim, q, up, here):
        self.hop_copy(dim, q, up, here).start()

    def last(self, k):
        self.hop(0, k, [(None,) + self.place.pos[1:]])

    def finish(self):
        for wait in self.waits:
            wait()
        self.waits = []


class Ring:
    def __init__(self, me, devices, land, sems):
        self.after = (me + 1) % devices
        self.before = (me + devices - 1) % devices
        self.land, self.sems = land, sems

    def copies(self, to_before, to_after):
        return (
            remote(to_before, self.land.at[1], self.sems.at[0], self.sems.at[1], self.before),
            remote(to_after, self.land.at[0], self.sems.at[2], self.sems.at[3], self.after),
        )

    def start(self, to_before, to_after):
        for copy in self.copies(to_before, to_after):
            copy.start()

    def wait(self, to_before, to_after):
        for copy in self.copies(to_before, to_after):
            copy.wait_recv()

    def finish(self, to_before, to_after):
        for copy in self.copies(to_before, to_after):
            copy.wait_send()


def unit_shape(amount):
    across = min(amount, PANEL)
    return amount // across * BLOCK_ROWS, across * BLOCK_COLS


def own_unit(units, me, blocks):
    across = units.cols // BLOCK_COLS
    rows = []
    for a in range(units.rows // BLOCK_ROWS):
        row = [blocks[a * across + b].astype(bf16) for b in range(across)]
        rows.append(jnp.concatenate(row, axis=1))
    units.put(me, jnp.concatenate(rows, axis=0))


def network(
    idx_ref,
    pack_ref,
    blocks_ref,
    late_in,
    energy_ref,
    forces_ref,
    vector_ref,
    first_out,
    late_out,
    first_w,
    late_w,
    hot,
    z_t,
    z_r,
    geo,
    yrow,
    env_b,
    ee_t,
    en2_t,
    s1_t,
    s2_t,
    gam,
    dlt,
    coef,
    ds_t,
    de_t,
    dy,
    dg,
    dw_t,
    dw_r,
    dpf,
    den,
    lat,
    hid,
    low0,
    act1,
    sl1,
    low1,
    act2,
    sl2,
    low2,
    stage,
    halo,
    force_in,
    sides,
    vector_in,
    gather_sems,
    send_sems,
    late_sems,
    high_sems,
    low_sems,
    ring_sems,
    vector_sems,
    ready,
):
    s_r = dw_r
    fact = den

    wee_t = dw_t.at[:, 0:LATENT]
    we2_t = dw_t.at[0:128, 0:LATENT]
    devices = lax.axis_size("atoms")
    me = lax.axis_index("atoms")
    place = Place(devices)
    own_at = pack_ref.at[0:8]
    first_units = Units(first_w, *unit_shape(blocks_ref.shape[0]))
    late_units = Units(late_w, *unit_shape(late_in.shape[0]))
    gather_first = Gather(place, first_units, gather_sems.at[0], send_sems.at[0])
    gather_late = Gather(place, late_units, gather_sems.at[1], send_sems.at[1])
    middle = place.sizes[0] // 2
    top = place.sizes[0]
    sum_late = Reduce(place, late_units, 0, top, low2, sl2, late_sems, ready.at[0])
    sum_high = Reduce(place, first_units, middle, top, act2, sl1, high_sems, ready.at[1])
    sum_low = Reduce(place, first_units, 0, middle, low0, hid, low_sems, ready.at[2])
    link_halo = Ring(me, devices, halo, ring_sems.at[0])
    link_force = Ring(me, devices, force_in, ring_sems.at[1])

    barrier = pltpu.get_barrier_semaphore()

    def greet(j):
        pl.semaphore_signal(
            barrier, inc=1, device_id=((me + j + 1) % devices,), device_id_type=MESH
        )

    loop(devices - 1, greet)
    own_unit(first_units, me, blocks_ref)
    own_unit(late_units, me, late_in)
    pl.semaphore_wait(barrier, devices - 1)
    link_halo.start(own_at, own_at)
    gather_first.own(0, top, dims=(0,), core=False)
    gather_first.own(0, middle, dims=(2, 1))

    ids = lax.broadcasted_iota(jnp.int32, (3 * PLANE, LANES), 0)

    whole = PLANE * devices

    def find(t):
        near = idx_ref[:, lanes(t)] - (me - 1) * PLANE
        near = jnp.where(near < 0, near + whole, jnp.where(near >= whole, near - whole, near))
        hot[:, lanes(t)] = jnp.where(ids == near, 1.0, 0.0).astype(bf16)

    loop(TILES, find)
    link_halo.wait(own_at, own_at)
    own = pack_ref[0:8]
    lane = lax.broadcasted_iota(jnp.int32, (8, LANES), 1)
    row = lax.broadcasted_iota(jnp.int32, (8, LANES), 0)
    edge = spacing * devices
    x_row = row == 0
    before = halo[0] - jnp.where(x_row, jnp.where(me == 0, edge, 0.0), 0.0)
    after = halo[1] + jnp.where(x_row, jnp.where(me == devices - 1, edge, 0.0), 0.0)
    rank_y = ((lane & (PLANE - 1)) >> 3).astype(f32)
    rank_z = (lane & (SIDE - 1)).astype(f32)
    table = jnp.concatenate([jnp.where(lane < PLANE, before, own), after], axis=1)
    ranks = jnp.where(row == 4, rank_y, rank_z)
    table = jnp.where(
        jnp.concatenate([row, row], axis=1) < 4, table, jnp.concatenate([ranks, ranks], axis=1)
    )[:, : 3 * PLANE]
    ga, gb, gc = parts(table)
    got = nn(ga, hot[...]) + nn(gb, hot[...]) + nn(gc, hot[...])
    mine = jnp.concatenate([own] * TILES, axis=1)
    lane = lax.broadcasted_iota(jnp.int32, (1, ROWS), 1)
    slot = lane >> 6
    atom = lane & (PLANE - 1)

    def wrapped(step):
        return jnp.where(step > 1.5, -8.0, jnp.where(step < -1.5, 8.0, 0.0)) * spacing

    disp = [
        got[0:1] - mine[0:1],
        got[1:2] - mine[1:2] + wrapped(got[4:5] - (atom >> 3).astype(f32)),
        got[2:3] - mine[2:3] + wrapped(got[5:6] - (atom & (SIDE - 1)).astype(f32)),
    ]
    length = jnp.sqrt(disp[0] * disp[0] + disp[1] * disp[1] + disp[2] * disp[2])
    inverse = 1.0 / length
    unit = [disp[0] * inverse, disp[1] * inverse, disp[2] * inverse]
    angle = length * (math.pi / cutoff_radius)
    sin_k = [jnp.sin(angle)]
    cos_k = [jnp.cos(angle)]
    sin_k.append(2.0 * cos_k[0] * sin_k[0])
    cos_k.append(2.0 * cos_k[0] * cos_k[0] - 1.0)
    for k in range(2, BESSEL):
        sin_k.append(2.0 * cos_k[0] * sin_k[k - 1] - sin_k[k - 2])
        cos_k.append(2.0 * cos_k[0] * cos_k[k - 1] - cos_k[k - 2])
    sines = jnp.concatenate(sin_k, axis=0)
    cosines = jnp.concatenate(cos_k, axis=0)
    bessel = (math.sqrt(2.0 / cutoff_radius) * inverse) * sines
    scaled = length * (1.0 / cutoff_radius)
    t2 = scaled * scaled
    t4 = t2 * t2
    t5 = t4 * scaled
    t6 = t4 * t2
    envelope = 1.0 - 28.0 * t6 + 48.0 * (t6 * scaled) - 21.0 * (t4 * t4)
    denvelope = (-168.0 * t5 + 336.0 * t6 - 168.0 * (t6 * scaled)) * (1.0 / cutoff_radius)
    live = jnp.where(slot.astype(f32) < mine[4:5], 1.0, 0.0)

    kind = lax.broadcasted_iota(jnp.int32, (KINDS, LANES), 0).astype(f32)
    is_kind = kind == own[3:4]
    by_kind = own.T
    scale = jnp.sum(jnp.where(is_kind, by_kind[:KINDS, 6:7], 0.0), axis=0, keepdims=True)
    shift = jnp.sum(jnp.where(is_kind, by_kind[:KINDS, 7:8], 0.0), axis=0, keepdims=True)
    cot = jnp.concatenate([own[5:6] * scale] * TILES, axis=1) * live
    weight = cot * envelope

    root3 = math.sqrt(3.0)
    root15 = math.sqrt(15.0)
    root5 = math.sqrt(5.0)
    ux, uy, uz = unit
    yrow[0:8] = jnp.concatenate(
        [
            root3 * ux,
            root3 * uy,
            root3 * uz,
            root15 * ux * uy,
            root15 * uy * uz,
            0.5 * root5 * (3.0 * uz * uz - 1.0),
            root15 * ux * uz,
            0.5 * root15 * (ux * ux - uy * uy),
        ],
        axis=0,
    )
    yrow[8:16] = yrow[0:8] * (live * env_scale)
    yrow[16:17] = live * env_scale
    geo[0:8] = jnp.concatenate([ux, uy, uz, inverse, envelope, denvelope, live, cot], axis=0)
    geo[8:16] = math.sqrt(2.0 / cutoff_radius) * (
        (math.pi / cutoff_radius)
        * lax.broadcasted_iota(jnp.int32, (BESSEL, ROWS), 0).astype(f32)
        * cosines
        + (math.pi / cutoff_radius) * cosines
        - sines * inverse
    ) * inverse

    def one_hots(t):
        row = lax.broadcasted_iota(jnp.int32, (LANES, LANES), 0).astype(f32)
        here = jnp.where(row == own[3:4] + float(BESSEL), 1.0, 0.0)
        there = jnp.where(row == kinds_near[t] + float(BESSEL + SPECIES), 1.0, 0.0)
        return here + there

    kinds_near = [got[3:4, t * LANES : (t + 1) * LANES] for t in range(TILES)]
    for t in range(TILES):
        at = slice(t * LANES, (t + 1) * LANES)
        column = jnp.concatenate([bessel[:, at], one_hots(t)[BESSEL:]], axis=0)
        z_t[:, at] = column.astype(bf16)
        z_r[at, :] = column.T.astype(bf16)
        env_b[at, :] = jnp.broadcast_to(envelope[:, at], (LANES, LANES)).T
        fact[at, :] = jnp.broadcast_to(weight[:, at], (LANES, LANES)).T

    gather_first.line(0, middle)
    gather_first.line(middle, top, dims=(0,), core=False)
    gather_first.second(0, middle)
    gather_first.third(0, middle)
    gather_first.own(middle, top, dims=(2, 1))
    gather_first.line(middle, top, wait=False, dims=(2, 1))
    gather_first.across(0, middle)

    def twice(x):
        return jnp.concatenate([x] * (STRIP // LANES), axis=1)

    def in_body(n, r):
        pre = nn(z_r[r], cols_panel(first_w, W_INPUT, n))
        hid[r, panel(n, STRIP)] = (pre * sigmoid(pre)).astype(bf16)

    loop_panels(in_body)
    gather_first.second(middle, top)
    gather_late.own(0, top)

    def two_body(n, r):
        zero = nn(hid[r], cols_panel(first_w, W_TWO, n)) * twice(env_b[r])
        lat[r, panel(n, STRIP)] = zero
        low0[r, panel(n, STRIP)] = zero.astype(bf16)

    loop_panels(two_body)

    def transposed_product(out, weights, right, width=256):
        at = 0
        while at < ROWS:
            end = min(at + width, ROWS)
            out[:, at:end] = nt(weights, right[at:end, :])
            at = end

    gather_first.third(middle, top)
    gather_late.line(0, top, (1,))
    wee_t[0:128, :] = narrow(first_w, W_EMBED).T
    wee_t[128:256, :] = narrow(first_w, W_ENV_ONE).T
    transposed_product(ee_t, wee_t[...], low0)

    def environment(out, v0_ref, v0_at, v1_at):
        for m in range(9):
            total = None
            begin = v0_at if m == 0 else v1_at
            y = yrow[16:17, :] if m == 0 else yrow[7 + m : 8 + m, :]
            for t in range(TILES):
                at = slice(t * LANES, (t + 1) * LANES)
                term = v0_ref[begin : begin + CHANNELS, at] * y[:, at]
                total = term if total is None else total + term
            out[m] = halves(total)

    def put_scalars(t, s_t, rows):
        s_t[:, lanes(t)] = jnp.concatenate(rows, axis=0).astype(bf16)
        filled = jnp.concatenate(rows + [jnp.zeros_like(rows[0])], axis=0)
        flipped = filled.T.astype(bf16)
        s_r[lanes(t), :] = flipped

    def weighted(y, first, count, source, offset):
        total = None
        for m in range(count):
            term = y[first + m : first + m + 1] * source[offset + m]
            total = term if total is None else total + term
        return total

    gather_late.line(0, top, (2,))
    environment(gam, ee_t, 128, 192)

    def scalars_one(t):
        e0 = ee_t[0:64, lanes(t)]
        e1 = ee_t[64:128, lanes(t)]
        y = yrow[0:8, lanes(t)]
        put_scalars(
            t,
            s1_t,
            [e0 * gam[0], e1 * weighted(y, 0, 3, gam, 1), e1 * weighted(y, 3, 5, gam, 4)],
        )

    loop(TILES, scalars_one)

    gather_first.across(middle, top)
    gather_late.line(0, top, (3,))
    def pre_one(n, r):
        pre = nn(low0[r], cols_panel(first_w, W_LAT_ONE, n)) + nn(
            s_r[r, : 3 * CHANNELS], cols_panel(first_w, W_SCAL_ONE, n)
        )
        sig = sigmoid(pre)
        act = pre * sig
        act1[r, panel(n, STRIP)] = act.astype(bf16)
        sl1[r, panel(n, STRIP)] = (sig + act * (1.0 - sig)).astype(bf16)

    loop_panels(pre_one)
    gather_late.second(0, top)

    def out_one(n, r):
        new = (lat[r, panel(n, STRIP)] + nn(act1[r], cols_panel(first_w, W_OUT_ONE, n))) * half_root
        lat[r, panel(n, STRIP)] = new
        low1[r, panel(n, STRIP)] = new.astype(bf16)

    loop_panels(out_one)
    gather_late.third(0, top)
    we2_t[...] = narrow(first_w, W_ENV_TWO).T
    transposed_product(en2_t, we2_t[...], low1)
    environment(dlt, en2_t, 0, 64)

    g0 = gam[0]
    coef[0] = g0 * dlt[0]
    for m in range(3):
        a, b = 1 + (m + 1) % 3, 1 + (m + 2) % 3
        coef[1 + m] = g0 * dlt[1 + m] + (gam[a] * dlt[b] - gam[b] * dlt[a])
    coef[9] = gam[1] * dlt[1] + gam[2] * dlt[2] + gam[3] * dlt[3]
    second = None
    for m in range(4, 9):
        coef[m] = g0 * dlt[m]
        term = gam[m] * dlt[m]
        second = term if second is None else second + term
    coef[10] = second

    def scalars_two(t):
        e0 = ee_t[0:64, lanes(t)]
        e1 = ee_t[64:128, lanes(t)]
        y = yrow[0:8, lanes(t)]
        put_scalars(
            t,
            s2_t,
            [
                e0 * coef[0],
                e1 * weighted(y, 0, 3, coef, 1) + e0 * coef[9],
                e1 * weighted(y, 3, 5, coef, 4) + e0 * coef[10],
            ],
        )

    loop(TILES, scalars_two)

    gather_late.across(0, top)
    gather_first.finish()
    gather_late.finish()
    def pre_two(n, r):
        pre = nn(low1[r], cols_panel(late_w, W_LAT_TWO, n)) + nn(
            s_r[r, : 3 * CHANNELS], cols_panel(first_w, W_SCAL_TWO, n)
        )
        sig = sigmoid(pre)
        act = pre * sig
        act2[r, panel(n, STRIP)] = act.astype(bf16)
        sl2[r, panel(n, STRIP)] = (sig + act * (1.0 - sig)).astype(bf16)

    loop_panels(pre_two)

    def out_two(n, r):
        new = (lat[r, panel(n, STRIP)] + nn(act2[r], cols_panel(late_w, W_OUT_TWO, n))) * half_root
        low2[r, panel(n, STRIP)] = new.astype(bf16)

    loop_panels(out_two)

    vec = jnp.broadcast_to(pack_ref[8:9], (8, LANES))
    stage[...] = narrow(first_w, W_FINAL)

    def read_out(i):
        r = pl.ds(pl.multiple_of(i * 416, 16), 416)
        pre = nn(low2[r, :], stage[...])
        sig = sigmoid(pre)
        final_act = pre * sig
        dpf[r, :] = (fact[r, :] * vec[0:1] * (sig + final_act * (1.0 - sig))).astype(bf16)
        fact[r, :] = final_act

    loop(4, read_out)
    value = nt(vec, fact[...], highest)[0:1]
    geo_live = geo[6:7]
    geo_env = geo[4:5]
    geo_cot = geo[7:8]
    edge_energy = geo_live * geo_env * value
    summed = None
    for t in range(TILES):
        term = edge_energy[:, t * LANES : (t + 1) * LANES]
        summed = term if summed is None else summed + term
    energy_ref[...] = scale * halves(summed) + shift
    all_weights = jnp.broadcast_to(geo_cot * geo_env, (8, ROWS))
    vector_in[me] = nn(all_weights, fact[...], highest)

    def vector_copy(j, source):
        return remote(
            vector_in.at[me],
            vector_in.at[source],
            vector_sems.at[j],
            vector_sems.at[devices + source],
            (me + j) % devices,
        )

    loop(devices - 1, lambda i: vector_copy(i + 1, me).start())
    vector_waits = [
        lambda: loop(
            devices - 1,
            lambda i: vector_copy(i + 1, (me + devices - 1 - i) % devices).wait(),
        )
    ]
    geo[16:17] = geo_cot * value

    def big_grad(out, where, left, right):
        def step(i):
            grad = tn(left[:, panel(i, STRIP)], right[...])
            out[pl.ds(pl.multiple_of(where[0] + i * STRIP, 64), STRIP), :] = grad.astype(bf16)

        loop(LATENT // STRIP, step)

    def wide_grad(out, where, left, right):
        def step(n):
            out[where[0] : where[0] + where[1], panel(n)] = nn(
                left[...], right[:, panel(n)]
            ).astype(bf16)

        loop(4, step)

    def narrow_grad(left, right, put):
        def step(n):
            put(n, nn(left, right[:, panel(n)]).T.astype(bf16))

        loop(4, step)

    def put_narrow(where, n, grad):
        row = pl.multiple_of(where[0] + n // 2 * BLOCK_ROWS, BLOCK_ROWS)
        col = pl.multiple_of(n % 2 * 512, 512)
        first_w[pl.ds(row, BLOCK_ROWS), pl.ds(col, 512)] = jnp.concatenate(
            [grad[b * BLOCK_ROWS : (b + 1) * BLOCK_ROWS] for b in range(4)], axis=1
        )

    def put_stage(n, grad):
        stage[panel(n), :] = grad

    narrow_grad(dpf[...].T, low2, put_stage)

    def back_final(n, r):
        grad = nt(dpf[r], narrow_panel(first_w, W_FINAL, n)) * half_root
        lat[r, panel(n, STRIP)] = grad
        low2[r, panel(n, STRIP)] = grad.astype(bf16)

    loop_panels(back_final)
    loop(4, lambda n: put_narrow(W_FINAL, n, stage[panel(n), :]))

    def back_out_two(n, r):
        grad = nt(low2[r], rows_panel(late_w, W_OUT_TWO, n))
        sl2[r, panel(n, STRIP)] = (grad * sl2[r, panel(n, STRIP)].astype(f32)).astype(bf16)

    loop_panels(back_out_two)
    transposed_product(ds_t, first_w[W_SCAL_TWO[0] : W_SCAL_TWO[0] + W_SCAL_TWO[1], :], sl2)
    wide_grad(first_w, W_SCAL_TWO, s2_t, sl2)
    big_grad(late_w, W_OUT_TWO, act2, low2)

    dg[...] = jnp.zeros_like(dg)

    def tensors_two(t):
        e0 = ee_t[0:64, lanes(t)]
        e1 = ee_t[64:128, lanes(t)]
        y = yrow[0:8, lanes(t)]
        r0 = ds_t[0:64, lanes(t)]
        r1 = ds_t[64:128, lanes(t)]
        r2 = ds_t[128:192, lanes(t)]
        de_t[0:64, lanes(t)] = r0 * coef[0] + r1 * coef[9] + r2 * coef[10]
        de_t[64:128, lanes(t)] = r1 * weighted(y, 0, 3, coef, 1) + r2 * weighted(y, 3, 5, coef, 4)
        p1 = r1 * e1
        p2 = r2 * e1
        rows = []
        for m in range(8):
            p = p1 if m < 3 else p2
            rows.append(jnp.sum(p * coef[1 + m], axis=0, keepdims=True))
            dg[1 + m] += p * y[m : m + 1]
        dy[:, lanes(t)] = jnp.concatenate(rows, axis=0)
        dg[0] += r0 * e0
        dg[9] += r1 * e0
        dg[10] += r2 * e0

    loop(TILES, tensors_two)
    total = [halves(dg[m]) for m in range(11)]
    g0 = gam[0]
    d0 = dlt[0]
    new_g0 = total[0] * d0
    for m in range(1, 9):
        new_g0 = new_g0 + total[m] * dlt[m]
    dlt_grads = [total[0] * g0]
    gam_grads = [new_g0]
    for m in range(3):
        a, b = 1 + (m + 1) % 3, 1 + (m + 2) % 3
        dlt_grads.append(
            total[1 + m] * g0 + total[9] * gam[1 + m] + (total[a] * gam[b] - total[b] * gam[a])
        )
        gam_grads.append(total[9] * dlt[1 + m] + (dlt[a] * total[b] - dlt[b] * total[a]))
    for m in range(4, 9):
        dlt_grads.append(total[m] * g0 + total[10] * gam[m])
        gam_grads.append(total[10] * dlt[m])
    for m in range(9):
        dlt[m] = dlt_grads[m]
        dg[m] = gam_grads[m]

    def environment_back(t, grads, source, v1_at, at):
        y4 = yrow[8:16, lanes(t)]
        l4 = yrow[16:17, lanes(t)]
        v1 = source[v1_at : v1_at + 64, lanes(t)]
        low = l4 * grads[0]
        high = weighted(y4, 0, 8, grads, 1)
        both = jnp.concatenate([low, high], axis=0)
        dw_t[at : at + 128, lanes(t)] = both.astype(bf16)
        dw_r[lanes(t), at : at + 128] = both.T.astype(bf16)
        v1 = v1 * l4
        rows = [jnp.sum(v1 * grads[1 + m], axis=0, keepdims=True) for m in range(8)]
        dy[:, lanes(t)] += jnp.concatenate(rows, axis=0)

    loop(TILES, lambda t: environment_back(t, dlt, en2_t, 64, 128))

    def back_lat_two(n, r):
        grad = (
            lat[r, panel(n, STRIP)]
            + nt(sl2[r], rows_panel(late_w, W_LAT_TWO, n))
            + nt(dw_r[r, 128:256], narrow_panel(first_w, W_ENV_TWO, n))
        ) * half_root
        lat[r, panel(n, STRIP)] = grad
        act2[r, panel(n, STRIP)] = grad.astype(bf16)

    loop_panels(back_lat_two)
    big_grad(late_w, W_LAT_TWO, low1, sl2)
    narrow_grad(dw_t[128:256, :], low1, functools.partial(put_narrow, W_ENV_TWO))
    sum_late.start()

    def back_out_one(n, r):
        grad = nt(act2[r], rows_panel(first_w, W_OUT_ONE, n))
        sl1[r, panel(n, STRIP)] = (grad * sl1[r, panel(n, STRIP)].astype(f32)).astype(bf16)

    loop_panels(back_out_one)
    sum_late.pairs()
    big_grad(first_w, W_OUT_ONE, act1, act2)
    sum_late.along(2)
    transposed_product(ds_t, first_w[W_SCAL_ONE[0] : W_SCAL_ONE[0] + W_SCAL_ONE[1], :], sl1)
    wide_grad(first_w, W_SCAL_ONE, s1_t, sl1)
    sum_late.along(1)

    def tensors_one(t):
        e0 = ee_t[0:64, lanes(t)]
        e1 = ee_t[64:128, lanes(t)]
        y = yrow[0:8, lanes(t)]
        r0 = ds_t[0:64, lanes(t)]
        r1 = ds_t[64:128, lanes(t)]
        r2 = ds_t[128:192, lanes(t)]
        low = de_t[0:64, lanes(t)] + r0 * gam[0]
        high = (
            de_t[64:128, lanes(t)]
            + r1 * weighted(y, 0, 3, gam, 1)
            + r2 * weighted(y, 3, 5, gam, 4)
        )
        both = jnp.concatenate([low, high], axis=0)
        dw_t[0:128, lanes(t)] = both.astype(bf16)
        dw_r[lanes(t), 0:128] = both.T.astype(bf16)
        p1 = r1 * e1
        p2 = r2 * e1
        rows = []
        for m in range(8):
            p = p1 if m < 3 else p2
            rows.append(jnp.sum(p * gam[1 + m], axis=0, keepdims=True))
            coef[1 + m] += p * y[m : m + 1]
        dy[:, lanes(t)] += jnp.concatenate(rows, axis=0)
        coef[0] += r0 * e0

    for m in range(9):
        coef[m] = jnp.zeros((CHANNELS, LANES), f32)
    loop(TILES, tensors_one)
    for m in range(9):
        dg[m] = dg[m] + halves(coef[m])
    loop(TILES, lambda t: environment_back(t, dg, ee_t, 192, 128))
    sum_late.last(1)

    den[...] = jnp.zeros_like(den)

    def back_lat_one(n, r):
        both = jnp.concatenate(
            [narrow_panel(first_w, W_EMBED, n), narrow_panel(first_w, W_ENV_ONE, n)], axis=1
        )
        grad = (
            lat[r, panel(n, STRIP)]
            + nt(sl1[r], rows_panel(first_w, W_LAT_ONE, n))
            + nt(dw_r[r], both)
        )
        low1[r, panel(n, STRIP)] = (grad * twice(env_b[r])).astype(bf16)
        part = grad * low0[r, panel(n, STRIP)].astype(f32)
        for b in range(STRIP // LANES):
            den[r] += part[:, b * LANES : (b + 1) * LANES]

    loop_panels(back_lat_one)
    sum_late.last(2)
    big_grad(first_w, W_LAT_ONE, low0, sl1)
    sum_late.last(3)
    sum_high.start()
    narrow_grad(dw_t[0:128, :], low0, functools.partial(put_narrow, W_EMBED))
    narrow_grad(dw_t[128:256, :], low0, functools.partial(put_narrow, W_ENV_ONE))

    def back_two(n, r):
        grad = nt(low1[r], rows_panel(first_w, W_TWO, n))
        pre = nn(z_r[r], cols_panel(first_w, W_INPUT, n))
        sig = sigmoid(pre)
        act1[r, panel(n, STRIP)] = (grad * (sig + pre * sig * (1.0 - sig))).astype(bf16)

    loop_panels(back_two)
    sum_high.pairs()

    transposed_product(ds_t.at[0:64], first_w[0:64, :], act1)
    dbessel = ds_t[0:8, :]
    through = nt(jnp.ones((8, LANES), f32), den[...], highest)[0:1]
    ux, uy, uz = geo[0:1], geo[1:2], geo[2:3]
    inverse = geo[3:4]
    envelope = geo[4:5]
    denv = geo[16:17] + through / envelope
    dlength = jnp.sum(dbessel * geo[8:16], axis=0, keepdims=True) + denv * geo[5:6]
    g = [dy[m : m + 1, :] for m in range(8)]
    dux = root3 * g[0] + root15 * (uy * g[3] + uz * g[6] + ux * g[7])
    duy = root3 * g[1] + root15 * (ux * g[3] + uz * g[4] - uy * g[7])
    duz = root3 * g[2] + root15 * (uy * g[4] + ux * g[6]) + (3.0 * root5) * uz * g[5]
    along = dlength - (ux * dux + uy * duy + uz * duz) * inverse
    near = jnp.concatenate(
        [
            dux * inverse + ux * along,
            duy * inverse + uy * along,
            duz * inverse + uz * along,
            jnp.zeros((5, ROWS), f32),
        ],
        axis=0,
    )
    wide_grad(first_w, W_INPUT, z_t, act1)
    sum_high.along(2)
    summed = None
    for t in range(TILES):
        term = near[:, t * LANES : (t + 1) * LANES]
        summed = term if summed is None else summed + term
    centre = halves(summed)
    na, nb, nc = parts(near)
    spread = nt(na, hot[...]) + nt(nb, hot[...]) + nt(nc, hot[...])
    sides[0] = spread[:, :LANES]
    sides[1, :, 0:PLANE] = spread[:, LANES:]
    link_force.start(sides.at[0], sides.at[1])
    big_grad(first_w, W_TWO, hid, low1)
    sum_low.start()
    sum_high.along(1)
    sum_high.last(1)
    sum_low.pairs()
    sum_high.last(2)
    sum_low.along(2)
    sum_high.last(3)
    sum_low.along(1)
    link_force.wait(sides.at[0], sides.at[1])
    forces_ref[...] = (
        centre - pltpu.roll(sides[0], PLANE, 1) - force_in[1] - force_in[0]
    )
    for wait in vector_waits:
        wait()
    total = jnp.sum(vector_in[...], axis=0)
    normed = total * lax.rsqrt(jnp.sum(total[0:1] * total[0:1]) * (1.0 / FINAL) + epsilon)
    state = decay_rate * pack_ref[9:10] + (1.0 - decay_rate) * normed * normed
    vector_ref[0:1] = total[0:1]
    vector_ref[1:2] = state[0:1]
    vector_ref[2:3] = (pack_ref[8:9] - vector_rate * normed * lax.rsqrt(state + epsilon))[0:1]
    for k in range(1, 4):
        sum_low.last(k)

    first_out[...] = first_units.get(me)
    late_out[...] = late_units.get(me)
    for group in (sum_late, sum_high, sum_low):
        group.finish()
    link_halo.finish(own_at, own_at)
    link_force.finish(sides.at[0], sides.at[1])


def run_network(devices, idx, pack, blocks, late):
    S = jax.ShapeDtypeStruct
    wide = pltpu.VMEM((ROWS, LATENT), bf16)
    slab = pltpu.VMEM((ROWS, LANES), f32)
    panels = lambda amount: pltpu.VMEM((amount * devices // PANEL * BLOCK_ROWS, WIDE), bf16)
    scratch = [
        panels(blocks.shape[0]),
        panels(late.shape[0]),
        pltpu.VMEM((3 * PLANE, ROWS), bf16),
        pltpu.VMEM((LANES, ROWS), bf16),
        pltpu.VMEM((ROWS, LANES), bf16),
        pltpu.VMEM((24, ROWS), f32),
        pltpu.VMEM((24, ROWS), f32),
        slab,
        pltpu.VMEM((256, ROWS), f32),
        pltpu.VMEM((128, ROWS), f32),
        pltpu.VMEM((192, ROWS), bf16),
        pltpu.VMEM((192, ROWS), bf16),
        pltpu.VMEM((9, CHANNELS, LANES), f32),
        pltpu.VMEM((9, CHANNELS, LANES), f32),
        pltpu.VMEM((11, CHANNELS, LANES), f32),
        pltpu.VMEM((192, ROWS), f32),
        pltpu.VMEM((128, ROWS), f32),
        pltpu.VMEM((8, ROWS), f32),
        pltpu.VMEM((11, CHANNELS, LANES), f32),
        pltpu.VMEM((256, ROWS), bf16),
        pltpu.VMEM((ROWS, 256), bf16),
        pltpu.VMEM((ROWS, LANES), bf16),
        slab,
        pltpu.VMEM((ROWS, LATENT), f32),
    ] + [wide] * 8 + [
        pltpu.VMEM((LATENT, LANES), bf16),
        pltpu.VMEM((2, 8, LANES), f32),
        pltpu.VMEM((2, 8, LANES), f32),
        pltpu.VMEM((2, 8, LANES), f32),
        pltpu.VMEM((devices, 8, LANES), f32),
        pltpu.SemaphoreType.DMA((2, devices)),
        pltpu.SemaphoreType.DMA((2, Gather.sems(devices))),
        pltpu.SemaphoreType.DMA((Reduce.amount(devices, 4),)),
        pltpu.SemaphoreType.DMA((Reduce.amount(devices, 2),)),
        pltpu.SemaphoreType.DMA((Reduce.amount(devices, 2),)),
        pltpu.SemaphoreType.DMA((2, 4)),
        pltpu.SemaphoreType.DMA((2 * devices,)),
        pltpu.SemaphoreType.REGULAR((3, 7)),
    ]
    vmem = pl.BlockSpec(memory_space=pltpu.VMEM)
    return pl.pallas_call(
        network,
        out_shape=[
            S((1, LANES), f32),
            S((8, LANES), f32),
            S((8, LANES), f32),
            S(unit_shape(blocks.shape[0]), bf16),
            S(unit_shape(late.shape[0]), bf16),
        ],
        in_specs=[vmem] * 4,
        out_specs=[vmem] * 5,
        scratch_shapes=scratch,
        compiler_params=pltpu.CompilerParams(
            vmem_limit_bytes=63 << 20, collective_id=0, has_side_effects=True
        ),
        name="network",
    )(idx, pack, blocks, late)


def shampoo(
    energy,
    force,
    vectors,
    grads,
    left,
    right,
    left_root,
    right_root,
    master,
    late_grads,
    late_left,
    late_right,
    late_left_root,
    late_right_root,
    late_master,
    energy_out,
    force_out,
    vector_out,
    state_out,
    moved_out,
    *outs,
):
    energy_out[...] = energy[:, :PLANE]
    force_out[...] = force[0:3, :PLANE]
    vector_out[...] = vectors[0:1]
    state_out[...] = vectors[1:2]
    moved_out[...] = vectors[2:3]

    def block(panels, j, left, right, left_root, right_root, master, out):
        grad_out, left_out, right_out, master_out = out
        per = panels.shape[1] // BLOCK_COLS
        at = pl.program_id(0) * left.shape[0] + j
        row = pl.multiple_of(at // per * BLOCK_ROWS, BLOCK_ROWS)
        col = pl.multiple_of(at % per * BLOCK_COLS, BLOCK_COLS)
        held = panels[pl.ds(row, BLOCK_ROWS), pl.ds(col, BLOCK_COLS)]
        grad = held.astype(f32)
        grad_out[j] = grad
        size = 1.0 / (BLOCK_ROWS * BLOCK_COLS)
        scale = lax.rsqrt(jnp.sum(grad * grad, keepdims=True) * size + epsilon)
        square = (1.0 - decay_rate) * scale * scale
        left_out[j] = decay_rate * left[j] + square * nt(held, held)
        right_out[j] = decay_rate * right[j] + square * tn(held, held)
        la, lb, _ = parts(left_root[j])
        ra, rb, _ = parts(right_root[j])
        turned = (nn(la, held) + nn(lb, held)) * scale
        ta, tb, _ = parts(turned)
        step = nn(ta, ra) + (nn(ta, rb) + nn(tb, ra))
        slope = lax.rsqrt(jnp.sum(step * step, keepdims=True) * size + epsilon)
        master_out[j] = master[j] - (learn_rate * slope) * step

    for j in range(left.shape[0]):
        block(grads, j, left, right, left_root, right_root, master, outs[:4])
    for j in range(late_left.shape[0]):
        block(
            late_grads,
            j,
            late_left,
            late_right,
            late_left_root,
            late_right_root,
            late_master,
            outs[4:],
        )


def run_shampoo(energy, force, vectors, first, late):
    S = jax.ShapeDtypeStruct
    steps = min(4, late[1].shape[0])

    def whole(x):
        return pl.BlockSpec(x.shape, lambda i: (0,) * len(x.shape))

    def share(x):
        return pl.BlockSpec((x.shape[0] // steps,) + x.shape[1:], lambda i: (i, 0, 0))

    small = [S((1, PLANE), f32), S((3, PLANE), f32)] + [S((1, FINAL), f32)] * 3
    grown = []
    for group in (first, late):
        left, right, _, _, master = group[1:]
        grown += [S(x.shape, f32) for x in (master, left, right, master)]
    return pl.pallas_call(
        shampoo,
        grid=(steps,),
        out_shape=small + grown,
        in_specs=[whole(energy), whole(force), whole(vectors)]
        + [whole(first[0])]
        + [share(x) for x in first[1:]]
        + [whole(late[0])]
        + [share(x) for x in late[1:]],
        out_specs=[whole(x) for x in small] + [share(x) for x in grown],
        compiler_params=pltpu.CompilerParams(vmem_limit_bytes=32 << 20),
        name="shampoo",
    )(energy, force, vectors, *first, *late)


def local(
    positions,
    species,
    neighbours,
    counts,
    species_scale,
    species_shift,
    energy_cot,
    blocks,
    left,
    right,
    left_root,
    right_root,
    late_blocks,
    late_left,
    late_right,
    late_left_root,
    late_right_root,
    out_vector,
    vector_state,
):
    devices = lax.axis_size("atoms")
    small = [
        positions,
        species.astype(f32)[None],
        counts.astype(f32)[None],
        energy_cot[None],
    ]
    small = jnp.concatenate(small, axis=0)
    room = ((0, LANES - SPECIES),)
    pack = jnp.concatenate(
        [
            jnp.concatenate([small, small], axis=1),
            jnp.pad(species_scale, room)[None],
            jnp.pad(species_shift, room)[None],
            out_vector[None],
            vector_state[None],
            jnp.zeros((6, LANES), f32),
        ],
        axis=0,
    )
    idx = neighbours.reshape(PLANE, SLOTS).T.reshape(1, ROWS)
    energy, force, vectors, first_units, late_units = run_network(
        devices, idx, pack, blocks, late_blocks
    )
    out = run_shampoo(
        energy,
        force,
        vectors,
        (first_units, left, right, left_root, right_root, blocks),
        (late_units, late_left, late_right, late_left_root, late_right_root, late_blocks),
    )
    energies, forces, vector_grad, new_state, new_vector = out[:5]
    return (
        energies.reshape(-1),
        forces,
        *out[5:],
        vector_grad.reshape(-1),
        new_state.reshape(-1),
        new_vector.reshape(-1),
    )


def solution(mesh):
    row = P("atoms")
    block = P("atoms", None, None)
    placed = (
        (P(None, "atoms"), row, row, row, P(), P(), row)
        + (block,) * 10
        + (P(), P())
    )
    return jax.shard_map(
        local,
        mesh=mesh,
        in_specs=placed,
        out_specs=(row, P(None, "atoms")) + (block,) * 8 + (P(), P(), P()),
        check_vma=False,
    )
```

```python
import functools
import math

import jax
import jax.numpy as jnp
from jax import lax
from jax.experimental import pallas as pl
from jax.experimental.pallas import tpu as pltpu
from jax.sharding import PartitionSpec as P

SIDE = 8
SLOTS = 26
SPECIES = 60
BESSEL = 8
CHANNELS = 64
LATENT = 1024
FINAL = 128
BLOCK_ROWS = 64
BLOCK_COLS = 128
PLANE = SIDE * SIDE

f32 = jnp.float32
bf16 = jnp.bfloat16
highest = lax.Precision.HIGHEST
spacing = 1.6
cutoff_radius = 4.0
env_scale = 0.25
half_root = 0.7071067811865476
decay_rate = 0.5
learn_rate = 0.02
vector_rate = 0.03
epsilon = 1e-06

LANES = 128
ROWS = SLOTS * PLANE
TILES = ROWS // LANES
KINDS = 64

PANEL = 8
WIDE = PANEL * BLOCK_COLS
W_INPUT = (0, 128)
W_TWO = (128, 1024)
W_EMBED = (1152, 128)
W_ENV_ONE = (1280, 128)
W_LAT_ONE = (1408, 1024)
W_SCAL_ONE = (2432, 192)
W_OUT_ONE = (2624, 1024)
W_ENV_TWO = (3648, 128)
W_SCAL_TWO = (3776, 192)
W_FINAL = (3968, 128)
W_LAT_TWO = (0, 1024)
W_OUT_TWO = (1024, 1024)

MESH = pl.DeviceIdType.MESH


def nn(a, b, precision=None):
    return lax.dot_general(
        a, b, (((1,), (0,)), ((), ())), preferred_element_type=f32, precision=precision
    )


def nt(a, b, precision=None):
    return lax.dot_general(
        a, b, (((1,), (1,)), ((), ())), preferred_element_type=f32, precision=precision
    )


def tn(a, b):
    return lax.dot_general(a, b, (((0,), (0,)), ((), ())), preferred_element_type=f32)


def cols_panel(ref, where, n):
    return ref[where[0] : where[0] + where[1], panel(n, STRIP)]


def rows_panel(ref, where, n):
    return ref[pl.ds(pl.multiple_of(where[0] + n * STRIP, 64), STRIP), :]


def narrow(ref, where):
    pieces = []
    for j in range(LATENT // BLOCK_ROWS):
        row = where[0] + j // PANEL * BLOCK_ROWS
        col = j % PANEL * BLOCK_COLS
        pieces.append(ref[row : row + BLOCK_ROWS, col : col + BLOCK_COLS])
    return jnp.concatenate(pieces, axis=0)


def narrow_panel(ref, where, n):
    part = ref[pl.ds(pl.multiple_of(where[0] + n * BLOCK_ROWS, BLOCK_ROWS), BLOCK_ROWS), :]
    return jnp.concatenate([part[:, b * 128 : (b + 1) * 128] for b in range(PANEL)], axis=0)


def sigmoid(x):
    return 0.5 * jnp.tanh(0.5 * x) + 0.5


def halves(x):
    return x + pltpu.roll(x, PLANE, 1)


def lanes(t):
    return pl.ds(pl.multiple_of(t * LANES, LANES), LANES)


def panel(n, width=256):
    return pl.ds(pl.multiple_of(n * width, width), width)


STRIP = 512
CHUNKS = 2
PIECES = 4
CHUNK = ROWS // CHUNKS


def loop_panels(body):
    def step(n):
        for c in range(CHUNKS):
            body(n, slice(c * CHUNK, (c + 1) * CHUNK))

    loop(LATENT // STRIP, step)


def loop(count, body):
    def step(i, carry):
        body(i)
        return carry

    lax.fori_loop(0, count, step, 0)


def parts(x):
    a = x.astype(bf16)
    rest = x - a.astype(f32)
    b = rest.astype(bf16)
    c = (rest - b.astype(f32)).astype(bf16)
    return a, b, c


class Place:
    def __init__(self, devices):
        side = math.isqrt(devices // 8)
        self.devices = devices
        self.sizes = (4, side, side)
        me = lax.axis_index("atoms")
        core = me % 2
        chip = me // 2
        last = chip % side
        middle = chip // side % side
        self.me = me
        self.core = core
        self.pos = (
            chip // (side * side),
            last + core * (middle - last),
            middle + core * (last - middle),
        )
        self.half = (side * side, 1 + core * (side - 1), side + core * (1 - side))
        self.step = tuple(2 * h for h in self.half)
        self.sibling = me + 1 - 2 * core
        self.plain = (self.pos[0], middle, last)
        self.plain_step = (2 * side * side, 2 * side, 2)

    def owner(self, q):
        return q[0] * self.step[0] + q[1] * self.step[1] + q[2] * self.step[2] + self.core

    def near(self, dim, up):
        return self.me + self.step[dim] if up else self.me - self.step[dim]

    def has(self, dim, up):
        return self.pos[dim] < self.sizes[dim] - 1 if up else self.pos[dim] > 0

    def peers(self, dim):
        n, p = self.sizes[dim], self.plain[dim]
        return [(r, (p + r) % n, self.me + ((p + r) % n - p) * self.plain_step[dim]) for r in range(1, n)]


class Units:
    def __init__(self, ref, rows, cols, base=0, part=(0, 1)):
        self.ref, self.rows, self.cols = ref, rows, cols
        self.per = WIDE // cols
        self.base = base
        self.high = rows // part[1]
        self.off = part[0] * self.high

    def window(self, s):
        s = s + self.base
        if self.per == 1:
            row, col = s * self.rows, slice(None)
        else:
            row = s // self.per * self.rows
            col = pl.ds(pl.multiple_of(s % self.per * self.cols, self.cols), self.cols)
        return (pl.ds(pl.multiple_of(row + self.off, 16), self.high), col)

    def at(self, s):
        return self.ref.at[self.window(s)]

    def get(self, s):
        return self.ref[self.window(s)]

    def put(self, s, value):
        self.ref[self.window(s)] = value


def remote(src, dst, send, recv, device):
    return pltpu.make_async_remote_copy(
        src_ref=src,
        dst_ref=dst,
        send_sem=send,
        recv_sem=recv,
        device_id=(device,),
        device_id_type=MESH,
    )


def signal(sem, device):
    pl.semaphore_signal(sem, inc=1, device_id=(device,), device_id_type=MESH)


def others(place, dim):
    n, p = place.sizes[dim], place.pos[dim]
    if n == 2:
        return [(1 - p, None)]
    found = []
    for distance in range(1, n):
        found.append((p - distance, p >= distance))
        found.append((p + distance, p < n - distance))
    return found


def gated(cond, body):
    if cond is None:
        body()
    else:
        pl.when(cond)(body)


def both(a, b):
    return b if a is None else (a if b is None else a & b)


class Gather:
    def __init__(self, place, units, lo, hi, sems):
        self.place, self.units, self.lo, self.hi, self.sems = place, units, lo, hi, sems
        _, na, nb = place.sizes
        self.waits = []
        self.first_owner = 2 * lo * na * nb
        at = 2 * (hi - lo) * na * nb
        self.base = []
        for dim in range(3):
            length = (hi - lo) * (1, na, na * nb)[dim]
            self.base.append((at, at + length))
            at += 2 * length
        self.core_base = at

    @staticmethod
    def amount(devices, share):
        side = math.isqrt(devices // 8)
        return share * (2 + 2 * side + 5 * side * side)

    def linear(self, q, dim):
        _, na, nb = self.place.sizes
        q0 = q[0] - self.lo
        return (q0, q0 * na + q[1], (q0 * na + q[1]) * nb + q[2])[dim]

    def emit(self, cond, q, sem, device):
        owner = self.place.owner(q)

        def copy():
            piece = self.units.at(owner)
            return remote(
                piece, piece, self.sems.at[sem], self.sems.at[owner - self.first_owner], device
            )

        gated(cond, lambda: copy().start())
        self.waits.append(lambda: gated(cond, lambda: copy().wait_send()))

    def forward(self, cond, q, via, arrived):
        place = self.place
        for dim in (0, 2, 1):
            if dim < via or (arrived and dim == via and place.sizes[dim] == 2):
                continue
            if place.sizes[dim] == 2:
                toward = place.me + (1 - 2 * place.pos[dim]) * place.step[dim]
                self.emit(cond, q, self.base[dim][0] + self.linear(q, dim), toward)
                continue
            for up in (True, False):
                open_end = place.has(dim, up)
                if arrived and dim == via:
                    p = place.pos[dim]
                    open_end = open_end & ((q[dim] < p) if up else (q[dim] > p))
                self.emit(
                    both(cond, open_end),
                    q,
                    self.base[dim][0 if up else 1] + self.linear(q, dim),
                    place.near(dim, up),
                )
        self.emit(cond, q, self.core_base + self.linear(q, 2), place.sibling)

    def wait(self, cond, owner):
        piece = self.units.at(owner)
        gated(
            cond,
            lambda: remote(
                piece,
                piece,
                self.sems.at[self.core_base],
                self.sems.at[owner - self.first_owner],
                self.place.sibling,
            ).wait_recv(),
        )

    def own(self):
        p = self.place.pos
        cond = None
        if self.hi - self.lo != self.place.sizes[0]:
            cond = (p[0] >= self.lo) & (p[0] < self.hi)
        self.forward(cond, p, 0, False)

    def take(self, cond, q, via):
        self.wait(cond, self.place.owner(q))
        self.forward(cond, q, via, True)

    def line(self, distances=(1, 2, 3)):
        p = self.place.pos
        for distance in distances:
            for q0 in (p[0] - distance, p[0] + distance):
                self.take((q0 >= self.lo) & (q0 < self.hi), (q0, p[1], p[2]), 0)

    def second(self):
        for q0 in range(self.lo, self.hi):
            for qa, there in others(self.place, 1):
                self.take(there, (q0, qa, self.place.pos[2]), 1)

    def third(self):
        for qb, there in others(self.place, 2):
            for q0 in range(self.lo, self.hi):
                for qa in range(self.place.sizes[1]):
                    self.take(there, (q0, qa, qb), 2)

    def across(self):
        place = self.place
        per = place.sizes[1] * place.sizes[2]

        def body(j):
            self.wait(None, 2 * (self.lo * per + j) + 1 - place.core)

        loop((self.hi - self.lo) * per, body)

    def finish(self):
        for wait in self.waits:
            wait()
        self.waits = []


def landing(n):
    return 1 if n == 2 else n + 1


class Reduce:
    def __init__(self, place, units, lo, hi, land, sems, ready):
        self.place, self.units, self.lo, self.hi, self.land = place, units, lo, hi, land
        n0, na, nb = place.sizes
        self.count = (hi - lo) * na * nb
        lines = ((1, n0), (hi - lo, na), ((hi - lo) * na, nb))
        z_at = self.count
        b_at = z_at + landing(n0)
        a_at = b_at + lines[2][0] * landing(nb)
        self.land_at = (z_at, a_at, b_at)
        self.sems, self.ready = sems, ready
        at = 2 * self.count
        self.recv_at, self.up_at, self.down_at = [], [], []
        for units_here, n in lines:
            self.recv_at.append(at)
            at += units_here * landing(n)
            self.up_at.append(at)
            at += units_here * n
            self.down_at.append(at)
            at += units_here * n
        self.waits = []

    @staticmethod
    def slots(devices, share):
        side = math.isqrt(devices // 8)
        return share * side * side + landing(4) + share * (1 + side) * landing(side)

    @staticmethod
    def amount(devices, share):
        side = math.isqrt(devices // 8)
        total = 2 * share * side * side
        for units_here, n in ((1, 4), (share, side), (share * side, side)):
            total += units_here * (landing(n) + 2 * n)
        return total

    def stage(self, k):
        if k == 0:
            self.start()
        elif k == 1:
            self.pairs()
        elif k < 4:
            self.along(4 - k)
        else:
            self.hop(0, k - 3, [(None,) + self.place.pos[1:]])

    def unit(self, dim, q):
        na = self.place.sizes[1]
        return (0, q[0] - self.lo, (q[0] - self.lo) * na + q[1])[dim]

    def add(self, owner, slot):
        self.units.put(owner, self.units.get(owner) + self.land.get(slot))

    def start(self):
        place = self.place
        if self.ready is not None:
            signal(self.ready.at[0], place.sibling)
            for dim in range(3):
                for up in (True, False):
                    pl.when(place.has(dim, up))(
                        lambda dim=dim, up=up: signal(
                            self.ready.at[1 + 2 * dim + (1 if up else 0)], place.near(dim, up)
                        )
                    )
            pl.semaphore_wait(self.ready.at[0], 1)
        per = place.sizes[1] * place.sizes[2]

        def copy(j):
            owner = 2 * (self.lo * per + j) + 1 - place.core
            return remote(
                self.units.at(owner),
                self.land.at(j),
                self.sems.at[j],
                self.sems.at[self.count + j],
                place.sibling,
            )

        loop(self.count, lambda j: copy(j).start())
        self.waits.append(lambda: loop(self.count, lambda j: copy(j).wait_send()))

    def allow(self, dim):
        if self.ready is None:
            return
        for up in (True, False):
            pl.when(self.place.has(dim, up))(
                lambda up=up: pl.semaphore_wait(self.ready.at[1 + 2 * dim + (0 if up else 1)], 1)
            )

    def push(self, cond, dim, q, sem, slot, device):
        owner = self.place.owner(q)
        target = self.unit(dim, q) * landing(self.place.sizes[dim]) + slot

        def copy():
            return remote(
                self.units.at(owner),
                self.land.at(self.land_at[dim] + target),
                self.sems.at[sem],
                self.sems.at[self.recv_at[dim] + target],
                device,
            )

        gated(cond, lambda: copy().start())
        self.waits.append(lambda: gated(cond, lambda: copy().wait_send()))

    def pull(self, dim, q, slot):
        target = self.unit(dim, q) * landing(self.place.sizes[dim]) + slot
        piece = self.land.at(self.land_at[dim] + target)
        remote(
            piece,
            piece,
            self.sems.at[0],
            self.sems.at[self.recv_at[dim] + target],
            self.place.sibling,
        ).wait_recv()
        self.add(self.place.owner(q), self.land_at[dim] + target)

    def first(self, dim, q):
        place = self.place
        n, p = place.sizes[dim], place.pos[dim]
        u = self.unit(dim, q)
        if n == 2:
            toward = place.me + (1 - 2 * p) * place.step[dim]
            self.push(None, dim, q, self.up_at[dim] + u * n, 0, toward)
            return
        for up in (True, False):
            away = (q[dim] > 0) if up else (q[dim] < n - 1)
            self.push(
                (p == (0 if up else n - 1)) & away,
                dim,
                q,
                (self.up_at if up else self.down_at)[dim] + u * n + q[dim],
                self.slot_up(q[dim], 0) if up else self.slot_down(n, q[dim], n - 1),
                place.near(dim, up),
            )

    @staticmethod
    def slot_up(q, p):
        return q - (p + 1)

    @staticmethod
    def slot_down(n, q, p):
        to = p - 1
        return q + (n - to if to > 0 else 0)

    def order(self, dim):
        place = self.place
        if place.sizes[dim] == 2:
            return [1 - place.pos[dim], place.pos[dim]]
        return list(range(place.sizes[dim]))

    def mine(self, dim, at):
        return at is self.place.pos[dim]

    def pairs(self):
        place = self.place
        self.allow(2)
        for qb in self.order(2):
            for qa in self.order(1):
                for q0 in range(self.lo, self.hi):
                    q = (q0, qa, qb)
                    j = (q0 - self.lo) * place.half[0] + qa * place.half[1] + qb * place.half[2]
                    piece = self.land.at(j)
                    remote(
                        piece,
                        piece,
                        self.sems.at[0],
                        self.sems.at[self.count + j],
                        place.sibling,
                    ).wait_recv()
                    self.add(place.owner(q), j)
                    if not self.mine(2, qb):
                        self.first(2, q)

    def along(self, dim):
        place = self.place
        n, p = place.sizes[dim], place.pos[dim]
        self.allow(dim - 1)
        if dim == 2:
            rows = [(q0, qa) for qa in self.order(1) for q0 in range(self.lo, self.hi)]
        else:
            rows = [(q0,) for q0 in range(self.lo, self.hi)]

        def whole(row, at):
            return row + (at,) + place.pos[dim + 1 :]

        if n == 2:
            for row in rows:
                self.pull(dim, whole(row, p), 0)
                if not self.mine(dim - 1, row[dim - 1]):
                    self.first(dim - 1, whole(row, p))
        else:
            for k in range(1, n):
                self.hop(dim, k, [whole(row, None) for row in rows])
            for row in rows:
                self.first(dim - 1, whole(row, p))

    def hop(self, dim, k, rows):
        place = self.place
        n, p = place.sizes[dim], place.pos[dim]
        lo, hi = (self.lo, self.hi) if dim == 0 else (0, n)
        for up in (True, False):
            here = k if up else n - 1 - k
            cond = p == here
            span = range(max(lo, here), hi) if up else range(lo, min(hi, here + 1))
            if len(span) == 0:
                continue

            def receive(up=up, here=here, span=span):
                for row in rows:
                    for at in span:
                        slot = at - here if up else at + (n - here if here > 0 else 0)
                        q = row[:dim] + (at,) + row[dim + 1 :]
                        self.pull(dim, q, slot)
                        if at != here:
                            self.hop_copy(dim, q, up, here).start()

            pl.when(cond)(receive)
            for row in rows:
                for at in span:
                    if at != here:
                        q = row[:dim] + (at,) + row[dim + 1 :]
                        self.waits.append(
                            lambda cond=cond, q=q, up=up, here=here: pl.when(cond)(
                                lambda: self.hop_copy(dim, q, up, here).wait_send()
                            )
                        )

    def hop_copy(self, dim, q, up, here):
        place = self.place
        n = place.sizes[dim]
        u = self.unit(dim, q)
        slot = self.slot_up(q[dim], here) if up else self.slot_down(n, q[dim], here)
        target = u * landing(n) + slot
        return remote(
            self.units.at(place.owner(q)),
            self.land.at(self.land_at[dim] + target),
            self.sems.at[(self.up_at if up else self.down_at)[dim] + u * n + q[dim]],
            self.sems.at[self.recv_at[dim] + target],
            place.near(dim, up),
        )

    def finish(self):
        for wait in self.waits:
            wait()
        self.waits = []


class Total:
    def __init__(self, place, land, sems):
        self.place, self.land, self.sems = place, land, sems
        self.sizes = (2,) + place.sizes[::-1]
        self.at = [sum(self.sizes[:k]) for k in range(4)]
        self.waits = []

    @staticmethod
    def slots(devices):
        return 6 + 2 * math.isqrt(devices // 8)

    def lines(self, k):
        place = self.place
        if k == 0:
            return place.core, [(1, 1 - place.core, place.sibling)]
        return place.plain[3 - k], place.peers(3 - k)

    def send(self, k, value):
        p, peers = self.lines(k)
        here = self.land.at[self.at[k] + p]
        self.land[self.at[k] + p] = value
        half = self.at[3] + self.sizes[3]
        for r, _, device in peers:

            def copy(r=r, device=device):
                sems = self.sems
                return remote(
                    here, here, sems.at[self.at[k] + r], sems.at[half + self.at[k] + p], device
                )

            copy().start()
            self.waits.append(lambda copy=copy: copy().wait_send())

    def take(self, k):
        _, peers = self.lines(k)
        half = self.at[3] + self.sizes[3]
        for r, at, device in peers:
            there = self.land.at[self.at[k] + at]
            remote(
                there, there, self.sems.at[0], self.sems.at[half + self.at[k] + at], device
            ).wait_recv()
        total = self.land[self.at[k]]
        for s in range(1, self.sizes[k]):
            total = total + self.land[self.at[k] + s]
        return total

    def pass_on(self, k):
        value = self.take(k)
        if k < 3:
            self.send(k + 1, value)
        return value

    def finish(self):
        for wait in self.waits:
            wait()
        self.waits = []


class Ring:
    def __init__(self, me, devices, land, sems):
        self.after = (me + 1) % devices
        self.before = (me + devices - 1) % devices
        self.land, self.sems = land, sems

    def copies(self, to_before, to_after):
        return (
            remote(to_before, self.land.at[1], self.sems.at[0], self.sems.at[1], self.before),
            remote(to_after, self.land.at[0], self.sems.at[2], self.sems.at[3], self.after),
        )

    def start(self, to_before, to_after):
        for copy in self.copies(to_before, to_after):
            copy.start()

    def wait(self, to_before, to_after):
        for copy in self.copies(to_before, to_after):
            copy.wait_recv()

    def finish(self, to_before, to_after):
        for copy in self.copies(to_before, to_after):
            copy.wait_send()


def unit_shape(amount):
    across = min(amount, PANEL)
    return amount // across * BLOCK_ROWS, across * BLOCK_COLS


def own_unit(units, me, blocks):
    across = units.cols // BLOCK_COLS
    rows = []
    for a in range(units.rows // BLOCK_ROWS):
        row = [blocks[a * across + b].astype(bf16) for b in range(across)]
        rows.append(jnp.concatenate(row, axis=1))
    units.put(me, jnp.concatenate(rows, axis=0))


def network(
    idx_ref,
    positions_ref,
    species_ref,
    counts_ref,
    cot_ref,
    scale_ref,
    shift_ref,
    weight_ref,
    state_ref,
    blocks_ref,
    late_in,
    energy_ref,
    forces_ref,
    vector_ref,
    first_out,
    late_out,
    first_w,
    late_w,
    hot,
    z_t,
    z_r,
    geo,
    yrow,
    env_b,
    ee_t,
    en2_t,
    s1_t,
    s2_t,
    gam,
    dlt,
    coef,
    ds_t,
    de_t,
    dy,
    dg,
    dw_t,
    dw_r,
    dpf,
    den,
    lat,
    hid,
    low0,
    act1,
    sl1,
    low1,
    act2,
    sl2,
    low2,
    stage,
    halo,
    force_in,
    sides,
    vector_in,
    pack_ref,
    low_gather,
    mid_gather,
    high_gather,
    late_gather,
    late_sems,
    first_sems,
    low_sems,
    ring_sems,
    vector_sems,
    ready,
):
    s_r = dw_r
    fact = den

    wee_t = dw_t.at[:, 0:LATENT]
    we2_t = dw_t.at[0:128, 0:LATENT]
    devices = lax.axis_size("atoms")
    me = lax.axis_index("atoms")
    place = Place(devices)
    own_at = pack_ref.at[0:8]
    first_units = Units(first_w, *unit_shape(blocks_ref.shape[0]))
    late_units = Units(late_w, *unit_shape(late_in.shape[0]))
    top = place.sizes[0]
    middle = top // 2

    def pieces(k):
        return Units(first_w, first_units.rows, first_units.cols, part=(k, PIECES))

    def free(ref, units, k=0, count=1):
        slots = Reduce.slots(devices, 1)
        return Units(ref, units.rows // count, units.cols, base=k * slots)

    gather_low = [Gather(place, pieces(k), 0, 1, low_gather.at[k]) for k in range(PIECES)]
    gather_mid = Gather(place, first_units, 1, middle, mid_gather)
    gather_high = Gather(place, first_units, middle, top, high_gather)
    gather_late = Gather(place, late_units, 0, top, late_gather)
    sum_out = Reduce(
        place, late_units, middle, top, free(low2, late_units), late_sems.at[0], ready.at[0]
    )
    sum_lat = Reduce(
        place, late_units, 0, middle, free(sl2, late_units), late_sems.at[1], ready.at[1]
    )
    sum_first = {
        z: Reduce(place, first_units, z, z + 1, free(ref, first_units), first_sems.at[z - 1], ready.at[z + 1])
        for z, ref in ((3, act2), (2, sl1), (1, low0))
    }
    sum_low = [
        Reduce(
            place,
            pieces(k),
            0,
            1,
            free(hid, first_units, k, PIECES),
            low_sems.at[k],
            ready.at[5] if k == 0 else None,
        )
        for k in range(PIECES)
    ]
    link_halo = Ring(me, devices, halo, ring_sems.at[0])
    link_force = Ring(me, devices, force_in, ring_sems.at[1])
    sum_vector = Total(place, vector_in, vector_sems)

    barrier = pltpu.get_barrier_semaphore()
    partners = [place.sibling, link_halo.before, link_halo.after]
    for dim in range(3):
        partners += [device for _, _, device in place.peers(dim)]
    for device in partners:
        signal(barrier, device)
    for part in (slice(0, PLANE), slice(PLANE, LANES)):
        pack_ref[0:3, part] = positions_ref[...]
        pack_ref[3:4, part] = species_ref[...].astype(f32)
        pack_ref[4:5, part] = counts_ref[...].astype(f32)
        pack_ref[5:6, part] = cot_ref[...]
    pack_ref[6:16] = jnp.zeros((10, LANES), f32)
    pack_ref[6:7, 0:SPECIES] = scale_ref[...]
    pack_ref[7:8, 0:SPECIES] = shift_ref[...]
    pack_ref[8:9] = weight_ref[...]
    pack_ref[9:10] = state_ref[...]
    own_unit(first_units, me, blocks_ref)
    own_unit(late_units, me, late_in)
    pl.semaphore_wait(barrier, len(partners))
    link_halo.start(own_at, own_at)
    for part in gather_low:
        part.own()

    ids = lax.broadcasted_iota(jnp.int32, (3 * PLANE, LANES), 0)

    whole = PLANE * devices
    coef[0, :, 0:SLOTS] = idx_ref[...].astype(f32)
    listed = coef[0].T[: SLOTS + 6].astype(jnp.int32) - (me - 1) * PLANE
    listed = jnp.where(
        listed < 0, listed + whole, jnp.where(listed >= whole, listed - whole, listed)
    )
    for t in range(TILES):
        near = jnp.concatenate([listed[2 * t : 2 * t + 1], listed[2 * t + 1 : 2 * t + 2]], axis=1)
        hot[:, t * LANES : (t + 1) * LANES] = jnp.where(ids == near, 1.0, 0.0).astype(bf16)

    link_halo.wait(own_at, own_at)
    own = pack_ref[0:8]
    lane = lax.broadcasted_iota(jnp.int32, (8, LANES), 1)
    row = lax.broadcasted_iota(jnp.int32, (8, LANES), 0)
    edge = spacing * devices
    x_row = row == 0
    before = halo[0] - jnp.where(x_row, jnp.where(me == 0, edge, 0.0), 0.0)
    after = halo[1] + jnp.where(x_row, jnp.where(me == devices - 1, edge, 0.0), 0.0)
    rank_y = ((lane & (PLANE - 1)) >> 3).astype(f32)
    rank_z = (lane & (SIDE - 1)).astype(f32)
    table = jnp.concatenate([jnp.where(lane < PLANE, before, own), after], axis=1)
    ranks = jnp.where(row == 4, rank_y, rank_z)
    table = jnp.where(
        jnp.concatenate([row, row], axis=1) < 4, table, jnp.concatenate([ranks, ranks], axis=1)
    )[:, : 3 * PLANE]
    ga, gb, gc = parts(table)
    got = nn(ga, hot[...]) + nn(gb, hot[...]) + nn(gc, hot[...])
    mine = jnp.concatenate([own] * TILES, axis=1)
    lane = lax.broadcasted_iota(jnp.int32, (1, ROWS), 1)
    slot = lane >> 6
    atom = lane & (PLANE - 1)

    def wrapped(step):
        return jnp.where(step > 1.5, -8.0, jnp.where(step < -1.5, 8.0, 0.0)) * spacing

    for part in gather_low:
        part.line()
    gather_mid.own()
    disp = [
        got[0:1] - mine[0:1],
        got[1:2] - mine[1:2] + wrapped(got[4:5] - (atom >> 3).astype(f32)),
        got[2:3] - mine[2:3] + wrapped(got[5:6] - (atom & (SIDE - 1)).astype(f32)),
    ]
    length = jnp.sqrt(disp[0] * disp[0] + disp[1] * disp[1] + disp[2] * disp[2])
    inverse = 1.0 / length
    unit = [disp[0] * inverse, disp[1] * inverse, disp[2] * inverse]
    angle = length * (math.pi / cutoff_radius)
    sin_k = [jnp.sin(angle)]
    cos_k = [jnp.cos(angle)]
    sin_k.append(2.0 * cos_k[0] * sin_k[0])
    cos_k.append(2.0 * cos_k[0] * cos_k[0] - 1.0)
    for k in range(2, BESSEL):
        sin_k.append(2.0 * cos_k[0] * sin_k[k - 1] - sin_k[k - 2])
        cos_k.append(2.0 * cos_k[0] * cos_k[k - 1] - cos_k[k - 2])
    sines = jnp.concatenate(sin_k, axis=0)
    cosines = jnp.concatenate(cos_k, axis=0)
    bessel = (math.sqrt(2.0 / cutoff_radius) * inverse) * sines
    scaled = length * (1.0 / cutoff_radius)
    t2 = scaled * scaled
    t4 = t2 * t2
    t5 = t4 * scaled
    t6 = t4 * t2
    envelope = 1.0 - 28.0 * t6 + 48.0 * (t6 * scaled) - 21.0 * (t4 * t4)
    denvelope = (-168.0 * t5 + 336.0 * t6 - 168.0 * (t6 * scaled)) * (1.0 / cutoff_radius)
    live = jnp.where(slot.astype(f32) < mine[4:5], 1.0, 0.0)

    kind = lax.broadcasted_iota(jnp.int32, (KINDS, LANES), 0).astype(f32)
    is_kind = kind == own[3:4]
    by_kind = own.T
    scale = jnp.sum(jnp.where(is_kind, by_kind[:KINDS, 6:7], 0.0), axis=0, keepdims=True)
    shift = jnp.sum(jnp.where(is_kind, by_kind[:KINDS, 7:8], 0.0), axis=0, keepdims=True)
    cot = jnp.concatenate([own[5:6] * scale] * TILES, axis=1) * live
    weight = cot * envelope

    root3 = math.sqrt(3.0)
    root15 = math.sqrt(15.0)
    root5 = math.sqrt(5.0)
    ux, uy, uz = unit
    yrow[0:8] = jnp.concatenate(
        [
            root3 * ux,
            root3 * uy,
            root3 * uz,
            root15 * ux * uy,
            root15 * uy * uz,
            0.5 * root5 * (3.0 * uz * uz - 1.0),
            root15 * ux * uz,
            0.5 * root15 * (ux * ux - uy * uy),
        ],
        axis=0,
    )
    yrow[8:16] = yrow[0:8] * (live * env_scale)
    yrow[16:17] = live * env_scale
    geo[0:8] = jnp.concatenate([ux, uy, uz, inverse, envelope, denvelope, live, cot], axis=0)
    geo[8:16] = math.sqrt(2.0 / cutoff_radius) * (
        (math.pi / cutoff_radius)
        * lax.broadcasted_iota(jnp.int32, (BESSEL, ROWS), 0).astype(f32)
        * cosines
        + (math.pi / cutoff_radius) * cosines
        - sines * inverse
    ) * inverse

    for part in gather_low:
        part.second()
    gather_mid.line()
    gather_high.own()

    def one_hots(t):
        row = lax.broadcasted_iota(jnp.int32, (LANES, LANES), 0).astype(f32)
        here = jnp.where(row == own[3:4] + float(BESSEL), 1.0, 0.0)
        there = jnp.where(row == kinds_near[t] + float(BESSEL + SPECIES), 1.0, 0.0)
        return here + there

    kinds_near = [got[3:4, t * LANES : (t + 1) * LANES] for t in range(TILES)]
    for t in range(TILES):
        at = slice(t * LANES, (t + 1) * LANES)
        column = jnp.concatenate([bessel[:, at], one_hots(t)[BESSEL:]], axis=0)
        z_t[:, at] = column.astype(bf16)
        z_r[at, :] = column.T.astype(bf16)
        env_b[at, :] = jnp.broadcast_to(envelope[:, at], (LANES, LANES)).T
        fact[at, :] = jnp.broadcast_to(weight[:, at], (LANES, LANES)).T

    for part in gather_low:
        part.third()
    gather_mid.second()
    for part in gather_low:
        part.across()

    def twice(x):
        return jnp.concatenate([x] * (STRIP // LANES), axis=1)

    def in_body(n, r):
        pre = nn(z_r[r], cols_panel(first_w, W_INPUT, n))
        hid[r, panel(n, STRIP)] = (pre * sigmoid(pre)).astype(bf16)

    loop_panels(in_body)
    gather_mid.third()
    gather_high.line()
    gather_mid.across()

    def two_body(n, r):
        zero = nn(hid[r], cols_panel(first_w, W_TWO, n)) * twice(env_b[r])
        lat[r, panel(n, STRIP)] = zero
        low0[r, panel(n, STRIP)] = zero.astype(bf16)

    loop_panels(two_body)

    def transposed_product(out, weights, right, width=256):
        at = 0
        while at < ROWS:
            end = min(at + width, ROWS)
            out[:, at:end] = nt(weights, right[at:end, :])
            at = end

    gather_high.second()
    gather_late.own()
    wee_t[0:128, :] = narrow(first_w, W_EMBED).T
    wee_t[128:256, :] = narrow(first_w, W_ENV_ONE).T
    transposed_product(ee_t, wee_t[...], low0)

    def environment(out, v0_ref, v0_at, v1_at):
        for m in range(9):
            total = None
            begin = v0_at if m == 0 else v1_at
            y = yrow[16:17, :] if m == 0 else yrow[7 + m : 8 + m, :]
            for t in range(TILES):
                at = slice(t * LANES, (t + 1) * LANES)
                term = v0_ref[begin : begin + CHANNELS, at] * y[:, at]
                total = term if total is None else total + term
            out[m] = halves(total)

    def put_scalars(t, s_t, rows):
        s_t[:, lanes(t)] = jnp.concatenate(rows, axis=0).astype(bf16)
        filled = jnp.concatenate(rows + [jnp.zeros_like(rows[0])], axis=0)
        flipped = filled.T.astype(bf16)
        s_r[lanes(t), :] = flipped

    def weighted(y, first, count, source, offset):
        total = None
        for m in range(count):
            term = y[first + m : first + m + 1] * source[offset + m]
            total = term if total is None else total + term
        return total

    gather_high.third()
    gather_late.line((1,))
    environment(gam, ee_t, 128, 192)

    def scalars_one(t):
        e0 = ee_t[0:64, lanes(t)]
        e1 = ee_t[64:128, lanes(t)]
        y = yrow[0:8, lanes(t)]
        put_scalars(
            t,
            s1_t,
            [e0 * gam[0], e1 * weighted(y, 0, 3, gam, 1), e1 * weighted(y, 3, 5, gam, 4)],
        )

    loop(TILES, scalars_one)

    gather_late.line((2,))
    gather_high.across()
    def pre_one(n, r):
        pre = nn(low0[r], cols_panel(first_w, W_LAT_ONE, n)) + nn(
            s_r[r, : 3 * CHANNELS], cols_panel(first_w, W_SCAL_ONE, n)
        )
        sig = sigmoid(pre)
        act = pre * sig
        act1[r, panel(n, STRIP)] = act.astype(bf16)
        sl1[r, panel(n, STRIP)] = (sig + act * (1.0 - sig)).astype(bf16)

    loop_panels(pre_one)
    gather_late.line((3,))
    gather_late.second()

    def out_one(n, r):
        new = (lat[r, panel(n, STRIP)] + nn(act1[r], cols_panel(first_w, W_OUT_ONE, n))) * half_root
        lat[r, panel(n, STRIP)] = new
        low1[r, panel(n, STRIP)] = new.astype(bf16)

    loop_panels(out_one)
    gather_late.third()
    we2_t[...] = narrow(first_w, W_ENV_TWO).T
    transposed_product(en2_t, we2_t[...], low1)
    environment(dlt, en2_t, 0, 64)

    g0 = gam[0]
    coef[0] = g0 * dlt[0]
    for m in range(3):
        a, b = 1 + (m + 1) % 3, 1 + (m + 2) % 3
        coef[1 + m] = g0 * dlt[1 + m] + (gam[a] * dlt[b] - gam[b] * dlt[a])
    coef[9] = gam[1] * dlt[1] + gam[2] * dlt[2] + gam[3] * dlt[3]
    second = None
    for m in range(4, 9):
        coef[m] = g0 * dlt[m]
        term = gam[m] * dlt[m]
        second = term if second is None else second + term
    coef[10] = second

    def scalars_two(t):
        e0 = ee_t[0:64, lanes(t)]
        e1 = ee_t[64:128, lanes(t)]
        y = yrow[0:8, lanes(t)]
        put_scalars(
            t,
            s2_t,
            [
                e0 * coef[0],
                e1 * weighted(y, 0, 3, coef, 1) + e0 * coef[9],
                e1 * weighted(y, 3, 5, coef, 4) + e0 * coef[10],
            ],
        )

    loop(TILES, scalars_two)

    gather_late.across()
    for part in gather_low + [gather_mid, gather_high, gather_late]:
        part.finish()
    def pre_two(n, r):
        pre = nn(low1[r], cols_panel(late_w, W_LAT_TWO, n)) + nn(
            s_r[r, : 3 * CHANNELS], cols_panel(first_w, W_SCAL_TWO, n)
        )
        sig = sigmoid(pre)
        act = pre * sig
        act2[r, panel(n, STRIP)] = act.astype(bf16)
        sl2[r, panel(n, STRIP)] = (sig + act * (1.0 - sig)).astype(bf16)

    loop_panels(pre_two)

    def out_two(n, r):
        new = (lat[r, panel(n, STRIP)] + nn(act2[r], cols_panel(late_w, W_OUT_TWO, n))) * half_root
        low2[r, panel(n, STRIP)] = new.astype(bf16)

    loop_panels(out_two)

    vec = jnp.broadcast_to(pack_ref[8:9], (8, LANES))
    stage[...] = narrow(first_w, W_FINAL)

    def read_out(i):
        r = pl.ds(pl.multiple_of(i * 416, 16), 416)
        pre = nn(low2[r, :], stage[...])
        sig = sigmoid(pre)
        final_act = pre * sig
        dpf[r, :] = (fact[r, :] * vec[0:1] * (sig + final_act * (1.0 - sig))).astype(bf16)
        fact[r, :] = final_act

    loop(4, read_out)
    value = nt(vec, fact[...], highest)[0:1]
    geo_live = geo[6:7]
    geo_env = geo[4:5]
    geo_cot = geo[7:8]
    edge_energy = geo_live * geo_env * value
    summed = None
    for t in range(TILES):
        term = edge_energy[:, t * LANES : (t + 1) * LANES]
        summed = term if summed is None else summed + term
    energy_ref[...] = scale * halves(summed) + shift
    all_weights = jnp.broadcast_to(geo_cot * geo_env, (8, ROWS))
    sum_vector.send(0, nn(all_weights, fact[...], highest))
    geo[16:17] = geo_cot * value

    def big_grad(out, where, left, right):
        def step(i):
            grad = tn(left[:, panel(i, STRIP)], right[...])
            out[pl.ds(pl.multiple_of(where[0] + i * STRIP, 64), STRIP), :] = grad.astype(bf16)

        loop(LATENT // STRIP, step)

    def wide_grad(out, where, left, right):
        def step(n):
            out[where[0] : where[0] + where[1], panel(n)] = nn(
                left[...], right[:, panel(n)]
            ).astype(bf16)

        loop(4, step)

    def narrow_grad(left, right, put):
        def step(n):
            put(n, nn(left, right[:, panel(n)]).T.astype(bf16))

        loop(4, step)

    def put_narrow(where, n, grad):
        row = pl.multiple_of(where[0] + n // 2 * BLOCK_ROWS, BLOCK_ROWS)
        col = pl.multiple_of(n % 2 * 512, 512)
        first_w[pl.ds(row, BLOCK_ROWS), pl.ds(col, 512)] = jnp.concatenate(
            [grad[b * BLOCK_ROWS : (b + 1) * BLOCK_ROWS] for b in range(4)], axis=1
        )

    def put_stage(n, grad):
        stage[panel(n), :] = grad

    narrow_grad(dpf[...].T, low2, put_stage)

    def back_final(n, r):
        grad = nt(dpf[r], narrow_panel(first_w, W_FINAL, n)) * half_root
        lat[r, panel(n, STRIP)] = grad
        low2[r, panel(n, STRIP)] = grad.astype(bf16)

    loop_panels(back_final)
    loop(4, lambda n: put_narrow(W_FINAL, n, stage[panel(n), :]))

    def back_out_two(n, r):
        grad = nt(low2[r], rows_panel(late_w, W_OUT_TWO, n))
        sl2[r, panel(n, STRIP)] = (grad * sl2[r, panel(n, STRIP)].astype(f32)).astype(bf16)

    loop_panels(back_out_two)
    transposed_product(ds_t, first_w[W_SCAL_TWO[0] : W_SCAL_TWO[0] + W_SCAL_TWO[1], :], sl2)
    wide_grad(first_w, W_SCAL_TWO, s2_t, sl2)
    big_grad(late_w, W_OUT_TWO, act2, low2)
    sum_out.stage(0)
    sum_vector.pass_on(0)

    dg[...] = jnp.zeros_like(dg)

    def tensors_two(t):
        e0 = ee_t[0:64, lanes(t)]
        e1 = ee_t[64:128, lanes(t)]
        y = yrow[0:8, lanes(t)]
        r0 = ds_t[0:64, lanes(t)]
        r1 = ds_t[64:128, lanes(t)]
        r2 = ds_t[128:192, lanes(t)]
        de_t[0:64, lanes(t)] = r0 * coef[0] + r1 * coef[9] + r2 * coef[10]
        de_t[64:128, lanes(t)] = r1 * weighted(y, 0, 3, coef, 1) + r2 * weighted(y, 3, 5, coef, 4)
        p1 = r1 * e1
        p2 = r2 * e1
        rows = []
        for m in range(8):
            p = p1 if m < 3 else p2
            rows.append(jnp.sum(p * coef[1 + m], axis=0, keepdims=True))
            dg[1 + m] += p * y[m : m + 1]
        dy[:, lanes(t)] = jnp.concatenate(rows, axis=0)
        dg[0] += r0 * e0
        dg[9] += r1 * e0
        dg[10] += r2 * e0

    loop(TILES, tensors_two)
    total = [halves(dg[m]) for m in range(11)]
    g0 = gam[0]
    d0 = dlt[0]
    new_g0 = total[0] * d0
    for m in range(1, 9):
        new_g0 = new_g0 + total[m] * dlt[m]
    dlt_grads = [total[0] * g0]
    gam_grads = [new_g0]
    for m in range(3):
        a, b = 1 + (m + 1) % 3, 1 + (m + 2) % 3
        dlt_grads.append(
            total[1 + m] * g0 + total[9] * gam[1 + m] + (total[a] * gam[b] - total[b] * gam[a])
        )
        gam_grads.append(total[9] * dlt[1 + m] + (dlt[a] * total[b] - dlt[b] * total[a]))
    for m in range(4, 9):
        dlt_grads.append(total[m] * g0 + total[10] * gam[m])
        gam_grads.append(total[10] * dlt[m])
    for m in range(9):
        dlt[m] = dlt_grads[m]
        dg[m] = gam_grads[m]

    def environment_back(t, grads, source, v1_at, at):
        y4 = yrow[8:16, lanes(t)]
        l4 = yrow[16:17, lanes(t)]
        v1 = source[v1_at : v1_at + 64, lanes(t)]
        low = l4 * grads[0]
        high = weighted(y4, 0, 8, grads, 1)
        both = jnp.concatenate([low, high], axis=0)
        dw_t[at : at + 128, lanes(t)] = both.astype(bf16)
        dw_r[lanes(t), at : at + 128] = both.T.astype(bf16)
        v1 = v1 * l4
        rows = [jnp.sum(v1 * grads[1 + m], axis=0, keepdims=True) for m in range(8)]
        dy[:, lanes(t)] += jnp.concatenate(rows, axis=0)

    loop(TILES, lambda t: environment_back(t, dlt, en2_t, 64, 128))

    def back_lat_two(n, r):
        grad = (
            lat[r, panel(n, STRIP)]
            + nt(sl2[r], rows_panel(late_w, W_LAT_TWO, n))
            + nt(dw_r[r, 128:256], narrow_panel(first_w, W_ENV_TWO, n))
        ) * half_root
        lat[r, panel(n, STRIP)] = grad
        act2[r, panel(n, STRIP)] = grad.astype(bf16)

    sum_out.stage(1)
    loop_panels(back_lat_two)
    sum_out.stage(2)
    big_grad(late_w, W_LAT_TWO, low1, sl2)
    sum_out.stage(3)
    narrow_grad(dw_t[128:256, :], low1, functools.partial(put_narrow, W_ENV_TWO))
    sum_lat.stage(0)
    sum_vector.pass_on(1)

    def back_out_one(n, r):
        grad = nt(act2[r], rows_panel(first_w, W_OUT_ONE, n))
        sl1[r, panel(n, STRIP)] = (grad * sl1[r, panel(n, STRIP)].astype(f32)).astype(bf16)

    loop_panels(back_out_one)
    sum_out.stage(4)
    sum_lat.stage(1)
    big_grad(first_w, W_OUT_ONE, act1, act2)
    sum_first[3].stage(0)
    sum_out.stage(5)
    sum_lat.stage(2)
    transposed_product(ds_t, first_w[W_SCAL_ONE[0] : W_SCAL_ONE[0] + W_SCAL_ONE[1], :], sl1)
    wide_grad(first_w, W_SCAL_ONE, s1_t, sl1)
    sum_out.stage(6)
    sum_lat.stage(3)
    sum_first[3].stage(1)
    sum_vector.pass_on(2)

    def tensors_one(t):
        e0 = ee_t[0:64, lanes(t)]
        e1 = ee_t[64:128, lanes(t)]
        y = yrow[0:8, lanes(t)]
        r0 = ds_t[0:64, lanes(t)]
        r1 = ds_t[64:128, lanes(t)]
        r2 = ds_t[128:192, lanes(t)]
        low = de_t[0:64, lanes(t)] + r0 * gam[0]
        high = (
            de_t[64:128, lanes(t)]
            + r1 * weighted(y, 0, 3, gam, 1)
            + r2 * weighted(y, 3, 5, gam, 4)
        )
        both = jnp.concatenate([low, high], axis=0)
        dw_t[0:128, lanes(t)] = both.astype(bf16)
        dw_r[lanes(t), 0:128] = both.T.astype(bf16)
        p1 = r1 * e1
        p2 = r2 * e1
        rows = []
        for m in range(8):
            p = p1 if m < 3 else p2
            rows.append(jnp.sum(p * gam[1 + m], axis=0, keepdims=True))
            coef[1 + m] += p * y[m : m + 1]
        dy[:, lanes(t)] += jnp.concatenate(rows, axis=0)
        coef[0] += r0 * e0

    for m in range(9):
        coef[m] = jnp.zeros((CHANNELS, LANES), f32)
    loop(TILES, tensors_one)
    sum_lat.stage(4)
    sum_first[3].stage(2)
    for m in range(9):
        dg[m] = dg[m] + halves(coef[m])
    loop(TILES, lambda t: environment_back(t, dg, ee_t, 192, 128))
    sum_lat.stage(5)
    sum_first[3].stage(3)

    den[...] = jnp.zeros_like(den)

    def back_lat_one(n, r):
        both = jnp.concatenate(
            [narrow_panel(first_w, W_EMBED, n), narrow_panel(first_w, W_ENV_ONE, n)], axis=1
        )
        grad = (
            lat[r, panel(n, STRIP)]
            + nt(sl1[r], rows_panel(first_w, W_LAT_ONE, n))
            + nt(dw_r[r], both)
        )
        low1[r, panel(n, STRIP)] = (grad * twice(env_b[r])).astype(bf16)
        part = grad * low0[r, panel(n, STRIP)].astype(f32)
        for b in range(STRIP // LANES):
            den[r] += part[:, b * LANES : (b + 1) * LANES]

    loop_panels(back_lat_one)
    sum_lat.stage(6)
    sum_first[3].stage(4)
    big_grad(first_w, W_LAT_ONE, low0, sl1)
    sum_first[2].stage(0)
    sum_first[3].stage(5)
    narrow_grad(dw_t[0:128, :], low0, functools.partial(put_narrow, W_EMBED))
    narrow_grad(dw_t[128:256, :], low0, functools.partial(put_narrow, W_ENV_ONE))

    def back_two(n, r):
        grad = nt(low1[r], rows_panel(first_w, W_TWO, n))
        pre = nn(z_r[r], cols_panel(first_w, W_INPUT, n))
        sig = sigmoid(pre)
        act1[r, panel(n, STRIP)] = (grad * (sig + pre * sig * (1.0 - sig))).astype(bf16)

    sum_first[2].stage(1)
    sum_first[3].stage(6)
    loop_panels(back_two)
    sum_first[2].stage(2)
    big_grad(first_w, W_TWO, hid, low1)
    sum_first[1].stage(0)
    sum_first[2].stage(3)
    transposed_product(ds_t.at[0:64], first_w[0:64, :], act1)
    wide_grad(first_w, W_INPUT, z_t, act1)
    for part in sum_low:
        part.stage(0)
    sum_first[1].stage(1)

    dbessel = ds_t[0:8, :]
    through = nt(jnp.ones((8, LANES), f32), den[...], highest)[0:1]
    ux, uy, uz = geo[0:1], geo[1:2], geo[2:3]
    inverse = geo[3:4]
    envelope = geo[4:5]
    denv = geo[16:17] + through / envelope
    dlength = jnp.sum(dbessel * geo[8:16], axis=0, keepdims=True) + denv * geo[5:6]
    g = [dy[m : m + 1, :] for m in range(8)]
    dux = root3 * g[0] + root15 * (uy * g[3] + uz * g[6] + ux * g[7])
    duy = root3 * g[1] + root15 * (ux * g[3] + uz * g[4] - uy * g[7])
    duz = root3 * g[2] + root15 * (uy * g[4] + ux * g[6]) + (3.0 * root5) * uz * g[5]
    along = dlength - (ux * dux + uy * duy + uz * duz) * inverse
    near = jnp.concatenate(
        [
            dux * inverse + ux * along,
            duy * inverse + uy * along,
            duz * inverse + uz * along,
            jnp.zeros((5, ROWS), f32),
        ],
        axis=0,
    )
    sum_first[1].stage(2)
    sum_first[2].stage(4)
    for part in sum_low:
        part.stage(1)
    summed = None
    for t in range(TILES):
        term = near[:, t * LANES : (t + 1) * LANES]
        summed = term if summed is None else summed + term
    centre = halves(summed)
    na, nb, nc = parts(near)
    spread = nt(na, hot[...]) + nt(nb, hot[...]) + nt(nc, hot[...])
    sides[0] = spread[:, :LANES]
    sides[1, :, 0:PLANE] = spread[:, LANES:]
    link_force.start(sides.at[0], sides.at[1])
    sum_first[1].stage(3)
    sum_first[2].stage(5)
    for step in range(5 + PIECES - 1):
        if step == 1:
            sum_first[1].stage(4)
            sum_first[2].stage(6)
        if step in (3, 5):
            sum_first[1].stage(4 + step // 2)
        for k in range(PIECES):
            if 0 <= step - k < 5:
                sum_low[k].stage(2 + step - k)
    link_force.wait(sides.at[0], sides.at[1])
    forces_ref[...] = (
        centre - pltpu.roll(sides[0], PLANE, 1) - force_in[1] - force_in[0]
    )
    total = sum_vector.pass_on(3)
    normed = total * lax.rsqrt(jnp.sum(total[0:1] * total[0:1]) * (1.0 / FINAL) + epsilon)
    state = decay_rate * pack_ref[9:10] + (1.0 - decay_rate) * normed * normed
    vector_ref[0:1] = total[0:1]
    vector_ref[1:2] = state[0:1]
    vector_ref[2:3] = (pack_ref[8:9] - vector_rate * normed * lax.rsqrt(state + epsilon))[0:1]
    first_out[...] = first_units.get(me)
    late_out[...] = late_units.get(me)
    for group in [sum_out, sum_lat, sum_vector] + list(sum_first.values()) + sum_low:
        group.finish()
    link_halo.finish(own_at, own_at)
    link_force.finish(sides.at[0], sides.at[1])


def run_network(devices, small, blocks, late):
    S = jax.ShapeDtypeStruct
    wide = pltpu.VMEM((ROWS, LATENT), bf16)
    slab = pltpu.VMEM((ROWS, LANES), f32)
    panels = lambda amount: pltpu.VMEM((amount * devices // PANEL * BLOCK_ROWS, WIDE), bf16)
    scratch = [
        panels(blocks.shape[0]),
        panels(late.shape[0]),
        pltpu.VMEM((3 * PLANE, ROWS), bf16),
        pltpu.VMEM((LANES, ROWS), bf16),
        pltpu.VMEM((ROWS, LANES), bf16),
        pltpu.VMEM((24, ROWS), f32),
        pltpu.VMEM((24, ROWS), f32),
        slab,
        pltpu.VMEM((256, ROWS), f32),
        pltpu.VMEM((128, ROWS), f32),
        pltpu.VMEM((192, ROWS), bf16),
        pltpu.VMEM((192, ROWS), bf16),
        pltpu.VMEM((9, CHANNELS, LANES), f32),
        pltpu.VMEM((9, CHANNELS, LANES), f32),
        pltpu.VMEM((11, CHANNELS, LANES), f32),
        pltpu.VMEM((192, ROWS), f32),
        pltpu.VMEM((128, ROWS), f32),
        pltpu.VMEM((8, ROWS), f32),
        pltpu.VMEM((11, CHANNELS, LANES), f32),
        pltpu.VMEM((256, ROWS), bf16),
        pltpu.VMEM((ROWS, 256), bf16),
        pltpu.VMEM((ROWS, LANES), bf16),
        slab,
        pltpu.VMEM((ROWS, LATENT), f32),
    ] + [wide] * 8 + [
        pltpu.VMEM((LATENT, LANES), bf16),
        pltpu.VMEM((2, 8, LANES), f32),
        pltpu.VMEM((2, 8, LANES), f32),
        pltpu.VMEM((2, 8, LANES), f32),
        pltpu.VMEM((Total.slots(devices), 8, LANES), f32),
        pltpu.VMEM((16, LANES), f32),
        pltpu.SemaphoreType.DMA((PIECES, Gather.amount(devices, 1))),
        pltpu.SemaphoreType.DMA((Gather.amount(devices, 1),)),
        pltpu.SemaphoreType.DMA((Gather.amount(devices, 2),)),
        pltpu.SemaphoreType.DMA((Gather.amount(devices, 4),)),
        pltpu.SemaphoreType.DMA((2, Reduce.amount(devices, 2))),
        pltpu.SemaphoreType.DMA((3, Reduce.amount(devices, 1))),
        pltpu.SemaphoreType.DMA((PIECES, Reduce.amount(devices, 1))),
        pltpu.SemaphoreType.DMA((2, 4)),
        pltpu.SemaphoreType.DMA((2 * Total.slots(devices),)),
        pltpu.SemaphoreType.REGULAR((6, 7)),
    ]
    vmem = pl.BlockSpec(memory_space=pltpu.VMEM)
    return pl.pallas_call(
        network,
        out_shape=[
            S((1, LANES), f32),
            S((8, LANES), f32),
            S((8, LANES), f32),
            S(unit_shape(blocks.shape[0]), bf16),
            S(unit_shape(late.shape[0]), bf16),
        ],
        in_specs=[vmem] * (len(small) + 2),
        out_specs=[vmem] * 5,
        scratch_shapes=scratch,
        compiler_params=pltpu.CompilerParams(
            vmem_limit_bytes=63 << 20, collective_id=0, has_side_effects=True
        ),
        name="network",
    )(*small, blocks, late)


def shampoo(
    energy,
    force,
    vectors,
    grads,
    left,
    right,
    left_root,
    right_root,
    master,
    late_grads,
    late_left,
    late_right,
    late_left_root,
    late_right_root,
    late_master,
    energy_out,
    force_out,
    vector_out,
    state_out,
    moved_out,
    *outs,
):
    energy_out[...] = energy[:, :PLANE]
    force_out[...] = force[0:3, :PLANE]
    vector_out[...] = vectors[0:1]
    state_out[...] = vectors[1:2]
    moved_out[...] = vectors[2:3]

    def block(panels, j, left, right, left_root, right_root, master, out):
        grad_out, left_out, right_out, master_out = out
        per = panels.shape[1] // BLOCK_COLS
        at = pl.program_id(0) * left.shape[0] + j
        row = pl.multiple_of(at // per * BLOCK_ROWS, BLOCK_ROWS)
        col = pl.multiple_of(at % per * BLOCK_COLS, BLOCK_COLS)
        held = panels[pl.ds(row, BLOCK_ROWS), pl.ds(col, BLOCK_COLS)]
        grad = held.astype(f32)
        grad_out[j] = grad
        size = 1.0 / (BLOCK_ROWS * BLOCK_COLS)
        scale = lax.rsqrt(jnp.sum(grad * grad, keepdims=True) * size + epsilon)
        square = (1.0 - decay_rate) * scale * scale
        left_out[j] = decay_rate * left[j] + square * nt(held, held)
        right_out[j] = decay_rate * right[j] + square * tn(held, held)
        la, lb, _ = parts(left_root[j])
        ra, rb, _ = parts(right_root[j])
        turned = (nn(la, held) + nn(lb, held)) * scale
        ta, tb, _ = parts(turned)
        step = nn(ta, ra) + (nn(ta, rb) + nn(tb, ra))
        slope = lax.rsqrt(jnp.sum(step * step, keepdims=True) * size + epsilon)
        master_out[j] = master[j] - (learn_rate * slope) * step

    for j in range(left.shape[0]):
        block(grads, j, left, right, left_root, right_root, master, outs[:4])
    for j in range(late_left.shape[0]):
        block(
            late_grads,
            j,
            late_left,
            late_right,
            late_left_root,
            late_right_root,
            late_master,
            outs[4:],
        )


def run_shampoo(energy, force, vectors, first, late):
    S = jax.ShapeDtypeStruct
    steps = min(4, late[1].shape[0])

    def whole(x):
        return pl.BlockSpec(x.shape, lambda i: (0,) * len(x.shape))

    def share(x):
        return pl.BlockSpec((x.shape[0] // steps,) + x.shape[1:], lambda i: (i, 0, 0))

    small = [S((1, PLANE), f32), S((3, PLANE), f32)] + [S((1, FINAL), f32)] * 3
    grown = []
    for group in (first, late):
        left, right, _, _, master = group[1:]
        grown += [S(x.shape, f32) for x in (master, left, right, master)]
    return pl.pallas_call(
        shampoo,
        grid=(steps,),
        out_shape=small + grown,
        in_specs=[whole(energy), whole(force), whole(vectors)]
        + [whole(first[0])]
        + [share(x) for x in first[1:]]
        + [whole(late[0])]
        + [share(x) for x in late[1:]],
        out_specs=[whole(x) for x in small] + [share(x) for x in grown],
        compiler_params=pltpu.CompilerParams(vmem_limit_bytes=60 << 20),
        name="shampoo",
    )(energy, force, vectors, *first, *late)


def local(
    positions,
    species,
    neighbours,
    counts,
    species_scale,
    species_shift,
    energy_cot,
    blocks,
    left,
    right,
    left_root,
    right_root,
    late_blocks,
    late_left,
    late_right,
    late_left_root,
    late_right_root,
    out_vector,
    vector_state,
):
    devices = lax.axis_size("atoms")
    small = (
        neighbours.reshape(PLANE, SLOTS),
        positions,
        species[None],
        counts[None],
        energy_cot[None],
        species_scale[None],
        species_shift[None],
        out_vector[None],
        vector_state[None],
    )
    energy, force, vectors, first_units, late_units = run_network(
        devices, small, blocks, late_blocks
    )
    out = run_shampoo(
        energy,
        force,
        vectors,
        (first_units, left, right, left_root, right_root, blocks),
        (late_units, late_left, late_right, late_left_root, late_right_root, late_blocks),
    )
    energies, forces, vector_grad, new_state, new_vector = out[:5]
    return (
        energies.reshape(-1),
        forces,
        *out[5:],
        vector_grad.reshape(-1),
        new_state.reshape(-1),
        new_vector.reshape(-1),
    )


def solution(mesh):
    row = P("atoms")
    block = P("atoms", None, None)
    placed = (
        (P(None, "atoms"), row, row, row, P(), P(), row)
        + (block,) * 10
        + (P(), P())
    )
    return jax.shard_map(
        local,
        mesh=mesh,
        in_specs=placed,
        out_specs=(row, P(None, "atoms")) + (block,) * 8 + (P(), P(), P()),
        check_vma=False,
    )
```

```python
import functools
import math

import jax
import jax.numpy as jnp
from jax import lax
from jax.experimental import pallas as pl
from jax.experimental.pallas import tpu as pltpu
from jax.sharding import PartitionSpec as P

SIDE = 8
SLOTS = 26
SPECIES = 60
BESSEL = 8
CHANNELS = 64
LATENT = 1024
FINAL = 128
BLOCK_ROWS = 64
BLOCK_COLS = 128
PLANE = SIDE * SIDE

f32 = jnp.float32
bf16 = jnp.bfloat16
highest = lax.Precision.HIGHEST
spacing = 1.6
cutoff_radius = 4.0
env_scale = 0.25
half_root = 0.7071067811865476
decay_rate = 0.5
learn_rate = 0.02
vector_rate = 0.03
epsilon = 1e-06

LANES = 128
ROWS = SLOTS * PLANE
TILES = ROWS // LANES
KINDS = 64

PANEL = 8
WIDE = PANEL * BLOCK_COLS
W_INPUT = (0, 128)
W_TWO = (128, 1024)
W_EMBED = (1152, 128)
W_ENV_ONE = (1280, 128)
W_LAT_ONE = (1408, 1024)
W_SCAL_ONE = (2432, 192)
W_OUT_ONE = (2624, 1024)
W_ENV_TWO = (3648, 128)
W_SCAL_TWO = (3776, 192)
W_FINAL = (3968, 128)
W_LAT_TWO = (0, 1024)
W_OUT_TWO = (1024, 1024)

MESH = pl.DeviceIdType.MESH


def nn(a, b, precision=None):
    return lax.dot_general(
        a, b, (((1,), (0,)), ((), ())), preferred_element_type=f32, precision=precision
    )


def nt(a, b, precision=None):
    return lax.dot_general(
        a, b, (((1,), (1,)), ((), ())), preferred_element_type=f32, precision=precision
    )


def tn(a, b):
    return lax.dot_general(a, b, (((0,), (0,)), ((), ())), preferred_element_type=f32)


def cols_panel(ref, where, n):
    return ref[where[0] : where[0] + where[1], panel(n, STRIP)]


def rows_panel(ref, where, n):
    return ref[pl.ds(pl.multiple_of(where[0] + n * STRIP, 64), STRIP), :]


def narrow(ref, where):
    pieces = []
    for j in range(LATENT // BLOCK_ROWS):
        row = where[0] + j // PANEL * BLOCK_ROWS
        col = j % PANEL * BLOCK_COLS
        pieces.append(ref[row : row + BLOCK_ROWS, col : col + BLOCK_COLS])
    return jnp.concatenate(pieces, axis=0)


def narrow_panel(ref, where, n):
    part = ref[pl.ds(pl.multiple_of(where[0] + n * BLOCK_ROWS, BLOCK_ROWS), BLOCK_ROWS), :]
    return jnp.concatenate([part[:, b * 128 : (b + 1) * 128] for b in range(PANEL)], axis=0)


def sigmoid(x):
    return 0.5 * jnp.tanh(0.5 * x) + 0.5


def halves(x):
    return x + pltpu.roll(x, PLANE, 1)


def lanes(t):
    if isinstance(t, int):
        return pl.ds(t * LANES, LANES)
    return pl.ds(pl.multiple_of(t * LANES, LANES), LANES)


def panel(n, width=256):
    return pl.ds(pl.multiple_of(n * width, width), width)


STRIP = 512
CHUNKS = 2
PIECES = 4
CHUNK = ROWS // CHUNKS


def loop_panels(body):
    def step(n):
        for c in range(CHUNKS):
            body(n, slice(c * CHUNK, (c + 1) * CHUNK))

    loop(LATENT // STRIP, step)


def each(count, body):
    for i in range(count):
        body(i)


def loop(count, body):
    def step(i, carry):
        body(i)
        return carry

    lax.fori_loop(0, count, step, 0)


def parts(x):
    a = x.astype(bf16)
    rest = x - a.astype(f32)
    b = rest.astype(bf16)
    c = (rest - b.astype(f32)).astype(bf16)
    return a, b, c


class Place:
    def __init__(self, devices):
        side = math.isqrt(devices // 8)
        self.devices = devices
        self.sizes = (4, side, side)
        me = lax.axis_index("atoms")
        core = me % 2
        chip = me // 2
        last = chip % side
        middle = chip // side % side
        self.me = me
        self.core = core
        self.pos = (
            chip // (side * side),
            last + core * (middle - last),
            middle + core * (last - middle),
        )
        self.half = (side * side, 1 + core * (side - 1), side + core * (1 - side))
        self.step = tuple(2 * h for h in self.half)
        self.sibling = me + 1 - 2 * core
        self.plain = (self.pos[0], middle, last)
        self.plain_step = (2 * side * side, 2 * side, 2)

    def owner(self, q):
        return q[0] * self.step[0] + q[1] * self.step[1] + q[2] * self.step[2] + self.core

    def near(self, dim, up):
        return self.me + self.step[dim] if up else self.me - self.step[dim]

    def has(self, dim, up):
        return self.pos[dim] < self.sizes[dim] - 1 if up else self.pos[dim] > 0

    def peers(self, dim):
        n, p = self.sizes[dim], self.plain[dim]
        return [(r, (p + r) % n, self.me + ((p + r) % n - p) * self.plain_step[dim]) for r in range(1, n)]


class Units:
    def __init__(self, ref, rows, cols, base=0, part=(0, 1)):
        self.ref, self.rows, self.cols = ref, rows, cols
        self.per = WIDE // cols
        self.base = base
        self.high = rows // part[1]
        self.off = part[0] * self.high

    def window(self, s):
        s = s + self.base
        if self.per == 1:
            row, col = s * self.rows, slice(None)
        else:
            row = s // self.per * self.rows
            col = pl.ds(pl.multiple_of(s % self.per * self.cols, self.cols), self.cols)
        return (pl.ds(pl.multiple_of(row + self.off, 16), self.high), col)

    def at(self, s):
        return self.ref.at[self.window(s)]

    def get(self, s):
        return self.ref[self.window(s)]

    def put(self, s, value):
        self.ref[self.window(s)] = value


def remote(src, dst, send, recv, device):
    return pltpu.make_async_remote_copy(
        src_ref=src,
        dst_ref=dst,
        send_sem=send,
        recv_sem=recv,
        device_id=(device,),
        device_id_type=MESH,
    )


def signal(sem, device):
    pl.semaphore_signal(sem, inc=1, device_id=(device,), device_id_type=MESH)


def others(place, dim):
    n, p = place.sizes[dim], place.pos[dim]
    if n == 2:
        return [(1 - p, None)]
    found = []
    for distance in range(1, n):
        found.append((p - distance, p >= distance))
        found.append((p + distance, p < n - distance))
    return found


def gated(cond, body):
    if cond is None:
        body()
    else:
        pl.when(cond)(body)


def both(a, b):
    return b if a is None else (a if b is None else a & b)


class Gather:
    def __init__(self, place, units, lo, hi, sems, direct=False):
        self.place, self.units, self.lo, self.hi, self.sems = place, units, lo, hi, sems
        self.direct = direct
        _, na, nb = place.sizes
        self.waits = []
        self.first_owner = 2 * lo * na * nb
        at = 2 * (hi - lo) * na * nb
        self.base = []
        for dim in range(3):
            length = (hi - lo) * (1, na, na * nb)[dim]
            self.base.append((at, at + length))
            at += 2 * length
        self.core_base = at

    @staticmethod
    def amount(devices, share):
        side = math.isqrt(devices // 8)
        return share * (2 + 2 * side + 5 * side * side)

    def linear(self, q, dim):
        _, na, nb = self.place.sizes
        q0 = q[0] - self.lo
        return (q0, q0 * na + q[1], (q0 * na + q[1]) * nb + q[2])[dim]

    def emit(self, cond, q, sem, device):
        owner = self.place.owner(q)

        def copy():
            piece = self.units.at(owner)
            return remote(
                piece, piece, self.sems.at[sem], self.sems.at[owner - self.first_owner], device
            )

        gated(cond, lambda: copy().start())
        self.waits.append(lambda: gated(cond, lambda: copy().wait_send()))

    def forward(self, cond, q, via, arrived):
        place = self.place
        for dim in (0, 2, 1):
            if dim < via or (arrived and dim == via and place.sizes[dim] == 2):
                continue
            if dim == 0 and self.direct:
                if not arrived:
                    for r in range(1, 4):
                        device = place.me + ((place.pos[0] + r) % 4 - place.pos[0]) * place.step[0]
                        self.emit(cond, q, self.base[0][0] + r, device)
                continue
            if place.sizes[dim] == 2:
                toward = place.me + (1 - 2 * place.pos[dim]) * place.step[dim]
                self.emit(cond, q, self.base[dim][0] + self.linear(q, dim), toward)
                continue
            for up in (True, False):
                open_end = place.has(dim, up)
                if arrived and dim == via:
                    p = place.pos[dim]
                    open_end = open_end & ((q[dim] < p) if up else (q[dim] > p))
                self.emit(
                    both(cond, open_end),
                    q,
                    self.base[dim][0 if up else 1] + self.linear(q, dim),
                    place.near(dim, up),
                )
        self.emit(cond, q, self.core_base + self.linear(q, 2), place.sibling)

    def wait(self, cond, owner):
        piece = self.units.at(owner)
        gated(
            cond,
            lambda: remote(
                piece,
                piece,
                self.sems.at[self.core_base],
                self.sems.at[owner - self.first_owner],
                self.place.sibling,
            ).wait_recv(),
        )

    def own(self):
        p = self.place.pos
        cond = None
        if self.hi - self.lo != self.place.sizes[0]:
            cond = (p[0] >= self.lo) & (p[0] < self.hi)
        self.forward(cond, p, 0, False)

    def take(self, cond, q, via):
        self.wait(cond, self.place.owner(q))
        self.forward(cond, q, via, True)

    def line(self, distances=(1, 2, 3)):
        p = self.place.pos
        for distance in distances:
            for q0 in (p[0] - distance, p[0] + distance):
                self.take((q0 >= self.lo) & (q0 < self.hi), (q0, p[1], p[2]), 0)

    def second(self):
        for q0 in range(self.lo, self.hi):
            for qa, there in others(self.place, 1):
                self.take(there, (q0, qa, self.place.pos[2]), 1)

    def third(self):
        for qb, there in others(self.place, 2):
            for q0 in range(self.lo, self.hi):
                for qa in range(self.place.sizes[1]):
                    self.take(there, (q0, qa, qb), 2)

    def across(self):
        place = self.place
        per = place.sizes[1] * place.sizes[2]

        def body(j):
            self.wait(None, 2 * (self.lo * per + j) + 1 - place.core)

        loop((self.hi - self.lo) * per, body)

    def finish(self):
        for wait in self.waits:
            wait()
        self.waits = []


def landing(n):
    return 1 if n == 2 else n + 1


class Reduce:
    def __init__(self, place, units, lo, hi, land, sems, ready):
        self.place, self.units, self.lo, self.hi, self.land = place, units, lo, hi, land
        n0, na, nb = place.sizes
        self.count = (hi - lo) * na * nb
        lines = ((1, n0), (hi - lo, na), ((hi - lo) * na, nb))
        z_at = self.count
        b_at = z_at + landing(n0)
        a_at = b_at + lines[2][0] * landing(nb)
        self.land_at = (z_at, a_at, b_at)
        self.sems, self.ready = sems, ready
        at = 2 * self.count
        self.recv_at, self.up_at, self.down_at = [], [], []
        for units_here, n in lines:
            self.recv_at.append(at)
            at += units_here * landing(n)
            self.up_at.append(at)
            at += units_here * n
            self.down_at.append(at)
            at += units_here * n
        self.waits = []

    @staticmethod
    def slots(devices, share):
        side = math.isqrt(devices // 8)
        return share * side * side + landing(4) + share * (1 + side) * landing(side)

    @staticmethod
    def amount(devices, share):
        side = math.isqrt(devices // 8)
        total = 2 * share * side * side
        for units_here, n in ((1, 4), (share, side), (share * side, side)):
            total += units_here * (landing(n) + 2 * n)
        return total

    def stage(self, k):
        if k == 0:
            self.start()
        elif k == 1:
            self.pairs()
        elif k < 4:
            self.along(4 - k)
        else:
            self.hop(0, k - 3, [(None,) + self.place.pos[1:]])

    def unit(self, dim, q):
        na = self.place.sizes[1]
        return (0, q[0] - self.lo, (q[0] - self.lo) * na + q[1])[dim]

    def add(self, owner, slot):
        self.units.put(owner, self.units.get(owner) + self.land.get(slot))

    def start(self):
        place = self.place
        if self.ready is not None:
            signal(self.ready.at[0], place.sibling)
            for dim in range(3):
                for up in (True, False):
                    pl.when(place.has(dim, up))(
                        lambda dim=dim, up=up: signal(
                            self.ready.at[1 + 2 * dim + (1 if up else 0)], place.near(dim, up)
                        )
                    )
            pl.semaphore_wait(self.ready.at[0], 1)
        per = place.sizes[1] * place.sizes[2]

        def copy(j):
            owner = 2 * (self.lo * per + j) + 1 - place.core
            return remote(
                self.units.at(owner),
                self.land.at(j),
                self.sems.at[j],
                self.sems.at[self.count + j],
                place.sibling,
            )

        loop(self.count, lambda j: copy(j).start())
        self.waits.append(lambda: loop(self.count, lambda j: copy(j).wait_send()))

    def allow(self, dim):
        if self.ready is None:
            return
        for up in (True, False):
            pl.when(self.place.has(dim, up))(
                lambda up=up: pl.semaphore_wait(self.ready.at[1 + 2 * dim + (0 if up else 1)], 1)
            )

    def push(self, cond, dim, q, sem, slot, device):
        owner = self.place.owner(q)
        target = self.unit(dim, q) * landing(self.place.sizes[dim]) + slot

        def copy():
            return remote(
                self.units.at(owner),
                self.land.at(self.land_at[dim] + target),
                self.sems.at[sem],
                self.sems.at[self.recv_at[dim] + target],
                device,
            )

        gated(cond, lambda: copy().start())
        self.waits.append(lambda: gated(cond, lambda: copy().wait_send()))

    def pull(self, dim, q, slot):
        target = self.unit(dim, q) * landing(self.place.sizes[dim]) + slot
        piece = self.land.at(self.land_at[dim] + target)
        remote(
            piece,
            piece,
            self.sems.at[0],
            self.sems.at[self.recv_at[dim] + target],
            self.place.sibling,
        ).wait_recv()
        self.add(self.place.owner(q), self.land_at[dim] + target)

    def first(self, dim, q):
        place = self.place
        n, p = place.sizes[dim], place.pos[dim]
        u = self.unit(dim, q)
        if n == 2:
            toward = place.me + (1 - 2 * p) * place.step[dim]
            self.push(None, dim, q, self.up_at[dim] + u * n, 0, toward)
            return
        for up in (True, False):
            away = (q[dim] > 0) if up else (q[dim] < n - 1)
            self.push(
                (p == (0 if up else n - 1)) & away,
                dim,
                q,
                (self.up_at if up else self.down_at)[dim] + u * n + q[dim],
                self.slot_up(q[dim], 0) if up else self.slot_down(n, q[dim], n - 1),
                place.near(dim, up),
            )

    @staticmethod
    def slot_up(q, p):
        return q - (p + 1)

    @staticmethod
    def slot_down(n, q, p):
        to = p - 1
        return q + (n - to if to > 0 else 0)

    def order(self, dim):
        place = self.place
        if place.sizes[dim] == 2:
            return [1 - place.pos[dim], place.pos[dim]]
        return list(range(place.sizes[dim]))

    def mine(self, dim, at):
        return at is self.place.pos[dim]

    def pairs(self):
        place = self.place
        self.allow(2)
        for qb in self.order(2):
            for qa in self.order(1):
                for q0 in range(self.lo, self.hi):
                    q = (q0, qa, qb)
                    j = (q0 - self.lo) * place.half[0] + qa * place.half[1] + qb * place.half[2]
                    piece = self.land.at(j)
                    remote(
                        piece,
                        piece,
                        self.sems.at[0],
                        self.sems.at[self.count + j],
                        place.sibling,
                    ).wait_recv()
                    self.add(place.owner(q), j)
                    if not self.mine(2, qb):
                        self.first(2, q)

    def along(self, dim):
        place = self.place
        n, p = place.sizes[dim], place.pos[dim]
        self.allow(dim - 1)
        if dim == 2:
            rows = [(q0, qa) for qa in self.order(1) for q0 in range(self.lo, self.hi)]
        else:
            rows = [(q0,) for q0 in range(self.lo, self.hi)]

        def whole(row, at):
            return row + (at,) + place.pos[dim + 1 :]

        if n == 2:
            for row in rows:
                self.pull(dim, whole(row, p), 0)
                if not self.mine(dim - 1, row[dim - 1]):
                    self.first(dim - 1, whole(row, p))
        else:
            for k in range(1, n):
                self.hop(dim, k, [whole(row, None) for row in rows])
            for row in rows:
                self.first(dim - 1, whole(row, p))

    def hop(self, dim, k, rows):
        place = self.place
        n, p = place.sizes[dim], place.pos[dim]
        lo, hi = (self.lo, self.hi) if dim == 0 else (0, n)
        for up in (True, False):
            here = k if up else n - 1 - k
            cond = p == here
            span = range(max(lo, here), hi) if up else range(lo, min(hi, here + 1))
            if len(span) == 0:
                continue

            def receive(up=up, here=here, span=span):
                for row in rows:
                    for at in span:
                        slot = at - here if up else at + (n - here if here > 0 else 0)
                        q = row[:dim] + (at,) + row[dim + 1 :]
                        self.pull(dim, q, slot)
                        if at != here:
                            self.hop_copy(dim, q, up, here).start()

            pl.when(cond)(receive)
            for row in rows:
                for at in span:
                    if at != here:
                        q = row[:dim] + (at,) + row[dim + 1 :]
                        self.waits.append(
                            lambda cond=cond, q=q, up=up, here=here: pl.when(cond)(
                                lambda: self.hop_copy(dim, q, up, here).wait_send()
                            )
                        )

    def hop_copy(self, dim, q, up, here):
        place = self.place
        n = place.sizes[dim]
        u = self.unit(dim, q)
        slot = self.slot_up(q[dim], here) if up else self.slot_down(n, q[dim], here)
        target = u * landing(n) + slot
        return remote(
            self.units.at(place.owner(q)),
            self.land.at(self.land_at[dim] + target),
            self.sems.at[(self.up_at if up else self.down_at)[dim] + u * n + q[dim]],
            self.sems.at[self.recv_at[dim] + target],
            place.near(dim, up),
        )

    def finish(self):
        for wait in self.waits:
            wait()
        self.waits = []


class Total:
    def __init__(self, place, land, sems):
        self.place, self.land, self.sems = place, land, sems
        self.sizes = (2,) + place.sizes[::-1]
        self.at = [sum(self.sizes[:k]) for k in range(4)]
        self.waits = []

    @staticmethod
    def slots(devices):
        return 6 + 2 * math.isqrt(devices // 8)

    def lines(self, k):
        place = self.place
        if k == 0:
            return place.core, [(1, 1 - place.core, place.sibling)]
        return place.plain[3 - k], place.peers(3 - k)

    def send(self, k, value):
        p, peers = self.lines(k)
        here = self.land.at[self.at[k] + p]
        self.land[self.at[k] + p] = value
        half = self.at[3] + self.sizes[3]
        for r, _, device in peers:

            def copy(r=r, device=device):
                sems = self.sems
                return remote(
                    here, here, sems.at[self.at[k] + r], sems.at[half + self.at[k] + p], device
                )

            copy().start()
            self.waits.append(lambda copy=copy: copy().wait_send())

    def take(self, k):
        _, peers = self.lines(k)
        half = self.at[3] + self.sizes[3]
        for r, at, device in peers:
            there = self.land.at[self.at[k] + at]
            remote(
                there, there, self.sems.at[0], self.sems.at[half + self.at[k] + at], device
            ).wait_recv()
        total = self.land[self.at[k]]
        for s in range(1, self.sizes[k]):
            total = total + self.land[self.at[k] + s]
        return total

    def pass_on(self, k):
        value = self.take(k)
        if k < 3:
            self.send(k + 1, value)
        return value

    def finish(self):
        for wait in self.waits:
            wait()
        self.waits = []


class Ring:
    def __init__(self, me, devices, land, sems):
        self.after = (me + 1) % devices
        self.before = (me + devices - 1) % devices
        self.land, self.sems = land, sems

    def copies(self, to_before, to_after):
        return (
            remote(to_before, self.land.at[1], self.sems.at[0], self.sems.at[1], self.before),
            remote(to_after, self.land.at[0], self.sems.at[2], self.sems.at[3], self.after),
        )

    def start(self, to_before, to_after):
        for copy in self.copies(to_before, to_after):
            copy.start()

    def wait(self, to_before, to_after):
        for copy in self.copies(to_before, to_after):
            copy.wait_recv()

    def finish(self, to_before, to_after):
        for copy in self.copies(to_before, to_after):
            copy.wait_send()


def unit_shape(amount):
    across = min(amount, PANEL)
    return amount // across * BLOCK_ROWS, across * BLOCK_COLS


def own_unit(units, me, blocks):
    across = units.cols // BLOCK_COLS
    rows = []
    for a in range(units.rows // BLOCK_ROWS):
        row = [blocks[a * across + b].astype(bf16) for b in range(across)]
        rows.append(jnp.concatenate(row, axis=1))
    units.put(me, jnp.concatenate(rows, axis=0))


def network(
    idx_ref,
    positions_ref,
    species_ref,
    counts_ref,
    cot_ref,
    scale_ref,
    shift_ref,
    weight_ref,
    state_ref,
    blocks_ref,
    late_in,
    energy_ref,
    forces_ref,
    vector_ref,
    first_out,
    late_out,
    first_w,
    late_w,
    hot,
    z_t,
    z_r,
    geo,
    yrow,
    env_b,
    ee_t,
    en2_t,
    s1_t,
    s2_t,
    gam,
    dlt,
    coef,
    ds_t,
    de_t,
    dy,
    dg,
    dw_t,
    dw_r,
    dpf,
    den,
    lat,
    hid,
    low0,
    act1,
    sl1,
    low1,
    act2,
    sl2,
    low2,
    stage,
    halo,
    force_in,
    sides,
    vector_in,
    pack_ref,
    low_gather,
    mid_gather,
    high_gather,
    late_gather,
    late_sems,
    first_sems,
    ring_sems,
    vector_sems,
    ready,
):
    s_r = dw_r
    fact = den

    wee_t = dw_t.at[:, 0:LATENT]
    we2_t = dw_t.at[0:128, 0:LATENT]
    devices = lax.axis_size("atoms")
    me = lax.axis_index("atoms")
    place = Place(devices)
    own_at = pack_ref.at[0:8]
    first_units = Units(first_w, *unit_shape(blocks_ref.shape[0]))
    late_units = Units(late_w, *unit_shape(late_in.shape[0]))
    top = place.sizes[0]
    middle = top // 2

    def pieces(k):
        return Units(first_w, first_units.rows, first_units.cols, part=(k, PIECES))

    def free(ref, units, k=0, count=1):
        slots = Reduce.slots(devices, 1)
        return Units(ref, units.rows // count, units.cols, base=k * slots)

    gather_low = [Gather(place, pieces(k), 0, 1, low_gather.at[k]) for k in range(PIECES)]
    gather_mid = Gather(place, first_units, 1, middle, mid_gather)
    gather_high = Gather(place, first_units, middle, top, high_gather)
    gather_late = Gather(place, late_units, 0, top, late_gather, True)
    sum_out = Reduce(
        place, late_units, middle, top, free(low2, late_units), late_sems.at[0], ready.at[0]
    )
    sum_lat = Reduce(
        place, late_units, 0, middle, free(sl2, late_units), late_sems.at[1], ready.at[1]
    )
    sum_first = [
        [
            Reduce(
                place,
                pieces(k),
                z,
                z + 1,
                free(ref, first_units, k, PIECES),
                first_sems.at[PIECES * z + k],
                ready.at[2 + z] if k == 0 else None,
            )
            for k in range(PIECES)
        ]
        for z, ref in enumerate((hid, low0, sl1, act2))
    ]

    def advance(z, stage):
        for part in sum_first[z]:
            part.stage(stage)
    link_halo = Ring(me, devices, halo, ring_sems.at[0])
    link_force = Ring(me, devices, force_in, ring_sems.at[1])
    sum_vector = Total(place, vector_in, vector_sems)

    barrier = pltpu.get_barrier_semaphore()
    partners = [place.sibling, link_halo.before, link_halo.after]
    for dim in range(3):
        partners += [device for _, _, device in place.peers(dim)]
    for device in partners:
        signal(barrier, device)
    for part in (slice(0, PLANE), slice(PLANE, LANES)):
        pack_ref[0:3, part] = positions_ref[...]
        pack_ref[3:4, part] = species_ref[...].astype(f32)
        pack_ref[4:5, part] = counts_ref[...].astype(f32)
        pack_ref[5:6, part] = cot_ref[...]
    pack_ref[6:16] = jnp.zeros((10, LANES), f32)
    pack_ref[6:7, 0:SPECIES] = scale_ref[...]
    pack_ref[7:8, 0:SPECIES] = shift_ref[...]
    pack_ref[8:9] = weight_ref[...]
    pack_ref[9:10] = state_ref[...]
    own_unit(first_units, me, blocks_ref)
    own_unit(late_units, me, late_in)
    pl.semaphore_wait(barrier, len(partners))
    link_halo.start(own_at, own_at)
    for part in gather_low:
        part.own()

    ids = lax.broadcasted_iota(jnp.int32, (3 * PLANE, LANES), 0)

    whole = PLANE * devices
    coef[0, :, 0:SLOTS] = idx_ref[...].astype(f32)
    listed = coef[0].T[: SLOTS + 6].astype(jnp.int32) - (me - 1) * PLANE
    listed = jnp.where(
        listed < 0, listed + whole, jnp.where(listed >= whole, listed - whole, listed)
    )
    for t in range(TILES):
        near = jnp.concatenate([listed[2 * t : 2 * t + 1], listed[2 * t + 1 : 2 * t + 2]], axis=1)
        hot[:, t * LANES : (t + 1) * LANES] = jnp.where(ids == near, 1.0, 0.0).astype(bf16)

    link_halo.wait(own_at, own_at)
    own = pack_ref[0:8]
    lane = lax.broadcasted_iota(jnp.int32, (8, LANES), 1)
    row = lax.broadcasted_iota(jnp.int32, (8, LANES), 0)
    edge = spacing * devices
    x_row = row == 0
    before = halo[0] - jnp.where(x_row, jnp.where(me == 0, edge, 0.0), 0.0)
    after = halo[1] + jnp.where(x_row, jnp.where(me == devices - 1, edge, 0.0), 0.0)
    rank_y = ((lane & (PLANE - 1)) >> 3).astype(f32)
    rank_z = (lane & (SIDE - 1)).astype(f32)
    table = jnp.concatenate([jnp.where(lane < PLANE, before, own), after], axis=1)
    ranks = jnp.where(row == 4, rank_y, rank_z)
    table = jnp.where(
        jnp.concatenate([row, row], axis=1) < 4, table, jnp.concatenate([ranks, ranks], axis=1)
    )[:, : 3 * PLANE]
    ga, gb, gc = parts(table)
    got = nn(ga, hot[...]) + nn(gb, hot[...]) + nn(gc, hot[...])
    mine = jnp.concatenate([own] * TILES, axis=1)
    lane = lax.broadcasted_iota(jnp.int32, (1, ROWS), 1)
    slot = lane >> 6
    atom = lane & (PLANE - 1)

    def wrapped(step):
        return jnp.where(step > 1.5, -8.0, jnp.where(step < -1.5, 8.0, 0.0)) * spacing

    for part in gather_low:
        part.line()
    gather_mid.own()
    disp = [
        got[0:1] - mine[0:1],
        got[1:2] - mine[1:2] + wrapped(got[4:5] - (atom >> 3).astype(f32)),
        got[2:3] - mine[2:3] + wrapped(got[5:6] - (atom & (SIDE - 1)).astype(f32)),
    ]
    length = jnp.sqrt(disp[0] * disp[0] + disp[1] * disp[1] + disp[2] * disp[2])
    inverse = 1.0 / length
    unit = [disp[0] * inverse, disp[1] * inverse, disp[2] * inverse]
    angle = length * (math.pi / cutoff_radius)
    sin_k = [jnp.sin(angle)]
    cos_k = [jnp.cos(angle)]
    sin_k.append(2.0 * cos_k[0] * sin_k[0])
    cos_k.append(2.0 * cos_k[0] * cos_k[0] - 1.0)
    for k in range(2, BESSEL):
        sin_k.append(2.0 * cos_k[0] * sin_k[k - 1] - sin_k[k - 2])
        cos_k.append(2.0 * cos_k[0] * cos_k[k - 1] - cos_k[k - 2])
    sines = jnp.concatenate(sin_k, axis=0)
    cosines = jnp.concatenate(cos_k, axis=0)
    bessel = (math.sqrt(2.0 / cutoff_radius) * inverse) * sines
    scaled = length * (1.0 / cutoff_radius)
    t2 = scaled * scaled
    t4 = t2 * t2
    t5 = t4 * scaled
    t6 = t4 * t2
    envelope = 1.0 - 28.0 * t6 + 48.0 * (t6 * scaled) - 21.0 * (t4 * t4)
    denvelope = (-168.0 * t5 + 336.0 * t6 - 168.0 * (t6 * scaled)) * (1.0 / cutoff_radius)
    live = jnp.where(slot.astype(f32) < mine[4:5], 1.0, 0.0)

    kind = lax.broadcasted_iota(jnp.int32, (KINDS, LANES), 0).astype(f32)
    is_kind = kind == own[3:4]
    by_kind = own.T
    scale = jnp.sum(jnp.where(is_kind, by_kind[:KINDS, 6:7], 0.0), axis=0, keepdims=True)
    shift = jnp.sum(jnp.where(is_kind, by_kind[:KINDS, 7:8], 0.0), axis=0, keepdims=True)
    cot = jnp.concatenate([own[5:6] * scale] * TILES, axis=1) * live
    weight = cot * envelope

    root3 = math.sqrt(3.0)
    root15 = math.sqrt(15.0)
    root5 = math.sqrt(5.0)
    ux, uy, uz = unit
    yrow[0:8] = jnp.concatenate(
        [
            root3 * ux,
            root3 * uy,
            root3 * uz,
            root15 * ux * uy,
            root15 * uy * uz,
            0.5 * root5 * (3.0 * uz * uz - 1.0),
            root15 * ux * uz,
            0.5 * root15 * (ux * ux - uy * uy),
        ],
        axis=0,
    )
    yrow[8:16] = yrow[0:8] * (live * env_scale)
    yrow[16:17] = live * env_scale
    geo[0:8] = jnp.concatenate([ux, uy, uz, inverse, envelope, denvelope, live, cot], axis=0)
    geo[8:16] = math.sqrt(2.0 / cutoff_radius) * (
        (math.pi / cutoff_radius)
        * lax.broadcasted_iota(jnp.int32, (BESSEL, ROWS), 0).astype(f32)
        * cosines
        + (math.pi / cutoff_radius) * cosines
        - sines * inverse
    ) * inverse

    for part in gather_low:
        part.second()
    gather_mid.line()
    gather_high.own()

    def one_hots(t):
        row = lax.broadcasted_iota(jnp.int32, (LANES, LANES), 0).astype(f32)
        here = jnp.where(row == own[3:4] + float(BESSEL), 1.0, 0.0)
        there = jnp.where(row == kinds_near[t] + float(BESSEL + SPECIES), 1.0, 0.0)
        return here + there

    kinds_near = [got[3:4, t * LANES : (t + 1) * LANES] for t in range(TILES)]
    for t in range(TILES):
        at = slice(t * LANES, (t + 1) * LANES)
        column = jnp.concatenate([bessel[:, at], one_hots(t)[BESSEL:]], axis=0)
        z_t[:, at] = column.astype(bf16)
        z_r[at, :] = column.T.astype(bf16)
        env_b[at, :] = jnp.broadcast_to(envelope[:, at], (LANES, LANES)).T
        fact[at, :] = jnp.broadcast_to(weight[:, at], (LANES, LANES)).T

    for part in gather_low:
        part.third()
    gather_mid.second()
    gather_high.line((1,))
    for part in gather_low:
        part.across()

    def twice(x):
        return jnp.concatenate([x] * (STRIP // LANES), axis=1)

    def in_body(n, r):
        pre = nn(z_r[r], cols_panel(first_w, W_INPUT, n))
        hid[r, panel(n, STRIP)] = (pre * sigmoid(pre)).astype(bf16)

    loop_panels(in_body)
    gather_mid.third()
    gather_high.line((2,))
    gather_high.line((3,))
    gather_high.second()
    gather_late.own()
    gather_mid.across()

    def two_body(n, r):
        zero = nn(hid[r], cols_panel(first_w, W_TWO, n)) * twice(env_b[r])
        lat[r, panel(n, STRIP)] = zero
        low0[r, panel(n, STRIP)] = zero.astype(bf16)

    loop_panels(two_body)

    def transposed_product(out, weights, right, width=256):
        at = 0
        while at < ROWS:
            end = min(at + width, ROWS)
            out[:, at:end] = nt(weights, right[at:end, :])
            at = end

    gather_high.third()
    wee_t[0:128, :] = narrow(first_w, W_EMBED).T
    wee_t[128:256, :] = narrow(first_w, W_ENV_ONE).T
    transposed_product(ee_t, wee_t[...], low0)

    def environment(out, v0_ref, v0_at, v1_at):
        for m in range(9):
            total = None
            begin = v0_at if m == 0 else v1_at
            y = yrow[16:17, :] if m == 0 else yrow[7 + m : 8 + m, :]
            for t in range(TILES):
                at = slice(t * LANES, (t + 1) * LANES)
                term = v0_ref[begin : begin + CHANNELS, at] * y[:, at]
                total = term if total is None else total + term
            out[m] = halves(total)

    def put_scalars(t, s_t, rows):
        s_t[:, lanes(t)] = jnp.concatenate(rows, axis=0).astype(bf16)
        filled = jnp.concatenate(rows + [jnp.zeros_like(rows[0])], axis=0)
        flipped = filled.T.astype(bf16)
        s_r[lanes(t), :] = flipped

    def weighted(y, first, count, source, offset):
        total = None
        for m in range(count):
            term = y[first + m : first + m + 1] * source[offset + m]
            total = term if total is None else total + term
        return total

    gather_late.line()
    environment(gam, ee_t, 128, 192)

    def scalars_one(t):
        e0 = ee_t[0:64, lanes(t)]
        e1 = ee_t[64:128, lanes(t)]
        y = yrow[0:8, lanes(t)]
        put_scalars(
            t,
            s1_t,
            [e0 * gam[0], e1 * weighted(y, 0, 3, gam, 1), e1 * weighted(y, 3, 5, gam, 4)],
        )

    each(TILES, scalars_one)

    gather_late.second()
    gather_high.across()
    def pre_one(n, r):
        pre = nn(low0[r], cols_panel(first_w, W_LAT_ONE, n)) + nn(
            s_r[r, : 3 * CHANNELS], cols_panel(first_w, W_SCAL_ONE, n)
        )
        sig = sigmoid(pre)
        act = pre * sig
        act1[r, panel(n, STRIP)] = act.astype(bf16)
        sl1[r, panel(n, STRIP)] = (sig + act * (1.0 - sig)).astype(bf16)

    loop_panels(pre_one)
    gather_late.third()

    def out_one(n, r):
        new = (lat[r, panel(n, STRIP)] + nn(act1[r], cols_panel(first_w, W_OUT_ONE, n))) * half_root
        lat[r, panel(n, STRIP)] = new
        low1[r, panel(n, STRIP)] = new.astype(bf16)

    loop_panels(out_one)
    we2_t[...] = narrow(first_w, W_ENV_TWO).T
    transposed_product(en2_t, we2_t[...], low1)
    environment(dlt, en2_t, 0, 64)

    g0 = gam[0]
    coef[0] = g0 * dlt[0]
    for m in range(3):
        a, b = 1 + (m + 1) % 3, 1 + (m + 2) % 3
        coef[1 + m] = g0 * dlt[1 + m] + (gam[a] * dlt[b] - gam[b] * dlt[a])
    coef[9] = gam[1] * dlt[1] + gam[2] * dlt[2] + gam[3] * dlt[3]
    second = None
    for m in range(4, 9):
        coef[m] = g0 * dlt[m]
        term = gam[m] * dlt[m]
        second = term if second is None else second + term
    coef[10] = second

    def scalars_two(t):
        e0 = ee_t[0:64, lanes(t)]
        e1 = ee_t[64:128, lanes(t)]
        y = yrow[0:8, lanes(t)]
        put_scalars(
            t,
            s2_t,
            [
                e0 * coef[0],
                e1 * weighted(y, 0, 3, coef, 1) + e0 * coef[9],
                e1 * weighted(y, 3, 5, coef, 4) + e0 * coef[10],
            ],
        )

    each(TILES, scalars_two)

    gather_late.across()
    for part in gather_low + [gather_mid, gather_high, gather_late]:
        part.finish()
    def pre_two(n, r):
        pre = nn(low1[r], cols_panel(late_w, W_LAT_TWO, n)) + nn(
            s_r[r, : 3 * CHANNELS], cols_panel(first_w, W_SCAL_TWO, n)
        )
        sig = sigmoid(pre)
        act = pre * sig
        act2[r, panel(n, STRIP)] = act.astype(bf16)
        sl2[r, panel(n, STRIP)] = (sig + act * (1.0 - sig)).astype(bf16)

    loop_panels(pre_two)

    def out_two(n, r):
        new = (lat[r, panel(n, STRIP)] + nn(act2[r], cols_panel(late_w, W_OUT_TWO, n))) * half_root
        low2[r, panel(n, STRIP)] = new.astype(bf16)

    loop_panels(out_two)

    vec = jnp.broadcast_to(pack_ref[8:9], (8, LANES))
    stage[...] = narrow(first_w, W_FINAL)

    def read_out(i):
        r = pl.ds(pl.multiple_of(i * 416, 16), 416)
        pre = nn(low2[r, :], stage[...])
        sig = sigmoid(pre)
        final_act = pre * sig
        dpf[r, :] = (fact[r, :] * vec[0:1] * (sig + final_act * (1.0 - sig))).astype(bf16)
        fact[r, :] = final_act

    loop(4, read_out)
    value = nt(vec, fact[...], highest)[0:1]
    geo_live = geo[6:7]
    geo_env = geo[4:5]
    geo_cot = geo[7:8]
    edge_energy = geo_live * geo_env * value
    summed = None
    for t in range(TILES):
        term = edge_energy[:, t * LANES : (t + 1) * LANES]
        summed = term if summed is None else summed + term
    energy_ref[...] = scale * halves(summed) + shift
    all_weights = jnp.broadcast_to(geo_cot * geo_env, (8, ROWS))
    sum_vector.send(0, nn(all_weights, fact[...], highest))
    geo[16:17] = geo_cot * value

    def big_grad(out, where, left, right):
        def step(i):
            grad = tn(left[:, panel(i, STRIP)], right[...])
            out[pl.ds(pl.multiple_of(where[0] + i * STRIP, 64), STRIP), :] = grad.astype(bf16)

        loop(LATENT // STRIP, step)

    def wide_grad(out, where, left, right):
        def step(n):
            out[where[0] : where[0] + where[1], panel(n)] = nn(
                left[...], right[:, panel(n)]
            ).astype(bf16)

        loop(4, step)

    def narrow_grad(left, right, put):
        def step(n):
            put(n, nn(left, right[:, panel(n)]).T.astype(bf16))

        loop(4, step)

    def put_narrow(where, n, grad):
        row = pl.multiple_of(where[0] + n // 2 * BLOCK_ROWS, BLOCK_ROWS)
        col = pl.multiple_of(n % 2 * 512, 512)
        first_w[pl.ds(row, BLOCK_ROWS), pl.ds(col, 512)] = jnp.concatenate(
            [grad[b * BLOCK_ROWS : (b + 1) * BLOCK_ROWS] for b in range(4)], axis=1
        )

    def put_stage(n, grad):
        stage[panel(n), :] = grad

    narrow_grad(dpf[...].T, low2, put_stage)

    def back_final(n, r):
        grad = nt(dpf[r], narrow_panel(first_w, W_FINAL, n)) * half_root
        lat[r, panel(n, STRIP)] = grad
        low2[r, panel(n, STRIP)] = grad.astype(bf16)

    loop_panels(back_final)
    loop(4, lambda n: put_narrow(W_FINAL, n, stage[panel(n), :]))

    def back_out_two(n, r):
        grad = nt(low2[r], rows_panel(late_w, W_OUT_TWO, n))
        sl2[r, panel(n, STRIP)] = (grad * sl2[r, panel(n, STRIP)].astype(f32)).astype(bf16)

    loop_panels(back_out_two)
    transposed_product(ds_t, first_w[W_SCAL_TWO[0] : W_SCAL_TWO[0] + W_SCAL_TWO[1], :], sl2)
    wide_grad(first_w, W_SCAL_TWO, s2_t, sl2)
    big_grad(late_w, W_OUT_TWO, act2, low2)
    sum_out.stage(0)
    sum_vector.pass_on(0)

    dg[...] = jnp.zeros_like(dg)

    def tensors_two(t):
        e0 = ee_t[0:64, lanes(t)]
        e1 = ee_t[64:128, lanes(t)]
        y = yrow[0:8, lanes(t)]
        r0 = ds_t[0:64, lanes(t)]
        r1 = ds_t[64:128, lanes(t)]
        r2 = ds_t[128:192, lanes(t)]
        de_t[0:64, lanes(t)] = r0 * coef[0] + r1 * coef[9] + r2 * coef[10]
        de_t[64:128, lanes(t)] = r1 * weighted(y, 0, 3, coef, 1) + r2 * weighted(y, 3, 5, coef, 4)
        p1 = r1 * e1
        p2 = r2 * e1
        rows = []
        for m in range(8):
            p = p1 if m < 3 else p2
            rows.append(jnp.sum(p * coef[1 + m], axis=0, keepdims=True))
            dg[1 + m] += p * y[m : m + 1]
        dy[:, lanes(t)] = jnp.concatenate(rows, axis=0)
        dg[0] += r0 * e0
        dg[9] += r1 * e0
        dg[10] += r2 * e0

    each(TILES, tensors_two)
    sum_out.stage(1)
    total = [halves(dg[m]) for m in range(11)]
    g0 = gam[0]
    d0 = dlt[0]
    new_g0 = total[0] * d0
    for m in range(1, 9):
        new_g0 = new_g0 + total[m] * dlt[m]
    dlt_grads = [total[0] * g0]
    gam_grads = [new_g0]
    for m in range(3):
        a, b = 1 + (m + 1) % 3, 1 + (m + 2) % 3
        dlt_grads.append(
            total[1 + m] * g0 + total[9] * gam[1 + m] + (total[a] * gam[b] - total[b] * gam[a])
        )
        gam_grads.append(total[9] * dlt[1 + m] + (dlt[a] * total[b] - dlt[b] * total[a]))
    for m in range(4, 9):
        dlt_grads.append(total[m] * g0 + total[10] * gam[m])
        gam_grads.append(total[10] * dlt[m])
    for m in range(9):
        dlt[m] = dlt_grads[m]
        dg[m] = gam_grads[m]

    def environment_back(t, grads, source, v1_at, at):
        y4 = yrow[8:16, lanes(t)]
        l4 = yrow[16:17, lanes(t)]
        v1 = source[v1_at : v1_at + 64, lanes(t)]
        low = l4 * grads[0]
        high = weighted(y4, 0, 8, grads, 1)
        both = jnp.concatenate([low, high], axis=0)
        dw_t[at : at + 128, lanes(t)] = both.astype(bf16)
        dw_r[lanes(t), at : at + 128] = both.T.astype(bf16)
        v1 = v1 * l4
        rows = [jnp.sum(v1 * grads[1 + m], axis=0, keepdims=True) for m in range(8)]
        dy[:, lanes(t)] += jnp.concatenate(rows, axis=0)

    each(TILES, lambda t: environment_back(t, dlt, en2_t, 64, 128))

    def back_lat_two(n, r):
        grad = (
            lat[r, panel(n, STRIP)]
            + nt(sl2[r], rows_panel(late_w, W_LAT_TWO, n))
            + nt(dw_r[r, 128:256], narrow_panel(first_w, W_ENV_TWO, n))
        ) * half_root
        lat[r, panel(n, STRIP)] = grad
        act2[r, panel(n, STRIP)] = grad.astype(bf16)

    loop_panels(back_lat_two)
    sum_out.stage(2)
    big_grad(late_w, W_LAT_TWO, low1, sl2)
    sum_out.stage(3)
    narrow_grad(dw_t[128:256, :], low1, functools.partial(put_narrow, W_ENV_TWO))
    sum_lat.stage(0)
    sum_vector.pass_on(1)

    def back_out_one(n, r):
        grad = nt(act2[r], rows_panel(first_w, W_OUT_ONE, n))
        sl1[r, panel(n, STRIP)] = (grad * sl1[r, panel(n, STRIP)].astype(f32)).astype(bf16)

    loop_panels(back_out_one)
    sum_out.stage(4)
    sum_lat.stage(1)
    big_grad(first_w, W_OUT_ONE, act1, act2)
    advance(3, 0)
    sum_out.stage(5)
    sum_lat.stage(2)
    transposed_product(ds_t, first_w[W_SCAL_ONE[0] : W_SCAL_ONE[0] + W_SCAL_ONE[1], :], sl1)
    wide_grad(first_w, W_SCAL_ONE, s1_t, sl1)
    sum_out.stage(6)
    sum_lat.stage(3)
    advance(3, 1)
    sum_vector.pass_on(2)

    def tensors_one(t):
        e0 = ee_t[0:64, lanes(t)]
        e1 = ee_t[64:128, lanes(t)]
        y = yrow[0:8, lanes(t)]
        r0 = ds_t[0:64, lanes(t)]
        r1 = ds_t[64:128, lanes(t)]
        r2 = ds_t[128:192, lanes(t)]
        low = de_t[0:64, lanes(t)] + r0 * gam[0]
        high = (
            de_t[64:128, lanes(t)]
            + r1 * weighted(y, 0, 3, gam, 1)
            + r2 * weighted(y, 3, 5, gam, 4)
        )
        both = jnp.concatenate([low, high], axis=0)
        dw_t[0:128, lanes(t)] = both.astype(bf16)
        dw_r[lanes(t), 0:128] = both.T.astype(bf16)
        p1 = r1 * e1
        p2 = r2 * e1
        rows = []
        for m in range(8):
            p = p1 if m < 3 else p2
            rows.append(jnp.sum(p * gam[1 + m], axis=0, keepdims=True))
            coef[1 + m] += p * y[m : m + 1]
        dy[:, lanes(t)] += jnp.concatenate(rows, axis=0)
        coef[0] += r0 * e0

    for m in range(9):
        coef[m] = jnp.zeros((CHANNELS, LANES), f32)
    each(TILES, tensors_one)
    sum_lat.stage(4)
    advance(3, 2)
    for m in range(9):
        dg[m] = dg[m] + halves(coef[m])
    each(TILES, lambda t: environment_back(t, dg, ee_t, 192, 128))
    sum_lat.stage(5)
    advance(3, 3)

    den[...] = jnp.zeros_like(den)

    def back_lat_one(n, r):
        both = jnp.concatenate(
            [narrow_panel(first_w, W_EMBED, n), narrow_panel(first_w, W_ENV_ONE, n)], axis=1
        )
        grad = (
            lat[r, panel(n, STRIP)]
            + nt(sl1[r], rows_panel(first_w, W_LAT_ONE, n))
            + nt(dw_r[r], both)
        )
        low1[r, panel(n, STRIP)] = (grad * twice(env_b[r])).astype(bf16)
        part = grad * low0[r, panel(n, STRIP)].astype(f32)
        for b in range(STRIP // LANES):
            den[r] += part[:, b * LANES : (b + 1) * LANES]

    loop_panels(back_lat_one)
    sum_lat.stage(6)
    advance(3, 4)

    def back_two(n, r):
        grad = nt(low1[r], rows_panel(first_w, W_TWO, n))
        pre = nn(z_r[r], cols_panel(first_w, W_INPUT, n))
        sig = sigmoid(pre)
        act1[r, panel(n, STRIP)] = (grad * (sig + pre * sig * (1.0 - sig))).astype(bf16)

    loop_panels(back_two)
    advance(3, 5)
    big_grad(first_w, W_TWO, hid, low1)
    transposed_product(ds_t.at[0:64], first_w[0:64, :], act1)
    wide_grad(first_w, W_INPUT, z_t, act1)
    advance(0, 0)
    advance(3, 6)
    narrow_grad(dw_t[0:128, :], low0, functools.partial(put_narrow, W_EMBED))
    narrow_grad(dw_t[128:256, :], low0, functools.partial(put_narrow, W_ENV_ONE))
    advance(0, 1)
    big_grad(first_w, W_LAT_ONE, low0, sl1)
    advance(1, 0)
    advance(2, 0)
    advance(0, 2)

    dbessel = ds_t[0:8, :]
    through = nt(jnp.ones((8, LANES), f32), den[...], highest)[0:1]
    ux, uy, uz = geo[0:1], geo[1:2], geo[2:3]
    inverse = geo[3:4]
    envelope = geo[4:5]
    denv = geo[16:17] + through / envelope
    dlength = jnp.sum(dbessel * geo[8:16], axis=0, keepdims=True) + denv * geo[5:6]
    g = [dy[m : m + 1, :] for m in range(8)]
    dux = root3 * g[0] + root15 * (uy * g[3] + uz * g[6] + ux * g[7])
    duy = root3 * g[1] + root15 * (ux * g[3] + uz * g[4] - uy * g[7])
    duz = root3 * g[2] + root15 * (uy * g[4] + ux * g[6]) + (3.0 * root5) * uz * g[5]
    along = dlength - (ux * dux + uy * duy + uz * duz) * inverse
    near = jnp.concatenate(
        [
            dux * inverse + ux * along,
            duy * inverse + uy * along,
            duz * inverse + uz * along,
            jnp.zeros((5, ROWS), f32),
        ],
        axis=0,
    )
    advance(1, 1)
    advance(2, 1)
    advance(0, 3)
    summed = None
    for t in range(TILES):
        term = near[:, t * LANES : (t + 1) * LANES]
        summed = term if summed is None else summed + term
    centre = halves(summed)
    na, nb, nc = parts(near)
    spread = nt(na, hot[...]) + nt(nb, hot[...]) + nt(nc, hot[...])
    sides[0] = spread[:, :LANES]
    sides[1, :, 0:PLANE] = spread[:, LANES:]
    link_force.start(sides.at[0], sides.at[1])
    for step in range(5 + PIECES - 1):
        for k in range(PIECES):
            if 0 <= step - k < 3:
                sum_first[0][k].stage(4 + step - k)
            if 0 <= step - k < 5:
                sum_first[1][k].stage(2 + step - k)
                sum_first[2][k].stage(2 + step - k)
    link_force.wait(sides.at[0], sides.at[1])
    forces_ref[...] = (
        centre - pltpu.roll(sides[0], PLANE, 1) - force_in[1] - force_in[0]
    )
    total = sum_vector.pass_on(3)
    normed = total * lax.rsqrt(jnp.sum(total[0:1] * total[0:1]) * (1.0 / FINAL) + epsilon)
    state = decay_rate * pack_ref[9:10] + (1.0 - decay_rate) * normed * normed
    vector_ref[0:1] = total[0:1]
    vector_ref[1:2] = state[0:1]
    vector_ref[2:3] = (pack_ref[8:9] - vector_rate * normed * lax.rsqrt(state + epsilon))[0:1]
    first_out[...] = first_units.get(me)
    late_out[...] = late_units.get(me)
    for group in sum((list(parts) for parts in sum_first), [sum_out, sum_lat, sum_vector]):
        group.finish()
    link_halo.finish(own_at, own_at)
    link_force.finish(sides.at[0], sides.at[1])


def run_network(devices, small, blocks, late):
    S = jax.ShapeDtypeStruct
    wide = pltpu.VMEM((ROWS, LATENT), bf16)
    slab = pltpu.VMEM((ROWS, LANES), f32)
    panels = lambda amount: pltpu.VMEM((amount * devices // PANEL * BLOCK_ROWS, WIDE), bf16)
    scratch = [
        panels(blocks.shape[0]),
        panels(late.shape[0]),
        pltpu.VMEM((3 * PLANE, ROWS), bf16),
        pltpu.VMEM((LANES, ROWS), bf16),
        pltpu.VMEM((ROWS, LANES), bf16),
        pltpu.VMEM((24, ROWS), f32),
        pltpu.VMEM((24, ROWS), f32),
        slab,
        pltpu.VMEM((256, ROWS), f32),
        pltpu.VMEM((128, ROWS), f32),
        pltpu.VMEM((192, ROWS), bf16),
        pltpu.VMEM((192, ROWS), bf16),
        pltpu.VMEM((9, CHANNELS, LANES), f32),
        pltpu.VMEM((9, CHANNELS, LANES), f32),
        pltpu.VMEM((11, CHANNELS, LANES), f32),
        pltpu.VMEM((192, ROWS), f32),
        pltpu.VMEM((128, ROWS), f32),
        pltpu.VMEM((8, ROWS), f32),
        pltpu.VMEM((11, CHANNELS, LANES), f32),
        pltpu.VMEM((256, ROWS), bf16),
        pltpu.VMEM((ROWS, 256), bf16),
        pltpu.VMEM((ROWS, LANES), bf16),
        slab,
        pltpu.VMEM((ROWS, LATENT), f32),
    ] + [wide] * 8 + [
        pltpu.VMEM((LATENT, LANES), bf16),
        pltpu.VMEM((2, 8, LANES), f32),
        pltpu.VMEM((2, 8, LANES), f32),
        pltpu.VMEM((2, 8, LANES), f32),
        pltpu.VMEM((Total.slots(devices), 8, LANES), f32),
        pltpu.VMEM((16, LANES), f32),
        pltpu.SemaphoreType.DMA((PIECES, Gather.amount(devices, 1))),
        pltpu.SemaphoreType.DMA((Gather.amount(devices, 1),)),
        pltpu.SemaphoreType.DMA((Gather.amount(devices, 2),)),
        pltpu.SemaphoreType.DMA((Gather.amount(devices, 4),)),
        pltpu.SemaphoreType.DMA((2, Reduce.amount(devices, 2))),
        pltpu.SemaphoreType.DMA((4 * PIECES, Reduce.amount(devices, 1))),
        pltpu.SemaphoreType.DMA((2, 4)),
        pltpu.SemaphoreType.DMA((2 * Total.slots(devices),)),
        pltpu.SemaphoreType.REGULAR((6, 7)),
    ]
    vmem = pl.BlockSpec(memory_space=pltpu.VMEM)
    return pl.pallas_call(
        network,
        out_shape=[
            S((1, LANES), f32),
            S((8, LANES), f32),
            S((8, LANES), f32),
            S(unit_shape(blocks.shape[0]), bf16),
            S(unit_shape(late.shape[0]), bf16),
        ],
        in_specs=[vmem] * (len(small) + 2),
        out_specs=[vmem] * 5,
        scratch_shapes=scratch,
        compiler_params=pltpu.CompilerParams(
            vmem_limit_bytes=63 << 20, collective_id=0, has_side_effects=True
        ),
        name="network",
    )(*small, blocks, late)


def shampoo(
    energy,
    force,
    vectors,
    grads,
    left,
    right,
    left_root,
    right_root,
    master,
    late_grads,
    late_left,
    late_right,
    late_left_root,
    late_right_root,
    late_master,
    energy_out,
    force_out,
    vector_out,
    state_out,
    moved_out,
    *outs,
):
    energy_out[...] = energy[:, :PLANE]
    force_out[...] = force[0:3, :PLANE]
    vector_out[...] = vectors[0:1]
    state_out[...] = vectors[1:2]
    moved_out[...] = vectors[2:3]

    todo = []
    for j in range(left.shape[0]):
        todo.append((grads, j, left, right, left_root, right_root, master) + outs[:4])
    for j in range(late_left.shape[0]):
        todo.append(
            (late_grads, j, late_left, late_right, late_left_root, late_right_root, late_master)
            + outs[4:]
        )
    size = 1.0 / (BLOCK_ROWS * BLOCK_COLS)
    held, scales, steps = [], [], []
    for panels, j, left, *_ in todo:
        per = panels.shape[1] // BLOCK_COLS
        at = pl.program_id(0) * left.shape[0] + j
        row = pl.multiple_of(at // per * BLOCK_ROWS, BLOCK_ROWS)
        col = pl.multiple_of(at % per * BLOCK_COLS, BLOCK_COLS)
        held.append(panels[pl.ds(row, BLOCK_ROWS), pl.ds(col, BLOCK_COLS)])
    for g, (_, j, *_, grad_out, left_out, right_out, master_out) in zip(held, todo):
        grad = g.astype(f32)
        grad_out[j] = grad
        scales.append(lax.rsqrt(jnp.sum(grad * grad, keepdims=True) * size + epsilon))
    turned = []
    for g, (_, j, left, right, left_root, *_) in zip(held, todo):
        la, lb, _ = parts(left_root[j])
        turned.append(nn(la, g) + nn(lb, g))
    for g, s, (_, j, left, right, *_, grad_out, left_out, right_out, master_out) in zip(
        held, scales, todo
    ):
        square = (1.0 - decay_rate) * s * s
        left_out[j] = decay_rate * left[j] + square * nt(g, g)
        right_out[j] = decay_rate * right[j] + square * tn(g, g)
    for turn, s, (_, j, left, right, left_root, right_root, *_) in zip(turned, scales, todo):
        ra, rb, _ = parts(right_root[j])
        ta, tb, _ = parts(turn * s)
        steps.append(nn(ta, ra) + (nn(ta, rb) + nn(tb, ra)))
    for step, (_, j, left, right, left_root, right_root, master, *_, master_out) in zip(steps, todo):
        slope = lax.rsqrt(jnp.sum(step * step, keepdims=True) * size + epsilon)
        master_out[j] = master[j] - (learn_rate * slope) * step


def run_shampoo(energy, force, vectors, first, late):
    S = jax.ShapeDtypeStruct
    steps = min(4, late[1].shape[0])

    def whole(x):
        return pl.BlockSpec(x.shape, lambda i: (0,) * len(x.shape))

    def share(x):
        return pl.BlockSpec((x.shape[0] // steps,) + x.shape[1:], lambda i: (i, 0, 0))

    small = [S((1, PLANE), f32), S((3, PLANE), f32)] + [S((1, FINAL), f32)] * 3
    grown = []
    for group in (first, late):
        left, right, _, _, master = group[1:]
        grown += [S(x.shape, f32) for x in (master, left, right, master)]
    return pl.pallas_call(
        shampoo,
        grid=(steps,),
        out_shape=small + grown,
        in_specs=[whole(energy), whole(force), whole(vectors)]
        + [whole(first[0])]
        + [share(x) for x in first[1:]]
        + [whole(late[0])]
        + [share(x) for x in late[1:]],
        out_specs=[whole(x) for x in small] + [share(x) for x in grown],
        compiler_params=pltpu.CompilerParams(vmem_limit_bytes=60 << 20),
        name="shampoo",
    )(energy, force, vectors, *first, *late)


def local(
    positions,
    species,
    neighbours,
    counts,
    species_scale,
    species_shift,
    energy_cot,
    blocks,
    left,
    right,
    left_root,
    right_root,
    late_blocks,
    late_left,
    late_right,
    late_left_root,
    late_right_root,
    out_vector,
    vector_state,
):
    devices = lax.axis_size("atoms")
    small = (
        neighbours.reshape(PLANE, SLOTS),
        positions,
        species[None],
        counts[None],
        energy_cot[None],
        species_scale[None],
        species_shift[None],
        out_vector[None],
        vector_state[None],
    )
    energy, force, vectors, first_units, late_units = run_network(
        devices, small, blocks, late_blocks
    )
    out = run_shampoo(
        energy,
        force,
        vectors,
        (first_units, left, right, left_root, right_root, blocks),
        (late_units, late_left, late_right, late_left_root, late_right_root, late_blocks),
    )
    energies, forces, vector_grad, new_state, new_vector = out[:5]
    return (
        energies.reshape(-1),
        forces,
        *out[5:],
        vector_grad.reshape(-1),
        new_state.reshape(-1),
        new_vector.reshape(-1),
    )


def solution(mesh):
    row = P("atoms")
    block = P("atoms", None, None)
    placed = (
        (P(None, "atoms"), row, row, row, P(), P(), row)
        + (block,) * 10
        + (P(), P())
    )
    return jax.shard_map(
        local,
        mesh=mesh,
        in_specs=placed,
        out_specs=(row, P(None, "atoms")) + (block,) * 8 + (P(), P(), P()),
        check_vma=False,
    )
```

```python
import functools
import math

import jax
import jax.numpy as jnp
from jax import lax
from jax.experimental import pallas as pl
from jax.experimental.pallas import tpu as pltpu
from jax.sharding import PartitionSpec as P

SIDE = 8
SLOTS = 26
SPECIES = 60
BESSEL = 8
CHANNELS = 64
LATENT = 1024
FINAL = 128
BLOCK_ROWS = 64
BLOCK_COLS = 128
PLANE = SIDE * SIDE

f32 = jnp.float32
bf16 = jnp.bfloat16
highest = lax.Precision.HIGHEST
spacing = 1.6
cutoff_radius = 4.0
env_scale = 0.25
half_root = 0.7071067811865476
decay_rate = 0.5
learn_rate = 0.02
vector_rate = 0.03
epsilon = 1e-06

LANES = 128
ROWS = SLOTS * PLANE
TILES = ROWS // LANES
KINDS = 64

PANEL = 8
WIDE = PANEL * BLOCK_COLS
W_INPUT = (0, 128)
W_TWO = (128, 1024)
W_EMBED = (1152, 128)
W_ENV_ONE = (1280, 128)
W_LAT_ONE = (1408, 1024)
W_SCAL_ONE = (2432, 192)
W_OUT_ONE = (2624, 1024)
W_ENV_TWO = (3648, 128)
W_SCAL_TWO = (3776, 192)
W_FINAL = (3968, 128)
W_LAT_TWO = (0, 1024)
W_OUT_TWO = (1024, 1024)

MESH = pl.DeviceIdType.MESH


def nn(a, b, precision=None):
    return lax.dot_general(
        a, b, (((1,), (0,)), ((), ())), preferred_element_type=f32, precision=precision
    )


def nt(a, b, precision=None):
    return lax.dot_general(
        a, b, (((1,), (1,)), ((), ())), preferred_element_type=f32, precision=precision
    )


def tn(a, b):
    return lax.dot_general(a, b, (((0,), (0,)), ((), ())), preferred_element_type=f32)


def cols_panel(ref, where, n):
    return ref[where[0] : where[0] + where[1], panel(n, STRIP)]


def rows_panel(ref, where, n):
    return ref[pl.ds(pl.multiple_of(where[0] + n * STRIP, 64), STRIP), :]


def narrow(ref, where):
    pieces = []
    for j in range(LATENT // BLOCK_ROWS):
        row = where[0] + j // PANEL * BLOCK_ROWS
        col = j % PANEL * BLOCK_COLS
        pieces.append(ref[row : row + BLOCK_ROWS, col : col + BLOCK_COLS])
    return jnp.concatenate(pieces, axis=0)


def narrow_panel(ref, where, n):
    part = ref[pl.ds(pl.multiple_of(where[0] + n * BLOCK_ROWS, BLOCK_ROWS), BLOCK_ROWS), :]
    return jnp.concatenate([part[:, b * 128 : (b + 1) * 128] for b in range(PANEL)], axis=0)


def sigmoid(x):
    return 0.5 * jnp.tanh(0.5 * x) + 0.5


def halves(x):
    return x + pltpu.roll(x, PLANE, 1)


def lanes(t):
    if isinstance(t, int):
        return pl.ds(t * LANES, LANES)
    return pl.ds(pl.multiple_of(t * LANES, LANES), LANES)


def panel(n, width=256):
    return pl.ds(pl.multiple_of(n * width, width), width)


STRIP = 512
CHUNKS = 2
PIECES = 4
SUM_PIECES = (2, 2, 2, 1)
CHUNK = ROWS // CHUNKS


def loop_panels(body):
    def step(n):
        for c in range(CHUNKS):
            body(n, slice(c * CHUNK, (c + 1) * CHUNK))

    loop(LATENT // STRIP, step)


def beside(count, step, tile):
    share = TILES // count

    def body(i):
        step(i)
        for u in range(share):
            tile(i * share + u)

    loop(count, body)
    for t in range(share * count, TILES):
        tile(t)


def loop(count, body):
    def step(i, carry):
        body(i)
        return carry

    lax.fori_loop(0, count, step, 0)


def parts(x):
    a = x.astype(bf16)
    rest = x - a.astype(f32)
    b = rest.astype(bf16)
    c = (rest - b.astype(f32)).astype(bf16)
    return a, b, c


class Place:
    def __init__(self, devices):
        side = math.isqrt(devices // 8)
        self.devices = devices
        self.sizes = (4, side, side)
        me = lax.axis_index("atoms")
        core = me % 2
        chip = me // 2
        last = chip % side
        middle = chip // side % side
        self.me = me
        self.core = core
        self.pos = (
            chip // (side * side),
            last + core * (middle - last),
            middle + core * (last - middle),
        )
        self.half = (side * side, 1 + core * (side - 1), side + core * (1 - side))
        self.step = tuple(2 * h for h in self.half)
        self.sibling = me + 1 - 2 * core
        self.plain = (self.pos[0], middle, last)
        self.plain_step = (2 * side * side, 2 * side, 2)

    def owner(self, q):
        return q[0] * self.step[0] + q[1] * self.step[1] + q[2] * self.step[2] + self.core

    def near(self, dim, up):
        return self.me + self.step[dim] if up else self.me - self.step[dim]

    def has(self, dim, up):
        return self.pos[dim] < self.sizes[dim] - 1 if up else self.pos[dim] > 0

    def peers(self, dim):
        n, p = self.sizes[dim], self.plain[dim]
        return [(r, (p + r) % n, self.me + ((p + r) % n - p) * self.plain_step[dim]) for r in range(1, n)]


class Units:
    def __init__(self, ref, rows, cols, base=0, part=(0, 1)):
        self.ref, self.rows, self.cols = ref, rows, cols
        self.per = WIDE // cols
        self.base = base
        self.high = rows // part[1]
        self.off = part[0] * self.high

    def window(self, s):
        s = s + self.base
        if self.per == 1:
            row, col = s * self.rows, slice(None)
        else:
            row = s // self.per * self.rows
            col = pl.ds(pl.multiple_of(s % self.per * self.cols, self.cols), self.cols)
        return (pl.ds(pl.multiple_of(row + self.off, 16), self.high), col)

    def at(self, s):
        return self.ref.at[self.window(s)]

    def get(self, s):
        return self.ref[self.window(s)]

    def put(self, s, value):
        self.ref[self.window(s)] = value

    def stretch(self, count):
        return self.ref.at[pl.ds(0, count * self.high // self.per), slice(None)]


def remote(src, dst, send, recv, device):
    return pltpu.make_async_remote_copy(
        src_ref=src,
        dst_ref=dst,
        send_sem=send,
        recv_sem=recv,
        device_id=(device,),
        device_id_type=MESH,
    )


def signal(sem, device):
    pl.semaphore_signal(sem, inc=1, device_id=(device,), device_id_type=MESH)


def others(place, dim):
    n, p = place.sizes[dim], place.pos[dim]
    if n == 2:
        return [(1 - p, None)]
    found = []
    for distance in range(1, n):
        found.append((p - distance, p >= distance))
        found.append((p + distance, p < n - distance))
    return found


def gated(cond, body):
    if cond is None:
        body()
    else:
        pl.when(cond)(body)


def both(a, b):
    return b if a is None else (a if b is None else a & b)


class Gather:
    def __init__(self, place, units, lo, hi, sems, direct=False):
        self.place, self.units, self.lo, self.hi, self.sems = place, units, lo, hi, sems
        self.direct = direct
        _, na, nb = place.sizes
        self.waits = []
        self.shared = 0
        self.first_owner = 2 * lo * na * nb
        at = 2 * (hi - lo) * na * nb
        self.shared_send, self.core_recv = at, at + 1
        at += 2
        self.base = []
        for dim in range(3):
            length = (hi - lo) * (1, na, na * nb)[dim]
            self.base.append((at, at + length))
            at += 2 * length
        self.core_base = at

    @staticmethod
    def amount(devices, share):
        side = math.isqrt(devices // 8)
        return 2 + share * (2 + 2 * side + 5 * side * side)

    def linear(self, q, dim):
        _, na, nb = self.place.sizes
        q0 = q[0] - self.lo
        return (q0, q0 * na + q[1], (q0 * na + q[1]) * nb + q[2])[dim]

    def emit(self, cond, q, sem, device, core=False):
        owner = self.place.owner(q)
        if cond is None:
            sem = self.shared_send
            self.shared += 1

        def copy():
            piece = self.units.at(owner)
            recv = self.core_recv if core else owner - self.first_owner
            return remote(piece, piece, self.sems.at[sem], self.sems.at[recv], device)

        gated(cond, lambda: copy().start())
        if cond is not None:
            self.waits.append(lambda: gated(cond, lambda: copy().wait_send()))

    def onward(self, cond, q):
        place, p = self.place, self.place.pos[0]
        for up in (True, False):
            away = (p >= q[0]) if up else (p <= q[0])
            self.emit(
                both(cond, away & place.has(0, up)),
                q,
                self.base[0][0 if up else 1] + self.linear(q, 0),
                place.near(0, up),
            )

    def sideways(self, cond, q, dims, via=None):
        place = self.place
        for dim in dims:
            if place.sizes[dim] == 2:
                if dim != via:
                    toward = place.me + (1 - 2 * place.pos[dim]) * place.step[dim]
                    self.emit(cond, q, self.base[dim][0] + self.linear(q, dim), toward)
                continue
            for up in (True, False):
                open_end = place.has(dim, up)
                if dim == via:
                    p = place.pos[dim]
                    open_end = open_end & ((q[dim] < p) if up else (q[dim] > p))
                self.emit(
                    both(cond, open_end),
                    q,
                    self.base[dim][0 if up else 1] + self.linear(q, dim),
                    place.near(dim, up),
                )
        self.emit(cond, q, self.core_base + self.linear(q, 2), place.sibling, True)

    def wait(self, cond, q):
        owner = self.place.owner(q)
        piece = self.units.at(owner)
        gated(
            cond,
            lambda: remote(
                piece,
                piece,
                self.sems.at[self.shared_send],
                self.sems.at[owner - self.first_owner],
                self.place.sibling,
            ).wait_recv(),
        )

    def own(self):
        place, p = self.place, self.place.pos
        if self.direct:
            for r in range(1, 4):
                self.emit(None, p, 0, place.me + ((p[0] + r) % 4 - p[0]) * place.step[0])
            return
        for q0 in range(self.lo, self.hi):
            self.onward(p[0] == q0, (q0, p[1], p[2]))

    def column(self):
        p = self.place.pos
        if self.direct:
            self.sideways(None, p, (2, 1))
            for r in range(1, 4):
                q = ((p[0] + r) % 4, p[1], p[2])
                self.wait(None, q)
                self.sideways(None, q, (2, 1))
            return
        for q0 in range(self.lo, self.hi):
            q = (q0, p[1], p[2])
            self.wait(p[0] != q0, q)
            self.onward(p[0] != q0, q)
            self.sideways(None, q, (2, 1))

    def second(self):
        for q0 in range(self.lo, self.hi):
            for qa, there in others(self.place, 1):
                q = (q0, qa, self.place.pos[2])
                self.wait(there, q)
                self.sideways(there, q, (2, 1), 1)

    def third(self):
        for qb, there in others(self.place, 2):
            for q0 in range(self.lo, self.hi):
                for qa in range(self.place.sizes[1]):
                    q = (q0, qa, qb)
                    self.wait(there, q)
                    self.sideways(there, q, (2,), 2)

    def across(self):
        _, na, nb = self.place.sizes
        piece = self.units.stretch((self.hi - self.lo) * na * nb)
        remote(
            piece,
            piece,
            self.sems.at[self.shared_send],
            self.sems.at[self.core_recv],
            self.place.sibling,
        ).wait_recv()

    def finish(self):
        for wait in self.waits:
            wait()
        if self.shared:
            piece = self.units.stretch(self.shared)
            remote(
                piece,
                piece,
                self.sems.at[self.shared_send],
                self.sems.at[self.core_recv],
                self.place.sibling,
            ).wait_send()
        self.waits, self.shared = [], 0


def landing(n):
    return 1 if n == 2 else n + 1


class Reduce:
    def __init__(self, place, units, lo, hi, land, sems, ready):
        self.place, self.units, self.lo, self.hi, self.land = place, units, lo, hi, land
        n0, na, nb = place.sizes
        self.count = (hi - lo) * na * nb
        lines = ((1, n0), (hi - lo, na), ((hi - lo) * na, nb))
        z_at = self.count
        b_at = z_at + landing(n0)
        a_at = b_at + lines[2][0] * landing(nb)
        self.land_at = (z_at, a_at, b_at)
        self.sems, self.ready = sems, ready
        self.shared = 0
        at = 4
        self.recv_at, self.up_at, self.down_at = [], [], []
        for units_here, n in lines:
            self.recv_at.append(at)
            at += units_here * landing(n)
            self.up_at.append(at)
            at += units_here * n
            self.down_at.append(at)
            at += units_here * n
        self.waits = []

    @staticmethod
    def slots(devices, share):
        side = math.isqrt(devices // 8)
        return share * side * side + landing(4) + share * (1 + side) * landing(side)

    @staticmethod
    def amount(devices, share):
        side = math.isqrt(devices // 8)
        total = 4
        for units_here, n in ((1, 4), (share, side), (share * side, side)):
            total += units_here * (landing(n) + 2 * n)
        return total

    def stage(self, k):
        if k == 0:
            self.start()
        elif k == 1:
            self.pairs()
        elif k < 4:
            self.along(4 - k)
        else:
            self.hop(0, k - 3, [(None,) + self.place.pos[1:]])

    def unit(self, dim, q):
        na = self.place.sizes[1]
        return (0, q[0] - self.lo, (q[0] - self.lo) * na + q[1])[dim]

    def add(self, owner, slot):
        self.units.put(owner, self.units.get(owner) + self.land.get(slot))

    def start(self):
        place = self.place
        if self.ready is not None:
            signal(self.ready.at[0], place.sibling)
            for dim in range(3):
                for up in (True, False):
                    pl.when(place.has(dim, up))(
                        lambda dim=dim, up=up: signal(
                            self.ready.at[1 + 2 * dim + (1 if up else 0)], place.near(dim, up)
                        )
                    )
            pl.semaphore_wait(self.ready.at[0], 1)
        per = place.sizes[1] * place.sizes[2]

        def copy(j):
            owner = 2 * (self.lo * per + j) + 1 - place.core
            return remote(
                self.units.at(owner), self.land.at(j), self.sems.at[0], self.sems.at[1], place.sibling
            )

        loop(self.count, lambda j: copy(j).start())
        self.shared += self.count

    def allow(self, dim):
        if self.ready is None:
            return
        for up in (True, False):
            pl.when(self.place.has(dim, up))(
                lambda up=up: pl.semaphore_wait(self.ready.at[1 + 2 * dim + (0 if up else 1)], 1)
            )

    def push(self, cond, dim, q, sem, slot, device):
        owner = self.place.owner(q)
        target = self.unit(dim, q) * landing(self.place.sizes[dim]) + slot
        recv = self.recv_at[dim] + target
        if cond is None:
            self.shared += 1
            sem, recv = 0, 1 + dim

        def copy():
            return remote(
                self.units.at(owner),
                self.land.at(self.land_at[dim] + target),
                self.sems.at[sem],
                self.sems.at[recv],
                device,
            )

        gated(cond, lambda: copy().start())
        if cond is not None:
            self.waits.append(lambda: gated(cond, lambda: copy().wait_send()))

    def arrived(self, sem, count):
        piece = self.land.stretch(count)
        remote(
            piece, piece, self.sems.at[0], self.sems.at[sem], self.place.sibling
        ).wait_recv()

    def pull(self, dim, q, slot):
        target = self.unit(dim, q) * landing(self.place.sizes[dim]) + slot
        piece = self.land.at(self.land_at[dim] + target)
        remote(
            piece,
            piece,
            self.sems.at[0],
            self.sems.at[self.recv_at[dim] + target],
            self.place.sibling,
        ).wait_recv()
        self.add(self.place.owner(q), self.land_at[dim] + target)

    def first(self, dim, q):
        place = self.place
        n, p = place.sizes[dim], place.pos[dim]
        u = self.unit(dim, q)
        if n == 2:
            toward = place.me + (1 - 2 * p) * place.step[dim]
            self.push(None, dim, q, self.up_at[dim] + u * n, 0, toward)
            return
        for up in (True, False):
            away = (q[dim] > 0) if up else (q[dim] < n - 1)
            self.push(
                (p == (0 if up else n - 1)) & away,
                dim,
                q,
                (self.up_at if up else self.down_at)[dim] + u * n + q[dim],
                self.slot_up(q[dim], 0) if up else self.slot_down(n, q[dim], n - 1),
                place.near(dim, up),
            )

    @staticmethod
    def slot_up(q, p):
        return q - (p + 1)

    @staticmethod
    def slot_down(n, q, p):
        to = p - 1
        return q + (n - to if to > 0 else 0)

    def order(self, dim):
        place = self.place
        if place.sizes[dim] == 2:
            return [1 - place.pos[dim], place.pos[dim]]
        return list(range(place.sizes[dim]))

    def mine(self, dim, at):
        return at is self.place.pos[dim]

    def pairs(self):
        place = self.place
        self.allow(2)
        self.arrived(1, self.count)
        for qb in self.order(2):
            for qa in self.order(1):
                for q0 in range(self.lo, self.hi):
                    q = (q0, qa, qb)
                    j = (q0 - self.lo) * place.half[0] + qa * place.half[1] + qb * place.half[2]
                    self.add(place.owner(q), j)
                    if not self.mine(2, qb):
                        self.first(2, q)

    def along(self, dim):
        place = self.place
        n, p = place.sizes[dim], place.pos[dim]
        self.allow(dim - 1)
        if dim == 2:
            rows = [(q0, qa) for qa in self.order(1) for q0 in range(self.lo, self.hi)]
        else:
            rows = [(q0,) for q0 in range(self.lo, self.hi)]

        def whole(row, at):
            return row + (at,) + place.pos[dim + 1 :]

        if n == 2:
            self.arrived(1 + dim, len(rows))
            for row in rows:
                q = whole(row, p)
                self.add(place.owner(q), self.land_at[dim] + self.unit(dim, q))
                if not self.mine(dim - 1, row[dim - 1]):
                    self.first(dim - 1, whole(row, p))
        else:
            for k in range(1, n):
                self.hop(dim, k, [whole(row, None) for row in rows])
            for row in rows:
                self.first(dim - 1, whole(row, p))

    def hop(self, dim, k, rows):
        place = self.place
        n, p = place.sizes[dim], place.pos[dim]
        lo, hi = (self.lo, self.hi) if dim == 0 else (0, n)
        for up in (True, False):
            here = k if up else n - 1 - k
            cond = p == here
            span = range(max(lo, here), hi) if up else range(lo, min(hi, here + 1))
            if len(span) == 0:
                continue

            def receive(up=up, here=here, span=span):
                for row in rows:
                    for at in span:
                        slot = at - here if up else at + (n - here if here > 0 else 0)
                        q = row[:dim] + (at,) + row[dim + 1 :]
                        self.pull(dim, q, slot)
                        if at != here:
                            self.hop_copy(dim, q, up, here).start()

            pl.when(cond)(receive)
            for row in rows:
                for at in span:
                    if at != here:
                        q = row[:dim] + (at,) + row[dim + 1 :]
                        self.waits.append(
                            lambda cond=cond, q=q, up=up, here=here: pl.when(cond)(
                                lambda: self.hop_copy(dim, q, up, here).wait_send()
                            )
                        )

    def hop_copy(self, dim, q, up, here):
        place = self.place
        n = place.sizes[dim]
        u = self.unit(dim, q)
        slot = self.slot_up(q[dim], here) if up else self.slot_down(n, q[dim], here)
        target = u * landing(n) + slot
        return remote(
            self.units.at(place.owner(q)),
            self.land.at(self.land_at[dim] + target),
            self.sems.at[(self.up_at if up else self.down_at)[dim] + u * n + q[dim]],
            self.sems.at[self.recv_at[dim] + target],
            place.near(dim, up),
        )

    def finish(self):
        for wait in self.waits:
            wait()
        piece = self.land.stretch(self.shared)
        remote(
            piece, piece, self.sems.at[0], self.sems.at[1], self.place.sibling
        ).wait_send()
        self.waits, self.shared = [], 0


class Total:
    def __init__(self, place, land, sems):
        self.place, self.land, self.sems = place, land, sems
        self.sizes = (2,) + place.sizes[::-1]
        self.at = [sum(self.sizes[:k]) for k in range(4)]
        self.waits = []

    @staticmethod
    def slots(devices):
        return 6 + 2 * math.isqrt(devices // 8)

    def lines(self, k):
        place = self.place
        if k == 0:
            return place.core, [(1, 1 - place.core, place.sibling)]
        return place.plain[3 - k], place.peers(3 - k)

    def send(self, k, value):
        p, peers = self.lines(k)
        here = self.land.at[self.at[k] + p]
        self.land[self.at[k] + p] = value
        half = self.at[3] + self.sizes[3]
        for r, _, device in peers:

            def copy(r=r, device=device):
                sems = self.sems
                return remote(
                    here, here, sems.at[self.at[k] + r], sems.at[half + self.at[k] + p], device
                )

            copy().start()
            self.waits.append(lambda copy=copy: copy().wait_send())

    def take(self, k):
        _, peers = self.lines(k)
        half = self.at[3] + self.sizes[3]
        for r, at, device in peers:
            there = self.land.at[self.at[k] + at]
            remote(
                there, there, self.sems.at[0], self.sems.at[half + self.at[k] + at], device
            ).wait_recv()
        total = self.land[self.at[k]]
        for s in range(1, self.sizes[k]):
            total = total + self.land[self.at[k] + s]
        return total

    def pass_on(self, k):
        value = self.take(k)
        if k < 3:
            self.send(k + 1, value)
        return value

    def finish(self):
        for wait in self.waits:
            wait()
        self.waits = []


class Ring:
    def __init__(self, me, devices, land, sems):
        self.after = (me + 1) % devices
        self.before = (me + devices - 1) % devices
        self.land, self.sems = land, sems

    def copies(self, to_before, to_after):
        return (
            remote(to_before, self.land.at[1], self.sems.at[0], self.sems.at[1], self.before),
            remote(to_after, self.land.at[0], self.sems.at[2], self.sems.at[3], self.after),
        )

    def start(self, to_before, to_after):
        for copy in self.copies(to_before, to_after):
            copy.start()

    def wait(self, to_before, to_after):
        for copy in self.copies(to_before, to_after):
            copy.wait_recv()

    def finish(self, to_before, to_after):
        for copy in self.copies(to_before, to_after):
            copy.wait_send()


def unit_shape(amount):
    across = min(amount, PANEL)
    return amount // across * BLOCK_ROWS, across * BLOCK_COLS


def own_unit(units, me, blocks):
    across = units.cols // BLOCK_COLS
    rows = []
    for a in range(units.rows // BLOCK_ROWS):
        row = [blocks[a * across + b].astype(bf16) for b in range(across)]
        rows.append(jnp.concatenate(row, axis=1))
    units.put(me, jnp.concatenate(rows, axis=0))


def network(
    idx_ref,
    positions_ref,
    species_ref,
    counts_ref,
    cot_ref,
    scale_ref,
    shift_ref,
    weight_ref,
    state_ref,
    blocks_ref,
    late_in,
    energy_ref,
    forces_ref,
    vector_ref,
    first_out,
    late_out,
    first_w,
    late_w,
    hot,
    z_t,
    z_r,
    geo,
    yrow,
    env_b,
    ee_t,
    en2_t,
    s1_t,
    s2_t,
    gam,
    dlt,
    coef,
    ds_t,
    de_t,
    dy,
    dg,
    dw_t,
    dw_r,
    dpf,
    den,
    lat,
    hid,
    low0,
    act1,
    sl1,
    low1,
    act2,
    sl2,
    low2,
    stage,
    halo,
    force_in,
    sides,
    vector_in,
    pack_ref,
    low_gather,
    mid_gather,
    high_gather,
    late_gather,
    late_sems,
    first_sems,
    ring_sems,
    vector_sems,
    ready,
):
    s_r = dw_r
    fact = den

    wee_t = dw_t.at[:, 0:LATENT]
    we2_t = dw_t.at[0:128, 0:LATENT]
    devices = lax.axis_size("atoms")
    me = lax.axis_index("atoms")
    place = Place(devices)
    own_at = pack_ref.at[0:8]
    first_units = Units(first_w, *unit_shape(blocks_ref.shape[0]))
    late_units = Units(late_w, *unit_shape(late_in.shape[0]))
    top = place.sizes[0]
    middle = top // 2

    def pieces(k, count):
        return Units(first_w, first_units.rows, first_units.cols, part=(k, count))

    def free(ref, units, k=0, count=1):
        slots = Reduce.slots(devices, 1)
        return Units(ref, units.rows // count, units.cols, base=k * slots)

    gather_low = [Gather(place, pieces(k, PIECES), 0, 1, low_gather.at[k]) for k in range(PIECES)]
    gather_mid = Gather(place, first_units, 1, middle, mid_gather)
    gather_high = Gather(place, first_units, middle, top, high_gather)
    gather_late = Gather(place, late_units, 0, top, late_gather, True)
    sum_out = Reduce(
        place, late_units, middle, top, free(low2, late_units), late_sems.at[0], ready.at[0]
    )
    sum_lat = Reduce(
        place, late_units, 0, middle, free(sl2, late_units), late_sems.at[1], ready.at[1]
    )
    sum_first = [
        [
            Reduce(
                place,
                pieces(k, SUM_PIECES[z]),
                z,
                z + 1,
                free(ref, first_units, k, SUM_PIECES[z]),
                first_sems.at[PIECES * z + k],
                ready.at[2 + z] if k == 0 else None,
            )
            for k in range(SUM_PIECES[z])
        ]
        for z, ref in enumerate((hid, low0, sl1, act2))
    ]

    def advance(z, stage):
        for part in sum_first[z]:
            part.stage(stage)
    link_halo = Ring(me, devices, halo, ring_sems.at[0])
    link_force = Ring(me, devices, force_in, ring_sems.at[1])
    sum_vector = Total(place, vector_in, vector_sems)

    barrier = pltpu.get_barrier_semaphore()
    partners = [place.sibling, link_halo.before, link_halo.after]
    for dim in range(3):
        partners += [device for _, _, device in place.peers(dim)]
    for device in partners:
        signal(barrier, device)
    for part in (slice(0, PLANE), slice(PLANE, LANES)):
        pack_ref[0:3, part] = positions_ref[...]
        pack_ref[3:4, part] = species_ref[...].astype(f32)
        pack_ref[4:5, part] = counts_ref[...].astype(f32)
        pack_ref[5:6, part] = cot_ref[...]
    pack_ref[6:16] = jnp.zeros((10, LANES), f32)
    pack_ref[6:7, 0:SPECIES] = scale_ref[...]
    pack_ref[7:8, 0:SPECIES] = shift_ref[...]
    pack_ref[8:9] = weight_ref[...]
    pack_ref[9:10] = state_ref[...]
    own_unit(first_units, me, blocks_ref)
    own_unit(late_units, me, late_in)
    pl.semaphore_wait(barrier, len(partners))
    link_halo.start(own_at, own_at)
    for part in gather_low:
        part.own()
    gather_high.own()
    for part in gather_low:
        part.column()

    ids = lax.broadcasted_iota(jnp.int32, (3 * PLANE, LANES), 0)

    whole = PLANE * devices
    coef[0, :, 0:SLOTS] = idx_ref[...].astype(f32)
    listed = coef[0].T[: SLOTS + 6].astype(jnp.int32) - (me - 1) * PLANE
    listed = jnp.where(
        listed < 0, listed + whole, jnp.where(listed >= whole, listed - whole, listed)
    )
    for t in range(TILES):
        near = jnp.concatenate([listed[2 * t : 2 * t + 1], listed[2 * t + 1 : 2 * t + 2]], axis=1)
        hot[:, t * LANES : (t + 1) * LANES] = jnp.where(ids == near, 1.0, 0.0).astype(bf16)

    link_halo.wait(own_at, own_at)
    own = pack_ref[0:8]
    lane = lax.broadcasted_iota(jnp.int32, (8, LANES), 1)
    row = lax.broadcasted_iota(jnp.int32, (8, LANES), 0)
    edge = spacing * devices
    x_row = row == 0
    before = halo[0] - jnp.where(x_row, jnp.where(me == 0, edge, 0.0), 0.0)
    after = halo[1] + jnp.where(x_row, jnp.where(me == devices - 1, edge, 0.0), 0.0)
    rank_y = ((lane & (PLANE - 1)) >> 3).astype(f32)
    rank_z = (lane & (SIDE - 1)).astype(f32)
    table = jnp.concatenate([jnp.where(lane < PLANE, before, own), after], axis=1)
    ranks = jnp.where(row == 4, rank_y, rank_z)
    table = jnp.where(
        jnp.concatenate([row, row], axis=1) < 4, table, jnp.concatenate([ranks, ranks], axis=1)
    )[:, : 3 * PLANE]
    ga, gb, gc = parts(table)
    got = nn(ga, hot[...]) + nn(gb, hot[...]) + nn(gc, hot[...])
    mine = jnp.concatenate([own] * TILES, axis=1)
    lane = lax.broadcasted_iota(jnp.int32, (1, ROWS), 1)
    slot = lane >> 6
    atom = lane & (PLANE - 1)
    for part in gather_low:
        part.second()
    gather_mid.own()

    def wrapped(step):
        return jnp.where(step > 1.5, -8.0, jnp.where(step < -1.5, 8.0, 0.0)) * spacing

    disp = [
        got[0:1] - mine[0:1],
        got[1:2] - mine[1:2] + wrapped(got[4:5] - (atom >> 3).astype(f32)),
        got[2:3] - mine[2:3] + wrapped(got[5:6] - (atom & (SIDE - 1)).astype(f32)),
    ]
    length = jnp.sqrt(disp[0] * disp[0] + disp[1] * disp[1] + disp[2] * disp[2])
    inverse = 1.0 / length
    unit = [disp[0] * inverse, disp[1] * inverse, disp[2] * inverse]
    angle = length * (math.pi / cutoff_radius)
    sin_k = [jnp.sin(angle)]
    cos_k = [jnp.cos(angle)]
    sin_k.append(2.0 * cos_k[0] * sin_k[0])
    cos_k.append(2.0 * cos_k[0] * cos_k[0] - 1.0)
    for k in range(2, BESSEL):
        sin_k.append(2.0 * cos_k[0] * sin_k[k - 1] - sin_k[k - 2])
        cos_k.append(2.0 * cos_k[0] * cos_k[k - 1] - cos_k[k - 2])
    sines = jnp.concatenate(sin_k, axis=0)
    cosines = jnp.concatenate(cos_k, axis=0)
    bessel = (math.sqrt(2.0 / cutoff_radius) * inverse) * sines
    scaled = length * (1.0 / cutoff_radius)
    t2 = scaled * scaled
    t4 = t2 * t2
    t5 = t4 * scaled
    t6 = t4 * t2
    envelope = 1.0 - 28.0 * t6 + 48.0 * (t6 * scaled) - 21.0 * (t4 * t4)
    denvelope = (-168.0 * t5 + 336.0 * t6 - 168.0 * (t6 * scaled)) * (1.0 / cutoff_radius)
    live = jnp.where(slot.astype(f32) < mine[4:5], 1.0, 0.0)

    kind = lax.broadcasted_iota(jnp.int32, (KINDS, LANES), 0).astype(f32)
    is_kind = kind == own[3:4]
    by_kind = own.T
    scale = jnp.sum(jnp.where(is_kind, by_kind[:KINDS, 6:7], 0.0), axis=0, keepdims=True)
    shift = jnp.sum(jnp.where(is_kind, by_kind[:KINDS, 7:8], 0.0), axis=0, keepdims=True)
    cot = jnp.concatenate([own[5:6] * scale] * TILES, axis=1) * live
    weight = cot * envelope

    root3 = math.sqrt(3.0)
    root15 = math.sqrt(15.0)
    root5 = math.sqrt(5.0)
    ux, uy, uz = unit
    yrow[0:8] = jnp.concatenate(
        [
            root3 * ux,
            root3 * uy,
            root3 * uz,
            root15 * ux * uy,
            root15 * uy * uz,
            0.5 * root5 * (3.0 * uz * uz - 1.0),
            root15 * ux * uz,
            0.5 * root15 * (ux * ux - uy * uy),
        ],
        axis=0,
    )
    yrow[8:16] = yrow[0:8] * (live * env_scale)
    yrow[16:17] = live * env_scale
    geo[0:8] = jnp.concatenate([ux, uy, uz, inverse, envelope, denvelope, live, cot], axis=0)
    geo[8:16] = math.sqrt(2.0 / cutoff_radius) * (
        (math.pi / cutoff_radius)
        * lax.broadcasted_iota(jnp.int32, (BESSEL, ROWS), 0).astype(f32)
        * cosines
        + (math.pi / cutoff_radius) * cosines
        - sines * inverse
    ) * inverse


    def one_hots(t):
        row = lax.broadcasted_iota(jnp.int32, (LANES, LANES), 0).astype(f32)
        here = jnp.where(row == own[3:4] + float(BESSEL), 1.0, 0.0)
        there = jnp.where(row == kinds_near[t] + float(BESSEL + SPECIES), 1.0, 0.0)
        return here + there

    kinds_near = [got[3:4, t * LANES : (t + 1) * LANES] for t in range(TILES)]
    gather_mid.column()
    for part in gather_low:
        part.third()
    for t in range(TILES):
        at = slice(t * LANES, (t + 1) * LANES)
        column = jnp.concatenate([bessel[:, at], one_hots(t)[BESSEL:]], axis=0)
        z_t[:, at] = column.astype(bf16)
        z_r[at, :] = column.T.astype(bf16)
        env_b[at, :] = jnp.broadcast_to(envelope[:, at], (LANES, LANES)).T
        fact[at, :] = jnp.broadcast_to(weight[:, at], (LANES, LANES)).T
    gather_mid.second()
    for part in gather_low:
        part.across()
    gather_high.column()


    def twice(x):
        return jnp.concatenate([x] * (STRIP // LANES), axis=1)

    def in_body(n, r):
        pre = nn(z_r[r], cols_panel(first_w, W_INPUT, n))
        hid[r, panel(n, STRIP)] = (pre * sigmoid(pre)).astype(bf16)

    loop_panels(in_body)
    gather_mid.third()
    gather_high.second()
    gather_late.own()
    gather_mid.across()

    def two_body(n, r):
        zero = nn(hid[r], cols_panel(first_w, W_TWO, n)) * twice(env_b[r])
        lat[r, panel(n, STRIP)] = zero
        low0[r, panel(n, STRIP)] = zero.astype(bf16)

    loop_panels(two_body)

    def transposed_product(out, weights, right, width=256):
        at = 0
        while at < ROWS:
            end = min(at + width, ROWS)
            out[:, at:end] = nt(weights, right[at:end, :])
            at = end

    wee_t[0:128, :] = narrow(first_w, W_EMBED).T
    wee_t[128:256, :] = narrow(first_w, W_ENV_ONE).T
    transposed_product(ee_t, wee_t[...], low0)
    gather_late.column()
    gather_high.third()

    def environment(out, v0_ref, v0_at, v1_at):
        for m in range(9):
            total = None
            begin = v0_at if m == 0 else v1_at
            y = yrow[16:17, :] if m == 0 else yrow[7 + m : 8 + m, :]
            for t in range(TILES):
                at = slice(t * LANES, (t + 1) * LANES)
                term = v0_ref[begin : begin + CHANNELS, at] * y[:, at]
                total = term if total is None else total + term
            out[m] = halves(total)

    def put_scalars(t, s_t, rows):
        s_t[:, lanes(t)] = jnp.concatenate(rows, axis=0).astype(bf16)
        filled = jnp.concatenate(rows + [jnp.zeros_like(rows[0])], axis=0)
        flipped = filled.T.astype(bf16)
        s_r[lanes(t), :] = flipped

    def weighted(y, first, count, source, offset):
        total = None
        for m in range(count):
            term = y[first + m : first + m + 1] * source[offset + m]
            total = term if total is None else total + term
        return total

    environment(gam, ee_t, 128, 192)

    def scalars_one(t):
        e0 = ee_t[0:64, lanes(t)]
        e1 = ee_t[64:128, lanes(t)]
        y = yrow[0:8, lanes(t)]
        put_scalars(
            t,
            s1_t,
            [e0 * gam[0], e1 * weighted(y, 0, 3, gam, 1), e1 * weighted(y, 3, 5, gam, 4)],
        )

    beside(6, lambda i: None, scalars_one)
    gather_high.across()

    def pre_one(n, r):
        pre = nn(low0[r], cols_panel(first_w, W_LAT_ONE, n)) + nn(
            s_r[r, : 3 * CHANNELS], cols_panel(first_w, W_SCAL_ONE, n)
        )
        sig = sigmoid(pre)
        act = pre * sig
        act1[r, panel(n, STRIP)] = act.astype(bf16)
        sl1[r, panel(n, STRIP)] = (sig + act * (1.0 - sig)).astype(bf16)

    loop_panels(pre_one)
    gather_late.second()

    def out_one(n, r):
        new = (lat[r, panel(n, STRIP)] + nn(act1[r], cols_panel(first_w, W_OUT_ONE, n))) * half_root
        lat[r, panel(n, STRIP)] = new
        low1[r, panel(n, STRIP)] = new.astype(bf16)

    loop_panels(out_one)
    gather_late.third()
    we2_t[...] = narrow(first_w, W_ENV_TWO).T
    transposed_product(en2_t, we2_t[...], low1)
    environment(dlt, en2_t, 0, 64)

    g0 = gam[0]
    coef[0] = g0 * dlt[0]
    for m in range(3):
        a, b = 1 + (m + 1) % 3, 1 + (m + 2) % 3
        coef[1 + m] = g0 * dlt[1 + m] + (gam[a] * dlt[b] - gam[b] * dlt[a])
    coef[9] = gam[1] * dlt[1] + gam[2] * dlt[2] + gam[3] * dlt[3]
    second = None
    for m in range(4, 9):
        coef[m] = g0 * dlt[m]
        term = gam[m] * dlt[m]
        second = term if second is None else second + term
    coef[10] = second

    def scalars_two(t):
        e0 = ee_t[0:64, lanes(t)]
        e1 = ee_t[64:128, lanes(t)]
        y = yrow[0:8, lanes(t)]
        put_scalars(
            t,
            s2_t,
            [
                e0 * coef[0],
                e1 * weighted(y, 0, 3, coef, 1) + e0 * coef[9],
                e1 * weighted(y, 3, 5, coef, 4) + e0 * coef[10],
            ],
        )

    beside(6, lambda i: None, scalars_two)
    gather_late.across()

    for part in gather_low + [gather_mid, gather_high, gather_late]:
        part.finish()
    def pre_two(n, r):
        pre = nn(low1[r], cols_panel(late_w, W_LAT_TWO, n)) + nn(
            s_r[r, : 3 * CHANNELS], cols_panel(first_w, W_SCAL_TWO, n)
        )
        sig = sigmoid(pre)
        act = pre * sig
        act2[r, panel(n, STRIP)] = act.astype(bf16)
        sl2[r, panel(n, STRIP)] = (sig + act * (1.0 - sig)).astype(bf16)

    loop_panels(pre_two)

    def out_two(n, r):
        new = (lat[r, panel(n, STRIP)] + nn(act2[r], cols_panel(late_w, W_OUT_TWO, n))) * half_root
        low2[r, panel(n, STRIP)] = new.astype(bf16)

    loop_panels(out_two)

    vec = jnp.broadcast_to(pack_ref[8:9], (8, LANES))
    stage[...] = narrow(first_w, W_FINAL)

    def read_out(i):
        r = pl.ds(pl.multiple_of(i * 416, 16), 416)
        pre = nn(low2[r, :], stage[...])
        sig = sigmoid(pre)
        final_act = pre * sig
        dpf[r, :] = (fact[r, :] * vec[0:1] * (sig + final_act * (1.0 - sig))).astype(bf16)
        fact[r, :] = final_act

    loop(4, read_out)
    value = nt(vec, fact[...], highest)[0:1]
    geo_live = geo[6:7]
    geo_env = geo[4:5]
    geo_cot = geo[7:8]
    edge_energy = geo_live * geo_env * value
    summed = None
    for t in range(TILES):
        term = edge_energy[:, t * LANES : (t + 1) * LANES]
        summed = term if summed is None else summed + term
    energy_ref[...] = scale * halves(summed) + shift
    all_weights = jnp.broadcast_to(geo_cot * geo_env, (8, ROWS))
    sum_vector.send(0, nn(all_weights, fact[...], highest))
    geo[16:17] = geo_cot * value

    def big_step(out, where, left, right):
        def step(i):
            grad = tn(left[:, panel(i, STRIP)], right[...])
            out[pl.ds(pl.multiple_of(where[0] + i * STRIP, 64), STRIP), :] = grad.astype(bf16)

        return step

    def big_grad(out, where, left, right):
        loop(LATENT // STRIP, big_step(out, where, left, right))

    def wide_step(out, where, left, right):
        def step(n):
            out[where[0] : where[0] + where[1], panel(n)] = nn(
                left[...], right[:, panel(n)]
            ).astype(bf16)

        return step

    def wide_grad(out, where, left, right):
        loop(4, wide_step(out, where, left, right))

    def narrow_grad(left, right, put):
        def step(n):
            put(n, nn(left, right[:, panel(n)]).T.astype(bf16))

        loop(4, step)

    def put_narrow(where, n, grad):
        row = pl.multiple_of(where[0] + n // 2 * BLOCK_ROWS, BLOCK_ROWS)
        col = pl.multiple_of(n % 2 * 512, 512)
        first_w[pl.ds(row, BLOCK_ROWS), pl.ds(col, 512)] = jnp.concatenate(
            [grad[b * BLOCK_ROWS : (b + 1) * BLOCK_ROWS] for b in range(4)], axis=1
        )

    def put_stage(n, grad):
        stage[panel(n), :] = grad

    narrow_grad(dpf[...].T, low2, put_stage)

    def back_final(n, r):
        grad = nt(dpf[r], narrow_panel(first_w, W_FINAL, n)) * half_root
        lat[r, panel(n, STRIP)] = grad
        low2[r, panel(n, STRIP)] = grad.astype(bf16)

    loop_panels(back_final)
    loop(4, lambda n: put_narrow(W_FINAL, n, stage[panel(n), :]))

    def back_out_two(n, r):
        grad = nt(low2[r], rows_panel(late_w, W_OUT_TWO, n))
        sl2[r, panel(n, STRIP)] = (grad * sl2[r, panel(n, STRIP)].astype(f32)).astype(bf16)

    loop_panels(back_out_two)
    transposed_product(ds_t, first_w[W_SCAL_TWO[0] : W_SCAL_TWO[0] + W_SCAL_TWO[1], :], sl2)

    dg[...] = jnp.zeros_like(dg)

    def tensors_two(t):
        e0 = ee_t[0:64, lanes(t)]
        e1 = ee_t[64:128, lanes(t)]
        y = yrow[0:8, lanes(t)]
        r0 = ds_t[0:64, lanes(t)]
        r1 = ds_t[64:128, lanes(t)]
        r2 = ds_t[128:192, lanes(t)]
        de_t[0:64, lanes(t)] = r0 * coef[0] + r1 * coef[9] + r2 * coef[10]
        de_t[64:128, lanes(t)] = r1 * weighted(y, 0, 3, coef, 1) + r2 * weighted(y, 3, 5, coef, 4)
        p1 = r1 * e1
        p2 = r2 * e1
        rows = []
        for m in range(8):
            p = p1 if m < 3 else p2
            rows.append(jnp.sum(p * coef[1 + m], axis=0, keepdims=True))
            dg[1 + m] += p * y[m : m + 1]
        dy[:, lanes(t)] = jnp.concatenate(rows, axis=0)
        dg[0] += r0 * e0
        dg[9] += r1 * e0
        dg[10] += r2 * e0

    beside(2, big_step(late_w, W_OUT_TWO, act2, low2), tensors_two)
    sum_out.stage(0)
    sum_vector.pass_on(0)
    total = [halves(dg[m]) for m in range(11)]
    g0 = gam[0]
    d0 = dlt[0]
    new_g0 = total[0] * d0
    for m in range(1, 9):
        new_g0 = new_g0 + total[m] * dlt[m]
    dlt_grads = [total[0] * g0]
    gam_grads = [new_g0]
    for m in range(3):
        a, b = 1 + (m + 1) % 3, 1 + (m + 2) % 3
        dlt_grads.append(
            total[1 + m] * g0 + total[9] * gam[1 + m] + (total[a] * gam[b] - total[b] * gam[a])
        )
        gam_grads.append(total[9] * dlt[1 + m] + (dlt[a] * total[b] - dlt[b] * total[a]))
    for m in range(4, 9):
        dlt_grads.append(total[m] * g0 + total[10] * gam[m])
        gam_grads.append(total[10] * dlt[m])
    for m in range(9):
        dlt[m] = dlt_grads[m]
        dg[m] = gam_grads[m]

    def environment_back(t, grads, source, v1_at, at):
        y4 = yrow[8:16, lanes(t)]
        l4 = yrow[16:17, lanes(t)]
        v1 = source[v1_at : v1_at + 64, lanes(t)]
        low = l4 * grads[0]
        high = weighted(y4, 0, 8, grads, 1)
        both = jnp.concatenate([low, high], axis=0)
        dw_t[at : at + 128, lanes(t)] = both.astype(bf16)
        dw_r[lanes(t), at : at + 128] = both.T.astype(bf16)
        v1 = v1 * l4
        rows = [jnp.sum(v1 * grads[1 + m], axis=0, keepdims=True) for m in range(8)]
        dy[:, lanes(t)] += jnp.concatenate(rows, axis=0)

    beside(
        4,
        wide_step(first_w, W_SCAL_TWO, s2_t, sl2),
        lambda t: environment_back(t, dlt, en2_t, 64, 128),
    )
    sum_out.stage(1)

    def back_lat_two(n, r):
        grad = (
            lat[r, panel(n, STRIP)]
            + nt(sl2[r], rows_panel(late_w, W_LAT_TWO, n))
            + nt(dw_r[r, 128:256], narrow_panel(first_w, W_ENV_TWO, n))
        ) * half_root
        lat[r, panel(n, STRIP)] = grad
        act2[r, panel(n, STRIP)] = grad.astype(bf16)

    loop_panels(back_lat_two)
    sum_out.stage(2)
    big_grad(late_w, W_LAT_TWO, low1, sl2)
    sum_out.stage(3)
    narrow_grad(dw_t[128:256, :], low1, functools.partial(put_narrow, W_ENV_TWO))
    sum_lat.stage(0)
    sum_vector.pass_on(1)

    def back_out_one(n, r):
        grad = nt(act2[r], rows_panel(first_w, W_OUT_ONE, n))
        sl1[r, panel(n, STRIP)] = (grad * sl1[r, panel(n, STRIP)].astype(f32)).astype(bf16)

    loop_panels(back_out_one)
    sum_out.stage(4)
    sum_lat.stage(1)
    transposed_product(ds_t, first_w[W_SCAL_ONE[0] : W_SCAL_ONE[0] + W_SCAL_ONE[1], :], sl1)

    def tensors_one(t):
        e0 = ee_t[0:64, lanes(t)]
        e1 = ee_t[64:128, lanes(t)]
        y = yrow[0:8, lanes(t)]
        r0 = ds_t[0:64, lanes(t)]
        r1 = ds_t[64:128, lanes(t)]
        r2 = ds_t[128:192, lanes(t)]
        low = de_t[0:64, lanes(t)] + r0 * gam[0]
        high = (
            de_t[64:128, lanes(t)]
            + r1 * weighted(y, 0, 3, gam, 1)
            + r2 * weighted(y, 3, 5, gam, 4)
        )
        both = jnp.concatenate([low, high], axis=0)
        dw_t[0:128, lanes(t)] = both.astype(bf16)
        dw_r[lanes(t), 0:128] = both.T.astype(bf16)
        p1 = r1 * e1
        p2 = r2 * e1
        rows = []
        for m in range(8):
            p = p1 if m < 3 else p2
            rows.append(jnp.sum(p * gam[1 + m], axis=0, keepdims=True))
            coef[1 + m] += p * y[m : m + 1]
        dy[:, lanes(t)] += jnp.concatenate(rows, axis=0)
        coef[0] += r0 * e0

    for m in range(9):
        coef[m] = jnp.zeros((CHANNELS, LANES), f32)
    beside(2, big_step(first_w, W_OUT_ONE, act1, act2), tensors_one)
    advance(3, 0)
    sum_out.stage(5)
    sum_lat.stage(2)
    sum_vector.pass_on(2)
    for m in range(9):
        dg[m] = dg[m] + halves(coef[m])
    beside(
        4,
        wide_step(first_w, W_SCAL_ONE, s1_t, sl1),
        lambda t: environment_back(t, dg, ee_t, 192, 128),
    )
    sum_out.stage(6)
    sum_lat.stage(3)
    advance(3, 1)

    den[...] = jnp.zeros_like(den)

    def back_lat_one(n, r):
        both = jnp.concatenate(
            [narrow_panel(first_w, W_EMBED, n), narrow_panel(first_w, W_ENV_ONE, n)], axis=1
        )
        grad = (
            lat[r, panel(n, STRIP)]
            + nt(sl1[r], rows_panel(first_w, W_LAT_ONE, n))
            + nt(dw_r[r], both)
        )
        low1[r, panel(n, STRIP)] = (grad * twice(env_b[r])).astype(bf16)
        part = grad * low0[r, panel(n, STRIP)].astype(f32)
        for b in range(STRIP // LANES):
            den[r] += part[:, b * LANES : (b + 1) * LANES]

    loop_panels(back_lat_one)
    sum_lat.stage(4)
    advance(3, 2)

    def back_two(n, r):
        grad = nt(low1[r], rows_panel(first_w, W_TWO, n))
        pre = nn(z_r[r], cols_panel(first_w, W_INPUT, n))
        sig = sigmoid(pre)
        act1[r, panel(n, STRIP)] = (grad * (sig + pre * sig * (1.0 - sig))).astype(bf16)

    loop_panels(back_two)
    sum_lat.stage(5)
    advance(3, 3)
    big_grad(first_w, W_TWO, hid, low1)
    sum_lat.stage(6)
    advance(3, 4)
    transposed_product(ds_t.at[0:64], first_w[0:64, :], act1)
    wide_grad(first_w, W_INPUT, z_t, act1)
    advance(0, 0)
    narrow_grad(dw_t[0:128, :], low0, functools.partial(put_narrow, W_EMBED))
    narrow_grad(dw_t[128:256, :], low0, functools.partial(put_narrow, W_ENV_ONE))
    advance(3, 5)
    advance(0, 1)
    big_grad(first_w, W_LAT_ONE, low0, sl1)
    advance(3, 6)
    advance(1, 0)
    advance(2, 0)
    advance(0, 2)

    dbessel = ds_t[0:8, :]
    through = nt(jnp.ones((8, LANES), f32), den[...], highest)[0:1]
    ux, uy, uz = geo[0:1], geo[1:2], geo[2:3]
    inverse = geo[3:4]
    envelope = geo[4:5]
    denv = geo[16:17] + through / envelope
    dlength = jnp.sum(dbessel * geo[8:16], axis=0, keepdims=True) + denv * geo[5:6]
    g = [dy[m : m + 1, :] for m in range(8)]
    dux = root3 * g[0] + root15 * (uy * g[3] + uz * g[6] + ux * g[7])
    duy = root3 * g[1] + root15 * (ux * g[3] + uz * g[4] - uy * g[7])
    duz = root3 * g[2] + root15 * (uy * g[4] + ux * g[6]) + (3.0 * root5) * uz * g[5]
    along = dlength - (ux * dux + uy * duy + uz * duz) * inverse
    near = jnp.concatenate(
        [
            dux * inverse + ux * along,
            duy * inverse + uy * along,
            duz * inverse + uz * along,
            jnp.zeros((5, ROWS), f32),
        ],
        axis=0,
    )
    advance(1, 1)
    advance(2, 1)
    advance(0, 3)
    summed = None
    for t in range(TILES):
        term = near[:, t * LANES : (t + 1) * LANES]
        summed = term if summed is None else summed + term
    centre = halves(summed)
    na, nb, nc = parts(near)
    spread = nt(na, hot[...]) + nt(nb, hot[...]) + nt(nc, hot[...])
    sides[0] = spread[:, :LANES]
    sides[1, :, 0:PLANE] = spread[:, LANES:]
    link_force.start(sides.at[0], sides.at[1])
    for step in range(5 + max(SUM_PIECES) - 1):
        for k in range(max(SUM_PIECES)):
            for z, after in ((0, 4), (1, 2), (2, 2)):
                if k < SUM_PIECES[z] and after <= after + step - k < 7:
                    sum_first[z][k].stage(after + step - k)
    link_force.wait(sides.at[0], sides.at[1])
    forces_ref[...] = (
        centre - pltpu.roll(sides[0], PLANE, 1) - force_in[1] - force_in[0]
    )
    total = sum_vector.pass_on(3)
    normed = total * lax.rsqrt(jnp.sum(total[0:1] * total[0:1]) * (1.0 / FINAL) + epsilon)
    state = decay_rate * pack_ref[9:10] + (1.0 - decay_rate) * normed * normed
    vector_ref[0:1] = total[0:1]
    vector_ref[1:2] = state[0:1]
    vector_ref[2:3] = (pack_ref[8:9] - vector_rate * normed * lax.rsqrt(state + epsilon))[0:1]
    first_out[...] = first_units.get(me)
    late_out[...] = late_units.get(me)
    for group in sum((list(parts) for parts in sum_first), [sum_out, sum_lat, sum_vector]):
        group.finish()
    link_halo.finish(own_at, own_at)
    link_force.finish(sides.at[0], sides.at[1])


def run_network(devices, small, blocks, late):
    S = jax.ShapeDtypeStruct
    wide = pltpu.VMEM((ROWS, LATENT), bf16)
    slab = pltpu.VMEM((ROWS, LANES), f32)
    panels = lambda amount: pltpu.VMEM((amount * devices // PANEL * BLOCK_ROWS, WIDE), bf16)
    scratch = [
        panels(blocks.shape[0]),
        panels(late.shape[0]),
        pltpu.VMEM((3 * PLANE, ROWS), bf16),
        pltpu.VMEM((LANES, ROWS), bf16),
        pltpu.VMEM((ROWS, LANES), bf16),
        pltpu.VMEM((24, ROWS), f32),
        pltpu.VMEM((24, ROWS), f32),
        slab,
        pltpu.VMEM((256, ROWS), f32),
        pltpu.VMEM((128, ROWS), f32),
        pltpu.VMEM((192, ROWS), bf16),
        pltpu.VMEM((192, ROWS), bf16),
        pltpu.VMEM((9, CHANNELS, LANES), f32),
        pltpu.VMEM((9, CHANNELS, LANES), f32),
        pltpu.VMEM((11, CHANNELS, LANES), f32),
        pltpu.VMEM((192, ROWS), f32),
        pltpu.VMEM((128, ROWS), f32),
        pltpu.VMEM((8, ROWS), f32),
        pltpu.VMEM((11, CHANNELS, LANES), f32),
        pltpu.VMEM((256, ROWS), bf16),
        pltpu.VMEM((ROWS, 256), bf16),
        pltpu.VMEM((ROWS, LANES), bf16),
        slab,
        pltpu.VMEM((ROWS, LATENT), f32),
    ] + [wide] * 8 + [
        pltpu.VMEM((LATENT, LANES), bf16),
        pltpu.VMEM((2, 8, LANES), f32),
        pltpu.VMEM((2, 8, LANES), f32),
        pltpu.VMEM((2, 8, LANES), f32),
        pltpu.VMEM((Total.slots(devices), 8, LANES), f32),
        pltpu.VMEM((16, LANES), f32),
        pltpu.SemaphoreType.DMA((PIECES, Gather.amount(devices, 1))),
        pltpu.SemaphoreType.DMA((Gather.amount(devices, 1),)),
        pltpu.SemaphoreType.DMA((Gather.amount(devices, 2),)),
        pltpu.SemaphoreType.DMA((Gather.amount(devices, 4),)),
        pltpu.SemaphoreType.DMA((2, Reduce.amount(devices, 2))),
        pltpu.SemaphoreType.DMA((4 * PIECES, Reduce.amount(devices, 1))),
        pltpu.SemaphoreType.DMA((2, 4)),
        pltpu.SemaphoreType.DMA((2 * Total.slots(devices),)),
        pltpu.SemaphoreType.REGULAR((6, 7)),
    ]
    vmem = pl.BlockSpec(memory_space=pltpu.VMEM)
    return pl.pallas_call(
        network,
        out_shape=[
            S((1, LANES), f32),
            S((8, LANES), f32),
            S((8, LANES), f32),
            S(unit_shape(blocks.shape[0]), bf16),
            S(unit_shape(late.shape[0]), bf16),
        ],
        in_specs=[vmem] * (len(small) + 2),
        out_specs=[vmem] * 5,
        scratch_shapes=scratch,
        compiler_params=pltpu.CompilerParams(
            vmem_limit_bytes=63 << 20, collective_id=0, has_side_effects=True
        ),
        name="network",
    )(*small, blocks, late)


def shampoo(
    energy,
    force,
    vectors,
    grads,
    left,
    right,
    left_root,
    right_root,
    master,
    late_grads,
    late_left,
    late_right,
    late_left_root,
    late_right_root,
    late_master,
    energy_out,
    force_out,
    vector_out,
    state_out,
    moved_out,
    *outs,
):
    energy_out[...] = energy[:, :PLANE]
    force_out[...] = force[0:3, :PLANE]
    vector_out[...] = vectors[0:1]
    state_out[...] = vectors[1:2]
    moved_out[...] = vectors[2:3]

    todo = []
    for j in range(left.shape[0]):
        todo.append((grads, j, left, right, left_root, right_root, master) + outs[:4])
    for j in range(late_left.shape[0]):
        todo.append(
            (late_grads, j, late_left, late_right, late_left_root, late_right_root, late_master)
            + outs[4:]
        )
    size = 1.0 / (BLOCK_ROWS * BLOCK_COLS)
    held, scales, steps = [], [], []
    for panels, j, left, *_ in todo:
        per = panels.shape[1] // BLOCK_COLS
        at = pl.program_id(0) * left.shape[0] + j
        row = pl.multiple_of(at // per * BLOCK_ROWS, BLOCK_ROWS)
        col = pl.multiple_of(at % per * BLOCK_COLS, BLOCK_COLS)
        held.append(panels[pl.ds(row, BLOCK_ROWS), pl.ds(col, BLOCK_COLS)])
    for g, (_, j, *_, grad_out, left_out, right_out, master_out) in zip(held, todo):
        grad = g.astype(f32)
        grad_out[j] = grad
        scales.append(lax.rsqrt(jnp.sum(grad * grad, keepdims=True) * size + epsilon))
    turned = []
    for g, (_, j, left, right, left_root, *_) in zip(held, todo):
        la, lb, _ = parts(left_root[j])
        turned.append(nn(la, g) + nn(lb, g))
    for g, s, (_, j, left, right, *_, grad_out, left_out, right_out, master_out) in zip(
        held, scales, todo
    ):
        square = (1.0 - decay_rate) * s * s
        left_out[j] = decay_rate * left[j] + square * nt(g, g)
        right_out[j] = decay_rate * right[j] + square * tn(g, g)
    for turn, s, (_, j, left, right, left_root, right_root, *_) in zip(turned, scales, todo):
        ra, rb, _ = parts(right_root[j])
        ta, tb, _ = parts(turn * s)
        steps.append(nn(ta, ra) + (nn(ta, rb) + nn(tb, ra)))
    for step, (_, j, left, right, left_root, right_root, master, *_, master_out) in zip(steps, todo):
        slope = lax.rsqrt(jnp.sum(step * step, keepdims=True) * size + epsilon)
        master_out[j] = master[j] - (learn_rate * slope) * step


def run_shampoo(energy, force, vectors, first, late):
    S = jax.ShapeDtypeStruct
    steps = min(4, late[1].shape[0])

    def whole(x):
        return pl.BlockSpec(x.shape, lambda i: (0,) * len(x.shape))

    def share(x):
        return pl.BlockSpec((x.shape[0] // steps,) + x.shape[1:], lambda i: (i, 0, 0))

    small = [S((1, PLANE), f32), S((3, PLANE), f32)] + [S((1, FINAL), f32)] * 3
    grown = []
    for group in (first, late):
        left, right, _, _, master = group[1:]
        grown += [S(x.shape, f32) for x in (master, left, right, master)]
    return pl.pallas_call(
        shampoo,
        grid=(steps,),
        out_shape=small + grown,
        in_specs=[whole(energy), whole(force), whole(vectors)]
        + [whole(first[0])]
        + [share(x) for x in first[1:]]
        + [whole(late[0])]
        + [share(x) for x in late[1:]],
        out_specs=[whole(x) for x in small] + [share(x) for x in grown],
        compiler_params=pltpu.CompilerParams(vmem_limit_bytes=60 << 20),
        name="shampoo",
    )(energy, force, vectors, *first, *late)


def local(
    positions,
    species,
    neighbours,
    counts,
    species_scale,
    species_shift,
    energy_cot,
    blocks,
    left,
    right,
    left_root,
    right_root,
    late_blocks,
    late_left,
    late_right,
    late_left_root,
    late_right_root,
    out_vector,
    vector_state,
):
    devices = lax.axis_size("atoms")
    small = (
        neighbours.reshape(PLANE, SLOTS),
        positions,
        species[None],
        counts[None],
        energy_cot[None],
        species_scale[None],
        species_shift[None],
        out_vector[None],
        vector_state[None],
    )
    energy, force, vectors, first_units, late_units = run_network(
        devices, small, blocks, late_blocks
    )
    out = run_shampoo(
        energy,
        force,
        vectors,
        (first_units, left, right, left_root, right_root, blocks),
        (late_units, late_left, late_right, late_left_root, late_right_root, late_blocks),
    )
    energies, forces, vector_grad, new_state, new_vector = out[:5]
    return (
        energies.reshape(-1),
        forces,
        *out[5:],
        vector_grad.reshape(-1),
        new_state.reshape(-1),
        new_vector.reshape(-1),
    )


def solution(mesh):
    row = P("atoms")
    block = P("atoms", None, None)
    placed = (
        (P(None, "atoms"), row, row, row, P(), P(), row)
        + (block,) * 10
        + (P(), P())
    )
    return jax.shard_map(
        local,
        mesh=mesh,
        in_specs=placed,
        out_specs=(row, P(None, "atoms")) + (block,) * 8 + (P(), P(), P()),
        check_vma=False,
    )
```

```python
import functools
import math

import jax
import jax.numpy as jnp
from jax import lax
from jax.experimental import pallas as pl
from jax.experimental.pallas import tpu as pltpu
from jax.sharding import PartitionSpec as P

SIDE = 8
SLOTS = 26
SPECIES = 60
BESSEL = 8
CHANNELS = 64
LATENT = 1024
FINAL = 128
BLOCK_ROWS = 64
BLOCK_COLS = 128
PLANE = SIDE * SIDE

f32 = jnp.float32
bf16 = jnp.bfloat16
highest = lax.Precision.HIGHEST
spacing = 1.6
cutoff_radius = 4.0
env_scale = 0.25
half_root = 0.7071067811865476
decay_rate = 0.5
learn_rate = 0.02
vector_rate = 0.03
epsilon = 1e-06

LANES = 128
ROWS = SLOTS * PLANE
TILES = ROWS // LANES
KINDS = 64

PANEL = 8
WIDE = PANEL * BLOCK_COLS
W_INPUT = (0, 128)
W_TWO = (128, 1024)
W_EMBED = (1152, 128)
W_ENV_ONE = (1280, 128)
W_LAT_ONE = (1408, 1024)
W_SCAL_ONE = (2432, 192)
W_OUT_ONE = (2624, 1024)
W_ENV_TWO = (3648, 128)
W_SCAL_TWO = (3776, 192)
W_FINAL = (3968, 128)
W_LAT_TWO = (0, 1024)
W_OUT_TWO = (1024, 1024)

MESH = pl.DeviceIdType.MESH


def nn(a, b, precision=None):
    return lax.dot_general(
        a, b, (((1,), (0,)), ((), ())), preferred_element_type=f32, precision=precision
    )


def nt(a, b, precision=None):
    return lax.dot_general(
        a, b, (((1,), (1,)), ((), ())), preferred_element_type=f32, precision=precision
    )


def tn(a, b):
    return lax.dot_general(a, b, (((0,), (0,)), ((), ())), preferred_element_type=f32)


def cols_panel(ref, where, n):
    return ref[where[0] : where[0] + where[1], panel(n, STRIP)]


def rows_panel(ref, where, n):
    return ref[pl.ds(pl.multiple_of(where[0] + n * STRIP, 64), STRIP), :]


def narrow(ref, where):
    pieces = []
    for j in range(LATENT // BLOCK_ROWS):
        row = where[0] + j // PANEL * BLOCK_ROWS
        col = j % PANEL * BLOCK_COLS
        pieces.append(ref[row : row + BLOCK_ROWS, col : col + BLOCK_COLS])
    return jnp.concatenate(pieces, axis=0)


def narrow_panel(ref, where, n):
    part = ref[pl.ds(pl.multiple_of(where[0] + n * BLOCK_ROWS, BLOCK_ROWS), BLOCK_ROWS), :]
    return jnp.concatenate([part[:, b * 128 : (b + 1) * 128] for b in range(PANEL)], axis=0)


def sigmoid(x):
    return 0.5 * jnp.tanh(0.5 * x) + 0.5


def halves(x):
    return x + pltpu.roll(x, PLANE, 1)


def lanes(t):
    if isinstance(t, int):
        return pl.ds(t * LANES, LANES)
    return pl.ds(pl.multiple_of(t * LANES, LANES), LANES)


def panel(n, width=256):
    return pl.ds(pl.multiple_of(n * width, width), width)


STRIP = 512
CHUNKS = 2
PIECES = 4
SUM_PIECES = (2, 2, 1, 1)
CHUNK = ROWS // CHUNKS


def loop_panels(body):
    def step(n):
        for c in range(CHUNKS):
            body(n, slice(c * CHUNK, (c + 1) * CHUNK))

    loop(LATENT // STRIP, step)


def beside(count, step, tile):
    share = TILES // count

    def body(i):
        step(i)
        for u in range(share):
            tile(i * share + u)

    loop(count, body)
    for t in range(share * count, TILES):
        tile(t)


def loop(count, body):
    def step(i, carry):
        body(i)
        return carry

    lax.fori_loop(0, count, step, 0)


def parts(x):
    a = x.astype(bf16)
    rest = x - a.astype(f32)
    b = rest.astype(bf16)
    c = (rest - b.astype(f32)).astype(bf16)
    return a, b, c


class Place:
    def __init__(self, devices):
        side = math.isqrt(devices // 8)
        self.devices = devices
        self.sizes = (4, side, side)
        me = lax.axis_index("atoms")
        core = me % 2
        chip = me // 2
        last = chip % side
        middle = chip // side % side
        self.me = me
        self.core = core
        self.pos = (
            chip // (side * side),
            last + core * (middle - last),
            middle + core * (last - middle),
        )
        self.half = (side * side, 1 + core * (side - 1), side + core * (1 - side))
        self.step = tuple(2 * h for h in self.half)
        self.sibling = me + 1 - 2 * core
        self.plain = (self.pos[0], middle, last)
        self.plain_step = (2 * side * side, 2 * side, 2)

    def owner(self, q):
        return q[0] * self.step[0] + q[1] * self.step[1] + q[2] * self.step[2] + self.core

    def near(self, dim, up):
        return self.me + self.step[dim] if up else self.me - self.step[dim]

    def has(self, dim, up):
        return self.pos[dim] < self.sizes[dim] - 1 if up else self.pos[dim] > 0

    def peers(self, dim):
        n, p = self.sizes[dim], self.plain[dim]
        return [(r, (p + r) % n, self.me + ((p + r) % n - p) * self.plain_step[dim]) for r in range(1, n)]


class Units:
    def __init__(self, ref, rows, cols, base=0, part=(0, 1)):
        self.ref, self.rows, self.cols = ref, rows, cols
        self.per = WIDE // cols
        self.base = base
        self.high = rows // part[1]
        self.off = part[0] * self.high

    def window(self, s):
        s = s + self.base
        if self.per == 1:
            row, col = s * self.rows, slice(None)
        else:
            row = s // self.per * self.rows
            col = pl.ds(pl.multiple_of(s % self.per * self.cols, self.cols), self.cols)
        return (pl.ds(pl.multiple_of(row + self.off, 16), self.high), col)

    def at(self, s):
        return self.ref.at[self.window(s)]

    def get(self, s):
        return self.ref[self.window(s)]

    def put(self, s, value):
        self.ref[self.window(s)] = value

    def stretch(self, count):
        return self.ref.at[pl.ds(0, count * self.high // self.per), slice(None)]


def remote(src, dst, send, recv, device):
    return pltpu.make_async_remote_copy(
        src_ref=src,
        dst_ref=dst,
        send_sem=send,
        recv_sem=recv,
        device_id=(device,),
        device_id_type=MESH,
    )


def signal(sem, device):
    pl.semaphore_signal(sem, inc=1, device_id=(device,), device_id_type=MESH)


def others(place, dim):
    n, p = place.sizes[dim], place.pos[dim]
    if n == 2:
        return [(1 - p, None)]
    found = []
    for distance in range(1, n):
        found.append((p - distance, p >= distance))
        found.append((p + distance, p < n - distance))
    return found


def gated(cond, body):
    if cond is None:
        body()
    else:
        pl.when(cond)(body)


def both(a, b):
    return b if a is None else (a if b is None else a & b)


class Gather:
    def __init__(self, place, units, lo, hi, sems, direct=False):
        self.place, self.units, self.lo, self.hi, self.sems = place, units, lo, hi, sems
        self.direct = direct
        _, na, nb = place.sizes
        self.waits = []
        self.shared = 0
        self.first_owner = 2 * lo * na * nb
        at = 2 * (hi - lo) * na * nb
        self.shared_send, self.core_recv = at, at + 1
        at += 2
        self.base = []
        for dim in range(3):
            length = (hi - lo) * (1, na, na * nb)[dim]
            self.base.append((at, at + length))
            at += 2 * length
        self.core_base = at

    @staticmethod
    def amount(devices, share):
        side = math.isqrt(devices // 8)
        return 2 + share * (2 + 2 * side + 5 * side * side)

    def linear(self, q, dim):
        _, na, nb = self.place.sizes
        q0 = q[0] - self.lo
        return (q0, q0 * na + q[1], (q0 * na + q[1]) * nb + q[2])[dim]

    def emit(self, cond, q, sem, device, core=False):
        owner = self.place.owner(q)
        if cond is None:
            sem = self.shared_send
            self.shared += 1

        def copy():
            piece = self.units.at(owner)
            recv = self.core_recv if core else owner - self.first_owner
            return remote(piece, piece, self.sems.at[sem], self.sems.at[recv], device)

        gated(cond, lambda: copy().start())
        if cond is not None:
            self.waits.append(lambda: gated(cond, lambda: copy().wait_send()))

    def onward(self, cond, q):
        place, p = self.place, self.place.pos[0]
        for up in (True, False):
            away = (p >= q[0]) if up else (p <= q[0])
            self.emit(
                both(cond, away & place.has(0, up)),
                q,
                self.base[0][0 if up else 1] + self.linear(q, 0),
                place.near(0, up),
            )

    def sideways(self, cond, q, dims, via=None):
        place = self.place
        for dim in dims:
            if place.sizes[dim] == 2:
                if dim != via:
                    toward = place.me + (1 - 2 * place.pos[dim]) * place.step[dim]
                    self.emit(cond, q, self.base[dim][0] + self.linear(q, dim), toward)
                continue
            for up in (True, False):
                open_end = place.has(dim, up)
                if dim == via:
                    p = place.pos[dim]
                    open_end = open_end & ((q[dim] < p) if up else (q[dim] > p))
                self.emit(
                    both(cond, open_end),
                    q,
                    self.base[dim][0 if up else 1] + self.linear(q, dim),
                    place.near(dim, up),
                )
        self.emit(cond, q, self.core_base + self.linear(q, 2), place.sibling, True)

    def wait(self, cond, q):
        owner = self.place.owner(q)
        piece = self.units.at(owner)
        gated(
            cond,
            lambda: remote(
                piece,
                piece,
                self.sems.at[self.shared_send],
                self.sems.at[owner - self.first_owner],
                self.place.sibling,
            ).wait_recv(),
        )

    def own(self):
        place, p = self.place, self.place.pos
        if self.direct:
            for r in range(1, 4):
                self.emit(None, p, 0, place.me + ((p[0] + r) % 4 - p[0]) * place.step[0])
            return
        for q0 in range(self.lo, self.hi):
            self.onward(p[0] == q0, (q0, p[1], p[2]))

    def column(self):
        p = self.place.pos
        if self.direct:
            self.sideways(None, p, (2, 1))
            for r in range(1, 4):
                q = ((p[0] + r) % 4, p[1], p[2])
                self.wait(None, q)
                self.sideways(None, q, (2, 1))
            return
        for q0 in range(self.lo, self.hi):
            q = (q0, p[1], p[2])
            self.wait(p[0] != q0, q)
            self.onward(p[0] != q0, q)
            self.sideways(None, q, (2, 1))

    def second(self):
        for q0 in range(self.lo, self.hi):
            for qa, there in others(self.place, 1):
                q = (q0, qa, self.place.pos[2])
                self.wait(there, q)
                self.sideways(there, q, (2, 1), 1)

    def third(self):
        for qb, there in others(self.place, 2):
            for q0 in range(self.lo, self.hi):
                for qa in range(self.place.sizes[1]):
                    q = (q0, qa, qb)
                    self.wait(there, q)
                    self.sideways(there, q, (2,), 2)

    def across(self):
        _, na, nb = self.place.sizes
        piece = self.units.stretch((self.hi - self.lo) * na * nb)
        remote(
            piece,
            piece,
            self.sems.at[self.shared_send],
            self.sems.at[self.core_recv],
            self.place.sibling,
        ).wait_recv()

    def finish(self):
        for wait in self.waits:
            wait()
        if self.shared:
            piece = self.units.stretch(self.shared)
            remote(
                piece,
                piece,
                self.sems.at[self.shared_send],
                self.sems.at[self.core_recv],
                self.place.sibling,
            ).wait_send()
        self.waits, self.shared = [], 0


def landing(n):
    return 1 if n == 2 else n + 1


class Reduce:
    def __init__(self, place, units, lo, hi, land, sems, ready):
        self.place, self.units, self.lo, self.hi, self.land = place, units, lo, hi, land
        n0, na, nb = place.sizes
        self.count = (hi - lo) * na * nb
        lines = ((1, n0), (hi - lo, na), ((hi - lo) * na, nb))
        z_at = self.count
        b_at = z_at + landing(n0)
        a_at = b_at + lines[2][0] * landing(nb)
        self.land_at = (z_at, a_at, b_at)
        self.sems, self.ready = sems, ready
        self.shared = 0
        at = 4
        self.recv_at, self.up_at, self.down_at = [], [], []
        for units_here, n in lines:
            self.recv_at.append(at)
            at += units_here * landing(n)
            self.up_at.append(at)
            at += units_here * n
            self.down_at.append(at)
            at += units_here * n
        self.waits = []

    @staticmethod
    def slots(devices, share):
        side = math.isqrt(devices // 8)
        return share * side * side + landing(4) + share * (1 + side) * landing(side)

    @staticmethod
    def amount(devices, share):
        side = math.isqrt(devices // 8)
        total = 4
        for units_here, n in ((1, 4), (share, side), (share * side, side)):
            total += units_here * (landing(n) + 2 * n)
        return total

    def stage(self, k):
        if k == 0:
            self.start()
        elif k == 1:
            self.pairs()
        elif k < 4:
            self.along(4 - k)
        else:
            self.hop(0, k - 3, [(None,) + self.place.pos[1:]])

    def unit(self, dim, q):
        na = self.place.sizes[1]
        return (0, q[0] - self.lo, (q[0] - self.lo) * na + q[1])[dim]

    def add(self, owner, slot):
        self.units.put(owner, self.units.get(owner) + self.land.get(slot))

    def start(self):
        place = self.place
        if self.ready is not None:
            signal(self.ready.at[0], place.sibling)
            for dim in range(3):
                for up in (True, False):
                    pl.when(place.has(dim, up))(
                        lambda dim=dim, up=up: signal(
                            self.ready.at[1 + 2 * dim + (1 if up else 0)], place.near(dim, up)
                        )
                    )
            pl.semaphore_wait(self.ready.at[0], 1)
        per = place.sizes[1] * place.sizes[2]

        def copy(j):
            owner = 2 * (self.lo * per + j) + 1 - place.core
            return remote(
                self.units.at(owner), self.land.at(j), self.sems.at[0], self.sems.at[1], place.sibling
            )

        loop(self.count, lambda j: copy(j).start())
        self.shared += self.count

    def allow(self, dim):
        if self.ready is None:
            return
        for up in (True, False):
            pl.when(self.place.has(dim, up))(
                lambda up=up: pl.semaphore_wait(self.ready.at[1 + 2 * dim + (0 if up else 1)], 1)
            )

    def push(self, cond, dim, q, sem, slot, device):
        owner = self.place.owner(q)
        target = self.unit(dim, q) * landing(self.place.sizes[dim]) + slot
        recv = self.recv_at[dim] + target
        if cond is None:
            self.shared += 1
            sem, recv = 0, 1 + dim

        def copy():
            return remote(
                self.units.at(owner),
                self.land.at(self.land_at[dim] + target),
                self.sems.at[sem],
                self.sems.at[recv],
                device,
            )

        gated(cond, lambda: copy().start())
        if cond is not None:
            self.waits.append(lambda: gated(cond, lambda: copy().wait_send()))

    def arrived(self, sem, count):
        piece = self.land.stretch(count)
        remote(
            piece, piece, self.sems.at[0], self.sems.at[sem], self.place.sibling
        ).wait_recv()

    def pull(self, dim, q, slot):
        target = self.unit(dim, q) * landing(self.place.sizes[dim]) + slot
        piece = self.land.at(self.land_at[dim] + target)
        remote(
            piece,
            piece,
            self.sems.at[0],
            self.sems.at[self.recv_at[dim] + target],
            self.place.sibling,
        ).wait_recv()
        self.add(self.place.owner(q), self.land_at[dim] + target)

    def first(self, dim, q):
        place = self.place
        n, p = place.sizes[dim], place.pos[dim]
        u = self.unit(dim, q)
        if n == 2:
            toward = place.me + (1 - 2 * p) * place.step[dim]
            self.push(None, dim, q, self.up_at[dim] + u * n, 0, toward)
            return
        for up in (True, False):
            away = (q[dim] > 0) if up else (q[dim] < n - 1)
            self.push(
                (p == (0 if up else n - 1)) & away,
                dim,
                q,
                (self.up_at if up else self.down_at)[dim] + u * n + q[dim],
                self.slot_up(q[dim], 0) if up else self.slot_down(n, q[dim], n - 1),
                place.near(dim, up),
            )

    @staticmethod
    def slot_up(q, p):
        return q - (p + 1)

    @staticmethod
    def slot_down(n, q, p):
        to = p - 1
        return q + (n - to if to > 0 else 0)

    def order(self, dim):
        place = self.place
        if place.sizes[dim] == 2:
            return [1 - place.pos[dim], place.pos[dim]]
        return list(range(place.sizes[dim]))

    def mine(self, dim, at):
        return at is self.place.pos[dim]

    def pairs(self):
        place = self.place
        self.allow(2)
        self.arrived(1, self.count)
        for qb in self.order(2):
            for qa in self.order(1):
                for q0 in range(self.lo, self.hi):
                    q = (q0, qa, qb)
                    j = (q0 - self.lo) * place.half[0] + qa * place.half[1] + qb * place.half[2]
                    self.add(place.owner(q), j)
                    if not self.mine(2, qb):
                        self.first(2, q)

    def along(self, dim):
        place = self.place
        n, p = place.sizes[dim], place.pos[dim]
        self.allow(dim - 1)
        if dim == 2:
            rows = [(q0, qa) for qa in self.order(1) for q0 in range(self.lo, self.hi)]
        else:
            rows = [(q0,) for q0 in range(self.lo, self.hi)]

        def whole(row, at):
            return row + (at,) + place.pos[dim + 1 :]

        if n == 2:
            self.arrived(1 + dim, len(rows))
            for row in rows:
                q = whole(row, p)
                self.add(place.owner(q), self.land_at[dim] + self.unit(dim, q))
                if not self.mine(dim - 1, row[dim - 1]):
                    self.first(dim - 1, whole(row, p))
        else:
            for k in range(1, n):
                self.hop(dim, k, [whole(row, None) for row in rows])
            for row in rows:
                self.first(dim - 1, whole(row, p))

    def hop(self, dim, k, rows):
        place = self.place
        n, p = place.sizes[dim], place.pos[dim]
        lo, hi = (self.lo, self.hi) if dim == 0 else (0, n)
        for up in (True, False):
            here = k if up else n - 1 - k
            cond = p == here
            span = range(max(lo, here), hi) if up else range(lo, min(hi, here + 1))
            if len(span) == 0:
                continue

            def receive(up=up, here=here, span=span):
                for row in rows:
                    for at in span:
                        slot = at - here if up else at + (n - here if here > 0 else 0)
                        q = row[:dim] + (at,) + row[dim + 1 :]
                        self.pull(dim, q, slot)
                        if at != here:
                            self.hop_copy(dim, q, up, here).start()

            pl.when(cond)(receive)
            for row in rows:
                for at in span:
                    if at != here:
                        q = row[:dim] + (at,) + row[dim + 1 :]
                        self.waits.append(
                            lambda cond=cond, q=q, up=up, here=here: pl.when(cond)(
                                lambda: self.hop_copy(dim, q, up, here).wait_send()
                            )
                        )

    def hop_copy(self, dim, q, up, here):
        place = self.place
        n = place.sizes[dim]
        u = self.unit(dim, q)
        slot = self.slot_up(q[dim], here) if up else self.slot_down(n, q[dim], here)
        target = u * landing(n) + slot
        return remote(
            self.units.at(place.owner(q)),
            self.land.at(self.land_at[dim] + target),
            self.sems.at[(self.up_at if up else self.down_at)[dim] + u * n + q[dim]],
            self.sems.at[self.recv_at[dim] + target],
            place.near(dim, up),
        )

    def finish(self):
        for wait in self.waits:
            wait()
        piece = self.land.stretch(self.shared)
        remote(
            piece, piece, self.sems.at[0], self.sems.at[1], self.place.sibling
        ).wait_send()
        self.waits, self.shared = [], 0


class Total:
    def __init__(self, place, land, sems):
        self.place, self.land, self.sems = place, land, sems
        self.sizes = (2,) + place.sizes[::-1]
        self.at = [sum(self.sizes[:k]) for k in range(4)]
        self.waits = []

    @staticmethod
    def slots(devices):
        return 6 + 2 * math.isqrt(devices // 8)

    def lines(self, k):
        place = self.place
        if k == 0:
            return place.core, [(1, 1 - place.core, place.sibling)]
        return place.plain[3 - k], place.peers(3 - k)

    def send(self, k, value):
        p, peers = self.lines(k)
        here = self.land.at[self.at[k] + p]
        self.land[self.at[k] + p] = value
        half = self.at[3] + self.sizes[3]
        for r, _, device in peers:

            def copy(r=r, device=device):
                sems = self.sems
                return remote(
                    here, here, sems.at[self.at[k] + r], sems.at[half + self.at[k] + p], device
                )

            copy().start()
            self.waits.append(lambda copy=copy: copy().wait_send())

    def take(self, k):
        _, peers = self.lines(k)
        half = self.at[3] + self.sizes[3]
        for r, at, device in peers:
            there = self.land.at[self.at[k] + at]
            remote(
                there, there, self.sems.at[0], self.sems.at[half + self.at[k] + at], device
            ).wait_recv()
        total = self.land[self.at[k]]
        for s in range(1, self.sizes[k]):
            total = total + self.land[self.at[k] + s]
        return total

    def pass_on(self, k):
        value = self.take(k)
        if k < 3:
            self.send(k + 1, value)
        return value

    def finish(self):
        for wait in self.waits:
            wait()
        self.waits = []


class Ring:
    def __init__(self, me, devices, land, sems):
        self.after = (me + 1) % devices
        self.before = (me + devices - 1) % devices
        self.land, self.sems = land, sems

    def copies(self, to_before, to_after):
        return (
            remote(to_before, self.land.at[1], self.sems.at[0], self.sems.at[1], self.before),
            remote(to_after, self.land.at[0], self.sems.at[2], self.sems.at[3], self.after),
        )

    def start(self, to_before, to_after):
        for copy in self.copies(to_before, to_after):
            copy.start()

    def wait(self, to_before, to_after):
        for copy in self.copies(to_before, to_after):
            copy.wait_recv()

    def finish(self, to_before, to_after):
        for copy in self.copies(to_before, to_after):
            copy.wait_send()


def unit_shape(amount):
    across = min(amount, PANEL)
    return amount // across * BLOCK_ROWS, across * BLOCK_COLS


def own_unit(units, me, blocks):
    across = units.cols // BLOCK_COLS
    rows = []
    for a in range(units.rows // BLOCK_ROWS):
        row = [blocks[a * across + b].astype(bf16) for b in range(across)]
        rows.append(jnp.concatenate(row, axis=1))
    units.put(me, jnp.concatenate(rows, axis=0))


def network(
    idx_ref,
    positions_ref,
    species_ref,
    counts_ref,
    cot_ref,
    scale_ref,
    shift_ref,
    weight_ref,
    state_ref,
    blocks_ref,
    late_in,
    energy_ref,
    forces_ref,
    vector_ref,
    first_out,
    late_out,
    first_w,
    late_w,
    hot,
    z_t,
    z_r,
    geo,
    yrow,
    env_b,
    ee_t,
    en2_t,
    s1_t,
    s2_t,
    gam,
    dlt,
    coef,
    ds_t,
    de_t,
    dy,
    dg,
    dw_t,
    dw_r,
    dpf,
    den,
    lat,
    hid,
    low0,
    act1,
    sl1,
    low1,
    act2,
    sl2,
    low2,
    stage,
    halo,
    force_in,
    sides,
    vector_in,
    pack_ref,
    low_gather,
    mid_gather,
    high_gather,
    late_gather,
    late_sems,
    first_sems,
    ring_sems,
    vector_sems,
    ready,
):
    s_r = dw_r
    fact = den

    wee_t = dw_t.at[:, 0:LATENT]
    we2_t = dw_t.at[0:128, 0:LATENT]
    devices = lax.axis_size("atoms")
    me = lax.axis_index("atoms")
    place = Place(devices)
    own_at = pack_ref.at[0:8]
    first_units = Units(first_w, *unit_shape(blocks_ref.shape[0]))
    late_units = Units(late_w, *unit_shape(late_in.shape[0]))
    top = place.sizes[0]
    middle = top // 2

    def pieces(k, count):
        return Units(first_w, first_units.rows, first_units.cols, part=(k, count))

    def free(ref, units, k=0, count=1):
        slots = Reduce.slots(devices, 1)
        return Units(ref, units.rows // count, units.cols, base=k * slots)

    gather_low = [Gather(place, pieces(k, PIECES), 0, 1, low_gather.at[k]) for k in range(PIECES)]
    gather_mid = Gather(place, first_units, 1, middle, mid_gather)
    gather_high = Gather(place, first_units, middle, top, high_gather)
    gather_late = Gather(place, late_units, 0, top, late_gather, True)
    sum_out = Reduce(
        place, late_units, middle, top, free(low2, late_units), late_sems.at[0], ready.at[0]
    )
    sum_lat = Reduce(
        place, late_units, 0, middle, free(sl2, late_units), late_sems.at[1], ready.at[1]
    )
    sum_first = [
        [
            Reduce(
                place,
                pieces(k, SUM_PIECES[z]),
                z,
                z + 1,
                free(ref, first_units, k, SUM_PIECES[z]),
                first_sems.at[PIECES * z + k],
                ready.at[2 + z] if k == 0 else None,
            )
            for k in range(SUM_PIECES[z])
        ]
        for z, ref in enumerate((hid, low0, low2, act2))
    ]

    def advance(z, stage):
        for part in sum_first[z]:
            part.stage(stage)
    link_halo = Ring(me, devices, halo, ring_sems.at[0])
    link_force = Ring(me, devices, force_in, ring_sems.at[1])
    sum_vector = Total(place, vector_in, vector_sems)

    barrier = pltpu.get_barrier_semaphore()
    partners = [place.sibling, link_halo.before, link_halo.after]
    for dim in range(3):
        partners += [device for _, _, device in place.peers(dim)]
    for device in partners:
        signal(barrier, device)
    for part in (slice(0, PLANE), slice(PLANE, LANES)):
        pack_ref[0:3, part] = positions_ref[...]
        pack_ref[3:4, part] = species_ref[...].astype(f32)
        pack_ref[4:5, part] = counts_ref[...].astype(f32)
        pack_ref[5:6, part] = cot_ref[...]
    pack_ref[6:16] = jnp.zeros((10, LANES), f32)
    pack_ref[6:7, 0:SPECIES] = scale_ref[...]
    pack_ref[7:8, 0:SPECIES] = shift_ref[...]
    pack_ref[8:9] = weight_ref[...]
    pack_ref[9:10] = state_ref[...]
    own_unit(first_units, me, blocks_ref)
    own_unit(late_units, me, late_in)
    pl.semaphore_wait(barrier, len(partners))
    link_halo.start(own_at, own_at)
    for part in gather_low:
        part.own()
    gather_high.own()
    for part in gather_low:
        part.column()

    ids = lax.broadcasted_iota(jnp.int32, (3 * PLANE, LANES), 0)

    whole = PLANE * devices
    coef[0, :, 0:SLOTS] = idx_ref[...].astype(f32)
    listed = coef[0].T[: SLOTS + 6].astype(jnp.int32) - (me - 1) * PLANE
    listed = jnp.where(
        listed < 0, listed + whole, jnp.where(listed >= whole, listed - whole, listed)
    )
    for t in range(TILES):
        near = jnp.concatenate([listed[2 * t : 2 * t + 1], listed[2 * t + 1 : 2 * t + 2]], axis=1)
        hot[:, t * LANES : (t + 1) * LANES] = jnp.where(ids == near, 1.0, 0.0).astype(bf16)

    link_halo.wait(own_at, own_at)
    own = pack_ref[0:8]
    lane = lax.broadcasted_iota(jnp.int32, (8, LANES), 1)
    row = lax.broadcasted_iota(jnp.int32, (8, LANES), 0)
    edge = spacing * devices
    x_row = row == 0
    before = halo[0] - jnp.where(x_row, jnp.where(me == 0, edge, 0.0), 0.0)
    after = halo[1] + jnp.where(x_row, jnp.where(me == devices - 1, edge, 0.0), 0.0)
    rank_y = ((lane & (PLANE - 1)) >> 3).astype(f32)
    rank_z = (lane & (SIDE - 1)).astype(f32)
    table = jnp.concatenate([jnp.where(lane < PLANE, before, own), after], axis=1)
    ranks = jnp.where(row == 4, rank_y, rank_z)
    table = jnp.where(
        jnp.concatenate([row, row], axis=1) < 4, table, jnp.concatenate([ranks, ranks], axis=1)
    )[:, : 3 * PLANE]
    ga, gb, gc = parts(table)
    got = nn(ga, hot[...]) + nn(gb, hot[...]) + nn(gc, hot[...])
    mine = jnp.concatenate([own] * TILES, axis=1)
    lane = lax.broadcasted_iota(jnp.int32, (1, ROWS), 1)
    slot = lane >> 6
    atom = lane & (PLANE - 1)
    for part in gather_low:
        part.second()
    gather_mid.own()

    def wrapped(step):
        return jnp.where(step > 1.5, -8.0, jnp.where(step < -1.5, 8.0, 0.0)) * spacing

    disp = [
        got[0:1] - mine[0:1],
        got[1:2] - mine[1:2] + wrapped(got[4:5] - (atom >> 3).astype(f32)),
        got[2:3] - mine[2:3] + wrapped(got[5:6] - (atom & (SIDE - 1)).astype(f32)),
    ]
    length = jnp.sqrt(disp[0] * disp[0] + disp[1] * disp[1] + disp[2] * disp[2])
    inverse = 1.0 / length
    unit = [disp[0] * inverse, disp[1] * inverse, disp[2] * inverse]
    angle = length * (math.pi / cutoff_radius)
    sin_k = [jnp.sin(angle)]
    cos_k = [jnp.cos(angle)]
    sin_k.append(2.0 * cos_k[0] * sin_k[0])
    cos_k.append(2.0 * cos_k[0] * cos_k[0] - 1.0)
    for k in range(2, BESSEL):
        sin_k.append(2.0 * cos_k[0] * sin_k[k - 1] - sin_k[k - 2])
        cos_k.append(2.0 * cos_k[0] * cos_k[k - 1] - cos_k[k - 2])
    sines = jnp.concatenate(sin_k, axis=0)
    cosines = jnp.concatenate(cos_k, axis=0)
    bessel = (math.sqrt(2.0 / cutoff_radius) * inverse) * sines
    scaled = length * (1.0 / cutoff_radius)
    t2 = scaled * scaled
    t4 = t2 * t2
    t5 = t4 * scaled
    t6 = t4 * t2
    envelope = 1.0 - 28.0 * t6 + 48.0 * (t6 * scaled) - 21.0 * (t4 * t4)
    denvelope = (-168.0 * t5 + 336.0 * t6 - 168.0 * (t6 * scaled)) * (1.0 / cutoff_radius)
    live = jnp.where(slot.astype(f32) < mine[4:5], 1.0, 0.0)

    kind = lax.broadcasted_iota(jnp.int32, (KINDS, LANES), 0).astype(f32)
    is_kind = kind == own[3:4]
    by_kind = own.T
    scale = jnp.sum(jnp.where(is_kind, by_kind[:KINDS, 6:7], 0.0), axis=0, keepdims=True)
    shift = jnp.sum(jnp.where(is_kind, by_kind[:KINDS, 7:8], 0.0), axis=0, keepdims=True)
    cot = jnp.concatenate([own[5:6] * scale] * TILES, axis=1) * live
    weight = cot * envelope

    root3 = math.sqrt(3.0)
    root15 = math.sqrt(15.0)
    root5 = math.sqrt(5.0)
    ux, uy, uz = unit
    yrow[0:8] = jnp.concatenate(
        [
            root3 * ux,
            root3 * uy,
            root3 * uz,
            root15 * ux * uy,
            root15 * uy * uz,
            0.5 * root5 * (3.0 * uz * uz - 1.0),
            root15 * ux * uz,
            0.5 * root15 * (ux * ux - uy * uy),
        ],
        axis=0,
    )
    yrow[8:16] = yrow[0:8] * (live * env_scale)
    yrow[16:17] = live * env_scale
    geo[0:8] = jnp.concatenate([ux, uy, uz, inverse, envelope, denvelope, live, cot], axis=0)
    geo[8:16] = math.sqrt(2.0 / cutoff_radius) * (
        (math.pi / cutoff_radius)
        * lax.broadcasted_iota(jnp.int32, (BESSEL, ROWS), 0).astype(f32)
        * cosines
        + (math.pi / cutoff_radius) * cosines
        - sines * inverse
    ) * inverse


    def one_hots(t):
        row = lax.broadcasted_iota(jnp.int32, (LANES, LANES), 0).astype(f32)
        here = jnp.where(row == own[3:4] + float(BESSEL), 1.0, 0.0)
        there = jnp.where(row == kinds_near[t] + float(BESSEL + SPECIES), 1.0, 0.0)
        return here + there

    kinds_near = [got[3:4, t * LANES : (t + 1) * LANES] for t in range(TILES)]
    gather_mid.column()
    for part in gather_low:
        part.third()
    for t in range(TILES):
        at = slice(t * LANES, (t + 1) * LANES)
        column = jnp.concatenate([bessel[:, at], one_hots(t)[BESSEL:]], axis=0)
        z_t[:, at] = column.astype(bf16)
        z_r[at, :] = column.T.astype(bf16)
        env_b[at, :] = jnp.broadcast_to(envelope[:, at], (LANES, LANES)).T
        fact[at, :] = jnp.broadcast_to(weight[:, at], (LANES, LANES)).T
    gather_mid.second()
    for part in gather_low:
        part.across()
    gather_high.column()


    def twice(x):
        return jnp.concatenate([x] * (STRIP // LANES), axis=1)

    def in_body(n, r):
        pre = nn(z_r[r], cols_panel(first_w, W_INPUT, n))
        hid[r, panel(n, STRIP)] = (pre * sigmoid(pre)).astype(bf16)

    loop_panels(in_body)
    gather_mid.third()
    gather_high.second()
    gather_late.own()
    gather_mid.across()

    def two_body(n, r):
        zero = nn(hid[r], cols_panel(first_w, W_TWO, n)) * twice(env_b[r])
        lat[r, panel(n, STRIP)] = zero
        low0[r, panel(n, STRIP)] = zero.astype(bf16)

    loop_panels(two_body)

    def transposed_product(out, weights, right, width=256):
        at = 0
        while at < ROWS:
            end = min(at + width, ROWS)
            out[:, at:end] = nt(weights, right[at:end, :])
            at = end

    wee_t[0:128, :] = narrow(first_w, W_EMBED).T
    wee_t[128:256, :] = narrow(first_w, W_ENV_ONE).T
    transposed_product(ee_t, wee_t[...], low0)
    gather_late.column()
    gather_high.third()

    def environment(out, v0_ref, v0_at, v1_at):
        for m in range(9):
            total = None
            begin = v0_at if m == 0 else v1_at
            y = yrow[16:17, :] if m == 0 else yrow[7 + m : 8 + m, :]
            for t in range(TILES):
                at = slice(t * LANES, (t + 1) * LANES)
                term = v0_ref[begin : begin + CHANNELS, at] * y[:, at]
                total = term if total is None else total + term
            out[m] = halves(total)

    def put_scalars(t, s_t, rows):
        s_t[:, lanes(t)] = jnp.concatenate(rows, axis=0).astype(bf16)
        filled = jnp.concatenate(rows + [jnp.zeros_like(rows[0])], axis=0)
        flipped = filled.T.astype(bf16)
        s_r[lanes(t), :] = flipped

    def weighted(y, first, count, source, offset):
        total = None
        for m in range(count):
            term = y[first + m : first + m + 1] * source[offset + m]
            total = term if total is None else total + term
        return total

    environment(gam, ee_t, 128, 192)

    def scalars_one(t):
        e0 = ee_t[0:64, lanes(t)]
        e1 = ee_t[64:128, lanes(t)]
        y = yrow[0:8, lanes(t)]
        put_scalars(
            t,
            s1_t,
            [e0 * gam[0], e1 * weighted(y, 0, 3, gam, 1), e1 * weighted(y, 3, 5, gam, 4)],
        )

    beside(6, lambda i: None, scalars_one)
    gather_high.across()

    def pre_one(n, r):
        pre = nn(low0[r], cols_panel(first_w, W_LAT_ONE, n)) + nn(
            s_r[r, : 3 * CHANNELS], cols_panel(first_w, W_SCAL_ONE, n)
        )
        sig = sigmoid(pre)
        act = pre * sig
        act1[r, panel(n, STRIP)] = act.astype(bf16)
        sl1[r, panel(n, STRIP)] = (sig + act * (1.0 - sig)).astype(bf16)

    loop_panels(pre_one)
    gather_late.second()

    def out_one(n, r):
        new = (lat[r, panel(n, STRIP)] + nn(act1[r], cols_panel(first_w, W_OUT_ONE, n))) * half_root
        lat[r, panel(n, STRIP)] = new
        low1[r, panel(n, STRIP)] = new.astype(bf16)

    loop_panels(out_one)
    gather_late.third()
    we2_t[...] = narrow(first_w, W_ENV_TWO).T
    transposed_product(en2_t, we2_t[...], low1)
    environment(dlt, en2_t, 0, 64)

    g0 = gam[0]
    coef[0] = g0 * dlt[0]
    for m in range(3):
        a, b = 1 + (m + 1) % 3, 1 + (m + 2) % 3
        coef[1 + m] = g0 * dlt[1 + m] + (gam[a] * dlt[b] - gam[b] * dlt[a])
    coef[9] = gam[1] * dlt[1] + gam[2] * dlt[2] + gam[3] * dlt[3]
    second = None
    for m in range(4, 9):
        coef[m] = g0 * dlt[m]
        term = gam[m] * dlt[m]
        second = term if second is None else second + term
    coef[10] = second

    def scalars_two(t):
        e0 = ee_t[0:64, lanes(t)]
        e1 = ee_t[64:128, lanes(t)]
        y = yrow[0:8, lanes(t)]
        put_scalars(
            t,
            s2_t,
            [
                e0 * coef[0],
                e1 * weighted(y, 0, 3, coef, 1) + e0 * coef[9],
                e1 * weighted(y, 3, 5, coef, 4) + e0 * coef[10],
            ],
        )

    beside(6, lambda i: None, scalars_two)
    gather_late.across()

    for part in gather_low + [gather_mid, gather_high, gather_late]:
        part.finish()
    def pre_two(n, r):
        pre = nn(low1[r], cols_panel(late_w, W_LAT_TWO, n)) + nn(
            s_r[r, : 3 * CHANNELS], cols_panel(first_w, W_SCAL_TWO, n)
        )
        sig = sigmoid(pre)
        act = pre * sig
        act2[r, panel(n, STRIP)] = act.astype(bf16)
        sl2[r, panel(n, STRIP)] = (sig + act * (1.0 - sig)).astype(bf16)

    loop_panels(pre_two)

    def out_two(n, r):
        new = (lat[r, panel(n, STRIP)] + nn(act2[r], cols_panel(late_w, W_OUT_TWO, n))) * half_root
        low2[r, panel(n, STRIP)] = new.astype(bf16)

    loop_panels(out_two)

    vec = jnp.broadcast_to(pack_ref[8:9], (8, LANES))
    stage[...] = narrow(first_w, W_FINAL)

    def read_out(i):
        r = pl.ds(pl.multiple_of(i * 416, 16), 416)
        pre = nn(low2[r, :], stage[...])
        sig = sigmoid(pre)
        final_act = pre * sig
        dpf[r, :] = (fact[r, :] * vec[0:1] * (sig + final_act * (1.0 - sig))).astype(bf16)
        fact[r, :] = final_act

    loop(4, read_out)
    value = nt(vec, fact[...], highest)[0:1]
    geo_live = geo[6:7]
    geo_env = geo[4:5]
    geo_cot = geo[7:8]
    edge_energy = geo_live * geo_env * value
    summed = None
    for t in range(TILES):
        term = edge_energy[:, t * LANES : (t + 1) * LANES]
        summed = term if summed is None else summed + term
    energy_ref[...] = scale * halves(summed) + shift
    all_weights = jnp.broadcast_to(geo_cot * geo_env, (8, ROWS))
    sum_vector.send(0, nn(all_weights, fact[...], highest))
    geo[16:17] = geo_cot * value

    def big_step(out, where, left, right):
        def step(i):
            grad = tn(left[:, panel(i, STRIP)], right[...])
            out[pl.ds(pl.multiple_of(where[0] + i * STRIP, 64), STRIP), :] = grad.astype(bf16)

        return step

    def big_grad(out, where, left, right):
        loop(LATENT // STRIP, big_step(out, where, left, right))

    def wide_step(out, where, left, right):
        def step(n):
            out[where[0] : where[0] + where[1], panel(n)] = nn(
                left[...], right[:, panel(n)]
            ).astype(bf16)

        return step

    def wide_grad(out, where, left, right):
        loop(4, wide_step(out, where, left, right))

    def narrow_grad(left, right, put):
        def step(n):
            put(n, nn(left, right[:, panel(n)]).T.astype(bf16))

        loop(4, step)

    def put_narrow(where, n, grad):
        row = pl.multiple_of(where[0] + n // 2 * BLOCK_ROWS, BLOCK_ROWS)
        col = pl.multiple_of(n % 2 * 512, 512)
        first_w[pl.ds(row, BLOCK_ROWS), pl.ds(col, 512)] = jnp.concatenate(
            [grad[b * BLOCK_ROWS : (b + 1) * BLOCK_ROWS] for b in range(4)], axis=1
        )

    def put_stage(n, grad):
        stage[panel(n), :] = grad

    def back_final(n, r):
        grad = nt(dpf[r], narrow_panel(first_w, W_FINAL, n)) * half_root
        lat[r, panel(n, STRIP)] = grad
        low2[r, panel(n, STRIP)] = grad.astype(bf16)

    def back_out_two(n, r):
        grad = nt(low2[r], rows_panel(late_w, W_OUT_TWO, n))
        sl2[r, panel(n, STRIP)] = (grad * sl2[r, panel(n, STRIP)].astype(f32)).astype(bf16)

    def tensors_two(t):
        e0 = ee_t[0:64, lanes(t)]
        e1 = ee_t[64:128, lanes(t)]
        y = yrow[0:8, lanes(t)]
        r0 = ds_t[0:64, lanes(t)]
        r1 = ds_t[64:128, lanes(t)]
        r2 = ds_t[128:192, lanes(t)]
        de_t[0:64, lanes(t)] = r0 * coef[0] + r1 * coef[9] + r2 * coef[10]
        de_t[64:128, lanes(t)] = r1 * weighted(y, 0, 3, coef, 1) + r2 * weighted(y, 3, 5, coef, 4)
        p1 = r1 * e1
        p2 = r2 * e1
        rows = []
        for m in range(8):
            p = p1 if m < 3 else p2
            rows.append(jnp.sum(p * coef[1 + m], axis=0, keepdims=True))
            dg[1 + m] += p * y[m : m + 1]
        dy[:, lanes(t)] = jnp.concatenate(rows, axis=0)
        dg[0] += r0 * e0
        dg[9] += r1 * e0
        dg[10] += r2 * e0

    def environment_back(t, grads, source, v1_at, at):
        y4 = yrow[8:16, lanes(t)]
        l4 = yrow[16:17, lanes(t)]
        v1 = source[v1_at : v1_at + 64, lanes(t)]
        low = l4 * grads[0]
        high = weighted(y4, 0, 8, grads, 1)
        both = jnp.concatenate([low, high], axis=0)
        dw_t[at : at + 128, lanes(t)] = both.astype(bf16)
        dw_r[lanes(t), at : at + 128] = both.T.astype(bf16)
        v1 = v1 * l4
        rows = [jnp.sum(v1 * grads[1 + m], axis=0, keepdims=True) for m in range(8)]
        dy[:, lanes(t)] += jnp.concatenate(rows, axis=0)

    def back_lat_two(n, r):
        grad = (
            lat[r, panel(n, STRIP)]
            + nt(sl2[r], rows_panel(late_w, W_LAT_TWO, n))
            + nt(dw_r[r, 128:256], narrow_panel(first_w, W_ENV_TWO, n))
        ) * half_root
        lat[r, panel(n, STRIP)] = grad
        act2[r, panel(n, STRIP)] = grad.astype(bf16)

    def back_out_one(n, r):
        grad = nt(act2[r], rows_panel(first_w, W_OUT_ONE, n))
        sl1[r, panel(n, STRIP)] = (grad * sl1[r, panel(n, STRIP)].astype(f32)).astype(bf16)

    def tensors_one(t):
        e0 = ee_t[0:64, lanes(t)]
        e1 = ee_t[64:128, lanes(t)]
        y = yrow[0:8, lanes(t)]
        r0 = ds_t[0:64, lanes(t)]
        r1 = ds_t[64:128, lanes(t)]
        r2 = ds_t[128:192, lanes(t)]
        low = de_t[0:64, lanes(t)] + r0 * gam[0]
        high = (
            de_t[64:128, lanes(t)]
            + r1 * weighted(y, 0, 3, gam, 1)
            + r2 * weighted(y, 3, 5, gam, 4)
        )
        both = jnp.concatenate([low, high], axis=0)
        dw_t[0:128, lanes(t)] = both.astype(bf16)
        dw_r[lanes(t), 0:128] = both.T.astype(bf16)
        p1 = r1 * e1
        p2 = r2 * e1
        rows = []
        for m in range(8):
            p = p1 if m < 3 else p2
            rows.append(jnp.sum(p * gam[1 + m], axis=0, keepdims=True))
            coef[1 + m] += p * y[m : m + 1]
        dy[:, lanes(t)] += jnp.concatenate(rows, axis=0)
        coef[0] += r0 * e0

    def back_lat_one(n, r):
        both = jnp.concatenate(
            [narrow_panel(first_w, W_EMBED, n), narrow_panel(first_w, W_ENV_ONE, n)], axis=1
        )
        grad = (
            lat[r, panel(n, STRIP)]
            + nt(sl1[r], rows_panel(first_w, W_LAT_ONE, n))
            + nt(dw_r[r], both)
        )
        low1[r, panel(n, STRIP)] = (grad * twice(env_b[r])).astype(bf16)
        part = grad * low0[r, panel(n, STRIP)].astype(f32)
        for b in range(STRIP // LANES):
            den[r] += part[:, b * LANES : (b + 1) * LANES]

    def back_two(n, r):
        grad = nt(low1[r], rows_panel(first_w, W_TWO, n))
        pre = nn(z_r[r], cols_panel(first_w, W_INPUT, n))
        sig = sigmoid(pre)
        act1[r, panel(n, STRIP)] = (grad * (sig + pre * sig * (1.0 - sig))).astype(bf16)

    def lat_one_grad(low, high):
        grad = tn(low0[:, low:high], sl1[...])
        first_w[W_LAT_ONE[0] + low : W_LAT_ONE[0] + high, :] = grad.astype(bf16)

    narrow_grad(dpf[...].T, low2, put_stage)
    loop_panels(back_final)
    loop(4, lambda n: put_narrow(W_FINAL, n, stage[panel(n), :]))
    loop_panels(back_out_two)
    transposed_product(ds_t, first_w[W_SCAL_TWO[0] : W_SCAL_TWO[0] + W_SCAL_TWO[1], :], sl2)
    dg[...] = jnp.zeros_like(dg)
    beside(2, big_step(late_w, W_OUT_TWO, act2, low2), tensors_two)
    sum_vector.pass_on(0)
    sum_out.stage(0)
    total = [halves(dg[m]) for m in range(11)]
    g0 = gam[0]
    d0 = dlt[0]
    new_g0 = total[0] * d0
    for m in range(1, 9):
        new_g0 = new_g0 + total[m] * dlt[m]
    dlt_grads = [total[0] * g0]
    gam_grads = [new_g0]
    for m in range(3):
        a, b = 1 + (m + 1) % 3, 1 + (m + 2) % 3
        dlt_grads.append(
            total[1 + m] * g0 + total[9] * gam[1 + m] + (total[a] * gam[b] - total[b] * gam[a])
        )
        gam_grads.append(total[9] * dlt[1 + m] + (dlt[a] * total[b] - dlt[b] * total[a]))
    for m in range(4, 9):
        dlt_grads.append(total[m] * g0 + total[10] * gam[m])
        gam_grads.append(total[10] * dlt[m])
    for m in range(9):
        dlt[m] = dlt_grads[m]
        dg[m] = gam_grads[m]
    beside(
        4,
        wide_step(first_w, W_SCAL_TWO, s2_t, sl2),
        lambda t: environment_back(t, dlt, en2_t, 64, 128),
    )
    sum_out.stage(1)
    loop_panels(back_lat_two)
    sum_out.stage(2)
    big_grad(late_w, W_LAT_TWO, low1, sl2)
    sum_vector.pass_on(1)
    sum_out.stage(3)
    sum_lat.stage(0)
    loop_panels(back_out_one)
    sum_out.stage(4)
    sum_lat.stage(1)
    transposed_product(ds_t, first_w[W_SCAL_ONE[0] : W_SCAL_ONE[0] + W_SCAL_ONE[1], :], sl1)
    narrow_grad(dw_t[128:256, :], low1, functools.partial(put_narrow, W_ENV_TWO))
    for m in range(9):
        coef[m] = jnp.zeros((CHANNELS, LANES), f32)
    beside(2, big_step(first_w, W_OUT_ONE, act1, act2), tensors_one)
    sum_vector.pass_on(2)
    sum_out.stage(5)
    sum_lat.stage(2)
    advance(3, 0)
    for m in range(9):
        dg[m] = dg[m] + halves(coef[m])
    beside(
        4,
        wide_step(first_w, W_SCAL_ONE, s1_t, sl1),
        lambda t: environment_back(t, dg, ee_t, 192, 128),
    )
    advance(3, 1)
    sum_out.stage(6)
    sum_lat.stage(3)
    den[...] = jnp.zeros_like(den)
    loop_panels(back_lat_one)
    lat_one_grad(640, 1024)
    sum_lat.stage(4)
    advance(3, 2)
    advance(2, 0)
    loop_panels(back_two)
    sum_lat.stage(5)
    advance(3, 3)
    advance(2, 1)
    big_grad(first_w, W_TWO, hid, low1)
    transposed_product(ds_t.at[0:64], first_w[0:64, :], act1)
    wide_grad(first_w, W_INPUT, z_t, act1)
    advance(0, 0)
    advance(2, 2)
    narrow_grad(dw_t[0:128, :], low0, functools.partial(put_narrow, W_EMBED))
    narrow_grad(dw_t[128:256, :], low0, functools.partial(put_narrow, W_ENV_ONE))
    advance(3, 4)
    advance(0, 1)
    dbessel = ds_t[0:8, :]
    through = nt(jnp.ones((8, LANES), f32), den[...], highest)[0:1]
    ux, uy, uz = geo[0:1], geo[1:2], geo[2:3]
    inverse = geo[3:4]
    envelope = geo[4:5]
    denv = geo[16:17] + through / envelope
    dlength = jnp.sum(dbessel * geo[8:16], axis=0, keepdims=True) + denv * geo[5:6]
    g = [dy[m : m + 1, :] for m in range(8)]
    dux = root3 * g[0] + root15 * (uy * g[3] + uz * g[6] + ux * g[7])
    duy = root3 * g[1] + root15 * (ux * g[3] + uz * g[4] - uy * g[7])
    duz = root3 * g[2] + root15 * (uy * g[4] + ux * g[6]) + (3.0 * root5) * uz * g[5]
    along = dlength - (ux * dux + uy * duy + uz * duz) * inverse
    near = jnp.concatenate(
        [
            dux * inverse + ux * along,
            duy * inverse + uy * along,
            duz * inverse + uz * along,
            jnp.zeros((5, ROWS), f32),
        ],
        axis=0,
    )
    summed = None
    for t in range(TILES):
        term = near[:, t * LANES : (t + 1) * LANES]
        summed = term if summed is None else summed + term
    centre = halves(summed)
    na, nb, nc = parts(near)
    spread = nt(na, hot[...]) + nt(nb, hot[...]) + nt(nc, hot[...])
    sides[0] = spread[:, :LANES]
    sides[1, :, 0:PLANE] = spread[:, LANES:]
    link_force.start(sides.at[0], sides.at[1])
    lat_one_grad(0, 384)
    lat_one_grad(384, 640)
    advance(1, 0)
    advance(3, 5)
    advance(2, 3)
    sum_lat.stage(6)
    advance(0, 2)
    advance(1, 1)
    advance(2, 4)
    advance(0, 3)
    advance(3, 6)
    advance(0, 4)
    for step in range(6):
        for k in range(max(SUM_PIECES[:3])):
            for z, after in ((0, 5), (1, 2), (2, 5)):
                if k < SUM_PIECES[z] and after <= after + step - k < 7:
                    sum_first[z][k].stage(after + step - k)
    link_force.wait(sides.at[0], sides.at[1])
    forces_ref[...] = (
        centre - pltpu.roll(sides[0], PLANE, 1) - force_in[1] - force_in[0]
    )
    total = sum_vector.pass_on(3)
    normed = total * lax.rsqrt(jnp.sum(total[0:1] * total[0:1]) * (1.0 / FINAL) + epsilon)
    state = decay_rate * pack_ref[9:10] + (1.0 - decay_rate) * normed * normed
    vector_ref[0:1] = total[0:1]
    vector_ref[1:2] = state[0:1]
    vector_ref[2:3] = (pack_ref[8:9] - vector_rate * normed * lax.rsqrt(state + epsilon))[0:1]
    first_out[...] = first_units.get(me)
    late_out[...] = late_units.get(me)
    for group in sum((list(parts) for parts in sum_first), [sum_out, sum_lat, sum_vector]):
        group.finish()
    link_halo.finish(own_at, own_at)
    link_force.finish(sides.at[0], sides.at[1])


def run_network(devices, small, blocks, late):
    S = jax.ShapeDtypeStruct
    wide = pltpu.VMEM((ROWS, LATENT), bf16)
    slab = pltpu.VMEM((ROWS, LANES), f32)
    panels = lambda amount: pltpu.VMEM((amount * devices // PANEL * BLOCK_ROWS, WIDE), bf16)
    scratch = [
        panels(blocks.shape[0]),
        panels(late.shape[0]),
        pltpu.VMEM((3 * PLANE, ROWS), bf16),
        pltpu.VMEM((LANES, ROWS), bf16),
        pltpu.VMEM((ROWS, LANES), bf16),
        pltpu.VMEM((24, ROWS), f32),
        pltpu.VMEM((24, ROWS), f32),
        slab,
        pltpu.VMEM((256, ROWS), f32),
        pltpu.VMEM((128, ROWS), f32),
        pltpu.VMEM((192, ROWS), bf16),
        pltpu.VMEM((192, ROWS), bf16),
        pltpu.VMEM((9, CHANNELS, LANES), f32),
        pltpu.VMEM((9, CHANNELS, LANES), f32),
        pltpu.VMEM((11, CHANNELS, LANES), f32),
        pltpu.VMEM((192, ROWS), f32),
        pltpu.VMEM((128, ROWS), f32),
        pltpu.VMEM((8, ROWS), f32),
        pltpu.VMEM((11, CHANNELS, LANES), f32),
        pltpu.VMEM((256, ROWS), bf16),
        pltpu.VMEM((ROWS, 256), bf16),
        pltpu.VMEM((ROWS, LANES), bf16),
        slab,
        pltpu.VMEM((ROWS, LATENT), f32),
    ] + [wide] * 8 + [
        pltpu.VMEM((LATENT, LANES), bf16),
        pltpu.VMEM((2, 8, LANES), f32),
        pltpu.VMEM((2, 8, LANES), f32),
        pltpu.VMEM((2, 8, LANES), f32),
        pltpu.VMEM((Total.slots(devices), 8, LANES), f32),
        pltpu.VMEM((16, LANES), f32),
        pltpu.SemaphoreType.DMA((PIECES, Gather.amount(devices, 1))),
        pltpu.SemaphoreType.DMA((Gather.amount(devices, 1),)),
        pltpu.SemaphoreType.DMA((Gather.amount(devices, 2),)),
        pltpu.SemaphoreType.DMA((Gather.amount(devices, 4),)),
        pltpu.SemaphoreType.DMA((2, Reduce.amount(devices, 2))),
        pltpu.SemaphoreType.DMA((4 * PIECES, Reduce.amount(devices, 1))),
        pltpu.SemaphoreType.DMA((2, 4)),
        pltpu.SemaphoreType.DMA((2 * Total.slots(devices),)),
        pltpu.SemaphoreType.REGULAR((6, 7)),
    ]
    vmem = pl.BlockSpec(memory_space=pltpu.VMEM)
    return pl.pallas_call(
        network,
        out_shape=[
            S((1, LANES), f32),
            S((8, LANES), f32),
            S((8, LANES), f32),
            S(unit_shape(blocks.shape[0]), bf16),
            S(unit_shape(late.shape[0]), bf16),
        ],
        in_specs=[vmem] * (len(small) + 2),
        out_specs=[vmem] * 5,
        scratch_shapes=scratch,
        compiler_params=pltpu.CompilerParams(
            vmem_limit_bytes=63 << 20, collective_id=0, has_side_effects=True
        ),
        name="network",
    )(*small, blocks, late)


def shampoo(
    energy,
    force,
    vectors,
    grads,
    left,
    right,
    left_root,
    right_root,
    master,
    late_grads,
    late_left,
    late_right,
    late_left_root,
    late_right_root,
    late_master,
    energy_out,
    force_out,
    vector_out,
    state_out,
    moved_out,
    *outs,
):
    energy_out[...] = energy[:, :PLANE]
    force_out[...] = force[0:3, :PLANE]
    vector_out[...] = vectors[0:1]
    state_out[...] = vectors[1:2]
    moved_out[...] = vectors[2:3]

    todo = []
    for j in range(left.shape[0]):
        todo.append((grads, j, left, right, left_root, right_root, master) + outs[:4])
    for j in range(late_left.shape[0]):
        todo.append(
            (late_grads, j, late_left, late_right, late_left_root, late_right_root, late_master)
            + outs[4:]
        )
    size = 1.0 / (BLOCK_ROWS * BLOCK_COLS)
    held, scales, steps = [], [], []
    for panels, j, left, *_ in todo:
        per = panels.shape[1] // BLOCK_COLS
        at = pl.program_id(0) * left.shape[0] + j
        row = pl.multiple_of(at // per * BLOCK_ROWS, BLOCK_ROWS)
        col = pl.multiple_of(at % per * BLOCK_COLS, BLOCK_COLS)
        held.append(panels[pl.ds(row, BLOCK_ROWS), pl.ds(col, BLOCK_COLS)])
    for g, (_, j, *_, grad_out, left_out, right_out, master_out) in zip(held, todo):
        grad = g.astype(f32)
        grad_out[j] = grad
        scales.append(lax.rsqrt(jnp.sum(grad * grad, keepdims=True) * size + epsilon))
    turned = []
    for g, (_, j, left, right, left_root, *_) in zip(held, todo):
        la, lb, _ = parts(left_root[j])
        turned.append(nn(la, g) + nn(lb, g))
    for g, s, (_, j, left, right, *_, grad_out, left_out, right_out, master_out) in zip(
        held, scales, todo
    ):
        square = (1.0 - decay_rate) * s * s
        left_out[j] = decay_rate * left[j] + square * nt(g, g)
        right_out[j] = decay_rate * right[j] + square * tn(g, g)
    for turn, s, (_, j, left, right, left_root, right_root, *_) in zip(turned, scales, todo):
        ra, rb, _ = parts(right_root[j])
        ta, tb, _ = parts(turn * s)
        steps.append(nn(ta, ra) + (nn(ta, rb) + nn(tb, ra)))
    for step, (_, j, left, right, left_root, right_root, master, *_, master_out) in zip(steps, todo):
        slope = lax.rsqrt(jnp.sum(step * step, keepdims=True) * size + epsilon)
        master_out[j] = master[j] - (learn_rate * slope) * step


def run_shampoo(energy, force, vectors, first, late):
    S = jax.ShapeDtypeStruct
    steps = min(2, late[1].shape[0])

    def whole(x):
        return pl.BlockSpec(x.shape, lambda i: (0,) * len(x.shape))

    def share(x):
        return pl.BlockSpec((x.shape[0] // steps,) + x.shape[1:], lambda i: (i, 0, 0))

    small = [S((1, PLANE), f32), S((3, PLANE), f32)] + [S((1, FINAL), f32)] * 3
    grown = []
    for group in (first, late):
        left, right, _, _, master = group[1:]
        grown += [S(x.shape, f32) for x in (master, left, right, master)]
    return pl.pallas_call(
        shampoo,
        grid=(steps,),
        out_shape=small + grown,
        in_specs=[whole(energy), whole(force), whole(vectors)]
        + [whole(first[0])]
        + [share(x) for x in first[1:]]
        + [whole(late[0])]
        + [share(x) for x in late[1:]],
        out_specs=[whole(x) for x in small] + [share(x) for x in grown],
        compiler_params=pltpu.CompilerParams(vmem_limit_bytes=60 << 20),
        name="shampoo",
    )(energy, force, vectors, *first, *late)


def local(
    positions,
    species,
    neighbours,
    counts,
    species_scale,
    species_shift,
    energy_cot,
    blocks,
    left,
    right,
    left_root,
    right_root,
    late_blocks,
    late_left,
    late_right,
    late_left_root,
    late_right_root,
    out_vector,
    vector_state,
):
    devices = lax.axis_size("atoms")
    small = (
        neighbours.reshape(PLANE, SLOTS),
        positions,
        species[None],
        counts[None],
        energy_cot[None],
        species_scale[None],
        species_shift[None],
        out_vector[None],
        vector_state[None],
    )
    energy, force, vectors, first_units, late_units = run_network(
        devices, small, blocks, late_blocks
    )
    out = run_shampoo(
        energy,
        force,
        vectors,
        (first_units, left, right, left_root, right_root, blocks),
        (late_units, late_left, late_right, late_left_root, late_right_root, late_blocks),
    )
    energies, forces, vector_grad, new_state, new_vector = out[:5]
    return (
        energies.reshape(-1),
        forces,
        *out[5:],
        vector_grad.reshape(-1),
        new_state.reshape(-1),
        new_vector.reshape(-1),
    )


def solution(mesh):
    row = P("atoms")
    block = P("atoms", None, None)
    placed = (
        (P(None, "atoms"), row, row, row, P(), P(), row)
        + (block,) * 10
        + (P(), P())
    )
    return jax.shard_map(
        local,
        mesh=mesh,
        in_specs=placed,
        out_specs=(row, P(None, "atoms")) + (block,) * 8 + (P(), P(), P()),
        check_vma=False,
    )
```

```python
import functools
import math

import jax
import jax.numpy as jnp
from jax import lax
from jax.experimental import pallas as pl
from jax.experimental.pallas import tpu as pltpu
from jax.sharding import PartitionSpec as P

SIDE = 8
SLOTS = 26
SPECIES = 60
BESSEL = 8
CHANNELS = 64
LATENT = 1024
FINAL = 128
BLOCK_ROWS = 64
BLOCK_COLS = 128
PLANE = SIDE * SIDE

f32 = jnp.float32
bf16 = jnp.bfloat16
highest = lax.Precision.HIGHEST
spacing = 1.6
cutoff_radius = 4.0
env_scale = 0.25
half_root = 0.7071067811865476
decay_rate = 0.5
learn_rate = 0.02
vector_rate = 0.03
epsilon = 1e-06

LANES = 128
ROWS = SLOTS * PLANE
TILES = ROWS // LANES
KINDS = 64

PANEL = 8
WIDE = PANEL * BLOCK_COLS
W_INPUT = (0, 128)
W_TWO = (128, 1024)
W_EMBED = (1152, 128)
W_ENV_ONE = (1280, 128)
W_LAT_ONE = (1408, 1024)
W_SCAL_ONE = (2432, 192)
W_OUT_ONE = (2624, 1024)
W_ENV_TWO = (3648, 128)
W_SCAL_TWO = (3776, 192)
W_FINAL = (3968, 128)
W_LAT_TWO = (0, 1024)
W_OUT_TWO = (1024, 1024)

MESH = pl.DeviceIdType.MESH


def nn(a, b, precision=None):
    return lax.dot_general(
        a, b, (((1,), (0,)), ((), ())), preferred_element_type=f32, precision=precision
    )


def nt(a, b, precision=None):
    return lax.dot_general(
        a, b, (((1,), (1,)), ((), ())), preferred_element_type=f32, precision=precision
    )


def tn(a, b):
    return lax.dot_general(a, b, (((0,), (0,)), ((), ())), preferred_element_type=f32)


def cols_panel(ref, where, n):
    return ref[where[0] : where[0] + where[1], panel(n, STRIP)]


def rows_panel(ref, where, n):
    return ref[pl.ds(pl.multiple_of(where[0] + n * STRIP, 64), STRIP), :]


def narrow(ref, where):
    pieces = []
    for j in range(LATENT // BLOCK_ROWS):
        row = where[0] + j // PANEL * BLOCK_ROWS
        col = j % PANEL * BLOCK_COLS
        pieces.append(ref[row : row + BLOCK_ROWS, col : col + BLOCK_COLS])
    return jnp.concatenate(pieces, axis=0)


def narrow_panel(ref, where, n):
    part = ref[pl.ds(pl.multiple_of(where[0] + n * BLOCK_ROWS, BLOCK_ROWS), BLOCK_ROWS), :]
    return jnp.concatenate([part[:, b * 128 : (b + 1) * 128] for b in range(PANEL)], axis=0)


def sigmoid(x):
    return 0.5 * jnp.tanh(0.5 * x) + 0.5


def halves(x):
    return x + pltpu.roll(x, PLANE, 1)


def lanes(t):
    if isinstance(t, int):
        return pl.ds(t * LANES, LANES)
    return pl.ds(pl.multiple_of(t * LANES, LANES), LANES)


def panel(n, width=256):
    return pl.ds(pl.multiple_of(n * width, width), width)


STRIP = 512
CHUNKS = 2
PIECES = 2
SUM_PIECES = (2, 2, 1, 1)
CHUNK = ROWS // CHUNKS


def loop_panels(body):
    def step(n):
        for c in range(CHUNKS):
            body(n, slice(c * CHUNK, (c + 1) * CHUNK))

    loop(LATENT // STRIP, step)


def beside(count, step, tile):
    share = TILES // count

    def body(i):
        step(i)
        for u in range(share):
            tile(i * share + u)

    loop(count, body)
    for t in range(share * count, TILES):
        tile(t)


def loop(count, body):
    def step(i, carry):
        body(i)
        return carry

    lax.fori_loop(0, count, step, 0)


def parts(x):
    a = x.astype(bf16)
    rest = x - a.astype(f32)
    b = rest.astype(bf16)
    c = (rest - b.astype(f32)).astype(bf16)
    return a, b, c


class Place:
    def __init__(self, devices):
        side = math.isqrt(devices // 8)
        self.devices = devices
        self.sizes = (4, side, side)
        me = lax.axis_index("atoms")
        core = me % 2
        chip = me // 2
        last = chip % side
        middle = chip // side % side
        self.me = me
        self.core = core
        self.pos = (
            chip // (side * side),
            last + core * (middle - last),
            middle + core * (last - middle),
        )
        self.half = (side * side, 1 + core * (side - 1), side + core * (1 - side))
        self.step = tuple(2 * h for h in self.half)
        self.sibling = me + 1 - 2 * core
        self.plain = (self.pos[0], middle, last)
        self.plain_step = (2 * side * side, 2 * side, 2)

    def owner(self, q):
        return q[0] * self.step[0] + q[1] * self.step[1] + q[2] * self.step[2] + self.core

    def near(self, dim, up):
        return self.me + self.step[dim] if up else self.me - self.step[dim]

    def has(self, dim, up):
        return self.pos[dim] < self.sizes[dim] - 1 if up else self.pos[dim] > 0

    def peers(self, dim):
        n, p = self.sizes[dim], self.plain[dim]
        return [(r, (p + r) % n, self.me + ((p + r) % n - p) * self.plain_step[dim]) for r in range(1, n)]


class Units:
    def __init__(self, ref, rows, cols, base=0, part=(0, 1)):
        self.ref, self.rows, self.cols = ref, rows, cols
        self.per = WIDE // cols
        self.base = base
        self.high = rows // part[1]
        self.off = part[0] * self.high

    def window(self, s):
        s = s + self.base
        if self.per == 1:
            row, col = s * self.rows, slice(None)
        else:
            row = s // self.per * self.rows
            col = pl.ds(pl.multiple_of(s % self.per * self.cols, self.cols), self.cols)
        return (pl.ds(pl.multiple_of(row + self.off, 16), self.high), col)

    def at(self, s):
        return self.ref.at[self.window(s)]

    def get(self, s):
        return self.ref[self.window(s)]

    def put(self, s, value):
        self.ref[self.window(s)] = value

    def stretch(self, count):
        return self.ref.at[pl.ds(0, count * self.high // self.per), slice(None)]


def remote(src, dst, send, recv, device):
    return pltpu.make_async_remote_copy(
        src_ref=src,
        dst_ref=dst,
        send_sem=send,
        recv_sem=recv,
        device_id=(device,),
        device_id_type=MESH,
    )


def signal(sem, device):
    pl.semaphore_signal(sem, inc=1, device_id=(device,), device_id_type=MESH)


def others(place, dim):
    n, p = place.sizes[dim], place.pos[dim]
    if n == 2:
        return [(1 - p, None)]
    found = []
    for distance in range(1, n):
        found.append((p - distance, p >= distance))
        found.append((p + distance, p < n - distance))
    return found


def gated(cond, body):
    if cond is None:
        body()
    else:
        pl.when(cond)(body)


def both(a, b):
    return b if a is None else (a if b is None else a & b)


class Gather:
    def __init__(self, place, units, lo, hi, sems, direct=False, eager=True):
        self.place, self.units, self.lo, self.hi, self.sems = place, units, lo, hi, sems
        self.direct, self.eager = direct, eager
        _, na, nb = place.sizes
        self.waits = []
        self.shared = 0
        self.first_owner = 2 * lo * na * nb
        at = 2 * (hi - lo) * na * nb
        self.shared_send, self.core_recv = at, at + 1
        at += 2
        self.base = []
        for dim in range(3):
            length = (hi - lo) * (1, na, na * nb)[dim]
            self.base.append((at, at + length))
            at += 2 * length
        self.core_base = at

    @staticmethod
    def amount(devices, share):
        side = math.isqrt(devices // 8)
        return 2 + share * (2 + 2 * side + 5 * side * side)

    def linear(self, q, dim):
        _, na, nb = self.place.sizes
        q0 = q[0] - self.lo
        return (q0, q0 * na + q[1], (q0 * na + q[1]) * nb + q[2])[dim]

    def emit(self, cond, q, sem, device, core=False, once=None):
        owner = self.place.owner(q)
        common = cond is None or once is not None
        if common:
            sem = self.shared_send
            self.shared += 1 if once is None else once

        def copy():
            piece = self.units.at(owner)
            recv = self.core_recv if core else owner - self.first_owner
            return remote(piece, piece, self.sems.at[sem], self.sems.at[recv], device)

        gated(cond, lambda: copy().start())
        if not common:
            self.waits.append(lambda: gated(cond, lambda: copy().wait_send()))

    def onward(self, cond, q):
        place, p = self.place, self.place.pos[0]
        for up in (True, False):
            away = (p >= q[0]) if up else (p <= q[0])
            self.emit(
                both(cond, away & place.has(0, up)),
                q,
                self.base[0][0 if up else 1] + self.linear(q, 0),
                place.near(0, up),
            )

    def sideways(self, cond, q, dims, via=None, once=None):
        place = self.place
        for dim in dims:
            if place.sizes[dim] == 2:
                if dim != via:
                    toward = place.me + (1 - 2 * place.pos[dim]) * place.step[dim]
                    self.emit(
                        cond, q, self.base[dim][0] + self.linear(q, dim), toward, False, once
                    )
                continue
            for up in (True, False):
                open_end = place.has(dim, up)
                if dim == via:
                    p = place.pos[dim]
                    open_end = open_end & ((q[dim] < p) if up else (q[dim] > p))
                self.emit(
                    both(cond, open_end),
                    q,
                    self.base[dim][0 if up else 1] + self.linear(q, dim),
                    place.near(dim, up),
                )
        self.emit(cond, q, self.core_base + self.linear(q, 2), place.sibling, True, once)

    def wait(self, cond, q):
        owner = self.place.owner(q)
        piece = self.units.at(owner)
        gated(
            cond,
            lambda: remote(
                piece,
                piece,
                self.sems.at[self.shared_send],
                self.sems.at[owner - self.first_owner],
                self.place.sibling,
            ).wait_recv(),
        )

    def own(self):
        place, p = self.place, self.place.pos
        if self.direct:
            for r in range(1, 4):
                self.emit(None, p, 0, place.me + ((p[0] + r) % 4 - p[0]) * place.step[0])
            self.sideways(None, p, (2, 1))
            return
        for q0 in range(self.lo, self.hi):
            q = (q0, p[1], p[2])
            self.onward(p[0] == q0, q)
            if self.eager:
                self.sideways(p[0] == q0, q, (2, 1), None, 1)

    def column(self):
        p = self.place.pos
        if self.direct:
            for r in range(1, 4):
                q = ((p[0] + r) % 4, p[1], p[2])
                self.wait(None, q)
                self.sideways(None, q, (2, 1))
            return
        for q0 in range(self.lo, self.hi):
            q = (q0, p[1], p[2])
            self.wait(p[0] != q0, q)
            self.onward(p[0] != q0, q)
            if self.eager:
                self.sideways(p[0] != q0, q, (2, 1), None, 0)
            else:
                self.sideways(None, q, (2, 1))

    def second(self):
        for q0 in range(self.lo, self.hi):
            for qa, there in others(self.place, 1):
                q = (q0, qa, self.place.pos[2])
                self.wait(there, q)
                self.sideways(there, q, (2, 1), 1)

    def third(self):
        for qb, there in others(self.place, 2):
            for q0 in range(self.lo, self.hi):
                for qa in range(self.place.sizes[1]):
                    q = (q0, qa, qb)
                    self.wait(there, q)
                    self.sideways(there, q, (2,), 2)

    def across(self):
        _, na, nb = self.place.sizes
        piece = self.units.stretch((self.hi - self.lo) * na * nb)
        remote(
            piece,
            piece,
            self.sems.at[self.shared_send],
            self.sems.at[self.core_recv],
            self.place.sibling,
        ).wait_recv()

    def finish(self):
        for wait in self.waits:
            wait()
        if self.shared:
            piece = self.units.stretch(self.shared)
            remote(
                piece,
                piece,
                self.sems.at[self.shared_send],
                self.sems.at[self.core_recv],
                self.place.sibling,
            ).wait_send()
        self.waits, self.shared = [], 0


def landing(n):
    return 1 if n == 2 else n + 1


class Reduce:
    def __init__(self, place, units, lo, hi, land, sems, ready):
        self.place, self.units, self.lo, self.hi, self.land = place, units, lo, hi, land
        n0, na, nb = place.sizes
        self.count = (hi - lo) * na * nb
        lines = ((1, n0), (hi - lo, na), ((hi - lo) * na, nb))
        z_at = self.count
        b_at = z_at + landing(n0)
        a_at = b_at + lines[2][0] * landing(nb)
        self.land_at = (z_at, a_at, b_at)
        self.sems, self.ready = sems, ready
        self.shared = 0
        at = 4
        self.recv_at, self.up_at, self.down_at = [], [], []
        for units_here, n in lines:
            self.recv_at.append(at)
            at += units_here * landing(n)
            self.up_at.append(at)
            at += units_here * n
            self.down_at.append(at)
            at += units_here * n
        self.waits = []

    @staticmethod
    def slots(devices, share):
        side = math.isqrt(devices // 8)
        return share * side * side + landing(4) + share * (1 + side) * landing(side)

    @staticmethod
    def amount(devices, share):
        side = math.isqrt(devices // 8)
        total = 4
        for units_here, n in ((1, 4), (share, side), (share * side, side)):
            total += units_here * (landing(n) + 2 * n)
        return total

    def stage(self, k):
        if k == 0:
            self.start()
        elif k == 1:
            self.pairs()
        elif k < 4:
            self.along(4 - k)
        else:
            self.hop(0, k - 3, [(None,) + self.place.pos[1:]])

    def unit(self, dim, q):
        na = self.place.sizes[1]
        return (0, q[0] - self.lo, (q[0] - self.lo) * na + q[1])[dim]

    def add(self, owner, slot):
        self.units.put(owner, self.units.get(owner) + self.land.get(slot))

    def start(self):
        place = self.place
        if self.ready is not None:
            signal(self.ready.at[0], place.sibling)
            for dim in range(3):
                for up in (True, False):
                    pl.when(place.has(dim, up))(
                        lambda dim=dim, up=up: signal(
                            self.ready.at[1 + 2 * dim + (1 if up else 0)], place.near(dim, up)
                        )
                    )
            pl.semaphore_wait(self.ready.at[0], 1)
        per = place.sizes[1] * place.sizes[2]

        def copy(j):
            owner = 2 * (self.lo * per + j) + 1 - place.core
            return remote(
                self.units.at(owner), self.land.at(j), self.sems.at[0], self.sems.at[1], place.sibling
            )

        loop(self.count, lambda j: copy(j).start())
        self.shared += self.count

    def allow(self, dim):
        if self.ready is None:
            return
        for up in (True, False):
            pl.when(self.place.has(dim, up))(
                lambda up=up: pl.semaphore_wait(self.ready.at[1 + 2 * dim + (0 if up else 1)], 1)
            )

    def push(self, cond, dim, q, sem, slot, device):
        owner = self.place.owner(q)
        target = self.unit(dim, q) * landing(self.place.sizes[dim]) + slot
        recv = self.recv_at[dim] + target
        if cond is None:
            self.shared += 1
            sem, recv = 0, 1 + dim

        def copy():
            return remote(
                self.units.at(owner),
                self.land.at(self.land_at[dim] + target),
                self.sems.at[sem],
                self.sems.at[recv],
                device,
            )

        gated(cond, lambda: copy().start())
        if cond is not None:
            self.waits.append(lambda: gated(cond, lambda: copy().wait_send()))

    def arrived(self, sem, count):
        piece = self.land.stretch(count)
        remote(
            piece, piece, self.sems.at[0], self.sems.at[sem], self.place.sibling
        ).wait_recv()

    def pull(self, dim, q, slot):
        target = self.unit(dim, q) * landing(self.place.sizes[dim]) + slot
        piece = self.land.at(self.land_at[dim] + target)
        remote(
            piece,
            piece,
            self.sems.at[0],
            self.sems.at[self.recv_at[dim] + target],
            self.place.sibling,
        ).wait_recv()
        self.add(self.place.owner(q), self.land_at[dim] + target)

    def first(self, dim, q):
        place = self.place
        n, p = place.sizes[dim], place.pos[dim]
        u = self.unit(dim, q)
        if n == 2:
            toward = place.me + (1 - 2 * p) * place.step[dim]
            self.push(None, dim, q, self.up_at[dim] + u * n, 0, toward)
            return
        for up in (True, False):
            away = (q[dim] > 0) if up else (q[dim] < n - 1)
            self.push(
                (p == (0 if up else n - 1)) & away,
                dim,
                q,
                (self.up_at if up else self.down_at)[dim] + u * n + q[dim],
                self.slot_up(q[dim], 0) if up else self.slot_down(n, q[dim], n - 1),
                place.near(dim, up),
            )

    @staticmethod
    def slot_up(q, p):
        return q - (p + 1)

    @staticmethod
    def slot_down(n, q, p):
        to = p - 1
        return q + (n - to if to > 0 else 0)

    def order(self, dim):
        place = self.place
        if place.sizes[dim] == 2:
            return [1 - place.pos[dim], place.pos[dim]]
        return list(range(place.sizes[dim]))

    def mine(self, dim, at):
        return at is self.place.pos[dim]

    def pairs(self):
        place = self.place
        self.allow(2)
        self.arrived(1, self.count)
        for qb in self.order(2):
            for qa in self.order(1):
                for q0 in range(self.lo, self.hi):
                    q = (q0, qa, qb)
                    j = (q0 - self.lo) * place.half[0] + qa * place.half[1] + qb * place.half[2]
                    self.add(place.owner(q), j)
                    if not self.mine(2, qb):
                        self.first(2, q)

    def along(self, dim):
        place = self.place
        n, p = place.sizes[dim], place.pos[dim]
        self.allow(dim - 1)
        if dim == 2:
            rows = [(q0, qa) for qa in self.order(1) for q0 in range(self.lo, self.hi)]
        else:
            rows = [(q0,) for q0 in range(self.lo, self.hi)]

        def whole(row, at):
            return row + (at,) + place.pos[dim + 1 :]

        if n == 2:
            self.arrived(1 + dim, len(rows))
            for row in rows:
                q = whole(row, p)
                self.add(place.owner(q), self.land_at[dim] + self.unit(dim, q))
                if not self.mine(dim - 1, row[dim - 1]):
                    self.first(dim - 1, whole(row, p))
        else:
            for k in range(1, n):
                self.hop(dim, k, [whole(row, None) for row in rows])
            for row in rows:
                self.first(dim - 1, whole(row, p))

    def hop(self, dim, k, rows):
        place = self.place
        n, p = place.sizes[dim], place.pos[dim]
        lo, hi = (self.lo, self.hi) if dim == 0 else (0, n)
        for up in (True, False):
            here = k if up else n - 1 - k
            cond = p == here
            span = range(max(lo, here), hi) if up else range(lo, min(hi, here + 1))
            if len(span) == 0:
                continue

            def receive(up=up, here=here, span=span):
                for row in rows:
                    for at in span:
                        slot = at - here if up else at + (n - here if here > 0 else 0)
                        q = row[:dim] + (at,) + row[dim + 1 :]
                        self.pull(dim, q, slot)
                        if at != here:
                            self.hop_copy(dim, q, up, here).start()

            pl.when(cond)(receive)
            for row in rows:
                for at in span:
                    if at != here:
                        q = row[:dim] + (at,) + row[dim + 1 :]
                        self.waits.append(
                            lambda cond=cond, q=q, up=up, here=here: pl.when(cond)(
                                lambda: self.hop_copy(dim, q, up, here).wait_send()
                            )
                        )

    def hop_copy(self, dim, q, up, here):
        place = self.place
        n = place.sizes[dim]
        u = self.unit(dim, q)
        slot = self.slot_up(q[dim], here) if up else self.slot_down(n, q[dim], here)
        target = u * landing(n) + slot
        return remote(
            self.units.at(place.owner(q)),
            self.land.at(self.land_at[dim] + target),
            self.sems.at[(self.up_at if up else self.down_at)[dim] + u * n + q[dim]],
            self.sems.at[self.recv_at[dim] + target],
            place.near(dim, up),
        )

    def finish(self):
        for wait in self.waits:
            wait()
        piece = self.land.stretch(self.shared)
        remote(
            piece, piece, self.sems.at[0], self.sems.at[1], self.place.sibling
        ).wait_send()
        self.waits, self.shared = [], 0


class Total:
    def __init__(self, place, land, sems):
        self.place, self.land, self.sems = place, land, sems
        self.sizes = (2,) + place.sizes[::-1]
        self.at = [sum(self.sizes[:k]) for k in range(4)]
        self.waits = []

    @staticmethod
    def slots(devices):
        return 6 + 2 * math.isqrt(devices // 8)

    def lines(self, k):
        place = self.place
        if k == 0:
            return place.core, [(1, 1 - place.core, place.sibling)]
        return place.plain[3 - k], place.peers(3 - k)

    def send(self, k, value):
        p, peers = self.lines(k)
        here = self.land.at[self.at[k] + p]
        self.land[self.at[k] + p] = value
        half = self.at[3] + self.sizes[3]
        for r, _, device in peers:

            def copy(r=r, device=device):
                sems = self.sems
                return remote(
                    here, here, sems.at[self.at[k] + r], sems.at[half + self.at[k] + p], device
                )

            copy().start()
            self.waits.append(lambda copy=copy: copy().wait_send())

    def take(self, k):
        _, peers = self.lines(k)
        half = self.at[3] + self.sizes[3]
        for r, at, device in peers:
            there = self.land.at[self.at[k] + at]
            remote(
                there, there, self.sems.at[0], self.sems.at[half + self.at[k] + at], device
            ).wait_recv()
        total = self.land[self.at[k]]
        for s in range(1, self.sizes[k]):
            total = total + self.land[self.at[k] + s]
        return total

    def pass_on(self, k):
        value = self.take(k)
        if k < 3:
            self.send(k + 1, value)
        return value

    def finish(self):
        for wait in self.waits:
            wait()
        self.waits = []


class Ring:
    def __init__(self, me, devices, land, sems):
        self.after = (me + 1) % devices
        self.before = (me + devices - 1) % devices
        self.land, self.sems = land, sems

    def copies(self, to_before, to_after):
        return (
            remote(to_before, self.land.at[1], self.sems.at[0], self.sems.at[1], self.before),
            remote(to_after, self.land.at[0], self.sems.at[2], self.sems.at[3], self.after),
        )

    def start(self, to_before, to_after):
        for copy in self.copies(to_before, to_after):
            copy.start()

    def wait(self, to_before, to_after):
        for copy in self.copies(to_before, to_after):
            copy.wait_recv()

    def finish(self, to_before, to_after):
        for copy in self.copies(to_before, to_after):
            copy.wait_send()


def unit_shape(amount):
    across = min(amount, PANEL)
    return amount // across * BLOCK_ROWS, across * BLOCK_COLS


def own_unit(units, me, blocks):
    across = units.cols // BLOCK_COLS
    rows = []
    for a in range(units.rows // BLOCK_ROWS):
        row = [blocks[a * across + b].astype(bf16) for b in range(across)]
        rows.append(jnp.concatenate(row, axis=1))
    units.put(me, jnp.concatenate(rows, axis=0))


def network(
    idx_ref,
    positions_ref,
    species_ref,
    counts_ref,
    cot_ref,
    scale_ref,
    shift_ref,
    weight_ref,
    state_ref,
    blocks_ref,
    late_in,
    energy_ref,
    forces_ref,
    vector_ref,
    first_out,
    late_out,
    first_w,
    late_w,
    hot,
    z_t,
    z_r,
    geo,
    yrow,
    env_b,
    ee_t,
    en2_t,
    s1_t,
    s2_t,
    gam,
    dlt,
    coef,
    ds_t,
    de_t,
    dy,
    dg,
    dw_t,
    dw_r,
    dpf,
    den,
    lat,
    hid,
    low0,
    act1,
    sl1,
    low1,
    act2,
    sl2,
    low2,
    stage,
    halo,
    force_in,
    sides,
    vector_in,
    pack_ref,
    low_gather,
    mid_gather,
    high_gather,
    late_gather,
    late_sems,
    first_sems,
    ring_sems,
    vector_sems,
    ready,
):
    s_r = dw_r
    fact = den

    wee_t = dw_t.at[:, 0:LATENT]
    we2_t = dw_t.at[0:128, 0:LATENT]
    devices = lax.axis_size("atoms")
    me = lax.axis_index("atoms")
    place = Place(devices)
    own_at = pack_ref.at[0:8]
    first_units = Units(first_w, *unit_shape(blocks_ref.shape[0]))
    late_units = Units(late_w, *unit_shape(late_in.shape[0]))
    top = place.sizes[0]
    middle = top // 2

    def pieces(k, count):
        return Units(first_w, first_units.rows, first_units.cols, part=(k, count))

    def free(ref, units, k=0, count=1):
        slots = Reduce.slots(devices, 1)
        return Units(ref, units.rows // count, units.cols, base=k * slots)

    gather_low = [Gather(place, pieces(k, PIECES), 0, 1, low_gather.at[k]) for k in range(PIECES)]
    gather_mid = Gather(place, first_units, 1, middle, mid_gather)
    gather_high = Gather(place, first_units, middle, top, high_gather)
    gather_late = Gather(place, late_units, 0, top, late_gather, True)
    sum_out = Reduce(
        place, late_units, middle, top, free(low2, late_units), late_sems.at[0], ready.at[0]
    )
    sum_lat = Reduce(
        place, late_units, 0, middle, free(sl2, late_units), late_sems.at[1], ready.at[1]
    )
    sum_first = [
        [
            Reduce(
                place,
                pieces(k, SUM_PIECES[z]),
                z,
                z + 1,
                free(ref, first_units, k, SUM_PIECES[z]),
                first_sems.at[PIECES * z + k],
                ready.at[2 + z] if k == 0 else None,
            )
            for k in range(SUM_PIECES[z])
        ]
        for z, ref in enumerate((hid, low0, low2, act2))
    ]

    def advance(z, stage):
        for part in sum_first[z]:
            part.stage(stage)
    link_halo = Ring(me, devices, halo, ring_sems.at[0])
    link_force = Ring(me, devices, force_in, ring_sems.at[1])
    sum_vector = Total(place, vector_in, vector_sems)

    barrier = pltpu.get_barrier_semaphore()
    partners = [place.sibling, link_halo.before, link_halo.after]
    for dim in range(3):
        partners += [device for _, _, device in place.peers(dim)]
    for device in partners:
        signal(barrier, device)
    for part in (slice(0, PLANE), slice(PLANE, LANES)):
        pack_ref[0:3, part] = positions_ref[...]
        pack_ref[3:4, part] = species_ref[...].astype(f32)
        pack_ref[4:5, part] = counts_ref[...].astype(f32)
        pack_ref[5:6, part] = cot_ref[...]
    pack_ref[6:16] = jnp.zeros((10, LANES), f32)
    pack_ref[6:7, 0:SPECIES] = scale_ref[...]
    pack_ref[7:8, 0:SPECIES] = shift_ref[...]
    pack_ref[8:9] = weight_ref[...]
    pack_ref[9:10] = state_ref[...]
    own_unit(first_units, me, blocks_ref)
    own_unit(late_units, me, late_in)
    pl.semaphore_wait(barrier, len(partners))
    link_halo.start(own_at, own_at)
    for part in gather_low:
        part.own()
    gather_high.own()

    ids = lax.broadcasted_iota(jnp.int32, (3 * PLANE, LANES), 0)

    whole = PLANE * devices
    coef[0, :, 0:SLOTS] = idx_ref[...].astype(f32)
    listed = coef[0].T[: SLOTS + 6].astype(jnp.int32) - (me - 1) * PLANE
    listed = jnp.where(
        listed < 0, listed + whole, jnp.where(listed >= whole, listed - whole, listed)
    )
    for t in range(TILES):
        near = jnp.concatenate([listed[2 * t : 2 * t + 1], listed[2 * t + 1 : 2 * t + 2]], axis=1)
        hot[:, t * LANES : (t + 1) * LANES] = jnp.where(ids == near, 1.0, 0.0).astype(bf16)

    link_halo.wait(own_at, own_at)
    own = pack_ref[0:8]
    lane = lax.broadcasted_iota(jnp.int32, (8, LANES), 1)
    row = lax.broadcasted_iota(jnp.int32, (8, LANES), 0)
    edge = spacing * devices
    x_row = row == 0
    before = halo[0] - jnp.where(x_row, jnp.where(me == 0, edge, 0.0), 0.0)
    after = halo[1] + jnp.where(x_row, jnp.where(me == devices - 1, edge, 0.0), 0.0)
    rank_y = ((lane & (PLANE - 1)) >> 3).astype(f32)
    rank_z = (lane & (SIDE - 1)).astype(f32)
    table = jnp.concatenate([jnp.where(lane < PLANE, before, own), after], axis=1)
    ranks = jnp.where(row == 4, rank_y, rank_z)
    table = jnp.where(
        jnp.concatenate([row, row], axis=1) < 4, table, jnp.concatenate([ranks, ranks], axis=1)
    )[:, : 3 * PLANE]
    ga, gb, gc = parts(table)
    got = nn(ga, hot[...]) + nn(gb, hot[...]) + nn(gc, hot[...])
    mine = jnp.concatenate([own] * TILES, axis=1)
    lane = lax.broadcasted_iota(jnp.int32, (1, ROWS), 1)
    slot = lane >> 6
    atom = lane & (PLANE - 1)
    for part in gather_low:
        part.column()
    for part in gather_low:
        part.second()
    gather_mid.own()
    gather_mid.column()

    def wrapped(step):
        return jnp.where(step > 1.5, -8.0, jnp.where(step < -1.5, 8.0, 0.0)) * spacing

    disp = [
        got[0:1] - mine[0:1],
        got[1:2] - mine[1:2] + wrapped(got[4:5] - (atom >> 3).astype(f32)),
        got[2:3] - mine[2:3] + wrapped(got[5:6] - (atom & (SIDE - 1)).astype(f32)),
    ]
    length = jnp.sqrt(disp[0] * disp[0] + disp[1] * disp[1] + disp[2] * disp[2])
    inverse = 1.0 / length
    unit = [disp[0] * inverse, disp[1] * inverse, disp[2] * inverse]
    angle = length * (math.pi / cutoff_radius)
    sin_k = [jnp.sin(angle)]
    cos_k = [jnp.cos(angle)]
    sin_k.append(2.0 * cos_k[0] * sin_k[0])
    cos_k.append(2.0 * cos_k[0] * cos_k[0] - 1.0)
    for k in range(2, BESSEL):
        sin_k.append(2.0 * cos_k[0] * sin_k[k - 1] - sin_k[k - 2])
        cos_k.append(2.0 * cos_k[0] * cos_k[k - 1] - cos_k[k - 2])
    sines = jnp.concatenate(sin_k, axis=0)
    cosines = jnp.concatenate(cos_k, axis=0)
    bessel = (math.sqrt(2.0 / cutoff_radius) * inverse) * sines
    scaled = length * (1.0 / cutoff_radius)
    t2 = scaled * scaled
    t4 = t2 * t2
    t5 = t4 * scaled
    t6 = t4 * t2
    envelope = 1.0 - 28.0 * t6 + 48.0 * (t6 * scaled) - 21.0 * (t4 * t4)
    denvelope = (-168.0 * t5 + 336.0 * t6 - 168.0 * (t6 * scaled)) * (1.0 / cutoff_radius)
    live = jnp.where(slot.astype(f32) < mine[4:5], 1.0, 0.0)

    kind = lax.broadcasted_iota(jnp.int32, (KINDS, LANES), 0).astype(f32)
    is_kind = kind == own[3:4]
    by_kind = own.T
    scale = jnp.sum(jnp.where(is_kind, by_kind[:KINDS, 6:7], 0.0), axis=0, keepdims=True)
    shift = jnp.sum(jnp.where(is_kind, by_kind[:KINDS, 7:8], 0.0), axis=0, keepdims=True)
    cot = jnp.concatenate([own[5:6] * scale] * TILES, axis=1) * live
    weight = cot * envelope

    root3 = math.sqrt(3.0)
    root15 = math.sqrt(15.0)
    root5 = math.sqrt(5.0)
    ux, uy, uz = unit
    yrow[0:8] = jnp.concatenate(
        [
            root3 * ux,
            root3 * uy,
            root3 * uz,
            root15 * ux * uy,
            root15 * uy * uz,
            0.5 * root5 * (3.0 * uz * uz - 1.0),
            root15 * ux * uz,
            0.5 * root15 * (ux * ux - uy * uy),
        ],
        axis=0,
    )
    yrow[8:16] = yrow[0:8] * (live * env_scale)
    yrow[16:17] = live * env_scale
    geo[0:8] = jnp.concatenate([ux, uy, uz, inverse, envelope, denvelope, live, cot], axis=0)
    geo[8:16] = math.sqrt(2.0 / cutoff_radius) * (
        (math.pi / cutoff_radius)
        * lax.broadcasted_iota(jnp.int32, (BESSEL, ROWS), 0).astype(f32)
        * cosines
        + (math.pi / cutoff_radius) * cosines
        - sines * inverse
    ) * inverse


    def one_hots(t):
        row = lax.broadcasted_iota(jnp.int32, (LANES, LANES), 0).astype(f32)
        here = jnp.where(row == own[3:4] + float(BESSEL), 1.0, 0.0)
        there = jnp.where(row == kinds_near[t] + float(BESSEL + SPECIES), 1.0, 0.0)
        return here + there

    kinds_near = [got[3:4, t * LANES : (t + 1) * LANES] for t in range(TILES)]
    gather_mid.second()
    for part in gather_low:
        part.third()
    gather_high.column()
    for t in range(TILES):
        at = slice(t * LANES, (t + 1) * LANES)
        column = jnp.concatenate([bessel[:, at], one_hots(t)[BESSEL:]], axis=0)
        z_t[:, at] = column.astype(bf16)
        z_r[at, :] = column.T.astype(bf16)
        env_b[at, :] = jnp.broadcast_to(envelope[:, at], (LANES, LANES)).T
        fact[at, :] = jnp.broadcast_to(weight[:, at], (LANES, LANES)).T
    for part in gather_low:
        part.across()


    def twice(x):
        return jnp.concatenate([x] * (STRIP // LANES), axis=1)

    def in_body(n, r):
        pre = nn(z_r[r], cols_panel(first_w, W_INPUT, n))
        hid[r, panel(n, STRIP)] = (pre * sigmoid(pre)).astype(bf16)

    loop_panels(in_body)
    gather_mid.third()
    gather_high.second()
    gather_late.own()
    gather_mid.across()

    def two_body(n, r):
        zero = nn(hid[r], cols_panel(first_w, W_TWO, n)) * twice(env_b[r])
        lat[r, panel(n, STRIP)] = zero
        low0[r, panel(n, STRIP)] = zero.astype(bf16)

    loop_panels(two_body)
    gather_high.third()

    def transposed_product(out, weights, right, width=256):
        at = 0
        while at < ROWS:
            end = min(at + width, ROWS)
            out[:, at:end] = nt(weights, right[at:end, :])
            at = end

    wee_t[0:128, :] = narrow(first_w, W_EMBED).T
    wee_t[128:256, :] = narrow(first_w, W_ENV_ONE).T
    transposed_product(ee_t, wee_t[...], low0)
    gather_late.column()

    def environment(out, v0_ref, v0_at, v1_at):
        for m in range(9):
            total = None
            begin = v0_at if m == 0 else v1_at
            y = yrow[16:17, :] if m == 0 else yrow[7 + m : 8 + m, :]
            for t in range(TILES):
                at = slice(t * LANES, (t + 1) * LANES)
                term = v0_ref[begin : begin + CHANNELS, at] * y[:, at]
                total = term if total is None else total + term
            out[m] = halves(total)

    def put_scalars(t, s_t, rows):
        s_t[:, lanes(t)] = jnp.concatenate(rows, axis=0).astype(bf16)
        filled = jnp.concatenate(rows + [jnp.zeros_like(rows[0])], axis=0)
        flipped = filled.T.astype(bf16)
        s_r[lanes(t), :] = flipped

    def weighted(y, first, count, source, offset):
        total = None
        for m in range(count):
            term = y[first + m : first + m + 1] * source[offset + m]
            total = term if total is None else total + term
        return total

    environment(gam, ee_t, 128, 192)

    def scalars_one(t):
        e0 = ee_t[0:64, lanes(t)]
        e1 = ee_t[64:128, lanes(t)]
        y = yrow[0:8, lanes(t)]
        put_scalars(
            t,
            s1_t,
            [e0 * gam[0], e1 * weighted(y, 0, 3, gam, 1), e1 * weighted(y, 3, 5, gam, 4)],
        )

    beside(6, lambda i: None, scalars_one)
    gather_high.across()

    def pre_one(n, r):
        pre = nn(low0[r], cols_panel(first_w, W_LAT_ONE, n)) + nn(
            s_r[r, : 3 * CHANNELS], cols_panel(first_w, W_SCAL_ONE, n)
        )
        sig = sigmoid(pre)
        act = pre * sig
        act1[r, panel(n, STRIP)] = act.astype(bf16)
        sl1[r, panel(n, STRIP)] = (sig + act * (1.0 - sig)).astype(bf16)

    loop_panels(pre_one)
    gather_late.second()

    def out_one(n, r):
        new = (lat[r, panel(n, STRIP)] + nn(act1[r], cols_panel(first_w, W_OUT_ONE, n))) * half_root
        lat[r, panel(n, STRIP)] = new
        low1[r, panel(n, STRIP)] = new.astype(bf16)

    loop_panels(out_one)
    gather_late.third()
    we2_t[...] = narrow(first_w, W_ENV_TWO).T
    transposed_product(en2_t, we2_t[...], low1)
    environment(dlt, en2_t, 0, 64)

    g0 = gam[0]
    coef[0] = g0 * dlt[0]
    for m in range(3):
        a, b = 1 + (m + 1) % 3, 1 + (m + 2) % 3
        coef[1 + m] = g0 * dlt[1 + m] + (gam[a] * dlt[b] - gam[b] * dlt[a])
    coef[9] = gam[1] * dlt[1] + gam[2] * dlt[2] + gam[3] * dlt[3]
    second = None
    for m in range(4, 9):
        coef[m] = g0 * dlt[m]
        term = gam[m] * dlt[m]
        second = term if second is None else second + term
    coef[10] = second

    def scalars_two(t):
        e0 = ee_t[0:64, lanes(t)]
        e1 = ee_t[64:128, lanes(t)]
        y = yrow[0:8, lanes(t)]
        put_scalars(
            t,
            s2_t,
            [
                e0 * coef[0],
                e1 * weighted(y, 0, 3, coef, 1) + e0 * coef[9],
                e1 * weighted(y, 3, 5, coef, 4) + e0 * coef[10],
            ],
        )

    beside(6, lambda i: None, scalars_two)
    gather_late.across()

    for part in gather_low + [gather_mid, gather_high, gather_late]:
        part.finish()
    def pre_two(n, r):
        pre = nn(low1[r], cols_panel(late_w, W_LAT_TWO, n)) + nn(
            s_r[r, : 3 * CHANNELS], cols_panel(first_w, W_SCAL_TWO, n)
        )
        sig = sigmoid(pre)
        act = pre * sig
        act2[r, panel(n, STRIP)] = act.astype(bf16)
        sl2[r, panel(n, STRIP)] = (sig + act * (1.0 - sig)).astype(bf16)

    loop_panels(pre_two)

    def out_two(n, r):
        new = (lat[r, panel(n, STRIP)] + nn(act2[r], cols_panel(late_w, W_OUT_TWO, n))) * half_root
        low2[r, panel(n, STRIP)] = new.astype(bf16)

    loop_panels(out_two)

    vec = jnp.broadcast_to(pack_ref[8:9], (8, LANES))
    stage[...] = narrow(first_w, W_FINAL)

    def read_out(i):
        r = pl.ds(pl.multiple_of(i * 416, 16), 416)
        pre = nn(low2[r, :], stage[...])
        sig = sigmoid(pre)
        final_act = pre * sig
        dpf[r, :] = (fact[r, :] * vec[0:1] * (sig + final_act * (1.0 - sig))).astype(bf16)
        fact[r, :] = final_act

    loop(4, read_out)
    value = nt(vec, fact[...], highest)[0:1]
    geo_live = geo[6:7]
    geo_env = geo[4:5]
    geo_cot = geo[7:8]
    edge_energy = geo_live * geo_env * value
    summed = None
    for t in range(TILES):
        term = edge_energy[:, t * LANES : (t + 1) * LANES]
        summed = term if summed is None else summed + term
    energy_ref[...] = scale * halves(summed) + shift
    all_weights = jnp.broadcast_to(geo_cot * geo_env, (8, ROWS))
    sum_vector.send(0, nn(all_weights, fact[...], highest))
    geo[16:17] = geo_cot * value

    def big_step(out, where, left, right):
        def step(i):
            grad = tn(left[:, panel(i, STRIP)], right[...])
            out[pl.ds(pl.multiple_of(where[0] + i * STRIP, 64), STRIP), :] = grad.astype(bf16)

        return step

    def big_grad(out, where, left, right):
        loop(LATENT // STRIP, big_step(out, where, left, right))

    def wide_step(out, where, left, right):
        def step(n):
            out[where[0] : where[0] + where[1], panel(n)] = nn(
                left[...], right[:, panel(n)]
            ).astype(bf16)

        return step

    def wide_grad(out, where, left, right):
        loop(4, wide_step(out, where, left, right))

    def narrow_grad(left, right, put):
        def step(n):
            put(n, nn(left, right[:, panel(n)]).T.astype(bf16))

        loop(4, step)

    def put_narrow(where, n, grad):
        row = pl.multiple_of(where[0] + n // 2 * BLOCK_ROWS, BLOCK_ROWS)
        col = pl.multiple_of(n % 2 * 512, 512)
        first_w[pl.ds(row, BLOCK_ROWS), pl.ds(col, 512)] = jnp.concatenate(
            [grad[b * BLOCK_ROWS : (b + 1) * BLOCK_ROWS] for b in range(4)], axis=1
        )

    def put_stage(n, grad):
        stage[panel(n), :] = grad

    def back_final(n, r):
        grad = nt(dpf[r], narrow_panel(first_w, W_FINAL, n)) * half_root
        lat[r, panel(n, STRIP)] = grad
        low2[r, panel(n, STRIP)] = grad.astype(bf16)

    def back_out_two(n, r):
        grad = nt(low2[r], rows_panel(late_w, W_OUT_TWO, n))
        sl2[r, panel(n, STRIP)] = (grad * sl2[r, panel(n, STRIP)].astype(f32)).astype(bf16)

    def tensors_two(t):
        e0 = ee_t[0:64, lanes(t)]
        e1 = ee_t[64:128, lanes(t)]
        y = yrow[0:8, lanes(t)]
        r0 = ds_t[0:64, lanes(t)]
        r1 = ds_t[64:128, lanes(t)]
        r2 = ds_t[128:192, lanes(t)]
        de_t[0:64, lanes(t)] = r0 * coef[0] + r1 * coef[9] + r2 * coef[10]
        de_t[64:128, lanes(t)] = r1 * weighted(y, 0, 3, coef, 1) + r2 * weighted(y, 3, 5, coef, 4)
        p1 = r1 * e1
        p2 = r2 * e1
        rows = []
        for m in range(8):
            p = p1 if m < 3 else p2
            rows.append(jnp.sum(p * coef[1 + m], axis=0, keepdims=True))
            dg[1 + m] += p * y[m : m + 1]
        dy[:, lanes(t)] = jnp.concatenate(rows, axis=0)
        dg[0] += r0 * e0
        dg[9] += r1 * e0
        dg[10] += r2 * e0

    def environment_back(t, grads, source, v1_at, at):
        y4 = yrow[8:16, lanes(t)]
        l4 = yrow[16:17, lanes(t)]
        v1 = source[v1_at : v1_at + 64, lanes(t)]
        low = l4 * grads[0]
        high = weighted(y4, 0, 8, grads, 1)
        both = jnp.concatenate([low, high], axis=0)
        dw_t[at : at + 128, lanes(t)] = both.astype(bf16)
        dw_r[lanes(t), at : at + 128] = both.T.astype(bf16)
        v1 = v1 * l4
        rows = [jnp.sum(v1 * grads[1 + m], axis=0, keepdims=True) for m in range(8)]
        dy[:, lanes(t)] += jnp.concatenate(rows, axis=0)

    def back_lat_two(n, r):
        grad = (
            lat[r, panel(n, STRIP)]
            + nt(sl2[r], rows_panel(late_w, W_LAT_TWO, n))
            + nt(dw_r[r, 128:256], narrow_panel(first_w, W_ENV_TWO, n))
        ) * half_root
        lat[r, panel(n, STRIP)] = grad
        act2[r, panel(n, STRIP)] = grad.astype(bf16)

    def back_out_one(n, r):
        grad = nt(act2[r], rows_panel(first_w, W_OUT_ONE, n))
        sl1[r, panel(n, STRIP)] = (grad * sl1[r, panel(n, STRIP)].astype(f32)).astype(bf16)

    def tensors_one(t):
        e0 = ee_t[0:64, lanes(t)]
        e1 = ee_t[64:128, lanes(t)]
        y = yrow[0:8, lanes(t)]
        r0 = ds_t[0:64, lanes(t)]
        r1 = ds_t[64:128, lanes(t)]
        r2 = ds_t[128:192, lanes(t)]
        low = de_t[0:64, lanes(t)] + r0 * gam[0]
        high = (
            de_t[64:128, lanes(t)]
            + r1 * weighted(y, 0, 3, gam, 1)
            + r2 * weighted(y, 3, 5, gam, 4)
        )
        both = jnp.concatenate([low, high], axis=0)
        dw_t[0:128, lanes(t)] = both.astype(bf16)
        dw_r[lanes(t), 0:128] = both.T.astype(bf16)
        p1 = r1 * e1
        p2 = r2 * e1
        rows = []
        for m in range(8):
            p = p1 if m < 3 else p2
            rows.append(jnp.sum(p * gam[1 + m], axis=0, keepdims=True))
            coef[1 + m] += p * y[m : m + 1]
        dy[:, lanes(t)] += jnp.concatenate(rows, axis=0)
        coef[0] += r0 * e0

    def back_lat_one(n, r):
        both = jnp.concatenate(
            [narrow_panel(first_w, W_EMBED, n), narrow_panel(first_w, W_ENV_ONE, n)], axis=1
        )
        grad = (
            lat[r, panel(n, STRIP)]
            + nt(sl1[r], rows_panel(first_w, W_LAT_ONE, n))
            + nt(dw_r[r], both)
        )
        low1[r, panel(n, STRIP)] = (grad * twice(env_b[r])).astype(bf16)
        part = grad * low0[r, panel(n, STRIP)].astype(f32)
        for b in range(STRIP // LANES):
            den[r] += part[:, b * LANES : (b + 1) * LANES]

    def back_two(n, r):
        grad = nt(low1[r], rows_panel(first_w, W_TWO, n))
        pre = nn(z_r[r], cols_panel(first_w, W_INPUT, n))
        sig = sigmoid(pre)
        act1[r, panel(n, STRIP)] = (grad * (sig + pre * sig * (1.0 - sig))).astype(bf16)

    def lat_one_grad(low, high):
        grad = tn(low0[:, low:high], sl1[...])
        first_w[W_LAT_ONE[0] + low : W_LAT_ONE[0] + high, :] = grad.astype(bf16)

    narrow_grad(dpf[...].T, low2, put_stage)
    loop_panels(back_final)
    loop(4, lambda n: put_narrow(W_FINAL, n, stage[panel(n), :]))
    loop_panels(back_out_two)
    transposed_product(ds_t, first_w[W_SCAL_TWO[0] : W_SCAL_TWO[0] + W_SCAL_TWO[1], :], sl2)
    dg[...] = jnp.zeros_like(dg)
    beside(2, big_step(late_w, W_OUT_TWO, act2, low2), tensors_two)
    sum_vector.pass_on(0)
    sum_out.stage(0)
    total = [halves(dg[m]) for m in range(11)]
    g0 = gam[0]
    d0 = dlt[0]
    new_g0 = total[0] * d0
    for m in range(1, 9):
        new_g0 = new_g0 + total[m] * dlt[m]
    dlt_grads = [total[0] * g0]
    gam_grads = [new_g0]
    for m in range(3):
        a, b = 1 + (m + 1) % 3, 1 + (m + 2) % 3
        dlt_grads.append(
            total[1 + m] * g0 + total[9] * gam[1 + m] + (total[a] * gam[b] - total[b] * gam[a])
        )
        gam_grads.append(total[9] * dlt[1 + m] + (dlt[a] * total[b] - dlt[b] * total[a]))
    for m in range(4, 9):
        dlt_grads.append(total[m] * g0 + total[10] * gam[m])
        gam_grads.append(total[10] * dlt[m])
    for m in range(9):
        dlt[m] = dlt_grads[m]
        dg[m] = gam_grads[m]
    beside(
        4,
        wide_step(first_w, W_SCAL_TWO, s2_t, sl2),
        lambda t: environment_back(t, dlt, en2_t, 64, 128),
    )
    sum_out.stage(1)
    loop_panels(back_lat_two)
    sum_out.stage(2)
    big_grad(late_w, W_LAT_TWO, low1, sl2)
    sum_vector.pass_on(1)
    sum_out.stage(3)
    sum_lat.stage(0)
    loop_panels(back_out_one)
    sum_out.stage(4)
    sum_lat.stage(1)
    transposed_product(ds_t, first_w[W_SCAL_ONE[0] : W_SCAL_ONE[0] + W_SCAL_ONE[1], :], sl1)
    narrow_grad(dw_t[128:256, :], low1, functools.partial(put_narrow, W_ENV_TWO))
    for m in range(9):
        coef[m] = jnp.zeros((CHANNELS, LANES), f32)
    beside(2, big_step(first_w, W_OUT_ONE, act1, act2), tensors_one)
    sum_vector.pass_on(2)
    sum_out.stage(5)
    sum_lat.stage(2)
    advance(3, 0)
    for m in range(9):
        dg[m] = dg[m] + halves(coef[m])
    beside(
        4,
        wide_step(first_w, W_SCAL_ONE, s1_t, sl1),
        lambda t: environment_back(t, dg, ee_t, 192, 128),
    )
    advance(3, 1)
    sum_out.stage(6)
    sum_lat.stage(3)
    den[...] = jnp.zeros_like(den)
    loop_panels(back_lat_one)
    lat_one_grad(640, 1024)
    sum_lat.stage(4)
    advance(3, 2)
    advance(2, 0)
    loop_panels(back_two)
    sum_lat.stage(5)
    advance(3, 3)
    advance(2, 1)
    big_grad(first_w, W_TWO, hid, low1)
    transposed_product(ds_t.at[0:64], first_w[0:64, :], act1)
    wide_grad(first_w, W_INPUT, z_t, act1)
    advance(0, 0)
    advance(2, 2)
    narrow_grad(dw_t[0:128, :], low0, functools.partial(put_narrow, W_EMBED))
    narrow_grad(dw_t[128:256, :], low0, functools.partial(put_narrow, W_ENV_ONE))
    advance(3, 4)
    advance(0, 1)
    dbessel = ds_t[0:8, :]
    through = nt(jnp.ones((8, LANES), f32), den[...], highest)[0:1]
    ux, uy, uz = geo[0:1], geo[1:2], geo[2:3]
    inverse = geo[3:4]
    envelope = geo[4:5]
    denv = geo[16:17] + through / envelope
    dlength = jnp.sum(dbessel * geo[8:16], axis=0, keepdims=True) + denv * geo[5:6]
    g = [dy[m : m + 1, :] for m in range(8)]
    dux = root3 * g[0] + root15 * (uy * g[3] + uz * g[6] + ux * g[7])
    duy = root3 * g[1] + root15 * (ux * g[3] + uz * g[4] - uy * g[7])
    duz = root3 * g[2] + root15 * (uy * g[4] + ux * g[6]) + (3.0 * root5) * uz * g[5]
    along = dlength - (ux * dux + uy * duy + uz * duz) * inverse
    near = jnp.concatenate(
        [
            dux * inverse + ux * along,
            duy * inverse + uy * along,
            duz * inverse + uz * along,
            jnp.zeros((5, ROWS), f32),
        ],
        axis=0,
    )
    summed = None
    for t in range(TILES):
        term = near[:, t * LANES : (t + 1) * LANES]
        summed = term if summed is None else summed + term
    centre = halves(summed)
    na, nb, nc = parts(near)
    spread = nt(na, hot[...]) + nt(nb, hot[...]) + nt(nc, hot[...])
    sides[0] = spread[:, :LANES]
    sides[1, :, 0:PLANE] = spread[:, LANES:]
    link_force.start(sides.at[0], sides.at[1])
    lat_one_grad(0, 384)
    lat_one_grad(384, 640)
    advance(1, 0)
    advance(3, 5)
    advance(2, 3)
    sum_lat.stage(6)
    advance(0, 2)
    advance(1, 1)
    advance(2, 4)
    advance(0, 3)
    advance(3, 6)
    advance(0, 4)
    for step in range(6):
        for k in range(max(SUM_PIECES[:3])):
            for z, after in ((0, 5), (1, 2), (2, 5)):
                if k < SUM_PIECES[z] and after <= after + step - k < 7:
                    sum_first[z][k].stage(after + step - k)
    link_force.wait(sides.at[0], sides.at[1])
    forces_ref[...] = (
        centre - pltpu.roll(sides[0], PLANE, 1) - force_in[1] - force_in[0]
    )
    total = sum_vector.pass_on(3)
    normed = total * lax.rsqrt(jnp.sum(total[0:1] * total[0:1]) * (1.0 / FINAL) + epsilon)
    state = decay_rate * pack_ref[9:10] + (1.0 - decay_rate) * normed * normed
    vector_ref[0:1] = total[0:1]
    vector_ref[1:2] = state[0:1]
    vector_ref[2:3] = (pack_ref[8:9] - vector_rate * normed * lax.rsqrt(state + epsilon))[0:1]
    first_out[...] = first_units.get(me)
    late_out[...] = late_units.get(me)
    for group in sum((list(parts) for parts in sum_first), [sum_out, sum_lat, sum_vector]):
        group.finish()
    link_halo.finish(own_at, own_at)
    link_force.finish(sides.at[0], sides.at[1])


def run_network(devices, small, blocks, late):
    S = jax.ShapeDtypeStruct
    wide = pltpu.VMEM((ROWS, LATENT), bf16)
    slab = pltpu.VMEM((ROWS, LANES), f32)
    panels = lambda amount: pltpu.VMEM((amount * devices // PANEL * BLOCK_ROWS, WIDE), bf16)
    scratch = [
        panels(blocks.shape[0]),
        panels(late.shape[0]),
        pltpu.VMEM((3 * PLANE, ROWS), bf16),
        pltpu.VMEM((LANES, ROWS), bf16),
        pltpu.VMEM((ROWS, LANES), bf16),
        pltpu.VMEM((24, ROWS), f32),
        pltpu.VMEM((24, ROWS), f32),
        slab,
        pltpu.VMEM((256, ROWS), f32),
        pltpu.VMEM((128, ROWS), f32),
        pltpu.VMEM((192, ROWS), bf16),
        pltpu.VMEM((192, ROWS), bf16),
        pltpu.VMEM((9, CHANNELS, LANES), f32),
        pltpu.VMEM((9, CHANNELS, LANES), f32),
        pltpu.VMEM((11, CHANNELS, LANES), f32),
        pltpu.VMEM((192, ROWS), f32),
        pltpu.VMEM((128, ROWS), f32),
        pltpu.VMEM((8, ROWS), f32),
        pltpu.VMEM((11, CHANNELS, LANES), f32),
        pltpu.VMEM((256, ROWS), bf16),
        pltpu.VMEM((ROWS, 256), bf16),
        pltpu.VMEM((ROWS, LANES), bf16),
        slab,
        pltpu.VMEM((ROWS, LATENT), f32),
    ] + [wide] * 8 + [
        pltpu.VMEM((LATENT, LANES), bf16),
        pltpu.VMEM((2, 8, LANES), f32),
        pltpu.VMEM((2, 8, LANES), f32),
        pltpu.VMEM((2, 8, LANES), f32),
        pltpu.VMEM((Total.slots(devices), 8, LANES), f32),
        pltpu.VMEM((16, LANES), f32),
        pltpu.SemaphoreType.DMA((PIECES, Gather.amount(devices, 1))),
        pltpu.SemaphoreType.DMA((Gather.amount(devices, 1),)),
        pltpu.SemaphoreType.DMA((Gather.amount(devices, 2),)),
        pltpu.SemaphoreType.DMA((Gather.amount(devices, 4),)),
        pltpu.SemaphoreType.DMA((2, Reduce.amount(devices, 2))),
        pltpu.SemaphoreType.DMA((4 * PIECES, Reduce.amount(devices, 1))),
        pltpu.SemaphoreType.DMA((2, 4)),
        pltpu.SemaphoreType.DMA((2 * Total.slots(devices),)),
        pltpu.SemaphoreType.REGULAR((6, 7)),
    ]
    vmem = pl.BlockSpec(memory_space=pltpu.VMEM)
    return pl.pallas_call(
        network,
        out_shape=[
            S((1, LANES), f32),
            S((8, LANES), f32),
            S((8, LANES), f32),
            S(unit_shape(blocks.shape[0]), bf16),
            S(unit_shape(late.shape[0]), bf16),
        ],
        in_specs=[vmem] * (len(small) + 2),
        out_specs=[vmem] * 5,
        scratch_shapes=scratch,
        compiler_params=pltpu.CompilerParams(
            vmem_limit_bytes=63 << 20, collective_id=0, has_side_effects=True
        ),
        name="network",
    )(*small, blocks, late)


def shampoo(
    energy,
    force,
    vectors,
    grads,
    left,
    right,
    left_root,
    right_root,
    master,
    late_grads,
    late_left,
    late_right,
    late_left_root,
    late_right_root,
    late_master,
    energy_out,
    force_out,
    vector_out,
    state_out,
    moved_out,
    *outs,
):
    energy_out[...] = energy[:, :PLANE]
    force_out[...] = force[0:3, :PLANE]
    vector_out[...] = vectors[0:1]
    state_out[...] = vectors[1:2]
    moved_out[...] = vectors[2:3]

    todo = []
    for j in range(left.shape[0]):
        todo.append((grads, j, left, right, left_root, right_root, master) + outs[:4])
    for j in range(late_left.shape[0]):
        todo.append(
            (late_grads, j, late_left, late_right, late_left_root, late_right_root, late_master)
            + outs[4:]
        )
    size = 1.0 / (BLOCK_ROWS * BLOCK_COLS)
    held, scales, steps = [], [], []
    for panels, j, left, *_ in todo:
        per = panels.shape[1] // BLOCK_COLS
        at = pl.program_id(0) * left.shape[0] + j
        row = pl.multiple_of(at // per * BLOCK_ROWS, BLOCK_ROWS)
        col = pl.multiple_of(at % per * BLOCK_COLS, BLOCK_COLS)
        held.append(panels[pl.ds(row, BLOCK_ROWS), pl.ds(col, BLOCK_COLS)])
    for g, (_, j, *_, grad_out, left_out, right_out, master_out) in zip(held, todo):
        grad = g.astype(f32)
        grad_out[j] = grad
        scales.append(lax.rsqrt(jnp.sum(grad * grad, keepdims=True) * size + epsilon))
    turned = []
    for g, (_, j, left, right, left_root, *_) in zip(held, todo):
        la, lb, _ = parts(left_root[j])
        turned.append(nn(la, g) + nn(lb, g))
    for g, s, (_, j, left, right, *_, grad_out, left_out, right_out, master_out) in zip(
        held, scales, todo
    ):
        square = (1.0 - decay_rate) * s * s
        left_out[j] = decay_rate * left[j] + square * nt(g, g)
        right_out[j] = decay_rate * right[j] + square * tn(g, g)
    for turn, s, (_, j, left, right, left_root, right_root, *_) in zip(turned, scales, todo):
        ra, rb, _ = parts(right_root[j])
        ta, tb, _ = parts(turn * s)
        steps.append(nn(ta, ra) + (nn(ta, rb) + nn(tb, ra)))
    for step, (_, j, left, right, left_root, right_root, master, *_, master_out) in zip(steps, todo):
        slope = lax.rsqrt(jnp.sum(step * step, keepdims=True) * size + epsilon)
        master_out[j] = master[j] - (learn_rate * slope) * step


def run_shampoo(energy, force, vectors, first, late):
    S = jax.ShapeDtypeStruct
    steps = min(2, late[1].shape[0])

    def whole(x):
        return pl.BlockSpec(x.shape, lambda i: (0,) * len(x.shape))

    def share(x):
        return pl.BlockSpec((x.shape[0] // steps,) + x.shape[1:], lambda i: (i, 0, 0))

    small = [S((1, PLANE), f32), S((3, PLANE), f32)] + [S((1, FINAL), f32)] * 3
    grown = []
    for group in (first, late):
        left, right, _, _, master = group[1:]
        grown += [S(x.shape, f32) for x in (master, left, right, master)]
    return pl.pallas_call(
        shampoo,
        grid=(steps,),
        out_shape=small + grown,
        in_specs=[whole(energy), whole(force), whole(vectors)]
        + [whole(first[0])]
        + [share(x) for x in first[1:]]
        + [whole(late[0])]
        + [share(x) for x in late[1:]],
        out_specs=[whole(x) for x in small] + [share(x) for x in grown],
        compiler_params=pltpu.CompilerParams(vmem_limit_bytes=60 << 20),
        name="shampoo",
    )(energy, force, vectors, *first, *late)


def local(
    positions,
    species,
    neighbours,
    counts,
    species_scale,
    species_shift,
    energy_cot,
    blocks,
    left,
    right,
    left_root,
    right_root,
    late_blocks,
    late_left,
    late_right,
    late_left_root,
    late_right_root,
    out_vector,
    vector_state,
):
    devices = lax.axis_size("atoms")
    small = (
        neighbours.reshape(PLANE, SLOTS),
        positions,
        species[None],
        counts[None],
        energy_cot[None],
        species_scale[None],
        species_shift[None],
        out_vector[None],
        vector_state[None],
    )
    energy, force, vectors, first_units, late_units = run_network(
        devices, small, blocks, late_blocks
    )
    out = run_shampoo(
        energy,
        force,
        vectors,
        (first_units, left, right, left_root, right_root, blocks),
        (late_units, late_left, late_right, late_left_root, late_right_root, late_blocks),
    )
    energies, forces, vector_grad, new_state, new_vector = out[:5]
    return (
        energies.reshape(-1),
        forces,
        *out[5:],
        vector_grad.reshape(-1),
        new_state.reshape(-1),
        new_vector.reshape(-1),
    )


def solution(mesh):
    row = P("atoms")
    block = P("atoms", None, None)
    placed = (
        (P(None, "atoms"), row, row, row, P(), P(), row)
        + (block,) * 10
        + (P(), P())
    )
    return jax.shard_map(
        local,
        mesh=mesh,
        in_specs=placed,
        out_specs=(row, P(None, "atoms")) + (block,) * 8 + (P(), P(), P()),
        check_vma=False,
    )
```

```python
import functools
import math

import jax
import jax.numpy as jnp
from jax import lax
from jax.experimental import pallas as pl
from jax.experimental.pallas import tpu as pltpu
from jax.sharding import PartitionSpec as P

SIDE = 8
SLOTS = 26
SPECIES = 60
BESSEL = 8
CHANNELS = 64
LATENT = 1024
FINAL = 128
BLOCK_ROWS = 64
BLOCK_COLS = 128
PLANE = SIDE * SIDE

f32 = jnp.float32
bf16 = jnp.bfloat16
highest = lax.Precision.HIGHEST
spacing = 1.6
cutoff_radius = 4.0
env_scale = 0.25
half_root = 0.7071067811865476
decay_rate = 0.5
learn_rate = 0.02
vector_rate = 0.03
epsilon = 1e-06

LANES = 128
ROWS = SLOTS * PLANE
TILES = ROWS // LANES
KINDS = 64

PANEL = 8
WIDE = PANEL * BLOCK_COLS
W_INPUT = (0, 128)
W_TWO = (128, 1024)
W_EMBED = (1152, 128)
W_ENV_ONE = (1280, 128)
W_LAT_ONE = (1408, 1024)
W_SCAL_ONE = (2432, 192)
W_OUT_ONE = (2624, 1024)
W_ENV_TWO = (3648, 128)
W_SCAL_TWO = (3776, 192)
W_FINAL = (3968, 128)
W_LAT_TWO = (0, 1024)
W_OUT_TWO = (1024, 1024)

MESH = pl.DeviceIdType.MESH


def nn(a, b, precision=None):
    return lax.dot_general(
        a, b, (((1,), (0,)), ((), ())), preferred_element_type=f32, precision=precision
    )


def nt(a, b, precision=None):
    return lax.dot_general(
        a, b, (((1,), (1,)), ((), ())), preferred_element_type=f32, precision=precision
    )


def tn(a, b):
    return lax.dot_general(a, b, (((0,), (0,)), ((), ())), preferred_element_type=f32)


def cols_panel(ref, where, n):
    return ref[where[0] : where[0] + where[1], panel(n, STRIP)]


def rows_panel(ref, where, n):
    return ref[pl.ds(pl.multiple_of(where[0] + n * STRIP, 64), STRIP), :]


def narrow(ref, where):
    pieces = []
    for j in range(LATENT // BLOCK_ROWS):
        row = where[0] + j // PANEL * BLOCK_ROWS
        col = j % PANEL * BLOCK_COLS
        pieces.append(ref[row : row + BLOCK_ROWS, col : col + BLOCK_COLS])
    return jnp.concatenate(pieces, axis=0)


def narrow_panel(ref, where, n):
    part = ref[pl.ds(pl.multiple_of(where[0] + n * BLOCK_ROWS, BLOCK_ROWS), BLOCK_ROWS), :]
    return jnp.concatenate([part[:, b * 128 : (b + 1) * 128] for b in range(PANEL)], axis=0)


def sigmoid(x):
    return 0.5 * jnp.tanh(0.5 * x) + 0.5


def halves(x):
    return x + pltpu.roll(x, PLANE, 1)


def lanes(t):
    if isinstance(t, int):
        return pl.ds(t * LANES, LANES)
    return pl.ds(pl.multiple_of(t * LANES, LANES), LANES)


def panel(n, width=256):
    return pl.ds(pl.multiple_of(n * width, width), width)


STRIP = 512
CHUNKS = 4
PIECES = 2
SUM_PIECES = (2, 2, 1, 1)
CHUNK = ROWS // CHUNKS


def loop_panels(body):
    def step(n):
        for c in range(CHUNKS):
            body(n, slice(c * CHUNK, (c + 1) * CHUNK))

    loop(LATENT // STRIP, step)


def beside(count, step, tile):
    share = TILES // count

    def body(i):
        step(i)
        for u in range(share):
            tile(i * share + u)

    loop(count, body)
    for t in range(share * count, TILES):
        tile(t)


def loop(count, body):
    def step(i, carry):
        body(i)
        return carry

    lax.fori_loop(0, count, step, 0)


def parts(x):
    a = x.astype(bf16)
    rest = x - a.astype(f32)
    b = rest.astype(bf16)
    c = (rest - b.astype(f32)).astype(bf16)
    return a, b, c


class Place:
    def __init__(self, devices):
        side = math.isqrt(devices // 8)
        self.devices = devices
        self.sizes = (4, side, side)
        me = lax.axis_index("atoms")
        core = me % 2
        chip = me // 2
        last = chip % side
        middle = chip // side % side
        self.me = me
        self.core = core
        self.pos = (
            chip // (side * side),
            last + core * (middle - last),
            middle + core * (last - middle),
        )
        self.half = (side * side, 1 + core * (side - 1), side + core * (1 - side))
        self.step = tuple(2 * h for h in self.half)
        self.sibling = me + 1 - 2 * core
        self.plain = (self.pos[0], middle, last)
        self.plain_step = (2 * side * side, 2 * side, 2)

    def owner(self, q):
        return q[0] * self.step[0] + q[1] * self.step[1] + q[2] * self.step[2] + self.core

    def near(self, dim, up):
        return self.me + self.step[dim] if up else self.me - self.step[dim]

    def has(self, dim, up):
        return self.pos[dim] < self.sizes[dim] - 1 if up else self.pos[dim] > 0

    def peers(self, dim):
        n, p = self.sizes[dim], self.plain[dim]
        return [(r, (p + r) % n, self.me + ((p + r) % n - p) * self.plain_step[dim]) for r in range(1, n)]


class Units:
    def __init__(self, ref, rows, cols, base=0, part=(0, 1)):
        self.ref, self.rows, self.cols = ref, rows, cols
        self.per = WIDE // cols
        self.base = base
        self.high = rows // part[1]
        self.off = part[0] * self.high

    def window(self, s):
        s = s + self.base
        if self.per == 1:
            row, col = s * self.rows, slice(None)
        else:
            row = s // self.per * self.rows
            col = pl.ds(pl.multiple_of(s % self.per * self.cols, self.cols), self.cols)
        return (pl.ds(pl.multiple_of(row + self.off, 16), self.high), col)

    def at(self, s):
        return self.ref.at[self.window(s)]

    def get(self, s):
        return self.ref[self.window(s)]

    def put(self, s, value):
        self.ref[self.window(s)] = value

    def stretch(self, count):
        return self.ref.at[pl.ds(0, count * self.high // self.per), slice(None)]


def remote(src, dst, send, recv, device):
    return pltpu.make_async_remote_copy(
        src_ref=src,
        dst_ref=dst,
        send_sem=send,
        recv_sem=recv,
        device_id=(device,),
        device_id_type=MESH,
    )


def signal(sem, device):
    pl.semaphore_signal(sem, inc=1, device_id=(device,), device_id_type=MESH)


def others(place, dim):
    n, p = place.sizes[dim], place.pos[dim]
    if n == 2:
        return [(1 - p, None)]
    found = []
    for distance in range(1, n):
        found.append((p - distance, p >= distance))
        found.append((p + distance, p < n - distance))
    return found


def gated(cond, body):
    if cond is None:
        body()
    else:
        pl.when(cond)(body)


def both(a, b):
    return b if a is None else (a if b is None else a & b)


class Gather:
    def __init__(self, place, units, lo, hi, sems, direct=False, eager=True):
        self.place, self.units, self.lo, self.hi, self.sems = place, units, lo, hi, sems
        self.direct, self.eager = direct, eager
        _, na, nb = place.sizes
        self.waits = []
        self.shared = 0
        self.first_owner = 2 * lo * na * nb
        at = 2 * (hi - lo) * na * nb
        self.shared_send, self.core_recv = at, at + 1
        at += 2
        self.base = []
        for dim in range(3):
            length = (hi - lo) * (1, na, na * nb)[dim]
            self.base.append((at, at + length))
            at += 2 * length
        self.core_base = at

    @staticmethod
    def amount(devices, share):
        side = math.isqrt(devices // 8)
        return 2 + share * (2 + 2 * side + 5 * side * side)

    def linear(self, q, dim):
        _, na, nb = self.place.sizes
        q0 = q[0] - self.lo
        return (q0, q0 * na + q[1], (q0 * na + q[1]) * nb + q[2])[dim]

    def emit(self, cond, q, sem, device, core=False, once=None):
        owner = self.place.owner(q)
        common = cond is None or once is not None
        if common:
            sem = self.shared_send
            self.shared += 1 if once is None else once

        def copy():
            piece = self.units.at(owner)
            recv = self.core_recv if core else owner - self.first_owner
            return remote(piece, piece, self.sems.at[sem], self.sems.at[recv], device)

        gated(cond, lambda: copy().start())
        if not common:
            self.waits.append(lambda: gated(cond, lambda: copy().wait_send()))

    def onward(self, cond, q):
        place, p = self.place, self.place.pos[0]
        for up in (True, False):
            away = (p >= q[0]) if up else (p <= q[0])
            self.emit(
                both(cond, away & place.has(0, up)),
                q,
                self.base[0][0 if up else 1] + self.linear(q, 0),
                place.near(0, up),
            )

    def sideways(self, cond, q, dims, via=None, once=None):
        place = self.place
        for dim in dims:
            if place.sizes[dim] == 2:
                if dim != via:
                    toward = place.me + (1 - 2 * place.pos[dim]) * place.step[dim]
                    self.emit(
                        cond, q, self.base[dim][0] + self.linear(q, dim), toward, False, once
                    )
                continue
            for up in (True, False):
                open_end = place.has(dim, up)
                if dim == via:
                    p = place.pos[dim]
                    open_end = open_end & ((q[dim] < p) if up else (q[dim] > p))
                self.emit(
                    both(cond, open_end),
                    q,
                    self.base[dim][0 if up else 1] + self.linear(q, dim),
                    place.near(dim, up),
                )
        self.emit(cond, q, self.core_base + self.linear(q, 2), place.sibling, True, once)

    def wait(self, cond, q):
        owner = self.place.owner(q)
        piece = self.units.at(owner)
        gated(
            cond,
            lambda: remote(
                piece,
                piece,
                self.sems.at[self.shared_send],
                self.sems.at[owner - self.first_owner],
                self.place.sibling,
            ).wait_recv(),
        )

    def own(self):
        place, p = self.place, self.place.pos
        if self.direct:
            for r in range(1, 4):
                self.emit(None, p, 0, place.me + ((p[0] + r) % 4 - p[0]) * place.step[0])
            self.sideways(None, p, (2, 1))
            return
        for q0 in range(self.lo, self.hi):
            q = (q0, p[1], p[2])
            self.onward(p[0] == q0, q)
            if self.eager:
                self.sideways(p[0] == q0, q, (2, 1), None, 1)

    def column(self):
        p = self.place.pos
        if self.direct:
            for r in range(1, 4):
                q = ((p[0] + r) % 4, p[1], p[2])
                self.wait(None, q)
                self.sideways(None, q, (2, 1))
            return
        for q0 in range(self.lo, self.hi):
            q = (q0, p[1], p[2])
            self.wait(p[0] != q0, q)
            self.onward(p[0] != q0, q)
            if self.eager:
                self.sideways(p[0] != q0, q, (2, 1), None, 0)
            else:
                self.sideways(None, q, (2, 1))

    def second(self):
        for q0 in range(self.lo, self.hi):
            for qa, there in others(self.place, 1):
                q = (q0, qa, self.place.pos[2])
                self.wait(there, q)
                self.sideways(there, q, (2, 1), 1)

    def third(self):
        for qb, there in others(self.place, 2):
            for q0 in range(self.lo, self.hi):
                for qa in range(self.place.sizes[1]):
                    q = (q0, qa, qb)
                    self.wait(there, q)
                    self.sideways(there, q, (2,), 2)

    def across(self):
        _, na, nb = self.place.sizes
        piece = self.units.stretch((self.hi - self.lo) * na * nb)
        remote(
            piece,
            piece,
            self.sems.at[self.shared_send],
            self.sems.at[self.core_recv],
            self.place.sibling,
        ).wait_recv()

    def finish(self):
        for wait in self.waits:
            wait()
        if self.shared:
            piece = self.units.stretch(self.shared)
            remote(
                piece,
                piece,
                self.sems.at[self.shared_send],
                self.sems.at[self.core_recv],
                self.place.sibling,
            ).wait_send()
        self.waits, self.shared = [], 0


def landing(n):
    return 1 if n == 2 else n + 1


class Reduce:
    def __init__(self, place, units, lo, hi, land, sems, ready):
        self.place, self.units, self.lo, self.hi, self.land = place, units, lo, hi, land
        n0, na, nb = place.sizes
        self.count = (hi - lo) * na * nb
        lines = ((1, n0), (hi - lo, na), ((hi - lo) * na, nb))
        z_at = self.count
        b_at = z_at + landing(n0)
        a_at = b_at + lines[2][0] * landing(nb)
        self.land_at = (z_at, a_at, b_at)
        self.sems, self.ready = sems, ready
        self.shared = 0
        at = 4
        self.recv_at, self.up_at, self.down_at = [], [], []
        for units_here, n in lines:
            self.recv_at.append(at)
            at += units_here * landing(n)
            self.up_at.append(at)
            at += units_here * n
            self.down_at.append(at)
            at += units_here * n
        self.waits = []

    @staticmethod
    def slots(devices, share):
        side = math.isqrt(devices // 8)
        return share * side * side + landing(4) + share * (1 + side) * landing(side)

    @staticmethod
    def amount(devices, share):
        side = math.isqrt(devices // 8)
        total = 4
        for units_here, n in ((1, 4), (share, side), (share * side, side)):
            total += units_here * (landing(n) + 2 * n)
        return total

    def stage(self, k):
        if k == 0:
            self.start()
        elif k == 1:
            self.pairs()
        elif k < 4:
            self.along(4 - k)
        else:
            self.hop(0, k - 3, [(None,) + self.place.pos[1:]])

    def unit(self, dim, q):
        na = self.place.sizes[1]
        return (0, q[0] - self.lo, (q[0] - self.lo) * na + q[1])[dim]

    def add(self, owner, slot):
        self.units.put(owner, self.units.get(owner) + self.land.get(slot))

    def start(self):
        place = self.place
        if self.ready is not None:
            signal(self.ready.at[0], place.sibling)
            for dim in range(3):
                for up in (True, False):
                    pl.when(place.has(dim, up))(
                        lambda dim=dim, up=up: signal(
                            self.ready.at[1 + 2 * dim + (1 if up else 0)], place.near(dim, up)
                        )
                    )
            pl.semaphore_wait(self.ready.at[0], 1)
        per = place.sizes[1] * place.sizes[2]

        def copy(j):
            owner = 2 * (self.lo * per + j) + 1 - place.core
            return remote(
                self.units.at(owner), self.land.at(j), self.sems.at[0], self.sems.at[1], place.sibling
            )

        loop(self.count, lambda j: copy(j).start())
        self.shared += self.count

    def allow(self, dim):
        if self.ready is None:
            return
        for up in (True, False):
            pl.when(self.place.has(dim, up))(
                lambda up=up: pl.semaphore_wait(self.ready.at[1 + 2 * dim + (0 if up else 1)], 1)
            )

    def push(self, cond, dim, q, sem, slot, device):
        owner = self.place.owner(q)
        target = self.unit(dim, q) * landing(self.place.sizes[dim]) + slot
        recv = self.recv_at[dim] + target
        if cond is None:
            self.shared += 1
            sem, recv = 0, 1 + dim

        def copy():
            return remote(
                self.units.at(owner),
                self.land.at(self.land_at[dim] + target),
                self.sems.at[sem],
                self.sems.at[recv],
                device,
            )

        gated(cond, lambda: copy().start())
        if cond is not None:
            self.waits.append(lambda: gated(cond, lambda: copy().wait_send()))

    def arrived(self, sem, count):
        piece = self.land.stretch(count)
        remote(
            piece, piece, self.sems.at[0], self.sems.at[sem], self.place.sibling
        ).wait_recv()

    def pull(self, dim, q, slot):
        target = self.unit(dim, q) * landing(self.place.sizes[dim]) + slot
        piece = self.land.at(self.land_at[dim] + target)
        remote(
            piece,
            piece,
            self.sems.at[0],
            self.sems.at[self.recv_at[dim] + target],
            self.place.sibling,
        ).wait_recv()
        self.add(self.place.owner(q), self.land_at[dim] + target)

    def first(self, dim, q):
        place = self.place
        n, p = place.sizes[dim], place.pos[dim]
        u = self.unit(dim, q)
        if n == 2:
            toward = place.me + (1 - 2 * p) * place.step[dim]
            self.push(None, dim, q, self.up_at[dim] + u * n, 0, toward)
            return
        for up in (True, False):
            away = (q[dim] > 0) if up else (q[dim] < n - 1)
            self.push(
                (p == (0 if up else n - 1)) & away,
                dim,
                q,
                (self.up_at if up else self.down_at)[dim] + u * n + q[dim],
                self.slot_up(q[dim], 0) if up else self.slot_down(n, q[dim], n - 1),
                place.near(dim, up),
            )

    @staticmethod
    def slot_up(q, p):
        return q - (p + 1)

    @staticmethod
    def slot_down(n, q, p):
        to = p - 1
        return q + (n - to if to > 0 else 0)

    def order(self, dim):
        place = self.place
        if place.sizes[dim] == 2:
            return [1 - place.pos[dim], place.pos[dim]]
        return list(range(place.sizes[dim]))

    def mine(self, dim, at):
        return at is self.place.pos[dim]

    def pairs(self):
        place = self.place
        self.allow(2)
        self.arrived(1, self.count)
        for qb in self.order(2):
            for qa in self.order(1):
                for q0 in range(self.lo, self.hi):
                    q = (q0, qa, qb)
                    j = (q0 - self.lo) * place.half[0] + qa * place.half[1] + qb * place.half[2]
                    self.add(place.owner(q), j)
                    if not self.mine(2, qb):
                        self.first(2, q)

    def along(self, dim):
        place = self.place
        n, p = place.sizes[dim], place.pos[dim]
        self.allow(dim - 1)
        if dim == 2:
            rows = [(q0, qa) for qa in self.order(1) for q0 in range(self.lo, self.hi)]
        else:
            rows = [(q0,) for q0 in range(self.lo, self.hi)]

        def whole(row, at):
            return row + (at,) + place.pos[dim + 1 :]

        if n == 2:
            self.arrived(1 + dim, len(rows))
            for row in rows:
                q = whole(row, p)
                self.add(place.owner(q), self.land_at[dim] + self.unit(dim, q))
                if not self.mine(dim - 1, row[dim - 1]):
                    self.first(dim - 1, whole(row, p))
        else:
            for k in range(1, n):
                self.hop(dim, k, [whole(row, None) for row in rows])
            for row in rows:
                self.first(dim - 1, whole(row, p))

    def hop(self, dim, k, rows):
        place = self.place
        n, p = place.sizes[dim], place.pos[dim]
        lo, hi = (self.lo, self.hi) if dim == 0 else (0, n)
        for up in (True, False):
            here = k if up else n - 1 - k
            cond = p == here
            span = range(max(lo, here), hi) if up else range(lo, min(hi, here + 1))
            if len(span) == 0:
                continue

            def receive(up=up, here=here, span=span):
                for row in rows:
                    for at in span:
                        slot = at - here if up else at + (n - here if here > 0 else 0)
                        q = row[:dim] + (at,) + row[dim + 1 :]
                        self.pull(dim, q, slot)
                        if at != here:
                            self.hop_copy(dim, q, up, here).start()

            pl.when(cond)(receive)
            for row in rows:
                for at in span:
                    if at != here:
                        q = row[:dim] + (at,) + row[dim + 1 :]
                        self.waits.append(
                            lambda cond=cond, q=q, up=up, here=here: pl.when(cond)(
                                lambda: self.hop_copy(dim, q, up, here).wait_send()
                            )
                        )

    def hop_copy(self, dim, q, up, here):
        place = self.place
        n = place.sizes[dim]
        u = self.unit(dim, q)
        slot = self.slot_up(q[dim], here) if up else self.slot_down(n, q[dim], here)
        target = u * landing(n) + slot
        return remote(
            self.units.at(place.owner(q)),
            self.land.at(self.land_at[dim] + target),
            self.sems.at[(self.up_at if up else self.down_at)[dim] + u * n + q[dim]],
            self.sems.at[self.recv_at[dim] + target],
            place.near(dim, up),
        )

    def finish(self):
        for wait in self.waits:
            wait()
        piece = self.land.stretch(self.shared)
        remote(
            piece, piece, self.sems.at[0], self.sems.at[1], self.place.sibling
        ).wait_send()
        self.waits, self.shared = [], 0


class Total:
    def __init__(self, place, land, sems):
        self.place, self.land, self.sems = place, land, sems
        self.sizes = (2,) + place.sizes[::-1]
        self.at = [sum(self.sizes[:k]) for k in range(4)]
        self.waits = []

    @staticmethod
    def slots(devices):
        return 6 + 2 * math.isqrt(devices // 8)

    def lines(self, k):
        place = self.place
        if k == 0:
            return place.core, [(1, 1 - place.core, place.sibling)]
        return place.plain[3 - k], place.peers(3 - k)

    def send(self, k, value):
        p, peers = self.lines(k)
        here = self.land.at[self.at[k] + p]
        self.land[self.at[k] + p] = value
        half = self.at[3] + self.sizes[3]
        for r, _, device in peers:

            def copy(r=r, device=device):
                sems = self.sems
                return remote(
                    here, here, sems.at[self.at[k] + r], sems.at[half + self.at[k] + p], device
                )

            copy().start()
            self.waits.append(lambda copy=copy: copy().wait_send())

    def take(self, k):
        _, peers = self.lines(k)
        half = self.at[3] + self.sizes[3]
        for r, at, device in peers:
            there = self.land.at[self.at[k] + at]
            remote(
                there, there, self.sems.at[0], self.sems.at[half + self.at[k] + at], device
            ).wait_recv()
        total = self.land[self.at[k]]
        for s in range(1, self.sizes[k]):
            total = total + self.land[self.at[k] + s]
        return total

    def pass_on(self, k):
        value = self.take(k)
        if k < 3:
            self.send(k + 1, value)
        return value

    def finish(self):
        for wait in self.waits:
            wait()
        self.waits = []


class Ring:
    def __init__(self, me, devices, land, sems):
        self.after = (me + 1) % devices
        self.before = (me + devices - 1) % devices
        self.land, self.sems = land, sems

    def copies(self, to_before, to_after):
        return (
            remote(to_before, self.land.at[1], self.sems.at[0], self.sems.at[1], self.before),
            remote(to_after, self.land.at[0], self.sems.at[2], self.sems.at[3], self.after),
        )

    def start(self, to_before, to_after):
        for copy in self.copies(to_before, to_after):
            copy.start()

    def wait(self, to_before, to_after):
        for copy in self.copies(to_before, to_after):
            copy.wait_recv()

    def finish(self, to_before, to_after):
        for copy in self.copies(to_before, to_after):
            copy.wait_send()


def unit_shape(amount):
    across = min(amount, PANEL)
    return amount // across * BLOCK_ROWS, across * BLOCK_COLS


def own_unit(units, me, blocks):
    across = units.cols // BLOCK_COLS
    rows = []
    for a in range(units.rows // BLOCK_ROWS):
        row = [blocks[a * across + b].astype(bf16) for b in range(across)]
        rows.append(jnp.concatenate(row, axis=1))
    units.put(me, jnp.concatenate(rows, axis=0))


def network(
    idx_ref,
    positions_ref,
    species_ref,
    counts_ref,
    cot_ref,
    scale_ref,
    shift_ref,
    weight_ref,
    state_ref,
    blocks_ref,
    late_in,
    energy_ref,
    forces_ref,
    vector_ref,
    first_out,
    late_out,
    first_w,
    late_w,
    hot,
    z_t,
    z_r,
    geo,
    yrow,
    env_b,
    ee_t,
    en2_t,
    s1_t,
    s2_t,
    gam,
    dlt,
    coef,
    ds_t,
    de_t,
    dy,
    dg,
    dw_t,
    dw_r,
    dpf,
    den,
    lat,
    hid,
    low0,
    act1,
    sl1,
    low1,
    act2,
    sl2,
    low2,
    stage,
    halo,
    force_in,
    sides,
    vector_in,
    pack_ref,
    low_gather,
    mid_gather,
    high_gather,
    late_gather,
    late_sems,
    first_sems,
    ring_sems,
    vector_sems,
    ready,
):
    s_r = dw_r
    fact = den

    wee_t = dw_t.at[:, 0:LATENT]
    we2_t = dw_t.at[0:128, 0:LATENT]
    devices = lax.axis_size("atoms")
    me = lax.axis_index("atoms")
    place = Place(devices)
    own_at = pack_ref.at[0:8]
    first_units = Units(first_w, *unit_shape(blocks_ref.shape[0]))
    late_units = Units(late_w, *unit_shape(late_in.shape[0]))
    top = place.sizes[0]
    middle = top // 2

    def pieces(k, count):
        return Units(first_w, first_units.rows, first_units.cols, part=(k, count))

    def free(ref, units, k=0, count=1):
        slots = Reduce.slots(devices, 1)
        return Units(ref, units.rows // count, units.cols, base=k * slots)

    gather_low = [Gather(place, pieces(k, PIECES), 0, 1, low_gather.at[k]) for k in range(PIECES)]
    gather_mid = Gather(place, first_units, 1, middle, mid_gather)
    gather_high = Gather(place, first_units, middle, top, high_gather)
    gather_late = Gather(place, late_units, 0, top, late_gather, True)
    sum_out = Reduce(
        place, late_units, middle, top, free(low2, late_units), late_sems.at[0], ready.at[0]
    )
    sum_lat = Reduce(
        place, late_units, 0, middle, free(sl2, late_units), late_sems.at[1], ready.at[1]
    )
    sum_first = [
        [
            Reduce(
                place,
                pieces(k, SUM_PIECES[z]),
                z,
                z + 1,
                free(ref, first_units, k, SUM_PIECES[z]),
                first_sems.at[PIECES * z + k],
                ready.at[2 + z] if k == 0 else None,
            )
            for k in range(SUM_PIECES[z])
        ]
        for z, ref in enumerate((hid, low0, low2, act2))
    ]

    def advance(z, stage):
        for part in sum_first[z]:
            part.stage(stage)
    link_halo = Ring(me, devices, halo, ring_sems.at[0])
    link_force = Ring(me, devices, force_in, ring_sems.at[1])
    sum_vector = Total(place, vector_in, vector_sems)

    barrier = pltpu.get_barrier_semaphore()
    partners = [place.sibling, link_halo.before, link_halo.after]
    for dim in range(3):
        partners += [device for _, _, device in place.peers(dim)]
    for device in partners:
        signal(barrier, device)
    for part in (slice(0, PLANE), slice(PLANE, LANES)):
        pack_ref[0:3, part] = positions_ref[...]
        pack_ref[3:4, part] = species_ref[...].astype(f32)
        pack_ref[4:5, part] = counts_ref[...].astype(f32)
        pack_ref[5:6, part] = cot_ref[...]
    pack_ref[6:16] = jnp.zeros((10, LANES), f32)
    pack_ref[6:7, 0:SPECIES] = scale_ref[...]
    pack_ref[7:8, 0:SPECIES] = shift_ref[...]
    pack_ref[8:9] = weight_ref[...]
    pack_ref[9:10] = state_ref[...]
    own_unit(first_units, me, blocks_ref)
    own_unit(late_units, me, late_in)
    pl.semaphore_wait(barrier, len(partners))
    link_halo.start(own_at, own_at)
    for part in gather_low:
        part.own()
    gather_high.own()

    ids = lax.broadcasted_iota(jnp.int32, (3 * PLANE, LANES), 0)

    whole = PLANE * devices
    coef[0, :, 0:SLOTS] = idx_ref[...].astype(f32)
    listed = coef[0].T[: SLOTS + 6].astype(jnp.int32) - (me - 1) * PLANE
    listed = jnp.where(
        listed < 0, listed + whole, jnp.where(listed >= whole, listed - whole, listed)
    )
    for t in range(TILES):
        near = jnp.concatenate([listed[2 * t : 2 * t + 1], listed[2 * t + 1 : 2 * t + 2]], axis=1)
        hot[:, t * LANES : (t + 1) * LANES] = jnp.where(ids == near, 1.0, 0.0).astype(bf16)

    link_halo.wait(own_at, own_at)
    own = pack_ref[0:8]
    lane = lax.broadcasted_iota(jnp.int32, (8, LANES), 1)
    row = lax.broadcasted_iota(jnp.int32, (8, LANES), 0)
    edge = spacing * devices
    x_row = row == 0
    before = halo[0] - jnp.where(x_row, jnp.where(me == 0, edge, 0.0), 0.0)
    after = halo[1] + jnp.where(x_row, jnp.where(me == devices - 1, edge, 0.0), 0.0)
    rank_y = ((lane & (PLANE - 1)) >> 3).astype(f32)
    rank_z = (lane & (SIDE - 1)).astype(f32)
    table = jnp.concatenate([jnp.where(lane < PLANE, before, own), after], axis=1)
    ranks = jnp.where(row == 4, rank_y, rank_z)
    table = jnp.where(
        jnp.concatenate([row, row], axis=1) < 4, table, jnp.concatenate([ranks, ranks], axis=1)
    )[:, : 3 * PLANE]
    ga, gb, gc = parts(table)
    got = nn(ga, hot[...]) + nn(gb, hot[...]) + nn(gc, hot[...])
    mine = jnp.concatenate([own] * TILES, axis=1)
    lane = lax.broadcasted_iota(jnp.int32, (1, ROWS), 1)
    slot = lane >> 6
    atom = lane & (PLANE - 1)
    for part in gather_low:
        part.column()
    for part in gather_low:
        part.second()
    gather_mid.own()
    gather_mid.column()

    def wrapped(step):
        return jnp.where(step > 1.5, -8.0, jnp.where(step < -1.5, 8.0, 0.0)) * spacing

    disp = [
        got[0:1] - mine[0:1],
        got[1:2] - mine[1:2] + wrapped(got[4:5] - (atom >> 3).astype(f32)),
        got[2:3] - mine[2:3] + wrapped(got[5:6] - (atom & (SIDE - 1)).astype(f32)),
    ]
    length = jnp.sqrt(disp[0] * disp[0] + disp[1] * disp[1] + disp[2] * disp[2])
    inverse = 1.0 / length
    unit = [disp[0] * inverse, disp[1] * inverse, disp[2] * inverse]
    angle = length * (math.pi / cutoff_radius)
    sin_k = [jnp.sin(angle)]
    cos_k = [jnp.cos(angle)]
    sin_k.append(2.0 * cos_k[0] * sin_k[0])
    cos_k.append(2.0 * cos_k[0] * cos_k[0] - 1.0)
    for k in range(2, BESSEL):
        sin_k.append(2.0 * cos_k[0] * sin_k[k - 1] - sin_k[k - 2])
        cos_k.append(2.0 * cos_k[0] * cos_k[k - 1] - cos_k[k - 2])
    sines = jnp.concatenate(sin_k, axis=0)
    cosines = jnp.concatenate(cos_k, axis=0)
    bessel = (math.sqrt(2.0 / cutoff_radius) * inverse) * sines
    scaled = length * (1.0 / cutoff_radius)
    t2 = scaled * scaled
    t4 = t2 * t2
    t5 = t4 * scaled
    t6 = t4 * t2
    envelope = 1.0 - 28.0 * t6 + 48.0 * (t6 * scaled) - 21.0 * (t4 * t4)
    denvelope = (-168.0 * t5 + 336.0 * t6 - 168.0 * (t6 * scaled)) * (1.0 / cutoff_radius)
    live = jnp.where(slot.astype(f32) < mine[4:5], 1.0, 0.0)

    kind = lax.broadcasted_iota(jnp.int32, (KINDS, LANES), 0).astype(f32)
    is_kind = kind == own[3:4]
    by_kind = own.T
    scale = jnp.sum(jnp.where(is_kind, by_kind[:KINDS, 6:7], 0.0), axis=0, keepdims=True)
    shift = jnp.sum(jnp.where(is_kind, by_kind[:KINDS, 7:8], 0.0), axis=0, keepdims=True)
    cot = jnp.concatenate([own[5:6] * scale] * TILES, axis=1) * live
    weight = cot * envelope

    root3 = math.sqrt(3.0)
    root15 = math.sqrt(15.0)
    root5 = math.sqrt(5.0)
    ux, uy, uz = unit
    yrow[0:8] = jnp.concatenate(
        [
            root3 * ux,
            root3 * uy,
            root3 * uz,
            root15 * ux * uy,
            root15 * uy * uz,
            0.5 * root5 * (3.0 * uz * uz - 1.0),
            root15 * ux * uz,
            0.5 * root15 * (ux * ux - uy * uy),
        ],
        axis=0,
    )
    yrow[8:16] = yrow[0:8] * (live * env_scale)
    yrow[16:17] = live * env_scale
    geo[0:8] = jnp.concatenate([ux, uy, uz, inverse, envelope, denvelope, live, cot], axis=0)
    geo[8:16] = math.sqrt(2.0 / cutoff_radius) * (
        (math.pi / cutoff_radius)
        * lax.broadcasted_iota(jnp.int32, (BESSEL, ROWS), 0).astype(f32)
        * cosines
        + (math.pi / cutoff_radius) * cosines
        - sines * inverse
    ) * inverse


    def one_hots(t):
        row = lax.broadcasted_iota(jnp.int32, (LANES, LANES), 0).astype(f32)
        here = jnp.where(row == own[3:4] + float(BESSEL), 1.0, 0.0)
        there = jnp.where(row == kinds_near[t] + float(BESSEL + SPECIES), 1.0, 0.0)
        return here + there

    kinds_near = [got[3:4, t * LANES : (t + 1) * LANES] for t in range(TILES)]
    gather_mid.second()
    for part in gather_low:
        part.third()
    gather_high.column()
    for t in range(TILES):
        at = slice(t * LANES, (t + 1) * LANES)
        column = jnp.concatenate([bessel[:, at], one_hots(t)[BESSEL:]], axis=0)
        z_t[:, at] = column.astype(bf16)
        z_r[at, :] = column.T.astype(bf16)
        env_b[at, :] = jnp.broadcast_to(envelope[:, at], (LANES, LANES)).T
        fact[at, :] = jnp.broadcast_to(weight[:, at], (LANES, LANES)).T
    for part in gather_low:
        part.across()


    def twice(x):
        return jnp.concatenate([x] * (STRIP // LANES), axis=1)

    def in_body(n, r):
        pre = nn(z_r[r], cols_panel(first_w, W_INPUT, n))
        hid[r, panel(n, STRIP)] = (pre * sigmoid(pre)).astype(bf16)

    loop_panels(in_body)
    gather_mid.third()
    gather_high.second()
    gather_late.own()
    gather_mid.across()

    def two_body(n, r):
        zero = nn(hid[r], cols_panel(first_w, W_TWO, n)) * twice(env_b[r])
        lat[r, panel(n, STRIP)] = zero
        low0[r, panel(n, STRIP)] = zero.astype(bf16)

    loop_panels(two_body)
    gather_high.third()

    def transposed_product(out, weights, right, width=256):
        at = 0
        while at < ROWS:
            end = min(at + width, ROWS)
            out[:, at:end] = nt(weights, right[at:end, :])
            at = end

    wee_t[0:128, :] = narrow(first_w, W_EMBED).T
    wee_t[128:256, :] = narrow(first_w, W_ENV_ONE).T
    transposed_product(ee_t, wee_t[...], low0)
    gather_late.column()

    def environment(out, v0_ref, v0_at, v1_at):
        for m in range(9):
            total = None
            begin = v0_at if m == 0 else v1_at
            y = yrow[16:17, :] if m == 0 else yrow[7 + m : 8 + m, :]
            for t in range(TILES):
                at = slice(t * LANES, (t + 1) * LANES)
                term = v0_ref[begin : begin + CHANNELS, at] * y[:, at]
                total = term if total is None else total + term
            out[m] = halves(total)

    def put_scalars(t, s_t, rows):
        s_t[:, lanes(t)] = jnp.concatenate(rows, axis=0).astype(bf16)
        filled = jnp.concatenate(rows + [jnp.zeros_like(rows[0])], axis=0)
        flipped = filled.T.astype(bf16)
        s_r[lanes(t), :] = flipped

    def weighted(y, first, count, source, offset):
        total = None
        for m in range(count):
            term = y[first + m : first + m + 1] * source[offset + m]
            total = term if total is None else total + term
        return total

    environment(gam, ee_t, 128, 192)

    def scalars_one(t):
        e0 = ee_t[0:64, lanes(t)]
        e1 = ee_t[64:128, lanes(t)]
        y = yrow[0:8, lanes(t)]
        put_scalars(
            t,
            s1_t,
            [e0 * gam[0], e1 * weighted(y, 0, 3, gam, 1), e1 * weighted(y, 3, 5, gam, 4)],
        )

    beside(6, lambda i: None, scalars_one)
    gather_high.across()

    def pre_one(n, r):
        pre = nn(low0[r], cols_panel(first_w, W_LAT_ONE, n)) + nn(
            s_r[r, : 3 * CHANNELS], cols_panel(first_w, W_SCAL_ONE, n)
        )
        sig = sigmoid(pre)
        act = pre * sig
        act1[r, panel(n, STRIP)] = act.astype(bf16)
        sl1[r, panel(n, STRIP)] = (sig + act * (1.0 - sig)).astype(bf16)

    loop_panels(pre_one)
    gather_late.second()

    def out_one(n, r):
        new = (lat[r, panel(n, STRIP)] + nn(act1[r], cols_panel(first_w, W_OUT_ONE, n))) * half_root
        lat[r, panel(n, STRIP)] = new
        low1[r, panel(n, STRIP)] = new.astype(bf16)

    loop_panels(out_one)
    gather_late.third()
    we2_t[...] = narrow(first_w, W_ENV_TWO).T
    transposed_product(en2_t, we2_t[...], low1)
    environment(dlt, en2_t, 0, 64)

    g0 = gam[0]
    coef[0] = g0 * dlt[0]
    for m in range(3):
        a, b = 1 + (m + 1) % 3, 1 + (m + 2) % 3
        coef[1 + m] = g0 * dlt[1 + m] + (gam[a] * dlt[b] - gam[b] * dlt[a])
    coef[9] = gam[1] * dlt[1] + gam[2] * dlt[2] + gam[3] * dlt[3]
    second = None
    for m in range(4, 9):
        coef[m] = g0 * dlt[m]
        term = gam[m] * dlt[m]
        second = term if second is None else second + term
    coef[10] = second

    def scalars_two(t):
        e0 = ee_t[0:64, lanes(t)]
        e1 = ee_t[64:128, lanes(t)]
        y = yrow[0:8, lanes(t)]
        put_scalars(
            t,
            s2_t,
            [
                e0 * coef[0],
                e1 * weighted(y, 0, 3, coef, 1) + e0 * coef[9],
                e1 * weighted(y, 3, 5, coef, 4) + e0 * coef[10],
            ],
        )

    beside(6, lambda i: None, scalars_two)
    gather_late.across()

    for part in gather_low + [gather_mid, gather_high, gather_late]:
        part.finish()
    def pre_two(n, r):
        pre = nn(low1[r], cols_panel(late_w, W_LAT_TWO, n)) + nn(
            s_r[r, : 3 * CHANNELS], cols_panel(first_w, W_SCAL_TWO, n)
        )
        sig = sigmoid(pre)
        act = pre * sig
        act2[r, panel(n, STRIP)] = act.astype(bf16)
        sl2[r, panel(n, STRIP)] = (sig + act * (1.0 - sig)).astype(bf16)

    loop_panels(pre_two)

    def out_two(n, r):
        new = (lat[r, panel(n, STRIP)] + nn(act2[r], cols_panel(late_w, W_OUT_TWO, n))) * half_root
        low2[r, panel(n, STRIP)] = new.astype(bf16)

    loop_panels(out_two)

    vec = jnp.broadcast_to(pack_ref[8:9], (8, LANES))
    stage[...] = narrow(first_w, W_FINAL)

    def read_out(i):
        r = pl.ds(pl.multiple_of(i * 416, 16), 416)
        pre = nn(low2[r, :], stage[...])
        sig = sigmoid(pre)
        final_act = pre * sig
        dpf[r, :] = (fact[r, :] * vec[0:1] * (sig + final_act * (1.0 - sig))).astype(bf16)
        fact[r, :] = final_act

    loop(4, read_out)
    value = nt(vec, fact[...], highest)[0:1]
    geo_live = geo[6:7]
    geo_env = geo[4:5]
    geo_cot = geo[7:8]
    edge_energy = geo_live * geo_env * value
    summed = None
    for t in range(TILES):
        term = edge_energy[:, t * LANES : (t + 1) * LANES]
        summed = term if summed is None else summed + term
    energy_ref[...] = scale * halves(summed) + shift
    all_weights = jnp.broadcast_to(geo_cot * geo_env, (8, ROWS))
    sum_vector.send(0, nn(all_weights, fact[...], highest))
    geo[16:17] = geo_cot * value

    def big_step(out, where, left, right):
        def step(i):
            grad = tn(left[:, panel(i, STRIP)], right[...])
            out[pl.ds(pl.multiple_of(where[0] + i * STRIP, 64), STRIP), :] = grad.astype(bf16)

        return step

    def big_grad(out, where, left, right):
        loop(LATENT // STRIP, big_step(out, where, left, right))

    def wide_step(out, where, left, right):
        def step(n):
            out[where[0] : where[0] + where[1], panel(n)] = nn(
                left[...], right[:, panel(n)]
            ).astype(bf16)

        return step

    def wide_grad(out, where, left, right):
        loop(4, wide_step(out, where, left, right))

    def narrow_grad(left, right, put):
        def step(n):
            put(n, nn(left, right[:, panel(n)]).T.astype(bf16))

        loop(4, step)

    def put_narrow(where, n, grad):
        row = pl.multiple_of(where[0] + n // 2 * BLOCK_ROWS, BLOCK_ROWS)
        col = pl.multiple_of(n % 2 * 512, 512)
        first_w[pl.ds(row, BLOCK_ROWS), pl.ds(col, 512)] = jnp.concatenate(
            [grad[b * BLOCK_ROWS : (b + 1) * BLOCK_ROWS] for b in range(4)], axis=1
        )

    def put_stage(n, grad):
        stage[panel(n), :] = grad

    def back_final(n, r):
        grad = nt(dpf[r], narrow_panel(first_w, W_FINAL, n)) * half_root
        lat[r, panel(n, STRIP)] = grad
        low2[r, panel(n, STRIP)] = grad.astype(bf16)

    def back_out_two(n, r):
        grad = nt(low2[r], rows_panel(late_w, W_OUT_TWO, n))
        sl2[r, panel(n, STRIP)] = (grad * sl2[r, panel(n, STRIP)].astype(f32)).astype(bf16)

    def tensors_two(t):
        e0 = ee_t[0:64, lanes(t)]
        e1 = ee_t[64:128, lanes(t)]
        y = yrow[0:8, lanes(t)]
        r0 = ds_t[0:64, lanes(t)]
        r1 = ds_t[64:128, lanes(t)]
        r2 = ds_t[128:192, lanes(t)]
        de_t[0:64, lanes(t)] = r0 * coef[0] + r1 * coef[9] + r2 * coef[10]
        de_t[64:128, lanes(t)] = r1 * weighted(y, 0, 3, coef, 1) + r2 * weighted(y, 3, 5, coef, 4)
        p1 = r1 * e1
        p2 = r2 * e1
        rows = []
        for m in range(8):
            p = p1 if m < 3 else p2
            rows.append(jnp.sum(p * coef[1 + m], axis=0, keepdims=True))
            dg[1 + m] += p * y[m : m + 1]
        dy[:, lanes(t)] = jnp.concatenate(rows, axis=0)
        dg[0] += r0 * e0
        dg[9] += r1 * e0
        dg[10] += r2 * e0

    def environment_back(t, grads, source, v1_at, at):
        y4 = yrow[8:16, lanes(t)]
        l4 = yrow[16:17, lanes(t)]
        v1 = source[v1_at : v1_at + 64, lanes(t)]
        low = l4 * grads[0]
        high = weighted(y4, 0, 8, grads, 1)
        both = jnp.concatenate([low, high], axis=0)
        dw_t[at : at + 128, lanes(t)] = both.astype(bf16)
        dw_r[lanes(t), at : at + 128] = both.T.astype(bf16)
        v1 = v1 * l4
        rows = [jnp.sum(v1 * grads[1 + m], axis=0, keepdims=True) for m in range(8)]
        dy[:, lanes(t)] += jnp.concatenate(rows, axis=0)

    def back_lat_two(n, r):
        grad = (
            lat[r, panel(n, STRIP)]
            + nt(sl2[r], rows_panel(late_w, W_LAT_TWO, n))
            + nt(dw_r[r, 128:256], narrow_panel(first_w, W_ENV_TWO, n))
        ) * half_root
        lat[r, panel(n, STRIP)] = grad
        act2[r, panel(n, STRIP)] = grad.astype(bf16)

    def back_out_one(n, r):
        grad = nt(act2[r], rows_panel(first_w, W_OUT_ONE, n))
        sl1[r, panel(n, STRIP)] = (grad * sl1[r, panel(n, STRIP)].astype(f32)).astype(bf16)

    def tensors_one(t):
        e0 = ee_t[0:64, lanes(t)]
        e1 = ee_t[64:128, lanes(t)]
        y = yrow[0:8, lanes(t)]
        r0 = ds_t[0:64, lanes(t)]
        r1 = ds_t[64:128, lanes(t)]
        r2 = ds_t[128:192, lanes(t)]
        low = de_t[0:64, lanes(t)] + r0 * gam[0]
        high = (
            de_t[64:128, lanes(t)]
            + r1 * weighted(y, 0, 3, gam, 1)
            + r2 * weighted(y, 3, 5, gam, 4)
        )
        both = jnp.concatenate([low, high], axis=0)
        dw_t[0:128, lanes(t)] = both.astype(bf16)
        dw_r[lanes(t), 0:128] = both.T.astype(bf16)
        p1 = r1 * e1
        p2 = r2 * e1
        rows = []
        for m in range(8):
            p = p1 if m < 3 else p2
            rows.append(jnp.sum(p * gam[1 + m], axis=0, keepdims=True))
            coef[1 + m] += p * y[m : m + 1]
        dy[:, lanes(t)] += jnp.concatenate(rows, axis=0)
        coef[0] += r0 * e0

    def back_lat_one(n, r):
        both = jnp.concatenate(
            [narrow_panel(first_w, W_EMBED, n), narrow_panel(first_w, W_ENV_ONE, n)], axis=1
        )
        grad = (
            lat[r, panel(n, STRIP)]
            + nt(sl1[r], rows_panel(first_w, W_LAT_ONE, n))
            + nt(dw_r[r], both)
        )
        low1[r, panel(n, STRIP)] = (grad * twice(env_b[r])).astype(bf16)
        part = grad * low0[r, panel(n, STRIP)].astype(f32)
        for b in range(STRIP // LANES):
            den[r] += part[:, b * LANES : (b + 1) * LANES]

    def back_two(n, r):
        grad = nt(low1[r], rows_panel(first_w, W_TWO, n))
        pre = nn(z_r[r], cols_panel(first_w, W_INPUT, n))
        sig = sigmoid(pre)
        act1[r, panel(n, STRIP)] = (grad * (sig + pre * sig * (1.0 - sig))).astype(bf16)

    def lat_one_grad(low, high):
        grad = tn(low0[:, low:high], sl1[...])
        first_w[W_LAT_ONE[0] + low : W_LAT_ONE[0] + high, :] = grad.astype(bf16)

    narrow_grad(dpf[...].T, low2, put_stage)
    loop_panels(back_final)
    loop(4, lambda n: put_narrow(W_FINAL, n, stage[panel(n), :]))
    loop_panels(back_out_two)
    transposed_product(ds_t, first_w[W_SCAL_TWO[0] : W_SCAL_TWO[0] + W_SCAL_TWO[1], :], sl2)
    dg[...] = jnp.zeros_like(dg)
    beside(2, big_step(late_w, W_OUT_TWO, act2, low2), tensors_two)
    sum_vector.pass_on(0)
    sum_out.stage(0)
    total = [halves(dg[m]) for m in range(11)]
    g0 = gam[0]
    d0 = dlt[0]
    new_g0 = total[0] * d0
    for m in range(1, 9):
        new_g0 = new_g0 + total[m] * dlt[m]
    dlt_grads = [total[0] * g0]
    gam_grads = [new_g0]
    for m in range(3):
        a, b = 1 + (m + 1) % 3, 1 + (m + 2) % 3
        dlt_grads.append(
            total[1 + m] * g0 + total[9] * gam[1 + m] + (total[a] * gam[b] - total[b] * gam[a])
        )
        gam_grads.append(total[9] * dlt[1 + m] + (dlt[a] * total[b] - dlt[b] * total[a]))
    for m in range(4, 9):
        dlt_grads.append(total[m] * g0 + total[10] * gam[m])
        gam_grads.append(total[10] * dlt[m])
    for m in range(9):
        dlt[m] = dlt_grads[m]
        dg[m] = gam_grads[m]
    beside(
        4,
        wide_step(first_w, W_SCAL_TWO, s2_t, sl2),
        lambda t: environment_back(t, dlt, en2_t, 64, 128),
    )
    sum_out.stage(1)
    loop_panels(back_lat_two)
    sum_out.stage(2)
    big_grad(late_w, W_LAT_TWO, low1, sl2)
    sum_vector.pass_on(1)
    sum_out.stage(3)
    sum_lat.stage(0)
    loop_panels(back_out_one)
    sum_out.stage(4)
    sum_lat.stage(1)
    transposed_product(ds_t, first_w[W_SCAL_ONE[0] : W_SCAL_ONE[0] + W_SCAL_ONE[1], :], sl1)
    narrow_grad(dw_t[128:256, :], low1, functools.partial(put_narrow, W_ENV_TWO))
    for m in range(9):
        coef[m] = jnp.zeros((CHANNELS, LANES), f32)
    beside(2, big_step(first_w, W_OUT_ONE, act1, act2), tensors_one)
    sum_vector.pass_on(2)
    sum_out.stage(5)
    sum_lat.stage(2)
    advance(3, 0)
    for m in range(9):
        dg[m] = dg[m] + halves(coef[m])
    beside(
        4,
        wide_step(first_w, W_SCAL_ONE, s1_t, sl1),
        lambda t: environment_back(t, dg, ee_t, 192, 128),
    )
    advance(3, 1)
    sum_out.stage(6)
    sum_lat.stage(3)
    den[...] = jnp.zeros_like(den)
    loop_panels(back_lat_one)
    lat_one_grad(640, 1024)
    sum_lat.stage(4)
    advance(3, 2)
    advance(2, 0)
    loop_panels(back_two)
    sum_lat.stage(5)
    advance(3, 3)
    advance(2, 1)
    big_grad(first_w, W_TWO, hid, low1)
    transposed_product(ds_t.at[0:64], first_w[0:64, :], act1)
    wide_grad(first_w, W_INPUT, z_t, act1)
    advance(0, 0)
    advance(2, 2)
    narrow_grad(dw_t[0:128, :], low0, functools.partial(put_narrow, W_EMBED))
    narrow_grad(dw_t[128:256, :], low0, functools.partial(put_narrow, W_ENV_ONE))
    advance(3, 4)
    advance(0, 1)
    dbessel = ds_t[0:8, :]
    through = nt(jnp.ones((8, LANES), f32), den[...], highest)[0:1]
    ux, uy, uz = geo[0:1], geo[1:2], geo[2:3]
    inverse = geo[3:4]
    envelope = geo[4:5]
    denv = geo[16:17] + through / envelope
    dlength = jnp.sum(dbessel * geo[8:16], axis=0, keepdims=True) + denv * geo[5:6]
    g = [dy[m : m + 1, :] for m in range(8)]
    dux = root3 * g[0] + root15 * (uy * g[3] + uz * g[6] + ux * g[7])
    duy = root3 * g[1] + root15 * (ux * g[3] + uz * g[4] - uy * g[7])
    duz = root3 * g[2] + root15 * (uy * g[4] + ux * g[6]) + (3.0 * root5) * uz * g[5]
    along = dlength - (ux * dux + uy * duy + uz * duz) * inverse
    near = jnp.concatenate(
        [
            dux * inverse + ux * along,
            duy * inverse + uy * along,
            duz * inverse + uz * along,
            jnp.zeros((5, ROWS), f32),
        ],
        axis=0,
    )
    summed = None
    for t in range(TILES):
        term = near[:, t * LANES : (t + 1) * LANES]
        summed = term if summed is None else summed + term
    centre = halves(summed)
    na, nb, nc = parts(near)
    spread = nt(na, hot[...]) + nt(nb, hot[...]) + nt(nc, hot[...])
    sides[0] = spread[:, :LANES]
    sides[1, :, 0:PLANE] = spread[:, LANES:]
    link_force.start(sides.at[0], sides.at[1])
    lat_one_grad(0, 384)
    lat_one_grad(384, 640)
    advance(1, 0)
    advance(3, 5)
    advance(2, 3)
    sum_lat.stage(6)
    advance(0, 2)
    advance(1, 1)
    advance(2, 4)
    advance(0, 3)
    advance(3, 6)
    advance(0, 4)
    for step in range(6):
        for k in range(max(SUM_PIECES[:3])):
            for z, after in ((0, 5), (1, 2), (2, 5)):
                if k < SUM_PIECES[z] and after <= after + step - k < 7:
                    sum_first[z][k].stage(after + step - k)
    link_force.wait(sides.at[0], sides.at[1])
    forces_ref[...] = (
        centre - pltpu.roll(sides[0], PLANE, 1) - force_in[1] - force_in[0]
    )
    total = sum_vector.pass_on(3)
    normed = total * lax.rsqrt(jnp.sum(total[0:1] * total[0:1]) * (1.0 / FINAL) + epsilon)
    state = decay_rate * pack_ref[9:10] + (1.0 - decay_rate) * normed * normed
    vector_ref[0:1] = total[0:1]
    vector_ref[1:2] = state[0:1]
    vector_ref[2:3] = (pack_ref[8:9] - vector_rate * normed * lax.rsqrt(state + epsilon))[0:1]
    first_out[...] = first_units.get(me)
    late_out[...] = late_units.get(me)
    for group in sum((list(parts) for parts in sum_first), [sum_out, sum_lat, sum_vector]):
        group.finish()
    link_halo.finish(own_at, own_at)
    link_force.finish(sides.at[0], sides.at[1])


def run_network(devices, small, blocks, late):
    S = jax.ShapeDtypeStruct
    wide = pltpu.VMEM((ROWS, LATENT), bf16)
    slab = pltpu.VMEM((ROWS, LANES), f32)
    panels = lambda amount: pltpu.VMEM((amount * devices // PANEL * BLOCK_ROWS, WIDE), bf16)
    scratch = [
        panels(blocks.shape[0]),
        panels(late.shape[0]),
        pltpu.VMEM((3 * PLANE, ROWS), bf16),
        pltpu.VMEM((LANES, ROWS), bf16),
        pltpu.VMEM((ROWS, LANES), bf16),
        pltpu.VMEM((24, ROWS), f32),
        pltpu.VMEM((24, ROWS), f32),
        slab,
        pltpu.VMEM((256, ROWS), f32),
        pltpu.VMEM((128, ROWS), f32),
        pltpu.VMEM((192, ROWS), bf16),
        pltpu.VMEM((192, ROWS), bf16),
        pltpu.VMEM((9, CHANNELS, LANES), f32),
        pltpu.VMEM((9, CHANNELS, LANES), f32),
        pltpu.VMEM((11, CHANNELS, LANES), f32),
        pltpu.VMEM((192, ROWS), f32),
        pltpu.VMEM((128, ROWS), f32),
        pltpu.VMEM((8, ROWS), f32),
        pltpu.VMEM((11, CHANNELS, LANES), f32),
        pltpu.VMEM((256, ROWS), bf16),
        pltpu.VMEM((ROWS, 256), bf16),
        pltpu.VMEM((ROWS, LANES), bf16),
        slab,
        pltpu.VMEM((ROWS, LATENT), f32),
    ] + [wide] * 8 + [
        pltpu.VMEM((LATENT, LANES), bf16),
        pltpu.VMEM((2, 8, LANES), f32),
        pltpu.VMEM((2, 8, LANES), f32),
        pltpu.VMEM((2, 8, LANES), f32),
        pltpu.VMEM((Total.slots(devices), 8, LANES), f32),
        pltpu.VMEM((16, LANES), f32),
        pltpu.SemaphoreType.DMA((PIECES, Gather.amount(devices, 1))),
        pltpu.SemaphoreType.DMA((Gather.amount(devices, 1),)),
        pltpu.SemaphoreType.DMA((Gather.amount(devices, 2),)),
        pltpu.SemaphoreType.DMA((Gather.amount(devices, 4),)),
        pltpu.SemaphoreType.DMA((2, Reduce.amount(devices, 2))),
        pltpu.SemaphoreType.DMA((4 * PIECES, Reduce.amount(devices, 1))),
        pltpu.SemaphoreType.DMA((2, 4)),
        pltpu.SemaphoreType.DMA((2 * Total.slots(devices),)),
        pltpu.SemaphoreType.REGULAR((6, 7)),
    ]
    vmem = pl.BlockSpec(memory_space=pltpu.VMEM)
    return pl.pallas_call(
        network,
        out_shape=[
            S((1, LANES), f32),
            S((8, LANES), f32),
            S((8, LANES), f32),
            S(unit_shape(blocks.shape[0]), bf16),
            S(unit_shape(late.shape[0]), bf16),
        ],
        in_specs=[vmem] * (len(small) + 2),
        out_specs=[vmem] * 5,
        scratch_shapes=scratch,
        compiler_params=pltpu.CompilerParams(
            vmem_limit_bytes=63 << 20, collective_id=0, has_side_effects=True
        ),
        name="network",
    )(*small, blocks, late)


def shampoo(
    energy,
    force,
    vectors,
    grads,
    left,
    right,
    left_root,
    right_root,
    master,
    late_grads,
    late_left,
    late_right,
    late_left_root,
    late_right_root,
    late_master,
    energy_out,
    force_out,
    vector_out,
    state_out,
    moved_out,
    *outs,
):
    energy_out[...] = energy[:, :PLANE]
    force_out[...] = force[0:3, :PLANE]
    vector_out[...] = vectors[0:1]
    state_out[...] = vectors[1:2]
    moved_out[...] = vectors[2:3]

    todo = []
    for j in range(left.shape[0]):
        todo.append((grads, j, left, right, left_root, right_root, master) + outs[:4])
    for j in range(late_left.shape[0]):
        todo.append(
            (late_grads, j, late_left, late_right, late_left_root, late_right_root, late_master)
            + outs[4:]
        )
    size = 1.0 / (BLOCK_ROWS * BLOCK_COLS)
    held, scales, steps = [], [], []
    for panels, j, left, *_ in todo:
        per = panels.shape[1] // BLOCK_COLS
        at = pl.program_id(0) * left.shape[0] + j
        row = pl.multiple_of(at // per * BLOCK_ROWS, BLOCK_ROWS)
        col = pl.multiple_of(at % per * BLOCK_COLS, BLOCK_COLS)
        held.append(panels[pl.ds(row, BLOCK_ROWS), pl.ds(col, BLOCK_COLS)])
    for g, (_, j, *_, grad_out, left_out, right_out, master_out) in zip(held, todo):
        grad = g.astype(f32)
        grad_out[j] = grad
        scales.append(lax.rsqrt(jnp.sum(grad * grad, keepdims=True) * size + epsilon))
    turned = []
    for g, (_, j, left, right, left_root, *_) in zip(held, todo):
        la, lb, _ = parts(left_root[j])
        turned.append(nn(la, g) + nn(lb, g))
    for g, s, (_, j, left, right, *_, grad_out, left_out, right_out, master_out) in zip(
        held, scales, todo
    ):
        square = (1.0 - decay_rate) * s * s
        left_out[j] = decay_rate * left[j] + square * nt(g, g)
        right_out[j] = decay_rate * right[j] + square * tn(g, g)
    for turn, s, (_, j, left, right, left_root, right_root, *_) in zip(turned, scales, todo):
        ra, rb, _ = parts(right_root[j])
        ta, tb, _ = parts(turn * s)
        steps.append(nn(ta, ra) + (nn(ta, rb) + nn(tb, ra)))
    for step, (_, j, left, right, left_root, right_root, master, *_, master_out) in zip(steps, todo):
        slope = lax.rsqrt(jnp.sum(step * step, keepdims=True) * size + epsilon)
        master_out[j] = master[j] - (learn_rate * slope) * step


def run_shampoo(energy, force, vectors, first, late):
    S = jax.ShapeDtypeStruct
    steps = min(2, late[1].shape[0])

    def whole(x):
        return pl.BlockSpec(x.shape, lambda i: (0,) * len(x.shape))

    def share(x):
        return pl.BlockSpec((x.shape[0] // steps,) + x.shape[1:], lambda i: (i, 0, 0))

    small = [S((1, PLANE), f32), S((3, PLANE), f32)] + [S((1, FINAL), f32)] * 3
    grown = []
    for group in (first, late):
        left, right, _, _, master = group[1:]
        grown += [S(x.shape, f32) for x in (master, left, right, master)]
    return pl.pallas_call(
        shampoo,
        grid=(steps,),
        out_shape=small + grown,
        in_specs=[whole(energy), whole(force), whole(vectors)]
        + [whole(first[0])]
        + [share(x) for x in first[1:]]
        + [whole(late[0])]
        + [share(x) for x in late[1:]],
        out_specs=[whole(x) for x in small] + [share(x) for x in grown],
        compiler_params=pltpu.CompilerParams(vmem_limit_bytes=60 << 20),
        name="shampoo",
    )(energy, force, vectors, *first, *late)


def local(
    positions,
    species,
    neighbours,
    counts,
    species_scale,
    species_shift,
    energy_cot,
    blocks,
    left,
    right,
    left_root,
    right_root,
    late_blocks,
    late_left,
    late_right,
    late_left_root,
    late_right_root,
    out_vector,
    vector_state,
):
    devices = lax.axis_size("atoms")
    small = (
        neighbours.reshape(PLANE, SLOTS),
        positions,
        species[None],
        counts[None],
        energy_cot[None],
        species_scale[None],
        species_shift[None],
        out_vector[None],
        vector_state[None],
    )
    energy, force, vectors, first_units, late_units = run_network(
        devices, small, blocks, late_blocks
    )
    out = run_shampoo(
        energy,
        force,
        vectors,
        (first_units, left, right, left_root, right_root, blocks),
        (late_units, late_left, late_right, late_left_root, late_right_root, late_blocks),
    )
    energies, forces, vector_grad, new_state, new_vector = out[:5]
    return (
        energies.reshape(-1),
        forces,
        *out[5:],
        vector_grad.reshape(-1),
        new_state.reshape(-1),
        new_vector.reshape(-1),
    )


def solution(mesh):
    row = P("atoms")
    block = P("atoms", None, None)
    placed = (
        (P(None, "atoms"), row, row, row, P(), P(), row)
        + (block,) * 10
        + (P(), P())
    )
    return jax.shard_map(
        local,
        mesh=mesh,
        in_specs=placed,
        out_specs=(row, P(None, "atoms")) + (block,) * 8 + (P(), P(), P()),
        check_vma=False,
    )
```

```python
import functools
import math

import jax
import jax.numpy as jnp
from jax import lax
from jax.experimental import pallas as pl
from jax.experimental.pallas import tpu as pltpu
from jax.sharding import PartitionSpec as P

SIDE = 8
SLOTS = 26
SPECIES = 60
BESSEL = 8
CHANNELS = 64
LATENT = 1024
FINAL = 128
BLOCK_ROWS = 64
BLOCK_COLS = 128
PLANE = SIDE * SIDE

f32 = jnp.float32
bf16 = jnp.bfloat16
spacing = 1.6
cutoff_radius = 4.0
env_scale = 0.25
half_root = 0.7071067811865476
decay_rate = 0.5
learn_rate = 0.02
vector_rate = 0.03
epsilon = 1e-06

LANES = 128
ROWS = SLOTS * PLANE
TILES = ROWS // LANES
KINDS = 64

PANEL = 8
WIDE = PANEL * BLOCK_COLS
W_INPUT = (0, 128)
W_TWO = (128, 1024)
W_EMBED = (1152, 128)
W_ENV_ONE = (1280, 128)
W_LAT_ONE = (1408, 1024)
W_SCAL_ONE = (2432, 192)
W_OUT_ONE = (2624, 1024)
W_ENV_TWO = (3648, 128)
W_SCAL_TWO = (3776, 192)
W_FINAL = (3968, 128)
W_LAT_TWO = (0, 1024)
W_OUT_TWO = (1024, 1024)

MESH = pl.DeviceIdType.MESH


def nn(a, b):
    return lax.dot_general(a, b, (((1,), (0,)), ((), ())), preferred_element_type=f32)


def nt(a, b):
    return lax.dot_general(a, b, (((1,), (1,)), ((), ())), preferred_element_type=f32)


def tn(a, b):
    return lax.dot_general(a, b, (((0,), (0,)), ((), ())), preferred_element_type=f32)


def cols_panel(ref, where, n):
    return ref[where[0] : where[0] + where[1], panel(n, STRIP)]


def rows_panel(ref, where, n):
    return ref[pl.ds(pl.multiple_of(where[0] + n * STRIP, 64), STRIP), :]


def narrow(ref, where):
    pieces = []
    for j in range(LATENT // BLOCK_ROWS):
        row = where[0] + j // PANEL * BLOCK_ROWS
        col = j % PANEL * BLOCK_COLS
        pieces.append(ref[row : row + BLOCK_ROWS, col : col + BLOCK_COLS])
    return jnp.concatenate(pieces, axis=0)


def narrow_panel(ref, where, n):
    part = ref[pl.ds(pl.multiple_of(where[0] + n * BLOCK_ROWS, BLOCK_ROWS), BLOCK_ROWS), :]
    return jnp.concatenate([part[:, b * 128 : (b + 1) * 128] for b in range(PANEL)], axis=0)


def sigmoid(x):
    return 0.5 * jnp.tanh(0.5 * x) + 0.5


def halves(x):
    return x + pltpu.roll(x, PLANE, 1)


def lanes(t):
    if isinstance(t, int):
        return pl.ds(t * LANES, LANES)
    return pl.ds(pl.multiple_of(t * LANES, LANES), LANES)


def panel(n, width=256):
    return pl.ds(pl.multiple_of(n * width, width), width)


STRIP = 512
CHUNKS = 2
PIECES = 2
SUM_PIECES = (2, 2, 1, 1)
CHUNK = ROWS // CHUNKS


def loop_panels(body):
    def step(n):
        for c in range(CHUNKS):
            body(n, slice(c * CHUNK, (c + 1) * CHUNK))

    loop(LATENT // STRIP, step)


def beside(count, step, tile):
    share = TILES // count

    def body(i):
        step(i)
        for u in range(share):
            tile(i * share + u)

    loop(count, body)
    for t in range(share * count, TILES):
        tile(t)


def loop(count, body):
    def step(i, carry):
        body(i)
        return carry

    lax.fori_loop(0, count, step, 0)


def parts(x):
    a = x.astype(bf16)
    rest = x - a.astype(f32)
    b = rest.astype(bf16)
    c = (rest - b.astype(f32)).astype(bf16)
    return a, b, c


class Place:
    def __init__(self, devices):
        side = math.isqrt(devices // 8)
        self.devices = devices
        self.sizes = (4, side, side)
        me = lax.axis_index("atoms")
        core = me % 2
        chip = me // 2
        last = chip % side
        middle = chip // side % side
        self.me = me
        self.core = core
        self.pos = (
            chip // (side * side),
            last + core * (middle - last),
            middle + core * (last - middle),
        )
        self.half = (side * side, 1 + core * (side - 1), side + core * (1 - side))
        self.step = tuple(2 * h for h in self.half)
        self.sibling = me + 1 - 2 * core
        self.plain = (self.pos[0], middle, last)
        self.plain_step = (2 * side * side, 2 * side, 2)

    def owner(self, q):
        return q[0] * self.step[0] + q[1] * self.step[1] + q[2] * self.step[2] + self.core

    def near(self, dim, up):
        return self.me + self.step[dim] if up else self.me - self.step[dim]

    def has(self, dim, up):
        return self.pos[dim] < self.sizes[dim] - 1 if up else self.pos[dim] > 0

    def peers(self, dim):
        n, p = self.sizes[dim], self.plain[dim]
        return [(r, (p + r) % n, self.me + ((p + r) % n - p) * self.plain_step[dim]) for r in range(1, n)]


class Units:
    def __init__(self, ref, rows, cols, base=0, part=(0, 1)):
        self.ref, self.rows, self.cols = ref, rows, cols
        self.per = WIDE // cols
        self.base = base
        self.high = rows // part[1]
        self.off = part[0] * self.high

    def window(self, s):
        s = s + self.base
        if self.per == 1:
            row, col = s * self.rows, slice(None)
        else:
            row = s // self.per * self.rows
            col = pl.ds(pl.multiple_of(s % self.per * self.cols, self.cols), self.cols)
        return (pl.ds(pl.multiple_of(row + self.off, 16), self.high), col)

    def at(self, s):
        return self.ref.at[self.window(s)]

    def get(self, s):
        return self.ref[self.window(s)]

    def put(self, s, value):
        self.ref[self.window(s)] = value

    def stretch(self, count):
        return self.ref.at[pl.ds(0, count * self.high // self.per), slice(None)]


def remote(src, dst, send, recv, device):
    return pltpu.make_async_remote_copy(
        src_ref=src,
        dst_ref=dst,
        send_sem=send,
        recv_sem=recv,
        device_id=(device,),
        device_id_type=MESH,
    )


def signal(sem, device):
    pl.semaphore_signal(sem, inc=1, device_id=(device,), device_id_type=MESH)


def others(place, dim):
    n, p = place.sizes[dim], place.pos[dim]
    if n == 2:
        return [(1 - p, None)]
    found = []
    for distance in range(1, n):
        found.append((p - distance, p >= distance))
        found.append((p + distance, p < n - distance))
    return found


def gated(cond, body):
    if cond is None:
        body()
    else:
        pl.when(cond)(body)


def both(a, b):
    return b if a is None else (a if b is None else a & b)


class Gather:
    def __init__(self, place, units, lo, hi, sems, direct=False, eager=True):
        self.place, self.units, self.lo, self.hi, self.sems = place, units, lo, hi, sems
        self.direct, self.eager = direct, eager
        _, na, nb = place.sizes
        self.waits = []
        self.shared = 0
        self.first_owner = 2 * lo * na * nb
        at = 2 * (hi - lo) * na * nb
        self.shared_send, self.core_recv = at, at + 1
        at += 2
        self.base = []
        for dim in range(3):
            length = (hi - lo) * (1, na, na * nb)[dim]
            self.base.append((at, at + length))
            at += 2 * length
        self.core_base = at

    @staticmethod
    def amount(devices, share):
        side = math.isqrt(devices // 8)
        return 2 + share * (2 + 2 * side + 5 * side * side)

    def linear(self, q, dim):
        _, na, nb = self.place.sizes
        q0 = q[0] - self.lo
        return (q0, q0 * na + q[1], (q0 * na + q[1]) * nb + q[2])[dim]

    def emit(self, cond, q, sem, device, core=False, once=None):
        owner = self.place.owner(q)
        common = cond is None or once is not None
        if common:
            sem = self.shared_send
            self.shared += 1 if once is None else once

        def copy():
            piece = self.units.at(owner)
            recv = self.core_recv if core else owner - self.first_owner
            return remote(piece, piece, self.sems.at[sem], self.sems.at[recv], device)

        gated(cond, lambda: copy().start())
        if not common:
            self.waits.append(lambda: gated(cond, lambda: copy().wait_send()))

    def onward(self, cond, q):
        place, p = self.place, self.place.pos[0]
        for up in (True, False):
            away = (p >= q[0]) if up else (p <= q[0])
            self.emit(
                both(cond, away & place.has(0, up)),
                q,
                self.base[0][0 if up else 1] + self.linear(q, 0),
                place.near(0, up),
            )

    def sideways(self, cond, q, dims, via=None, once=None):
        place = self.place
        for dim in dims:
            if place.sizes[dim] == 2:
                if dim != via:
                    toward = place.me + (1 - 2 * place.pos[dim]) * place.step[dim]
                    self.emit(
                        cond, q, self.base[dim][0] + self.linear(q, dim), toward, False, once
                    )
                continue
            for up in (True, False):
                open_end = place.has(dim, up)
                if dim == via:
                    p = place.pos[dim]
                    open_end = open_end & ((q[dim] < p) if up else (q[dim] > p))
                self.emit(
                    both(cond, open_end),
                    q,
                    self.base[dim][0 if up else 1] + self.linear(q, dim),
                    place.near(dim, up),
                )
        self.emit(cond, q, self.core_base + self.linear(q, 2), place.sibling, True, once)

    def wait(self, cond, q):
        owner = self.place.owner(q)
        piece = self.units.at(owner)
        gated(
            cond,
            lambda: remote(
                piece,
                piece,
                self.sems.at[self.shared_send],
                self.sems.at[owner - self.first_owner],
                self.place.sibling,
            ).wait_recv(),
        )

    def own(self):
        place, p = self.place, self.place.pos
        if self.direct:
            for r in range(1, 4):
                self.emit(None, p, 0, place.me + ((p[0] + r) % 4 - p[0]) * place.step[0])
            self.sideways(None, p, (2, 1))
            return
        for q0 in range(self.lo, self.hi):
            q = (q0, p[1], p[2])
            self.onward(p[0] == q0, q)
            if self.eager:
                self.sideways(p[0] == q0, q, (2, 1), None, 1)

    def column(self):
        p = self.place.pos
        if self.direct:
            for r in range(1, 4):
                q = ((p[0] + r) % 4, p[1], p[2])
                self.wait(None, q)
                self.sideways(None, q, (2, 1))
            return
        for q0 in range(self.lo, self.hi):
            q = (q0, p[1], p[2])
            self.wait(p[0] != q0, q)
            self.onward(p[0] != q0, q)
            if self.eager:
                self.sideways(p[0] != q0, q, (2, 1), None, 0)
            else:
                self.sideways(None, q, (2, 1))

    def second(self):
        for q0 in range(self.lo, self.hi):
            for qa, there in others(self.place, 1):
                q = (q0, qa, self.place.pos[2])
                self.wait(there, q)
                self.sideways(there, q, (2, 1), 1)

    def third(self):
        for qb, there in others(self.place, 2):
            for q0 in range(self.lo, self.hi):
                for qa in range(self.place.sizes[1]):
                    q = (q0, qa, qb)
                    self.wait(there, q)
                    self.sideways(there, q, (2,), 2)

    def across(self):
        _, na, nb = self.place.sizes
        piece = self.units.stretch((self.hi - self.lo) * na * nb)
        remote(
            piece,
            piece,
            self.sems.at[self.shared_send],
            self.sems.at[self.core_recv],
            self.place.sibling,
        ).wait_recv()

    def finish(self):
        for wait in self.waits:
            wait()
        if self.shared:
            piece = self.units.stretch(self.shared)
            remote(
                piece,
                piece,
                self.sems.at[self.shared_send],
                self.sems.at[self.core_recv],
                self.place.sibling,
            ).wait_send()
        self.waits, self.shared = [], 0


def landing(n):
    return 1 if n == 2 else n + 1


class Reduce:
    def __init__(self, place, units, lo, hi, land, sems, ready):
        self.place, self.units, self.lo, self.hi, self.land = place, units, lo, hi, land
        n0, na, nb = place.sizes
        self.count = (hi - lo) * na * nb
        lines = ((1, n0), (hi - lo, na), ((hi - lo) * na, nb))
        z_at = self.count
        b_at = z_at + landing(n0)
        a_at = b_at + lines[2][0] * landing(nb)
        self.land_at = (z_at, a_at, b_at)
        self.sems, self.ready = sems, ready
        self.shared = 0
        at = 4
        self.recv_at, self.up_at, self.down_at = [], [], []
        for units_here, n in lines:
            self.recv_at.append(at)
            at += units_here * landing(n)
            self.up_at.append(at)
            at += units_here * n
            self.down_at.append(at)
            at += units_here * n
        self.waits = []

    @staticmethod
    def slots(devices, share):
        side = math.isqrt(devices // 8)
        return share * side * side + landing(4) + share * (1 + side) * landing(side)

    @staticmethod
    def amount(devices, share):
        side = math.isqrt(devices // 8)
        total = 4
        for units_here, n in ((1, 4), (share, side), (share * side, side)):
            total += units_here * (landing(n) + 2 * n)
        return total

    def stage(self, k):
        if k == 0:
            self.start()
        elif k == 1:
            self.pairs()
        elif k < 4:
            self.along(4 - k)
        else:
            self.hop(0, k - 3, [(None,) + self.place.pos[1:]])

    def unit(self, dim, q):
        na = self.place.sizes[1]
        return (0, q[0] - self.lo, (q[0] - self.lo) * na + q[1])[dim]

    def add(self, owner, slot):
        self.units.put(owner, self.units.get(owner) + self.land.get(slot))

    def start(self):
        place = self.place
        if self.ready is not None:
            signal(self.ready.at[0], place.sibling)
            for dim in range(3):
                for up in (True, False):
                    pl.when(place.has(dim, up))(
                        lambda dim=dim, up=up: signal(
                            self.ready.at[1 + 2 * dim + (1 if up else 0)], place.near(dim, up)
                        )
                    )
            pl.semaphore_wait(self.ready.at[0], 1)
        per = place.sizes[1] * place.sizes[2]

        def copy(j):
            owner = 2 * (self.lo * per + j) + 1 - place.core
            return remote(
                self.units.at(owner), self.land.at(j), self.sems.at[0], self.sems.at[1], place.sibling
            )

        loop(self.count, lambda j: copy(j).start())
        self.shared += self.count

    def allow(self, dim):
        if self.ready is None:
            return
        for up in (True, False):
            pl.when(self.place.has(dim, up))(
                lambda up=up: pl.semaphore_wait(self.ready.at[1 + 2 * dim + (0 if up else 1)], 1)
            )

    def push(self, cond, dim, q, sem, slot, device):
        owner = self.place.owner(q)
        target = self.unit(dim, q) * landing(self.place.sizes[dim]) + slot
        recv = self.recv_at[dim] + target
        if cond is None:
            self.shared += 1
            sem, recv = 0, 1 + dim

        def copy():
            return remote(
                self.units.at(owner),
                self.land.at(self.land_at[dim] + target),
                self.sems.at[sem],
                self.sems.at[recv],
                device,
            )

        gated(cond, lambda: copy().start())
        if cond is not None:
            self.waits.append(lambda: gated(cond, lambda: copy().wait_send()))

    def arrived(self, sem, count):
        piece = self.land.stretch(count)
        remote(
            piece, piece, self.sems.at[0], self.sems.at[sem], self.place.sibling
        ).wait_recv()

    def pull(self, dim, q, slot):
        target = self.unit(dim, q) * landing(self.place.sizes[dim]) + slot
        piece = self.land.at(self.land_at[dim] + target)
        remote(
            piece,
            piece,
            self.sems.at[0],
            self.sems.at[self.recv_at[dim] + target],
            self.place.sibling,
        ).wait_recv()
        self.add(self.place.owner(q), self.land_at[dim] + target)

    def first(self, dim, q):
        place = self.place
        n, p = place.sizes[dim], place.pos[dim]
        u = self.unit(dim, q)
        if n == 2:
            toward = place.me + (1 - 2 * p) * place.step[dim]
            self.push(None, dim, q, self.up_at[dim] + u * n, 0, toward)
            return
        for up in (True, False):
            away = (q[dim] > 0) if up else (q[dim] < n - 1)
            self.push(
                (p == (0 if up else n - 1)) & away,
                dim,
                q,
                (self.up_at if up else self.down_at)[dim] + u * n + q[dim],
                self.slot_up(q[dim], 0) if up else self.slot_down(n, q[dim], n - 1),
                place.near(dim, up),
            )

    @staticmethod
    def slot_up(q, p):
        return q - (p + 1)

    @staticmethod
    def slot_down(n, q, p):
        to = p - 1
        return q + (n - to if to > 0 else 0)

    def order(self, dim):
        place = self.place
        if place.sizes[dim] == 2:
            return [1 - place.pos[dim], place.pos[dim]]
        return list(range(place.sizes[dim]))

    def mine(self, dim, at):
        return at is self.place.pos[dim]

    def pairs(self):
        place = self.place
        self.allow(2)
        self.arrived(1, self.count)
        for qb in self.order(2):
            for qa in self.order(1):
                for q0 in range(self.lo, self.hi):
                    q = (q0, qa, qb)
                    j = (q0 - self.lo) * place.half[0] + qa * place.half[1] + qb * place.half[2]
                    self.add(place.owner(q), j)
                    if not self.mine(2, qb):
                        self.first(2, q)

    def along(self, dim):
        place = self.place
        n, p = place.sizes[dim], place.pos[dim]
        self.allow(dim - 1)
        if dim == 2:
            rows = [(q0, qa) for qa in self.order(1) for q0 in range(self.lo, self.hi)]
        else:
            rows = [(q0,) for q0 in range(self.lo, self.hi)]

        def whole(row, at):
            return row + (at,) + place.pos[dim + 1 :]

        if n == 2:
            self.arrived(1 + dim, len(rows))
            for row in rows:
                q = whole(row, p)
                self.add(place.owner(q), self.land_at[dim] + self.unit(dim, q))
                if not self.mine(dim - 1, row[dim - 1]):
                    self.first(dim - 1, whole(row, p))
        else:
            for k in range(1, n):
                self.hop(dim, k, [whole(row, None) for row in rows])
            for row in rows:
                self.first(dim - 1, whole(row, p))

    def hop(self, dim, k, rows):
        place = self.place
        n, p = place.sizes[dim], place.pos[dim]
        lo, hi = (self.lo, self.hi) if dim == 0 else (0, n)
        for up in (True, False):
            here = k if up else n - 1 - k
            cond = p == here
            span = range(max(lo, here), hi) if up else range(lo, min(hi, here + 1))
            if len(span) == 0:
                continue

            def receive(up=up, here=here, span=span):
                for row in rows:
                    for at in span:
                        slot = at - here if up else at + (n - here if here > 0 else 0)
                        q = row[:dim] + (at,) + row[dim + 1 :]
                        self.pull(dim, q, slot)
                        if at != here:
                            self.hop_copy(dim, q, up, here).start()

            pl.when(cond)(receive)
            for row in rows:
                for at in span:
                    if at != here:
                        q = row[:dim] + (at,) + row[dim + 1 :]
                        self.waits.append(
                            lambda cond=cond, q=q, up=up, here=here: pl.when(cond)(
                                lambda: self.hop_copy(dim, q, up, here).wait_send()
                            )
                        )

    def hop_copy(self, dim, q, up, here):
        place = self.place
        n = place.sizes[dim]
        u = self.unit(dim, q)
        slot = self.slot_up(q[dim], here) if up else self.slot_down(n, q[dim], here)
        target = u * landing(n) + slot
        return remote(
            self.units.at(place.owner(q)),
            self.land.at(self.land_at[dim] + target),
            self.sems.at[(self.up_at if up else self.down_at)[dim] + u * n + q[dim]],
            self.sems.at[self.recv_at[dim] + target],
            place.near(dim, up),
        )

    def finish(self):
        for wait in self.waits:
            wait()
        piece = self.land.stretch(self.shared)
        remote(
            piece, piece, self.sems.at[0], self.sems.at[1], self.place.sibling
        ).wait_send()
        self.waits, self.shared = [], 0


class Total:
    def __init__(self, place, land, sems):
        self.place, self.land, self.sems = place, land, sems
        self.sizes = (2,) + place.sizes[::-1]
        self.at = [sum(self.sizes[:k]) for k in range(4)]
        self.waits = []

    @staticmethod
    def slots(devices):
        return 6 + 2 * math.isqrt(devices // 8)

    def lines(self, k):
        place = self.place
        if k == 0:
            return place.core, [(1, 1 - place.core, place.sibling)]
        return place.plain[3 - k], place.peers(3 - k)

    def send(self, k, value):
        p, peers = self.lines(k)
        here = self.land.at[self.at[k] + p]
        self.land[self.at[k] + p] = value
        half = self.at[3] + self.sizes[3]
        for r, _, device in peers:

            def copy(r=r, device=device):
                sems = self.sems
                return remote(
                    here, here, sems.at[self.at[k] + r], sems.at[half + self.at[k] + p], device
                )

            copy().start()
            self.waits.append(lambda copy=copy: copy().wait_send())

    def take(self, k):
        _, peers = self.lines(k)
        half = self.at[3] + self.sizes[3]
        for r, at, device in peers:
            there = self.land.at[self.at[k] + at]
            remote(
                there, there, self.sems.at[0], self.sems.at[half + self.at[k] + at], device
            ).wait_recv()
        total = self.land[self.at[k]]
        for s in range(1, self.sizes[k]):
            total = total + self.land[self.at[k] + s]
        return total

    def pass_on(self, k):
        value = self.take(k)
        if k < 3:
            self.send(k + 1, value)
        return value

    def finish(self):
        for wait in self.waits:
            wait()
        self.waits = []


class Ring:
    def __init__(self, me, devices, land, sems):
        self.after = (me + 1) % devices
        self.before = (me + devices - 1) % devices
        self.land, self.sems = land, sems

    def copies(self, to_before, to_after):
        return (
            remote(to_before, self.land.at[1], self.sems.at[0], self.sems.at[1], self.before),
            remote(to_after, self.land.at[0], self.sems.at[2], self.sems.at[3], self.after),
        )

    def start(self, to_before, to_after):
        for copy in self.copies(to_before, to_after):
            copy.start()

    def wait(self, to_before, to_after):
        for copy in self.copies(to_before, to_after):
            copy.wait_recv()

    def finish(self, to_before, to_after):
        for copy in self.copies(to_before, to_after):
            copy.wait_send()


def unit_shape(amount):
    across = min(amount, PANEL)
    return amount // across * BLOCK_ROWS, across * BLOCK_COLS


def own_unit(units, me, blocks):
    across = units.cols // BLOCK_COLS
    rows = []
    for a in range(units.rows // BLOCK_ROWS):
        row = [blocks[a * across + b].astype(bf16) for b in range(across)]
        rows.append(jnp.concatenate(row, axis=1))
    units.put(me, jnp.concatenate(rows, axis=0))


def network(
    idx_ref,
    positions_ref,
    species_ref,
    counts_ref,
    cot_ref,
    scale_ref,
    shift_ref,
    weight_ref,
    state_ref,
    blocks_ref,
    late_in,
    energy_ref,
    forces_ref,
    vector_ref,
    first_out,
    late_out,
    first_w,
    late_w,
    hot,
    z_t,
    z_r,
    geo,
    yrow,
    env_b,
    ee_t,
    en2_t,
    s1_t,
    s2_t,
    gam,
    dlt,
    coef,
    ds_t,
    de_t,
    dy,
    dg,
    dw_t,
    dw_r,
    dpf,
    den,
    lat,
    hid,
    low0,
    act1,
    sl1,
    low1,
    act2,
    sl2,
    low2,
    stage,
    halo,
    force_in,
    sides,
    vector_in,
    pack_ref,
    low_gather,
    mid_gather,
    high_gather,
    late_gather,
    late_sems,
    first_sems,
    ring_sems,
    vector_sems,
    ready,
):
    s_r = dw_r
    fact = den

    wee_t = dw_t.at[:, 0:LATENT]
    we2_t = dw_t.at[0:128, 0:LATENT]
    devices = lax.axis_size("atoms")
    me = lax.axis_index("atoms")
    place = Place(devices)
    own_at = pack_ref.at[0:8]
    first_units = Units(first_w, *unit_shape(blocks_ref.shape[0]))
    late_units = Units(late_w, *unit_shape(late_in.shape[0]))
    top = place.sizes[0]
    middle = top // 2

    def pieces(k, count):
        return Units(first_w, first_units.rows, first_units.cols, part=(k, count))

    def free(ref, units, k=0, count=1):
        slots = Reduce.slots(devices, 1)
        return Units(ref, units.rows // count, units.cols, base=k * slots)

    gather_low = [Gather(place, pieces(k, PIECES), 0, 1, low_gather.at[k]) for k in range(PIECES)]
    gather_mid = Gather(place, first_units, 1, middle, mid_gather)
    gather_high = Gather(place, first_units, middle, top, high_gather)
    gather_late = Gather(place, late_units, 0, top, late_gather, True)
    sum_out = Reduce(
        place, late_units, middle, top, free(low2, late_units), late_sems.at[0], ready.at[0]
    )
    sum_lat = Reduce(
        place, late_units, 0, middle, free(sl2, late_units), late_sems.at[1], ready.at[1]
    )
    sum_first = [
        [
            Reduce(
                place,
                pieces(k, SUM_PIECES[z]),
                z,
                z + 1,
                free(ref, first_units, k, SUM_PIECES[z]),
                first_sems.at[PIECES * z + k],
                ready.at[2 + z] if k == 0 else None,
            )
            for k in range(SUM_PIECES[z])
        ]
        for z, ref in enumerate((hid, low0, low2, act2))
    ]

    def advance(z, stage):
        for part in sum_first[z]:
            part.stage(stage)
    link_halo = Ring(me, devices, halo, ring_sems.at[0])
    link_force = Ring(me, devices, force_in, ring_sems.at[1])
    sum_vector = Total(place, vector_in, vector_sems)

    barrier = pltpu.get_barrier_semaphore()
    partners = [place.sibling, link_halo.before, link_halo.after]
    for dim in range(3):
        partners += [device for _, _, device in place.peers(dim)]
    for device in partners:
        signal(barrier, device)
    for part in (slice(0, PLANE), slice(PLANE, LANES)):
        pack_ref[0:3, part] = positions_ref[...]
        pack_ref[3:4, part] = species_ref[...].astype(f32)
        pack_ref[4:5, part] = counts_ref[...].astype(f32)
        pack_ref[5:6, part] = cot_ref[...]
    pack_ref[6:16] = jnp.zeros((10, LANES), f32)
    pack_ref[6:7, 0:SPECIES] = scale_ref[...]
    pack_ref[7:8, 0:SPECIES] = shift_ref[...]
    pack_ref[8:9] = weight_ref[...]
    pack_ref[9:10] = state_ref[...]
    own_unit(first_units, me, blocks_ref)
    own_unit(late_units, me, late_in)
    pl.semaphore_wait(barrier, len(partners))
    link_halo.start(own_at, own_at)
    for part in gather_low:
        part.own()
    gather_high.own()

    ids = lax.broadcasted_iota(jnp.int32, (3 * PLANE, LANES), 0)

    whole = PLANE * devices
    coef[0, :, 0:SLOTS] = idx_ref[...].astype(f32)
    listed = coef[0].T[: SLOTS + 6].astype(jnp.int32) - (me - 1) * PLANE
    listed = jnp.where(
        listed < 0, listed + whole, jnp.where(listed >= whole, listed - whole, listed)
    )
    for t in range(TILES):
        near = jnp.concatenate([listed[2 * t : 2 * t + 1], listed[2 * t + 1 : 2 * t + 2]], axis=1)
        hot[:, t * LANES : (t + 1) * LANES] = jnp.where(ids == near, 1.0, 0.0).astype(bf16)

    link_halo.wait(own_at, own_at)
    own = pack_ref[0:8]
    lane = lax.broadcasted_iota(jnp.int32, (8, LANES), 1)
    row = lax.broadcasted_iota(jnp.int32, (8, LANES), 0)
    edge = spacing * devices
    x_row = row == 0
    before = halo[0] - jnp.where(x_row, jnp.where(me == 0, edge, 0.0), 0.0)
    after = halo[1] + jnp.where(x_row, jnp.where(me == devices - 1, edge, 0.0), 0.0)
    rank_y = ((lane & (PLANE - 1)) >> 3).astype(f32)
    rank_z = (lane & (SIDE - 1)).astype(f32)
    table = jnp.concatenate([jnp.where(lane < PLANE, before, own), after], axis=1)
    ranks = jnp.where(row == 4, rank_y, rank_z)
    table = jnp.where(
        jnp.concatenate([row, row], axis=1) < 4, table, jnp.concatenate([ranks, ranks], axis=1)
    )[:, : 3 * PLANE]
    ga, gb, gc = parts(table)
    got = nn(ga, hot[...]) + nn(gb, hot[...]) + nn(gc, hot[...])
    mine = jnp.concatenate([own] * TILES, axis=1)
    lane = lax.broadcasted_iota(jnp.int32, (1, ROWS), 1)
    slot = lane >> 6
    atom = lane & (PLANE - 1)
    for part in gather_low:
        part.column()
    for part in gather_low:
        part.second()
    gather_mid.own()
    gather_mid.column()

    def wrapped(step):
        return jnp.where(step > 1.5, -8.0, jnp.where(step < -1.5, 8.0, 0.0)) * spacing

    disp = [
        got[0:1] - mine[0:1],
        got[1:2] - mine[1:2] + wrapped(got[4:5] - (atom >> 3).astype(f32)),
        got[2:3] - mine[2:3] + wrapped(got[5:6] - (atom & (SIDE - 1)).astype(f32)),
    ]
    length = jnp.sqrt(disp[0] * disp[0] + disp[1] * disp[1] + disp[2] * disp[2])
    inverse = 1.0 / length
    unit = [disp[0] * inverse, disp[1] * inverse, disp[2] * inverse]
    angle = length * (math.pi / cutoff_radius)
    sin_k = [jnp.sin(angle)]
    cos_k = [jnp.cos(angle)]
    sin_k.append(2.0 * cos_k[0] * sin_k[0])
    cos_k.append(2.0 * cos_k[0] * cos_k[0] - 1.0)
    for k in range(2, BESSEL):
        sin_k.append(2.0 * cos_k[0] * sin_k[k - 1] - sin_k[k - 2])
        cos_k.append(2.0 * cos_k[0] * cos_k[k - 1] - cos_k[k - 2])
    sines = jnp.concatenate(sin_k, axis=0)
    cosines = jnp.concatenate(cos_k, axis=0)
    bessel = (math.sqrt(2.0 / cutoff_radius) * inverse) * sines
    scaled = length * (1.0 / cutoff_radius)
    t2 = scaled * scaled
    t4 = t2 * t2
    t5 = t4 * scaled
    t6 = t4 * t2
    envelope = 1.0 - 28.0 * t6 + 48.0 * (t6 * scaled) - 21.0 * (t4 * t4)
    denvelope = (-168.0 * t5 + 336.0 * t6 - 168.0 * (t6 * scaled)) * (1.0 / cutoff_radius)
    live = jnp.where(slot.astype(f32) < mine[4:5], 1.0, 0.0)

    kind = lax.broadcasted_iota(jnp.int32, (KINDS, LANES), 0).astype(f32)
    is_kind = kind == own[3:4]
    by_kind = own.T
    scale = jnp.sum(jnp.where(is_kind, by_kind[:KINDS, 6:7], 0.0), axis=0, keepdims=True)
    shift = jnp.sum(jnp.where(is_kind, by_kind[:KINDS, 7:8], 0.0), axis=0, keepdims=True)
    cot = jnp.concatenate([own[5:6] * scale] * TILES, axis=1) * live
    weight = cot * envelope

    root3 = math.sqrt(3.0)
    root15 = math.sqrt(15.0)
    root5 = math.sqrt(5.0)
    ux, uy, uz = unit
    yrow[0:8] = jnp.concatenate(
        [
            root3 * ux,
            root3 * uy,
            root3 * uz,
            root15 * ux * uy,
            root15 * uy * uz,
            0.5 * root5 * (3.0 * uz * uz - 1.0),
            root15 * ux * uz,
            0.5 * root15 * (ux * ux - uy * uy),
        ],
        axis=0,
    )
    yrow[8:16] = yrow[0:8] * (live * env_scale)
    yrow[16:17] = live * env_scale
    geo[0:8] = jnp.concatenate([ux, uy, uz, inverse, envelope, denvelope, live, cot], axis=0)
    geo[8:16] = math.sqrt(2.0 / cutoff_radius) * (
        (math.pi / cutoff_radius)
        * lax.broadcasted_iota(jnp.int32, (BESSEL, ROWS), 0).astype(f32)
        * cosines
        + (math.pi / cutoff_radius) * cosines
        - sines * inverse
    ) * inverse


    def one_hots(t):
        row = lax.broadcasted_iota(jnp.int32, (LANES, LANES), 0).astype(f32)
        here = jnp.where(row == own[3:4] + float(BESSEL), 1.0, 0.0)
        there = jnp.where(row == kinds_near[t] + float(BESSEL + SPECIES), 1.0, 0.0)
        return here + there

    kinds_near = [got[3:4, t * LANES : (t + 1) * LANES] for t in range(TILES)]
    gather_mid.second()
    for part in gather_low:
        part.third()
    gather_high.column()
    for t in range(TILES):
        at = slice(t * LANES, (t + 1) * LANES)
        column = jnp.concatenate([bessel[:, at], one_hots(t)[BESSEL:]], axis=0)
        z_t[:, at] = column.astype(bf16)
        z_r[at, :] = column.T.astype(bf16)
        env_b[at, :] = jnp.broadcast_to(envelope[:, at], (LANES, LANES)).T
        fact[at, :] = jnp.broadcast_to(weight[:, at], (LANES, LANES)).T
    for part in gather_low:
        part.across()


    def twice(x):
        return jnp.concatenate([x] * (STRIP // LANES), axis=1)

    def in_body(n, r):
        pre = nn(z_r[r], cols_panel(first_w, W_INPUT, n))
        hid[r, panel(n, STRIP)] = (pre * sigmoid(pre)).astype(bf16)

    loop_panels(in_body)
    gather_mid.third()
    gather_high.second()
    gather_late.own()
    gather_mid.across()

    def two_body(n, r):
        zero = nn(hid[r], cols_panel(first_w, W_TWO, n)) * twice(env_b[r])
        lat[r, panel(n, STRIP)] = zero
        low0[r, panel(n, STRIP)] = zero.astype(bf16)

    loop_panels(two_body)
    gather_high.third()

    def transposed_product(out, weights, right, width=256):
        at = 0
        while at < ROWS:
            end = min(at + width, ROWS)
            out[:, at:end] = nt(weights, right[at:end, :])
            at = end

    wee_t[0:128, :] = narrow(first_w, W_EMBED).T
    wee_t[128:256, :] = narrow(first_w, W_ENV_ONE).T
    transposed_product(ee_t, wee_t[...], low0)
    gather_late.column()

    def environment(out, v0_ref, v0_at, v1_at):
        for m in range(9):
            total = None
            begin = v0_at if m == 0 else v1_at
            y = yrow[16:17, :] if m == 0 else yrow[7 + m : 8 + m, :]
            for t in range(TILES):
                at = slice(t * LANES, (t + 1) * LANES)
                term = v0_ref[begin : begin + CHANNELS, at] * y[:, at]
                total = term if total is None else total + term
            out[m] = halves(total)

    def put_scalars(t, s_t, rows):
        s_t[:, lanes(t)] = jnp.concatenate(rows, axis=0).astype(bf16)
        filled = jnp.concatenate(rows + [jnp.zeros_like(rows[0])], axis=0)
        flipped = filled.T.astype(bf16)
        s_r[lanes(t), :] = flipped

    def weighted(y, first, count, source, offset):
        total = None
        for m in range(count):
            term = y[first + m : first + m + 1] * source[offset + m]
            total = term if total is None else total + term
        return total

    environment(gam, ee_t, 128, 192)

    def scalars_one(t):
        e0 = ee_t[0:64, lanes(t)]
        e1 = ee_t[64:128, lanes(t)]
        y = yrow[0:8, lanes(t)]
        put_scalars(
            t,
            s1_t,
            [e0 * gam[0], e1 * weighted(y, 0, 3, gam, 1), e1 * weighted(y, 3, 5, gam, 4)],
        )

    beside(6, lambda i: None, scalars_one)
    gather_high.across()

    def pre_one(n, r):
        pre = nn(low0[r], cols_panel(first_w, W_LAT_ONE, n)) + nn(
            s_r[r, : 3 * CHANNELS], cols_panel(first_w, W_SCAL_ONE, n)
        )
        sig = sigmoid(pre)
        act = pre * sig
        act1[r, panel(n, STRIP)] = act.astype(bf16)
        sl1[r, panel(n, STRIP)] = (sig + act * (1.0 - sig)).astype(bf16)

    loop_panels(pre_one)
    gather_late.second()

    def out_one(n, r):
        new = (lat[r, panel(n, STRIP)] + nn(act1[r], cols_panel(first_w, W_OUT_ONE, n))) * half_root
        lat[r, panel(n, STRIP)] = new
        low1[r, panel(n, STRIP)] = new.astype(bf16)

    loop_panels(out_one)
    gather_late.third()
    we2_t[...] = narrow(first_w, W_ENV_TWO).T
    transposed_product(en2_t, we2_t[...], low1)
    environment(dlt, en2_t, 0, 64)

    g0 = gam[0]
    coef[0] = g0 * dlt[0]
    for m in range(3):
        a, b = 1 + (m + 1) % 3, 1 + (m + 2) % 3
        coef[1 + m] = g0 * dlt[1 + m] + (gam[a] * dlt[b] - gam[b] * dlt[a])
    coef[9] = gam[1] * dlt[1] + gam[2] * dlt[2] + gam[3] * dlt[3]
    second = None
    for m in range(4, 9):
        coef[m] = g0 * dlt[m]
        term = gam[m] * dlt[m]
        second = term if second is None else second + term
    coef[10] = second

    def scalars_two(t):
        e0 = ee_t[0:64, lanes(t)]
        e1 = ee_t[64:128, lanes(t)]
        y = yrow[0:8, lanes(t)]
        put_scalars(
            t,
            s2_t,
            [
                e0 * coef[0],
                e1 * weighted(y, 0, 3, coef, 1) + e0 * coef[9],
                e1 * weighted(y, 3, 5, coef, 4) + e0 * coef[10],
            ],
        )

    beside(6, lambda i: None, scalars_two)
    gather_late.across()

    for part in gather_low + [gather_mid, gather_high, gather_late]:
        part.finish()
    def pre_two(n, r):
        pre = nn(low1[r], cols_panel(late_w, W_LAT_TWO, n)) + nn(
            s_r[r, : 3 * CHANNELS], cols_panel(first_w, W_SCAL_TWO, n)
        )
        sig = sigmoid(pre)
        act = pre * sig
        act2[r, panel(n, STRIP)] = act.astype(bf16)
        sl2[r, panel(n, STRIP)] = (sig + act * (1.0 - sig)).astype(bf16)

    loop_panels(pre_two)

    def out_two(n, r):
        new = (lat[r, panel(n, STRIP)] + nn(act2[r], cols_panel(late_w, W_OUT_TWO, n))) * half_root
        low2[r, panel(n, STRIP)] = new.astype(bf16)

    loop_panels(out_two)

    vec = jnp.broadcast_to(pack_ref[8:9], (8, LANES))
    stage[...] = narrow(first_w, W_FINAL)

    def read_out(i):
        r = pl.ds(pl.multiple_of(i * 416, 16), 416)
        pre = nn(low2[r, :], stage[...])
        sig = sigmoid(pre)
        final_act = pre * sig
        dpf[r, :] = (fact[r, :] * vec[0:1] * (sig + final_act * (1.0 - sig))).astype(bf16)
        fact[r, :] = final_act

    loop(4, read_out)
    fa, fb, _ = parts(fact[...])
    va, vb, _ = parts(vec)
    value = (nt(va, fa) + (nt(va, fb) + nt(vb, fa)))[0:1]
    geo_live = geo[6:7]
    geo_env = geo[4:5]
    geo_cot = geo[7:8]
    edge_energy = geo_live * geo_env * value
    summed = None
    for t in range(TILES):
        term = edge_energy[:, t * LANES : (t + 1) * LANES]
        summed = term if summed is None else summed + term
    energy_ref[...] = scale * halves(summed) + shift
    all_weights = jnp.broadcast_to(geo_cot * geo_env, (8, ROWS))
    wa, wb, _ = parts(all_weights)
    sum_vector.send(0, nn(wa, fa) + (nn(wa, fb) + nn(wb, fa)))
    geo[16:17] = geo_cot * value

    def big_step(out, where, left, right):
        def step(i):
            grad = tn(left[:, panel(i, STRIP)], right[...])
            out[pl.ds(pl.multiple_of(where[0] + i * STRIP, 64), STRIP), :] = grad.astype(bf16)

        return step

    def big_grad(out, where, left, right):
        loop(LATENT // STRIP, big_step(out, where, left, right))

    def wide_step(out, where, left, right):
        def step(n):
            out[where[0] : where[0] + where[1], panel(n)] = nn(
                left[...], right[:, panel(n)]
            ).astype(bf16)

        return step

    def wide_grad(out, where, left, right):
        loop(4, wide_step(out, where, left, right))

    def narrow_grad(left, right, put):
        def step(n):
            put(n, nn(left, right[:, panel(n)]).T.astype(bf16))

        loop(4, step)

    def put_narrow(where, n, grad):
        row = pl.multiple_of(where[0] + n // 2 * BLOCK_ROWS, BLOCK_ROWS)
        col = pl.multiple_of(n % 2 * 512, 512)
        first_w[pl.ds(row, BLOCK_ROWS), pl.ds(col, 512)] = jnp.concatenate(
            [grad[b * BLOCK_ROWS : (b + 1) * BLOCK_ROWS] for b in range(4)], axis=1
        )

    def put_stage(n, grad):
        stage[panel(n), :] = grad

    def back_final(n, r):
        grad = nt(dpf[r], narrow_panel(first_w, W_FINAL, n)) * half_root
        lat[r, panel(n, STRIP)] = grad
        low2[r, panel(n, STRIP)] = grad.astype(bf16)

    def back_out_two(n, r):
        grad = nt(low2[r], rows_panel(late_w, W_OUT_TWO, n))
        sl2[r, panel(n, STRIP)] = (grad * sl2[r, panel(n, STRIP)].astype(f32)).astype(bf16)

    def tensors_two(t):
        e0 = ee_t[0:64, lanes(t)]
        e1 = ee_t[64:128, lanes(t)]
        y = yrow[0:8, lanes(t)]
        r0 = ds_t[0:64, lanes(t)]
        r1 = ds_t[64:128, lanes(t)]
        r2 = ds_t[128:192, lanes(t)]
        de_t[0:64, lanes(t)] = r0 * coef[0] + r1 * coef[9] + r2 * coef[10]
        de_t[64:128, lanes(t)] = r1 * weighted(y, 0, 3, coef, 1) + r2 * weighted(y, 3, 5, coef, 4)
        p1 = r1 * e1
        p2 = r2 * e1
        rows = []
        for m in range(8):
            p = p1 if m < 3 else p2
            rows.append(jnp.sum(p * coef[1 + m], axis=0, keepdims=True))
            dg[1 + m] += p * y[m : m + 1]
        dy[:, lanes(t)] = jnp.concatenate(rows, axis=0)
        dg[0] += r0 * e0
        dg[9] += r1 * e0
        dg[10] += r2 * e0

    def environment_back(t, grads, source, v1_at, at):
        y4 = yrow[8:16, lanes(t)]
        l4 = yrow[16:17, lanes(t)]
        v1 = source[v1_at : v1_at + 64, lanes(t)]
        low = l4 * grads[0]
        high = weighted(y4, 0, 8, grads, 1)
        both = jnp.concatenate([low, high], axis=0)
        dw_t[at : at + 128, lanes(t)] = both.astype(bf16)
        dw_r[lanes(t), at : at + 128] = both.T.astype(bf16)
        v1 = v1 * l4
        rows = [jnp.sum(v1 * grads[1 + m], axis=0, keepdims=True) for m in range(8)]
        dy[:, lanes(t)] += jnp.concatenate(rows, axis=0)

    def back_lat_two(n, r):
        grad = (
            lat[r, panel(n, STRIP)]
            + nt(sl2[r], rows_panel(late_w, W_LAT_TWO, n))
            + nt(dw_r[r, 128:256], narrow_panel(first_w, W_ENV_TWO, n))
        ) * half_root
        lat[r, panel(n, STRIP)] = grad
        act2[r, panel(n, STRIP)] = grad.astype(bf16)

    def back_out_one(n, r):
        grad = nt(act2[r], rows_panel(first_w, W_OUT_ONE, n))
        sl1[r, panel(n, STRIP)] = (grad * sl1[r, panel(n, STRIP)].astype(f32)).astype(bf16)

    def tensors_one(t):
        e0 = ee_t[0:64, lanes(t)]
        e1 = ee_t[64:128, lanes(t)]
        y = yrow[0:8, lanes(t)]
        r0 = ds_t[0:64, lanes(t)]
        r1 = ds_t[64:128, lanes(t)]
        r2 = ds_t[128:192, lanes(t)]
        low = de_t[0:64, lanes(t)] + r0 * gam[0]
        high = (
            de_t[64:128, lanes(t)]
            + r1 * weighted(y, 0, 3, gam, 1)
            + r2 * weighted(y, 3, 5, gam, 4)
        )
        both = jnp.concatenate([low, high], axis=0)
        dw_t[0:128, lanes(t)] = both.astype(bf16)
        dw_r[lanes(t), 0:128] = both.T.astype(bf16)
        p1 = r1 * e1
        p2 = r2 * e1
        rows = []
        for m in range(8):
            p = p1 if m < 3 else p2
            rows.append(jnp.sum(p * gam[1 + m], axis=0, keepdims=True))
            coef[1 + m] += p * y[m : m + 1]
        dy[:, lanes(t)] += jnp.concatenate(rows, axis=0)
        coef[0] += r0 * e0

    def back_lat_one(n, r):
        both = jnp.concatenate(
            [narrow_panel(first_w, W_EMBED, n), narrow_panel(first_w, W_ENV_ONE, n)], axis=1
        )
        grad = (
            lat[r, panel(n, STRIP)]
            + nt(sl1[r], rows_panel(first_w, W_LAT_ONE, n))
            + nt(dw_r[r], both)
        )
        low1[r, panel(n, STRIP)] = (grad * twice(env_b[r])).astype(bf16)
        part = grad * low0[r, panel(n, STRIP)].astype(f32)
        for b in range(STRIP // LANES):
            den[r] += part[:, b * LANES : (b + 1) * LANES]

    def back_two(n, r):
        grad = nt(low1[r], rows_panel(first_w, W_TWO, n))
        pre = nn(z_r[r], cols_panel(first_w, W_INPUT, n))
        sig = sigmoid(pre)
        act1[r, panel(n, STRIP)] = (grad * (sig + pre * sig * (1.0 - sig))).astype(bf16)

    def lat_one_grad(low, high):
        grad = tn(low0[:, low:high], sl1[...])
        first_w[W_LAT_ONE[0] + low : W_LAT_ONE[0] + high, :] = grad.astype(bf16)

    narrow_grad(dpf[...].T, low2, put_stage)
    loop_panels(back_final)
    loop(4, lambda n: put_narrow(W_FINAL, n, stage[panel(n), :]))
    loop_panels(back_out_two)
    transposed_product(ds_t, first_w[W_SCAL_TWO[0] : W_SCAL_TWO[0] + W_SCAL_TWO[1], :], sl2)
    dg[...] = jnp.zeros_like(dg)
    beside(2, big_step(late_w, W_OUT_TWO, act2, low2), tensors_two)
    sum_vector.pass_on(0)
    sum_out.stage(0)
    total = [halves(dg[m]) for m in range(11)]
    g0 = gam[0]
    d0 = dlt[0]
    new_g0 = total[0] * d0
    for m in range(1, 9):
        new_g0 = new_g0 + total[m] * dlt[m]
    dlt_grads = [total[0] * g0]
    gam_grads = [new_g0]
    for m in range(3):
        a, b = 1 + (m + 1) % 3, 1 + (m + 2) % 3
        dlt_grads.append(
            total[1 + m] * g0 + total[9] * gam[1 + m] + (total[a] * gam[b] - total[b] * gam[a])
        )
        gam_grads.append(total[9] * dlt[1 + m] + (dlt[a] * total[b] - dlt[b] * total[a]))
    for m in range(4, 9):
        dlt_grads.append(total[m] * g0 + total[10] * gam[m])
        gam_grads.append(total[10] * dlt[m])
    for m in range(9):
        dlt[m] = dlt_grads[m]
        dg[m] = gam_grads[m]
    beside(
        4,
        wide_step(first_w, W_SCAL_TWO, s2_t, sl2),
        lambda t: environment_back(t, dlt, en2_t, 64, 128),
    )
    sum_out.stage(1)
    loop_panels(back_lat_two)
    sum_out.stage(2)
    big_grad(late_w, W_LAT_TWO, low1, sl2)
    sum_vector.pass_on(1)
    sum_out.stage(3)
    sum_lat.stage(0)
    loop_panels(back_out_one)
    sum_out.stage(4)
    sum_lat.stage(1)
    transposed_product(ds_t, first_w[W_SCAL_ONE[0] : W_SCAL_ONE[0] + W_SCAL_ONE[1], :], sl1)
    narrow_grad(dw_t[128:256, :], low1, functools.partial(put_narrow, W_ENV_TWO))
    for m in range(9):
        coef[m] = jnp.zeros((CHANNELS, LANES), f32)
    beside(2, big_step(first_w, W_OUT_ONE, act1, act2), tensors_one)
    sum_vector.pass_on(2)
    sum_out.stage(5)
    sum_lat.stage(2)
    advance(3, 0)
    for m in range(9):
        dg[m] = dg[m] + halves(coef[m])
    beside(
        4,
        wide_step(first_w, W_SCAL_ONE, s1_t, sl1),
        lambda t: environment_back(t, dg, ee_t, 192, 128),
    )
    advance(3, 1)
    sum_out.stage(6)
    sum_lat.stage(3)
    den[...] = jnp.zeros_like(den)
    loop_panels(back_lat_one)
    lat_one_grad(640, 1024)
    sum_lat.stage(4)
    advance(3, 2)
    advance(2, 0)
    loop_panels(back_two)
    sum_lat.stage(5)
    advance(3, 3)
    advance(2, 1)
    big_grad(first_w, W_TWO, hid, low1)
    transposed_product(ds_t.at[0:64], first_w[0:64, :], act1)
    wide_grad(first_w, W_INPUT, z_t, act1)
    advance(0, 0)
    advance(2, 2)
    narrow_grad(dw_t[0:128, :], low0, functools.partial(put_narrow, W_EMBED))
    narrow_grad(dw_t[128:256, :], low0, functools.partial(put_narrow, W_ENV_ONE))
    advance(3, 4)
    advance(0, 1)
    lat_one_grad(0, 384)
    lat_one_grad(384, 640)
    advance(1, 0)
    advance(3, 5)
    advance(2, 3)
    sum_lat.stage(6)
    advance(0, 2)
    dbessel = ds_t[0:8, :]
    da, db, _ = parts(den[...])
    ones = jnp.ones((8, LANES), bf16)
    through = (nt(ones, da) + nt(ones, db))[0:1]
    ux, uy, uz = geo[0:1], geo[1:2], geo[2:3]
    inverse = geo[3:4]
    envelope = geo[4:5]
    denv = geo[16:17] + through / envelope
    dlength = jnp.sum(dbessel * geo[8:16], axis=0, keepdims=True) + denv * geo[5:6]
    g = [dy[m : m + 1, :] for m in range(8)]
    dux = root3 * g[0] + root15 * (uy * g[3] + uz * g[6] + ux * g[7])
    duy = root3 * g[1] + root15 * (ux * g[3] + uz * g[4] - uy * g[7])
    duz = root3 * g[2] + root15 * (uy * g[4] + ux * g[6]) + (3.0 * root5) * uz * g[5]
    along = dlength - (ux * dux + uy * duy + uz * duz) * inverse
    near = jnp.concatenate(
        [
            dux * inverse + ux * along,
            duy * inverse + uy * along,
            duz * inverse + uz * along,
            jnp.zeros((5, ROWS), f32),
        ],
        axis=0,
    )
    summed = None
    for t in range(TILES):
        term = near[:, t * LANES : (t + 1) * LANES]
        summed = term if summed is None else summed + term
    centre = halves(summed)
    na, nb, nc = parts(near)
    spread = nt(na, hot[...]) + nt(nb, hot[...]) + nt(nc, hot[...])
    sides[0] = spread[:, :LANES]
    sides[1, :, 0:PLANE] = spread[:, LANES:]
    link_force.start(sides.at[0], sides.at[1])
    advance(1, 1)
    advance(2, 4)
    advance(0, 3)
    advance(3, 6)
    advance(0, 4)
    for step in range(6):
        for k in range(max(SUM_PIECES[:3])):
            for z, after in ((0, 5), (1, 2), (2, 5)):
                if k < SUM_PIECES[z] and after <= after + step - k < 7:
                    sum_first[z][k].stage(after + step - k)
    link_force.wait(sides.at[0], sides.at[1])
    forces_ref[...] = (
        centre - pltpu.roll(sides[0], PLANE, 1) - force_in[1] - force_in[0]
    )
    total = sum_vector.pass_on(3)
    normed = total * lax.rsqrt(jnp.sum(total[0:1] * total[0:1]) * (1.0 / FINAL) + epsilon)
    state = decay_rate * pack_ref[9:10] + (1.0 - decay_rate) * normed * normed
    vector_ref[0:1] = total[0:1]
    vector_ref[1:2] = state[0:1]
    vector_ref[2:3] = (pack_ref[8:9] - vector_rate * normed * lax.rsqrt(state + epsilon))[0:1]
    first_out[...] = first_units.get(me)
    late_out[...] = late_units.get(me)
    for group in sum((list(parts) for parts in sum_first), [sum_out, sum_lat, sum_vector]):
        group.finish()
    link_halo.finish(own_at, own_at)
    link_force.finish(sides.at[0], sides.at[1])


def run_network(devices, small, blocks, late):
    S = jax.ShapeDtypeStruct
    wide = pltpu.VMEM((ROWS, LATENT), bf16)
    slab = pltpu.VMEM((ROWS, LANES), f32)
    panels = lambda amount: pltpu.VMEM((amount * devices // PANEL * BLOCK_ROWS, WIDE), bf16)
    scratch = [
        panels(blocks.shape[0]),
        panels(late.shape[0]),
        pltpu.VMEM((3 * PLANE, ROWS), bf16),
        pltpu.VMEM((LANES, ROWS), bf16),
        pltpu.VMEM((ROWS, LANES), bf16),
        pltpu.VMEM((24, ROWS), f32),
        pltpu.VMEM((24, ROWS), f32),
        slab,
        pltpu.VMEM((256, ROWS), f32),
        pltpu.VMEM((128, ROWS), f32),
        pltpu.VMEM((192, ROWS), bf16),
        pltpu.VMEM((192, ROWS), bf16),
        pltpu.VMEM((9, CHANNELS, LANES), f32),
        pltpu.VMEM((9, CHANNELS, LANES), f32),
        pltpu.VMEM((11, CHANNELS, LANES), f32),
        pltpu.VMEM((192, ROWS), f32),
        pltpu.VMEM((128, ROWS), f32),
        pltpu.VMEM((8, ROWS), f32),
        pltpu.VMEM((11, CHANNELS, LANES), f32),
        pltpu.VMEM((256, ROWS), bf16),
        pltpu.VMEM((ROWS, 256), bf16),
        pltpu.VMEM((ROWS, LANES), bf16),
        slab,
        pltpu.VMEM((ROWS, LATENT), f32),
    ] + [wide] * 8 + [
        pltpu.VMEM((LATENT, LANES), bf16),
        pltpu.VMEM((2, 8, LANES), f32),
        pltpu.VMEM((2, 8, LANES), f32),
        pltpu.VMEM((2, 8, LANES), f32),
        pltpu.VMEM((Total.slots(devices), 8, LANES), f32),
        pltpu.VMEM((16, LANES), f32),
        pltpu.SemaphoreType.DMA((PIECES, Gather.amount(devices, 1))),
        pltpu.SemaphoreType.DMA((Gather.amount(devices, 1),)),
        pltpu.SemaphoreType.DMA((Gather.amount(devices, 2),)),
        pltpu.SemaphoreType.DMA((Gather.amount(devices, 4),)),
        pltpu.SemaphoreType.DMA((2, Reduce.amount(devices, 2))),
        pltpu.SemaphoreType.DMA((4 * PIECES, Reduce.amount(devices, 1))),
        pltpu.SemaphoreType.DMA((2, 4)),
        pltpu.SemaphoreType.DMA((2 * Total.slots(devices),)),
        pltpu.SemaphoreType.REGULAR((6, 7)),
    ]
    vmem = pl.BlockSpec(memory_space=pltpu.VMEM)
    return pl.pallas_call(
        network,
        out_shape=[
            S((1, LANES), f32),
            S((8, LANES), f32),
            S((8, LANES), f32),
            S(unit_shape(blocks.shape[0]), bf16),
            S(unit_shape(late.shape[0]), bf16),
        ],
        in_specs=[vmem] * (len(small) + 2),
        out_specs=[vmem] * 5,
        scratch_shapes=scratch,
        compiler_params=pltpu.CompilerParams(
            vmem_limit_bytes=63 << 20, collective_id=0, has_side_effects=True
        ),
        name="network",
    )(*small, blocks, late)


def shampoo(
    energy,
    force,
    vectors,
    grads,
    left,
    right,
    left_root,
    right_root,
    master,
    late_grads,
    late_left,
    late_right,
    late_left_root,
    late_right_root,
    late_master,
    energy_out,
    force_out,
    vector_out,
    state_out,
    moved_out,
    *outs,
):
    energy_out[...] = energy[:, :PLANE]
    force_out[...] = force[0:3, :PLANE]
    vector_out[...] = vectors[0:1]
    state_out[...] = vectors[1:2]
    moved_out[...] = vectors[2:3]

    todo = []
    for j in range(left.shape[0]):
        todo.append((grads, j, left, right, left_root, right_root, master) + outs[:4])
    for j in range(late_left.shape[0]):
        todo.append(
            (late_grads, j, late_left, late_right, late_left_root, late_right_root, late_master)
            + outs[4:]
        )
    size = 1.0 / (BLOCK_ROWS * BLOCK_COLS)
    held, scales, steps = [], [], []
    for panels, j, left, *_ in todo:
        per = panels.shape[1] // BLOCK_COLS
        at = pl.program_id(0) * left.shape[0] + j
        row = pl.multiple_of(at // per * BLOCK_ROWS, BLOCK_ROWS)
        col = pl.multiple_of(at % per * BLOCK_COLS, BLOCK_COLS)
        held.append(panels[pl.ds(row, BLOCK_ROWS), pl.ds(col, BLOCK_COLS)])
    for g, (_, j, *_, grad_out, left_out, right_out, master_out) in zip(held, todo):
        grad = g.astype(f32)
        grad_out[j] = grad
        scales.append(lax.rsqrt(jnp.sum(grad * grad, keepdims=True) * size + epsilon))
    turned = []
    for g, (_, j, left, right, left_root, *_) in zip(held, todo):
        turned.append(nn(left_root[j].astype(bf16), g))
    for g, s, (_, j, left, right, *_, grad_out, left_out, right_out, master_out) in zip(
        held, scales, todo
    ):
        square = (1.0 - decay_rate) * s * s
        left_out[j] = decay_rate * left[j] + square * nt(g, g)
        right_out[j] = decay_rate * right[j] + square * tn(g, g)
    for turn, s, (_, j, left, right, left_root, right_root, *_) in zip(turned, scales, todo):
        steps.append(nn((turn * s).astype(bf16), right_root[j].astype(bf16)))
    for step, (_, j, left, right, left_root, right_root, master, *_, master_out) in zip(steps, todo):
        slope = lax.rsqrt(jnp.sum(step * step, keepdims=True) * size + epsilon)
        master_out[j] = master[j] - (learn_rate * slope) * step


def run_shampoo(energy, force, vectors, first, late):
    S = jax.ShapeDtypeStruct
    steps = min(2, late[1].shape[0])

    def whole(x):
        return pl.BlockSpec(x.shape, lambda i: (0,) * len(x.shape))

    def share(x):
        return pl.BlockSpec((x.shape[0] // steps,) + x.shape[1:], lambda i: (i, 0, 0))

    small = [S((1, PLANE), f32), S((3, PLANE), f32)] + [S((1, FINAL), f32)] * 3
    grown = []
    for group in (first, late):
        left, right, _, _, master = group[1:]
        grown += [S(x.shape, f32) for x in (master, left, right, master)]
    return pl.pallas_call(
        shampoo,
        grid=(steps,),
        out_shape=small + grown,
        in_specs=[whole(energy), whole(force), whole(vectors)]
        + [whole(first[0])]
        + [share(x) for x in first[1:]]
        + [whole(late[0])]
        + [share(x) for x in late[1:]],
        out_specs=[whole(x) for x in small] + [share(x) for x in grown],
        compiler_params=pltpu.CompilerParams(vmem_limit_bytes=60 << 20),
        name="shampoo",
    )(energy, force, vectors, *first, *late)


def local(
    positions,
    species,
    neighbours,
    counts,
    species_scale,
    species_shift,
    energy_cot,
    blocks,
    left,
    right,
    left_root,
    right_root,
    late_blocks,
    late_left,
    late_right,
    late_left_root,
    late_right_root,
    out_vector,
    vector_state,
):
    devices = lax.axis_size("atoms")
    small = (
        neighbours.reshape(PLANE, SLOTS),
        positions,
        species[None],
        counts[None],
        energy_cot[None],
        species_scale[None],
        species_shift[None],
        out_vector[None],
        vector_state[None],
    )
    energy, force, vectors, first_units, late_units = run_network(
        devices, small, blocks, late_blocks
    )
    out = run_shampoo(
        energy,
        force,
        vectors,
        (first_units, left, right, left_root, right_root, blocks),
        (late_units, late_left, late_right, late_left_root, late_right_root, late_blocks),
    )
    energies, forces, vector_grad, new_state, new_vector = out[:5]
    return (
        energies.reshape(-1),
        forces,
        *out[5:],
        vector_grad.reshape(-1),
        new_state.reshape(-1),
        new_vector.reshape(-1),
    )


def solution(mesh):
    row = P("atoms")
    block = P("atoms", None, None)
    placed = (
        (P(None, "atoms"), row, row, row, P(), P(), row)
        + (block,) * 10
        + (P(), P())
    )
    return jax.shard_map(
        local,
        mesh=mesh,
        in_specs=placed,
        out_specs=(row, P(None, "atoms")) + (block,) * 8 + (P(), P(), P()),
        check_vma=False,
    )
```

```python
import functools
import math

import jax
import jax.numpy as jnp
from jax import lax
from jax.experimental import pallas as pl
from jax.experimental.pallas import tpu as pltpu
from jax.sharding import PartitionSpec as P

SIDE = 8
SLOTS = 26
SPECIES = 60
BESSEL = 8
CHANNELS = 64
LATENT = 1024
FINAL = 128
BLOCK_ROWS = 64
BLOCK_COLS = 128
PLANE = SIDE * SIDE

f32 = jnp.float32
bf16 = jnp.bfloat16
spacing = 1.6
cutoff_radius = 4.0
env_scale = 0.25
half_root = 0.7071067811865476
decay_rate = 0.5
learn_rate = 0.02
vector_rate = 0.03
epsilon = 1e-06

LANES = 128
ROWS = SLOTS * PLANE
TILES = ROWS // LANES
KINDS = 64

PANEL = 8
WIDE = PANEL * BLOCK_COLS
W_INPUT = (0, 128)
W_TWO = (128, 1024)
W_EMBED = (1152, 128)
W_ENV_ONE = (1280, 128)
W_LAT_ONE = (1408, 1024)
W_SCAL_ONE = (2432, 192)
W_OUT_ONE = (2624, 1024)
W_ENV_TWO = (3648, 128)
W_SCAL_TWO = (3776, 192)
W_FINAL = (3968, 128)
W_LAT_TWO = (0, 1024)
W_OUT_TWO = (1024, 1024)

MESH = pl.DeviceIdType.MESH


def nn(a, b):
    return lax.dot_general(a, b, (((1,), (0,)), ((), ())), preferred_element_type=f32)


def nt(a, b):
    return lax.dot_general(a, b, (((1,), (1,)), ((), ())), preferred_element_type=f32)


def tn(a, b):
    return lax.dot_general(a, b, (((0,), (0,)), ((), ())), preferred_element_type=f32)


def cols_panel(ref, where, n):
    return ref[where[0] : where[0] + where[1], panel(n, STRIP)]


def rows_panel(ref, where, n):
    return ref[pl.ds(pl.multiple_of(where[0] + n * STRIP, 64), STRIP), :]


def narrow(ref, where):
    pieces = []
    for j in range(LATENT // BLOCK_ROWS):
        row = where[0] + j // PANEL * BLOCK_ROWS
        col = j % PANEL * BLOCK_COLS
        pieces.append(ref[row : row + BLOCK_ROWS, col : col + BLOCK_COLS])
    return jnp.concatenate(pieces, axis=0)


def narrow_panel(ref, where, n):
    part = ref[pl.ds(pl.multiple_of(where[0] + n * BLOCK_ROWS, BLOCK_ROWS), BLOCK_ROWS), :]
    return jnp.concatenate([part[:, b * 128 : (b + 1) * 128] for b in range(PANEL)], axis=0)


def sigmoid(x):
    return 0.5 * jnp.tanh(0.5 * x) + 0.5


def halves(x):
    return x + pltpu.roll(x, PLANE, 1)


def lanes(t):
    if isinstance(t, int):
        return pl.ds(t * LANES, LANES)
    return pl.ds(pl.multiple_of(t * LANES, LANES), LANES)


def panel(n, width=256):
    return pl.ds(pl.multiple_of(n * width, width), width)


STRIP = 512
CHUNKS = 2
PIECES = 2
SUM_PIECES = (2, 4, 1, 1)
CHUNK = ROWS // CHUNKS


def loop_panels(body):
    def step(n):
        for c in range(CHUNKS):
            body(n, slice(c * CHUNK, (c + 1) * CHUNK))

    loop(LATENT // STRIP, step)


def beside(count, step, tile):
    share = TILES // count

    def body(i):
        step(i)
        for u in range(share):
            tile(i * share + u)

    loop(count, body)
    for t in range(share * count, TILES):
        tile(t)


def loop(count, body):
    def step(i, carry):
        body(i)
        return carry

    lax.fori_loop(0, count, step, 0)


def parts(x):
    a = x.astype(bf16)
    rest = x - a.astype(f32)
    b = rest.astype(bf16)
    c = (rest - b.astype(f32)).astype(bf16)
    return a, b, c


class Place:
    def __init__(self, devices):
        side = math.isqrt(devices // 8)
        self.devices = devices
        self.sizes = (4, side, side)
        me = lax.axis_index("atoms")
        core = me % 2
        chip = me // 2
        last = chip % side
        middle = chip // side % side
        self.me = me
        self.core = core
        self.pos = (
            chip // (side * side),
            last + core * (middle - last),
            middle + core * (last - middle),
        )
        self.half = (side * side, 1 + core * (side - 1), side + core * (1 - side))
        self.step = tuple(2 * h for h in self.half)
        self.sibling = me + 1 - 2 * core
        self.plain = (self.pos[0], middle, last)
        self.plain_step = (2 * side * side, 2 * side, 2)

    def owner(self, q):
        return q[0] * self.step[0] + q[1] * self.step[1] + q[2] * self.step[2] + self.core

    def near(self, dim, up):
        return self.me + self.step[dim] if up else self.me - self.step[dim]

    def has(self, dim, up):
        return self.pos[dim] < self.sizes[dim] - 1 if up else self.pos[dim] > 0

    def peers(self, dim):
        n, p = self.sizes[dim], self.plain[dim]
        return [(r, (p + r) % n, self.me + ((p + r) % n - p) * self.plain_step[dim]) for r in range(1, n)]


class Units:
    def __init__(self, ref, rows, cols, base=0, part=(0, 1)):
        self.ref, self.rows, self.cols = ref, rows, cols
        self.per = WIDE // cols
        self.base = base
        self.high = rows // part[1]
        self.off = part[0] * self.high

    def window(self, s):
        s = s + self.base
        if self.per == 1:
            row, col = s * self.rows, slice(None)
        else:
            row = s // self.per * self.rows
            col = pl.ds(pl.multiple_of(s % self.per * self.cols, self.cols), self.cols)
        return (pl.ds(pl.multiple_of(row + self.off, 16), self.high), col)

    def at(self, s):
        return self.ref.at[self.window(s)]

    def get(self, s):
        return self.ref[self.window(s)]

    def put(self, s, value):
        self.ref[self.window(s)] = value

    def stretch(self, count):
        return self.ref.at[pl.ds(0, count * self.high // self.per), slice(None)]


def remote(src, dst, send, recv, device):
    return pltpu.make_async_remote_copy(
        src_ref=src,
        dst_ref=dst,
        send_sem=send,
        recv_sem=recv,
        device_id=(device,),
        device_id_type=MESH,
    )


def signal(sem, device):
    pl.semaphore_signal(sem, inc=1, device_id=(device,), device_id_type=MESH)


def others(place, dim):
    n, p = place.sizes[dim], place.pos[dim]
    if n == 2:
        return [(1 - p, None)]
    found = []
    for distance in range(1, n):
        found.append((p - distance, p >= distance))
        found.append((p + distance, p < n - distance))
    return found


def gated(cond, body):
    if cond is None:
        body()
    else:
        pl.when(cond)(body)


def both(a, b):
    return b if a is None else (a if b is None else a & b)


class Gather:
    def __init__(self, place, units, lo, hi, sems, direct=False, eager=True):
        self.place, self.units, self.lo, self.hi, self.sems = place, units, lo, hi, sems
        self.direct, self.eager = direct, eager
        _, na, nb = place.sizes
        self.waits = []
        self.shared = 0
        self.first_owner = 2 * lo * na * nb
        at = 2 * (hi - lo) * na * nb
        self.shared_send, self.core_recv = at, at + 1
        at += 2
        self.base = []
        for dim in range(3):
            length = (hi - lo) * (1, na, na * nb)[dim]
            self.base.append((at, at + length))
            at += 2 * length
        self.core_base = at

    @staticmethod
    def amount(devices, share):
        side = math.isqrt(devices // 8)
        return 2 + share * (2 + 2 * side + 5 * side * side)

    def linear(self, q, dim):
        _, na, nb = self.place.sizes
        q0 = q[0] - self.lo
        return (q0, q0 * na + q[1], (q0 * na + q[1]) * nb + q[2])[dim]

    def emit(self, cond, q, sem, device, core=False, once=None):
        owner = self.place.owner(q)
        common = cond is None or once is not None
        if common:
            sem = self.shared_send
            self.shared += 1 if once is None else once

        def copy():
            piece = self.units.at(owner)
            recv = self.core_recv if core else owner - self.first_owner
            return remote(piece, piece, self.sems.at[sem], self.sems.at[recv], device)

        gated(cond, lambda: copy().start())
        if not common:
            self.waits.append(lambda: gated(cond, lambda: copy().wait_send()))

    def onward(self, cond, q):
        place, p = self.place, self.place.pos[0]
        for up in (True, False):
            away = (p >= q[0]) if up else (p <= q[0])
            self.emit(
                both(cond, away & place.has(0, up)),
                q,
                self.base[0][0 if up else 1] + self.linear(q, 0),
                place.near(0, up),
            )

    def sideways(self, cond, q, dims, via=None, once=None):
        place = self.place
        for dim in dims:
            if place.sizes[dim] == 2:
                if dim != via:
                    toward = place.me + (1 - 2 * place.pos[dim]) * place.step[dim]
                    self.emit(
                        cond, q, self.base[dim][0] + self.linear(q, dim), toward, False, once
                    )
                continue
            for up in (True, False):
                open_end = place.has(dim, up)
                if dim == via:
                    p = place.pos[dim]
                    open_end = open_end & ((q[dim] < p) if up else (q[dim] > p))
                self.emit(
                    both(cond, open_end),
                    q,
                    self.base[dim][0 if up else 1] + self.linear(q, dim),
                    place.near(dim, up),
                )
        self.emit(cond, q, self.core_base + self.linear(q, 2), place.sibling, True, once)

    def wait(self, cond, q):
        owner = self.place.owner(q)
        piece = self.units.at(owner)
        gated(
            cond,
            lambda: remote(
                piece,
                piece,
                self.sems.at[self.shared_send],
                self.sems.at[owner - self.first_owner],
                self.place.sibling,
            ).wait_recv(),
        )

    def own(self):
        place, p = self.place, self.place.pos
        if self.direct:
            for r in range(1, 4):
                self.emit(None, p, 0, place.me + ((p[0] + r) % 4 - p[0]) * place.step[0])
            self.sideways(None, p, (2, 1))
            return
        for q0 in range(self.lo, self.hi):
            q = (q0, p[1], p[2])
            self.onward(p[0] == q0, q)
            if self.eager:
                self.sideways(p[0] == q0, q, (2, 1), None, 1)

    def column(self):
        p = self.place.pos
        if self.direct:
            for r in range(1, 4):
                q = ((p[0] + r) % 4, p[1], p[2])
                self.wait(None, q)
                self.sideways(None, q, (2, 1))
            return
        for q0 in range(self.lo, self.hi):
            q = (q0, p[1], p[2])
            self.wait(p[0] != q0, q)
            self.onward(p[0] != q0, q)
            if self.eager:
                self.sideways(p[0] != q0, q, (2, 1), None, 0)
            else:
                self.sideways(None, q, (2, 1))

    def second(self):
        for q0 in range(self.lo, self.hi):
            for qa, there in others(self.place, 1):
                q = (q0, qa, self.place.pos[2])
                self.wait(there, q)
                self.sideways(there, q, (2, 1), 1)

    def third(self):
        for qb, there in others(self.place, 2):
            for q0 in range(self.lo, self.hi):
                for qa in range(self.place.sizes[1]):
                    q = (q0, qa, qb)
                    self.wait(there, q)
                    self.sideways(there, q, (2,), 2)

    def across(self):
        _, na, nb = self.place.sizes
        piece = self.units.stretch((self.hi - self.lo) * na * nb)
        remote(
            piece,
            piece,
            self.sems.at[self.shared_send],
            self.sems.at[self.core_recv],
            self.place.sibling,
        ).wait_recv()

    def finish(self):
        for wait in self.waits:
            wait()
        if self.shared:
            piece = self.units.stretch(self.shared)
            remote(
                piece,
                piece,
                self.sems.at[self.shared_send],
                self.sems.at[self.core_recv],
                self.place.sibling,
            ).wait_send()
        self.waits, self.shared = [], 0


def landing(n):
    return 1 if n == 2 else n + 1


class Reduce:
    def __init__(self, place, units, lo, hi, land, sems, ready):
        self.place, self.units, self.lo, self.hi, self.land = place, units, lo, hi, land
        n0, na, nb = place.sizes
        self.count = (hi - lo) * na * nb
        lines = ((1, n0), (hi - lo, na), ((hi - lo) * na, nb))
        z_at = self.count
        b_at = z_at + landing(n0)
        a_at = b_at + lines[2][0] * landing(nb)
        self.land_at = (z_at, a_at, b_at)
        self.sems, self.ready = sems, ready
        self.shared = 0
        at = 4
        self.recv_at, self.up_at, self.down_at = [], [], []
        for units_here, n in lines:
            self.recv_at.append(at)
            at += units_here * landing(n)
            self.up_at.append(at)
            at += units_here * n
            self.down_at.append(at)
            at += units_here * n
        self.waits = []

    @staticmethod
    def slots(devices, share):
        side = math.isqrt(devices // 8)
        return share * side * side + landing(4) + share * (1 + side) * landing(side)

    @staticmethod
    def amount(devices, share):
        side = math.isqrt(devices // 8)
        total = 4
        for units_here, n in ((1, 4), (share, side), (share * side, side)):
            total += units_here * (landing(n) + 2 * n)
        return total

    def stage(self, k):
        if k == 0:
            self.start()
        elif k == 1:
            self.pairs()
        elif k < 4:
            self.along(4 - k)
        else:
            self.hop(0, k - 3, [(None,) + self.place.pos[1:]])

    def unit(self, dim, q):
        na = self.place.sizes[1]
        return (0, q[0] - self.lo, (q[0] - self.lo) * na + q[1])[dim]

    def add(self, owner, slot):
        self.units.put(owner, self.units.get(owner) + self.land.get(slot))

    def start(self):
        place = self.place
        if self.ready is not None:
            signal(self.ready.at[0], place.sibling)
            for dim in range(3):
                for up in (True, False):
                    pl.when(place.has(dim, up))(
                        lambda dim=dim, up=up: signal(
                            self.ready.at[1 + 2 * dim + (1 if up else 0)], place.near(dim, up)
                        )
                    )
            pl.semaphore_wait(self.ready.at[0], 1)
        per = place.sizes[1] * place.sizes[2]

        def copy(j):
            owner = 2 * (self.lo * per + j) + 1 - place.core
            return remote(
                self.units.at(owner), self.land.at(j), self.sems.at[0], self.sems.at[1], place.sibling
            )

        loop(self.count, lambda j: copy(j).start())
        self.shared += self.count

    def allow(self, dim):
        if self.ready is None:
            return
        for up in (True, False):
            pl.when(self.place.has(dim, up))(
                lambda up=up: pl.semaphore_wait(self.ready.at[1 + 2 * dim + (0 if up else 1)], 1)
            )

    def push(self, cond, dim, q, sem, slot, device):
        owner = self.place.owner(q)
        target = self.unit(dim, q) * landing(self.place.sizes[dim]) + slot
        recv = self.recv_at[dim] + target
        if cond is None:
            self.shared += 1
            sem, recv = 0, 1 + dim

        def copy():
            return remote(
                self.units.at(owner),
                self.land.at(self.land_at[dim] + target),
                self.sems.at[sem],
                self.sems.at[recv],
                device,
            )

        gated(cond, lambda: copy().start())
        if cond is not None:
            self.waits.append(lambda: gated(cond, lambda: copy().wait_send()))

    def arrived(self, sem, count):
        piece = self.land.stretch(count)
        remote(
            piece, piece, self.sems.at[0], self.sems.at[sem], self.place.sibling
        ).wait_recv()

    def pull(self, dim, q, slot):
        target = self.unit(dim, q) * landing(self.place.sizes[dim]) + slot
        piece = self.land.at(self.land_at[dim] + target)
        remote(
            piece,
            piece,
            self.sems.at[0],
            self.sems.at[self.recv_at[dim] + target],
            self.place.sibling,
        ).wait_recv()
        self.add(self.place.owner(q), self.land_at[dim] + target)

    def first(self, dim, q):
        place = self.place
        n, p = place.sizes[dim], place.pos[dim]
        u = self.unit(dim, q)
        if n == 2:
            toward = place.me + (1 - 2 * p) * place.step[dim]
            self.push(None, dim, q, self.up_at[dim] + u * n, 0, toward)
            return
        for up in (True, False):
            away = (q[dim] > 0) if up else (q[dim] < n - 1)
            self.push(
                (p == (0 if up else n - 1)) & away,
                dim,
                q,
                (self.up_at if up else self.down_at)[dim] + u * n + q[dim],
                self.slot_up(q[dim], 0) if up else self.slot_down(n, q[dim], n - 1),
                place.near(dim, up),
            )

    @staticmethod
    def slot_up(q, p):
        return q - (p + 1)

    @staticmethod
    def slot_down(n, q, p):
        to = p - 1
        return q + (n - to if to > 0 else 0)

    def order(self, dim):
        place = self.place
        if place.sizes[dim] == 2:
            return [1 - place.pos[dim], place.pos[dim]]
        return list(range(place.sizes[dim]))

    def mine(self, dim, at):
        return at is self.place.pos[dim]

    def pairs(self):
        place = self.place
        self.allow(2)
        self.arrived(1, self.count)
        for qb in self.order(2):
            for qa in self.order(1):
                for q0 in range(self.lo, self.hi):
                    q = (q0, qa, qb)
                    j = (q0 - self.lo) * place.half[0] + qa * place.half[1] + qb * place.half[2]
                    self.add(place.owner(q), j)
                    if not self.mine(2, qb):
                        self.first(2, q)

    def along(self, dim):
        place = self.place
        n, p = place.sizes[dim], place.pos[dim]
        self.allow(dim - 1)
        if dim == 2:
            rows = [(q0, qa) for qa in self.order(1) for q0 in range(self.lo, self.hi)]
        else:
            rows = [(q0,) for q0 in range(self.lo, self.hi)]

        def whole(row, at):
            return row + (at,) + place.pos[dim + 1 :]

        if n == 2:
            self.arrived(1 + dim, len(rows))
            for row in rows:
                q = whole(row, p)
                self.add(place.owner(q), self.land_at[dim] + self.unit(dim, q))
                if not self.mine(dim - 1, row[dim - 1]):
                    self.first(dim - 1, whole(row, p))
        else:
            for k in range(1, n):
                self.hop(dim, k, [whole(row, None) for row in rows])
            for row in rows:
                self.first(dim - 1, whole(row, p))

    def hop(self, dim, k, rows):
        place = self.place
        n, p = place.sizes[dim], place.pos[dim]
        lo, hi = (self.lo, self.hi) if dim == 0 else (0, n)
        for up in (True, False):
            here = k if up else n - 1 - k
            cond = p == here
            span = range(max(lo, here), hi) if up else range(lo, min(hi, here + 1))
            if len(span) == 0:
                continue

            def receive(up=up, here=here, span=span):
                for row in rows:
                    for at in span:
                        slot = at - here if up else at + (n - here if here > 0 else 0)
                        q = row[:dim] + (at,) + row[dim + 1 :]
                        self.pull(dim, q, slot)
                        if at != here:
                            self.hop_copy(dim, q, up, here).start()

            pl.when(cond)(receive)
            for row in rows:
                for at in span:
                    if at != here:
                        q = row[:dim] + (at,) + row[dim + 1 :]
                        self.waits.append(
                            lambda cond=cond, q=q, up=up, here=here: pl.when(cond)(
                                lambda: self.hop_copy(dim, q, up, here).wait_send()
                            )
                        )

    def hop_copy(self, dim, q, up, here):
        place = self.place
        n = place.sizes[dim]
        u = self.unit(dim, q)
        slot = self.slot_up(q[dim], here) if up else self.slot_down(n, q[dim], here)
        target = u * landing(n) + slot
        return remote(
            self.units.at(place.owner(q)),
            self.land.at(self.land_at[dim] + target),
            self.sems.at[(self.up_at if up else self.down_at)[dim] + u * n + q[dim]],
            self.sems.at[self.recv_at[dim] + target],
            place.near(dim, up),
        )

    def finish(self):
        for wait in self.waits:
            wait()
        piece = self.land.stretch(self.shared)
        remote(
            piece, piece, self.sems.at[0], self.sems.at[1], self.place.sibling
        ).wait_send()
        self.waits, self.shared = [], 0


class Total:
    def __init__(self, place, land, sems):
        self.place, self.land, self.sems = place, land, sems
        self.sizes = (2,) + place.sizes[::-1]
        self.at = [sum(self.sizes[:k]) for k in range(4)]
        self.waits = []

    @staticmethod
    def slots(devices):
        return 6 + 2 * math.isqrt(devices // 8)

    def lines(self, k):
        place = self.place
        if k == 0:
            return place.core, [(1, 1 - place.core, place.sibling)]
        return place.plain[3 - k], place.peers(3 - k)

    def send(self, k, value):
        p, peers = self.lines(k)
        here = self.land.at[self.at[k] + p]
        self.land[self.at[k] + p] = value
        half = self.at[3] + self.sizes[3]
        for r, _, device in peers:

            def copy(r=r, device=device):
                sems = self.sems
                return remote(
                    here, here, sems.at[self.at[k] + r], sems.at[half + self.at[k] + p], device
                )

            copy().start()
            self.waits.append(lambda copy=copy: copy().wait_send())

    def take(self, k):
        _, peers = self.lines(k)
        half = self.at[3] + self.sizes[3]
        for r, at, device in peers:
            there = self.land.at[self.at[k] + at]
            remote(
                there, there, self.sems.at[0], self.sems.at[half + self.at[k] + at], device
            ).wait_recv()
        total = self.land[self.at[k]]
        for s in range(1, self.sizes[k]):
            total = total + self.land[self.at[k] + s]
        return total

    def pass_on(self, k):
        value = self.take(k)
        if k < 3:
            self.send(k + 1, value)
        return value

    def finish(self):
        for wait in self.waits:
            wait()
        self.waits = []


class Ring:
    def __init__(self, me, devices, land, sems):
        self.after = (me + 1) % devices
        self.before = (me + devices - 1) % devices
        self.land, self.sems = land, sems

    def copies(self, to_before, to_after):
        return (
            remote(to_before, self.land.at[1], self.sems.at[0], self.sems.at[1], self.before),
            remote(to_after, self.land.at[0], self.sems.at[2], self.sems.at[3], self.after),
        )

    def start(self, to_before, to_after):
        for copy in self.copies(to_before, to_after):
            copy.start()

    def wait(self, to_before, to_after):
        for copy in self.copies(to_before, to_after):
            copy.wait_recv()

    def finish(self, to_before, to_after):
        for copy in self.copies(to_before, to_after):
            copy.wait_send()


def unit_shape(amount):
    across = min(amount, PANEL)
    return amount // across * BLOCK_ROWS, across * BLOCK_COLS


def own_unit(units, me, blocks):
    across = units.cols // BLOCK_COLS
    rows = []
    for a in range(units.rows // BLOCK_ROWS):
        row = [blocks[a * across + b].astype(bf16) for b in range(across)]
        rows.append(jnp.concatenate(row, axis=1))
    units.put(me, jnp.concatenate(rows, axis=0))


def network(
    idx_ref,
    positions_ref,
    species_ref,
    counts_ref,
    cot_ref,
    scale_ref,
    shift_ref,
    weight_ref,
    state_ref,
    blocks_ref,
    late_in,
    energy_ref,
    forces_ref,
    vector_ref,
    first_out,
    late_out,
    first_w,
    late_w,
    hot,
    z_t,
    z_r,
    geo,
    yrow,
    env_b,
    ee_t,
    en2_t,
    s1_t,
    s2_t,
    gam,
    dlt,
    coef,
    ds_t,
    de_t,
    dy,
    dg,
    dw_t,
    dw_r,
    dpf,
    den,
    lat,
    hid,
    low0,
    act1,
    sl1,
    low1,
    act2,
    sl2,
    low2,
    stage,
    halo,
    force_in,
    sides,
    vector_in,
    pack_ref,
    low_gather,
    mid_gather,
    high_gather,
    late_gather,
    late_sems,
    first_sems,
    ring_sems,
    vector_sems,
    ready,
):
    s_r = dw_r
    fact = den

    wee_t = dw_t.at[:, 0:LATENT]
    we2_t = dw_t.at[0:128, 0:LATENT]
    devices = lax.axis_size("atoms")
    me = lax.axis_index("atoms")
    place = Place(devices)
    own_at = pack_ref.at[0:8]
    first_units = Units(first_w, *unit_shape(blocks_ref.shape[0]))
    late_units = Units(late_w, *unit_shape(late_in.shape[0]))
    top = place.sizes[0]
    middle = top // 2

    def pieces(k, count):
        return Units(first_w, first_units.rows, first_units.cols, part=(k, count))

    def free(ref, units, k=0, count=1):
        slots = Reduce.slots(devices, 1)
        return Units(ref, units.rows // count, units.cols, base=k * slots)

    gather_low = [Gather(place, pieces(k, PIECES), 0, 1, low_gather.at[k]) for k in range(PIECES)]
    gather_mid = Gather(place, first_units, 1, middle, mid_gather)
    gather_high = Gather(place, first_units, middle, top, high_gather)
    gather_late = Gather(place, late_units, 0, top, late_gather, True)
    sum_out = Reduce(
        place, late_units, middle, top, free(low2, late_units), late_sems.at[0], ready.at[0]
    )
    sum_lat = Reduce(
        place, late_units, 0, middle, free(sl2, late_units), late_sems.at[1], ready.at[1]
    )
    sum_first = [
        [
            Reduce(
                place,
                pieces(k, SUM_PIECES[z]),
                z,
                z + 1,
                free(ref, first_units, k, SUM_PIECES[z]),
                first_sems.at[max(SUM_PIECES) * z + k],
                ready.at[2 + z] if k == 0 else None,
            )
            for k in range(SUM_PIECES[z])
        ]
        for z, ref in enumerate((hid, low0, low2, act2))
    ]

    def advance(z, stage):
        for part in sum_first[z]:
            part.stage(stage)
    link_halo = Ring(me, devices, halo, ring_sems.at[0])
    link_force = Ring(me, devices, force_in, ring_sems.at[1])
    sum_vector = Total(place, vector_in, vector_sems)

    barrier = pltpu.get_barrier_semaphore()
    partners = [place.sibling, link_halo.before, link_halo.after]
    for dim in range(3):
        partners += [device for _, _, device in place.peers(dim)]
    for device in partners:
        signal(barrier, device)
    for part in (slice(0, PLANE), slice(PLANE, LANES)):
        pack_ref[0:3, part] = positions_ref[...]
        pack_ref[3:4, part] = species_ref[...].astype(f32)
        pack_ref[4:5, part] = counts_ref[...].astype(f32)
        pack_ref[5:6, part] = cot_ref[...]
    pack_ref[6:16] = jnp.zeros((10, LANES), f32)
    pack_ref[6:7, 0:SPECIES] = scale_ref[...]
    pack_ref[7:8, 0:SPECIES] = shift_ref[...]
    pack_ref[8:9] = weight_ref[...]
    pack_ref[9:10] = state_ref[...]
    own_unit(first_units, me, blocks_ref)
    own_unit(late_units, me, late_in)
    pl.semaphore_wait(barrier, len(partners))
    link_halo.start(own_at, own_at)
    for part in gather_low:
        part.own()
    gather_high.own()

    ids = lax.broadcasted_iota(jnp.int32, (3 * PLANE, LANES), 0)

    whole = PLANE * devices
    coef[0, :, 0:SLOTS] = idx_ref[...].astype(f32)
    listed = coef[0].T[: SLOTS + 6].astype(jnp.int32) - (me - 1) * PLANE
    listed = jnp.where(
        listed < 0, listed + whole, jnp.where(listed >= whole, listed - whole, listed)
    )
    for t in range(TILES):
        near = jnp.concatenate([listed[2 * t : 2 * t + 1], listed[2 * t + 1 : 2 * t + 2]], axis=1)
        hot[:, t * LANES : (t + 1) * LANES] = jnp.where(ids == near, 1.0, 0.0).astype(bf16)

    link_halo.wait(own_at, own_at)
    own = pack_ref[0:8]
    lane = lax.broadcasted_iota(jnp.int32, (8, LANES), 1)
    row = lax.broadcasted_iota(jnp.int32, (8, LANES), 0)
    edge = spacing * devices
    x_row = row == 0
    before = halo[0] - jnp.where(x_row, jnp.where(me == 0, edge, 0.0), 0.0)
    after = halo[1] + jnp.where(x_row, jnp.where(me == devices - 1, edge, 0.0), 0.0)
    rank_y = ((lane & (PLANE - 1)) >> 3).astype(f32)
    rank_z = (lane & (SIDE - 1)).astype(f32)
    table = jnp.concatenate([jnp.where(lane < PLANE, before, own), after], axis=1)
    ranks = jnp.where(row == 4, rank_y, rank_z)
    table = jnp.where(
        jnp.concatenate([row, row], axis=1) < 4, table, jnp.concatenate([ranks, ranks], axis=1)
    )[:, : 3 * PLANE]
    ga, gb, gc = parts(table)
    got = nn(ga, hot[...]) + nn(gb, hot[...]) + nn(gc, hot[...])
    mine = jnp.concatenate([own] * TILES, axis=1)
    lane = lax.broadcasted_iota(jnp.int32, (1, ROWS), 1)
    slot = lane >> 6
    atom = lane & (PLANE - 1)
    for part in gather_low:
        part.column()
    for part in gather_low:
        part.second()
    gather_mid.own()
    gather_mid.column()

    def wrapped(step):
        return jnp.where(step > 1.5, -8.0, jnp.where(step < -1.5, 8.0, 0.0)) * spacing

    disp = [
        got[0:1] - mine[0:1],
        got[1:2] - mine[1:2] + wrapped(got[4:5] - (atom >> 3).astype(f32)),
        got[2:3] - mine[2:3] + wrapped(got[5:6] - (atom & (SIDE - 1)).astype(f32)),
    ]
    length = jnp.sqrt(disp[0] * disp[0] + disp[1] * disp[1] + disp[2] * disp[2])
    inverse = 1.0 / length
    unit = [disp[0] * inverse, disp[1] * inverse, disp[2] * inverse]
    angle = length * (math.pi / cutoff_radius)
    sin_k = [jnp.sin(angle)]
    cos_k = [jnp.cos(angle)]
    sin_k.append(2.0 * cos_k[0] * sin_k[0])
    cos_k.append(2.0 * cos_k[0] * cos_k[0] - 1.0)
    for k in range(2, BESSEL):
        sin_k.append(2.0 * cos_k[0] * sin_k[k - 1] - sin_k[k - 2])
        cos_k.append(2.0 * cos_k[0] * cos_k[k - 1] - cos_k[k - 2])
    sines = jnp.concatenate(sin_k, axis=0)
    cosines = jnp.concatenate(cos_k, axis=0)
    bessel = (math.sqrt(2.0 / cutoff_radius) * inverse) * sines
    scaled = length * (1.0 / cutoff_radius)
    t2 = scaled * scaled
    t4 = t2 * t2
    t5 = t4 * scaled
    t6 = t4 * t2
    envelope = 1.0 - 28.0 * t6 + 48.0 * (t6 * scaled) - 21.0 * (t4 * t4)
    denvelope = (-168.0 * t5 + 336.0 * t6 - 168.0 * (t6 * scaled)) * (1.0 / cutoff_radius)
    live = jnp.where(slot.astype(f32) < mine[4:5], 1.0, 0.0)

    kind = lax.broadcasted_iota(jnp.int32, (KINDS, LANES), 0).astype(f32)
    is_kind = kind == own[3:4]
    by_kind = own.T
    scale = jnp.sum(jnp.where(is_kind, by_kind[:KINDS, 6:7], 0.0), axis=0, keepdims=True)
    shift = jnp.sum(jnp.where(is_kind, by_kind[:KINDS, 7:8], 0.0), axis=0, keepdims=True)
    cot = jnp.concatenate([own[5:6] * scale] * TILES, axis=1) * live
    weight = cot * envelope

    root3 = math.sqrt(3.0)
    root15 = math.sqrt(15.0)
    root5 = math.sqrt(5.0)
    ux, uy, uz = unit
    yrow[0:8] = jnp.concatenate(
        [
            root3 * ux,
            root3 * uy,
            root3 * uz,
            root15 * ux * uy,
            root15 * uy * uz,
            0.5 * root5 * (3.0 * uz * uz - 1.0),
            root15 * ux * uz,
            0.5 * root15 * (ux * ux - uy * uy),
        ],
        axis=0,
    )
    yrow[8:16] = yrow[0:8] * (live * env_scale)
    yrow[16:17] = live * env_scale
    geo[0:8] = jnp.concatenate([ux, uy, uz, inverse, envelope, denvelope, live, cot], axis=0)
    geo[8:16] = math.sqrt(2.0 / cutoff_radius) * (
        (math.pi / cutoff_radius)
        * lax.broadcasted_iota(jnp.int32, (BESSEL, ROWS), 0).astype(f32)
        * cosines
        + (math.pi / cutoff_radius) * cosines
        - sines * inverse
    ) * inverse


    def one_hots(t):
        row = lax.broadcasted_iota(jnp.int32, (LANES, LANES), 0).astype(f32)
        here = jnp.where(row == own[3:4] + float(BESSEL), 1.0, 0.0)
        there = jnp.where(row == kinds_near[t] + float(BESSEL + SPECIES), 1.0, 0.0)
        return here + there

    kinds_near = [got[3:4, t * LANES : (t + 1) * LANES] for t in range(TILES)]
    gather_mid.second()
    for part in gather_low:
        part.third()
    gather_high.column()
    for t in range(TILES):
        at = slice(t * LANES, (t + 1) * LANES)
        column = jnp.concatenate([bessel[:, at], one_hots(t)[BESSEL:]], axis=0)
        z_t[:, at] = column.astype(bf16)
        z_r[at, :] = column.T.astype(bf16)
        env_b[at, :] = jnp.broadcast_to(envelope[:, at], (LANES, LANES)).T
        fact[at, :] = jnp.broadcast_to(weight[:, at], (LANES, LANES)).T
    for part in gather_low:
        part.across()


    def twice(x):
        return jnp.concatenate([x] * (STRIP // LANES), axis=1)

    def in_body(n, r):
        pre = nn(z_r[r], cols_panel(first_w, W_INPUT, n))
        hid[r, panel(n, STRIP)] = (pre * sigmoid(pre)).astype(bf16)

    loop_panels(in_body)
    gather_mid.third()
    gather_high.second()
    gather_late.own()
    gather_mid.across()

    def two_body(n, r):
        zero = nn(hid[r], cols_panel(first_w, W_TWO, n)) * twice(env_b[r])
        lat[r, panel(n, STRIP)] = zero
        low0[r, panel(n, STRIP)] = zero.astype(bf16)

    loop_panels(two_body)
    gather_high.third()

    def transposed_product(out, weights, right, width=256):
        at = 0
        while at < ROWS:
            end = min(at + width, ROWS)
            out[:, at:end] = nt(weights, right[at:end, :])
            at = end

    wee_t[0:128, :] = narrow(first_w, W_EMBED).T
    wee_t[128:256, :] = narrow(first_w, W_ENV_ONE).T
    transposed_product(ee_t, wee_t[...], low0)
    gather_late.column()

    def environment(out, v0_ref, v0_at, v1_at):
        for m in range(9):
            total = None
            begin = v0_at if m == 0 else v1_at
            y = yrow[16:17, :] if m == 0 else yrow[7 + m : 8 + m, :]
            for t in range(TILES):
                at = slice(t * LANES, (t + 1) * LANES)
                term = v0_ref[begin : begin + CHANNELS, at] * y[:, at]
                total = term if total is None else total + term
            out[m] = halves(total)

    def put_scalars(t, s_t, rows):
        s_t[:, lanes(t)] = jnp.concatenate(rows, axis=0).astype(bf16)
        filled = jnp.concatenate(rows + [jnp.zeros_like(rows[0])], axis=0)
        flipped = filled.T.astype(bf16)
        s_r[lanes(t), :] = flipped

    def weighted(y, first, count, source, offset):
        total = None
        for m in range(count):
            term = y[first + m : first + m + 1] * source[offset + m]
            total = term if total is None else total + term
        return total

    environment(gam, ee_t, 128, 192)

    def scalars_one(t):
        e0 = ee_t[0:64, lanes(t)]
        e1 = ee_t[64:128, lanes(t)]
        y = yrow[0:8, lanes(t)]
        put_scalars(
            t,
            s1_t,
            [e0 * gam[0], e1 * weighted(y, 0, 3, gam, 1), e1 * weighted(y, 3, 5, gam, 4)],
        )

    beside(6, lambda i: None, scalars_one)
    gather_high.across()

    def pre_one(n, r):
        pre = nn(low0[r], cols_panel(first_w, W_LAT_ONE, n)) + nn(
            s_r[r, : 3 * CHANNELS], cols_panel(first_w, W_SCAL_ONE, n)
        )
        sig = sigmoid(pre)
        act = pre * sig
        act1[r, panel(n, STRIP)] = act.astype(bf16)
        sl1[r, panel(n, STRIP)] = (sig + act * (1.0 - sig)).astype(bf16)

    loop_panels(pre_one)
    gather_late.second()

    def out_one(n, r):
        new = (lat[r, panel(n, STRIP)] + nn(act1[r], cols_panel(first_w, W_OUT_ONE, n))) * half_root
        lat[r, panel(n, STRIP)] = new
        low1[r, panel(n, STRIP)] = new.astype(bf16)

    loop_panels(out_one)
    gather_late.third()
    we2_t[...] = narrow(first_w, W_ENV_TWO).T
    transposed_product(en2_t, we2_t[...], low1)
    environment(dlt, en2_t, 0, 64)

    g0 = gam[0]
    coef[0] = g0 * dlt[0]
    for m in range(3):
        a, b = 1 + (m + 1) % 3, 1 + (m + 2) % 3
        coef[1 + m] = g0 * dlt[1 + m] + (gam[a] * dlt[b] - gam[b] * dlt[a])
    coef[9] = gam[1] * dlt[1] + gam[2] * dlt[2] + gam[3] * dlt[3]
    second = None
    for m in range(4, 9):
        coef[m] = g0 * dlt[m]
        term = gam[m] * dlt[m]
        second = term if second is None else second + term
    coef[10] = second

    def scalars_two(t):
        e0 = ee_t[0:64, lanes(t)]
        e1 = ee_t[64:128, lanes(t)]
        y = yrow[0:8, lanes(t)]
        put_scalars(
            t,
            s2_t,
            [
                e0 * coef[0],
                e1 * weighted(y, 0, 3, coef, 1) + e0 * coef[9],
                e1 * weighted(y, 3, 5, coef, 4) + e0 * coef[10],
            ],
        )

    beside(6, lambda i: None, scalars_two)
    gather_late.across()

    for part in gather_low + [gather_mid, gather_high, gather_late]:
        part.finish()
    def pre_two(n, r):
        pre = nn(low1[r], cols_panel(late_w, W_LAT_TWO, n)) + nn(
            s_r[r, : 3 * CHANNELS], cols_panel(first_w, W_SCAL_TWO, n)
        )
        sig = sigmoid(pre)
        act = pre * sig
        act2[r, panel(n, STRIP)] = act.astype(bf16)
        sl2[r, panel(n, STRIP)] = (sig + act * (1.0 - sig)).astype(bf16)

    loop_panels(pre_two)

    def out_two(n, r):
        new = (lat[r, panel(n, STRIP)] + nn(act2[r], cols_panel(late_w, W_OUT_TWO, n))) * half_root
        low2[r, panel(n, STRIP)] = new.astype(bf16)

    loop_panels(out_two)

    vec = jnp.broadcast_to(pack_ref[8:9], (8, LANES))
    stage[...] = narrow(first_w, W_FINAL)

    def read_out(i):
        r = pl.ds(pl.multiple_of(i * 416, 16), 416)
        pre = nn(low2[r, :], stage[...])
        sig = sigmoid(pre)
        final_act = pre * sig
        dpf[r, :] = (fact[r, :] * vec[0:1] * (sig + final_act * (1.0 - sig))).astype(bf16)
        fact[r, :] = final_act

    loop(4, read_out)
    fa, fb, _ = parts(fact[...])
    va, vb, _ = parts(vec)
    value = (nt(va, fa) + (nt(va, fb) + nt(vb, fa)))[0:1]
    geo_live = geo[6:7]
    geo_env = geo[4:5]
    geo_cot = geo[7:8]
    edge_energy = geo_live * geo_env * value
    summed = None
    for t in range(TILES):
        term = edge_energy[:, t * LANES : (t + 1) * LANES]
        summed = term if summed is None else summed + term
    energy_ref[...] = scale * halves(summed) + shift
    all_weights = jnp.broadcast_to(geo_cot * geo_env, (8, ROWS))
    wa, wb, _ = parts(all_weights)
    sum_vector.send(0, nn(wa, fa) + (nn(wa, fb) + nn(wb, fa)))
    geo[16:17] = geo_cot * value

    def big_step(out, where, left, right):
        def step(i):
            grad = tn(left[:, panel(i, STRIP)], right[...])
            out[pl.ds(pl.multiple_of(where[0] + i * STRIP, 64), STRIP), :] = grad.astype(bf16)

        return step

    def big_grad(out, where, left, right):
        loop(LATENT // STRIP, big_step(out, where, left, right))

    def wide_step(out, where, left, right):
        def step(n):
            out[where[0] : where[0] + where[1], panel(n)] = nn(
                left[...], right[:, panel(n)]
            ).astype(bf16)

        return step

    def wide_grad(out, where, left, right):
        loop(4, wide_step(out, where, left, right))

    def narrow_grad(left, right, put):
        def step(n):
            put(n, nn(left, right[:, panel(n)]).T.astype(bf16))

        loop(4, step)

    def put_narrow(where, n, grad):
        row = pl.multiple_of(where[0] + n // 2 * BLOCK_ROWS, BLOCK_ROWS)
        col = pl.multiple_of(n % 2 * 512, 512)
        first_w[pl.ds(row, BLOCK_ROWS), pl.ds(col, 512)] = jnp.concatenate(
            [grad[b * BLOCK_ROWS : (b + 1) * BLOCK_ROWS] for b in range(4)], axis=1
        )

    def put_stage(n, grad):
        stage[panel(n), :] = grad

    def back_final(n, r):
        grad = nt(dpf[r], narrow_panel(first_w, W_FINAL, n)) * half_root
        lat[r, panel(n, STRIP)] = grad
        low2[r, panel(n, STRIP)] = grad.astype(bf16)

    def back_out_two(n, r):
        grad = nt(low2[r], rows_panel(late_w, W_OUT_TWO, n))
        sl2[r, panel(n, STRIP)] = (grad * sl2[r, panel(n, STRIP)].astype(f32)).astype(bf16)

    def tensors_two(t):
        e0 = ee_t[0:64, lanes(t)]
        e1 = ee_t[64:128, lanes(t)]
        y = yrow[0:8, lanes(t)]
        r0 = ds_t[0:64, lanes(t)]
        r1 = ds_t[64:128, lanes(t)]
        r2 = ds_t[128:192, lanes(t)]
        de_t[0:64, lanes(t)] = r0 * coef[0] + r1 * coef[9] + r2 * coef[10]
        de_t[64:128, lanes(t)] = r1 * weighted(y, 0, 3, coef, 1) + r2 * weighted(y, 3, 5, coef, 4)
        p1 = r1 * e1
        p2 = r2 * e1
        rows = []
        for m in range(8):
            p = p1 if m < 3 else p2
            rows.append(jnp.sum(p * coef[1 + m], axis=0, keepdims=True))
            dg[1 + m] += p * y[m : m + 1]
        dy[:, lanes(t)] = jnp.concatenate(rows, axis=0)
        dg[0] += r0 * e0
        dg[9] += r1 * e0
        dg[10] += r2 * e0

    def environment_back(t, grads, source, v1_at, at):
        y4 = yrow[8:16, lanes(t)]
        l4 = yrow[16:17, lanes(t)]
        v1 = source[v1_at : v1_at + 64, lanes(t)]
        low = l4 * grads[0]
        high = weighted(y4, 0, 8, grads, 1)
        both = jnp.concatenate([low, high], axis=0)
        dw_t[at : at + 128, lanes(t)] = both.astype(bf16)
        dw_r[lanes(t), at : at + 128] = both.T.astype(bf16)
        v1 = v1 * l4
        rows = [jnp.sum(v1 * grads[1 + m], axis=0, keepdims=True) for m in range(8)]
        dy[:, lanes(t)] += jnp.concatenate(rows, axis=0)

    def back_lat_two(n, r):
        grad = (
            lat[r, panel(n, STRIP)]
            + nt(sl2[r], rows_panel(late_w, W_LAT_TWO, n))
            + nt(dw_r[r, 128:256], narrow_panel(first_w, W_ENV_TWO, n))
        ) * half_root
        lat[r, panel(n, STRIP)] = grad
        act2[r, panel(n, STRIP)] = grad.astype(bf16)

    def back_out_one(n, r):
        grad = nt(act2[r], rows_panel(first_w, W_OUT_ONE, n))
        sl1[r, panel(n, STRIP)] = (grad * sl1[r, panel(n, STRIP)].astype(f32)).astype(bf16)

    def tensors_one(t):
        e0 = ee_t[0:64, lanes(t)]
        e1 = ee_t[64:128, lanes(t)]
        y = yrow[0:8, lanes(t)]
        r0 = ds_t[0:64, lanes(t)]
        r1 = ds_t[64:128, lanes(t)]
        r2 = ds_t[128:192, lanes(t)]
        low = de_t[0:64, lanes(t)] + r0 * gam[0]
        high = (
            de_t[64:128, lanes(t)]
            + r1 * weighted(y, 0, 3, gam, 1)
            + r2 * weighted(y, 3, 5, gam, 4)
        )
        both = jnp.concatenate([low, high], axis=0)
        dw_t[0:128, lanes(t)] = both.astype(bf16)
        dw_r[lanes(t), 0:128] = both.T.astype(bf16)
        p1 = r1 * e1
        p2 = r2 * e1
        rows = []
        for m in range(8):
            p = p1 if m < 3 else p2
            rows.append(jnp.sum(p * gam[1 + m], axis=0, keepdims=True))
            coef[1 + m] += p * y[m : m + 1]
        dy[:, lanes(t)] += jnp.concatenate(rows, axis=0)
        coef[0] += r0 * e0

    def back_lat_one(n, r):
        both = jnp.concatenate(
            [narrow_panel(first_w, W_EMBED, n), narrow_panel(first_w, W_ENV_ONE, n)], axis=1
        )
        grad = (
            lat[r, panel(n, STRIP)]
            + nt(sl1[r], rows_panel(first_w, W_LAT_ONE, n))
            + nt(dw_r[r], both)
        )
        low1[r, panel(n, STRIP)] = (grad * twice(env_b[r])).astype(bf16)
        part = grad * low0[r, panel(n, STRIP)].astype(f32)
        for b in range(STRIP // LANES):
            den[r] += part[:, b * LANES : (b + 1) * LANES]

    def back_two(n, r):
        grad = nt(low1[r], rows_panel(first_w, W_TWO, n))
        pre = nn(z_r[r], cols_panel(first_w, W_INPUT, n))
        sig = sigmoid(pre)
        act1[r, panel(n, STRIP)] = (grad * (sig + pre * sig * (1.0 - sig))).astype(bf16)

    def lat_one_grad(low, high):
        grad = tn(low0[:, low:high], sl1[...])
        first_w[W_LAT_ONE[0] + low : W_LAT_ONE[0] + high, :] = grad.astype(bf16)

    narrow_grad(dpf[...].T, low2, put_stage)
    loop_panels(back_final)
    loop(4, lambda n: put_narrow(W_FINAL, n, stage[panel(n), :]))
    loop_panels(back_out_two)
    transposed_product(ds_t, first_w[W_SCAL_TWO[0] : W_SCAL_TWO[0] + W_SCAL_TWO[1], :], sl2)
    dg[...] = jnp.zeros_like(dg)
    beside(2, big_step(late_w, W_OUT_TWO, act2, low2), tensors_two)
    sum_vector.pass_on(0)
    sum_out.stage(0)
    total = [halves(dg[m]) for m in range(11)]
    g0 = gam[0]
    d0 = dlt[0]
    new_g0 = total[0] * d0
    for m in range(1, 9):
        new_g0 = new_g0 + total[m] * dlt[m]
    dlt_grads = [total[0] * g0]
    gam_grads = [new_g0]
    for m in range(3):
        a, b = 1 + (m + 1) % 3, 1 + (m + 2) % 3
        dlt_grads.append(
            total[1 + m] * g0 + total[9] * gam[1 + m] + (total[a] * gam[b] - total[b] * gam[a])
        )
        gam_grads.append(total[9] * dlt[1 + m] + (dlt[a] * total[b] - dlt[b] * total[a]))
    for m in range(4, 9):
        dlt_grads.append(total[m] * g0 + total[10] * gam[m])
        gam_grads.append(total[10] * dlt[m])
    for m in range(9):
        dlt[m] = dlt_grads[m]
        dg[m] = gam_grads[m]
    beside(
        4,
        wide_step(first_w, W_SCAL_TWO, s2_t, sl2),
        lambda t: environment_back(t, dlt, en2_t, 64, 128),
    )
    sum_out.stage(1)
    loop_panels(back_lat_two)
    sum_out.stage(2)
    big_grad(late_w, W_LAT_TWO, low1, sl2)
    sum_vector.pass_on(1)
    sum_out.stage(3)
    sum_lat.stage(0)
    loop_panels(back_out_one)
    sum_out.stage(4)
    narrow_grad(dw_t[128:256, :], low1, functools.partial(put_narrow, W_ENV_TWO))
    sum_lat.stage(1)
    transposed_product(ds_t, first_w[W_SCAL_ONE[0] : W_SCAL_ONE[0] + W_SCAL_ONE[1], :], sl1)
    for m in range(9):
        coef[m] = jnp.zeros((CHANNELS, LANES), f32)
    beside(2, big_step(first_w, W_OUT_ONE, act1, act2), tensors_one)
    sum_vector.pass_on(2)
    sum_out.stage(5)
    sum_lat.stage(2)
    advance(3, 0)
    for m in range(9):
        dg[m] = dg[m] + halves(coef[m])
    beside(
        4,
        wide_step(first_w, W_SCAL_ONE, s1_t, sl1),
        lambda t: environment_back(t, dg, ee_t, 192, 128),
    )
    sum_out.stage(6)
    sum_lat.stage(3)
    advance(3, 1)
    den[...] = jnp.zeros_like(den)
    loop_panels(back_lat_one)
    lat_one_grad(640, 1024)
    sum_lat.stage(4)
    advance(3, 2)
    advance(2, 0)
    loop_panels(back_two)
    advance(3, 3)
    transposed_product(ds_t.at[0:64], first_w[0:64, :], act1)
    sum_lat.stage(5)
    advance(2, 1)
    big_grad(first_w, W_TWO, hid, low1)
    wide_grad(first_w, W_INPUT, z_t, act1)
    advance(0, 0)
    advance(2, 2)
    narrow_grad(dw_t[0:128, :], low0, functools.partial(put_narrow, W_EMBED))
    narrow_grad(dw_t[128:256, :], low0, functools.partial(put_narrow, W_ENV_ONE))
    advance(3, 4)
    lat_one_grad(0, 384)
    lat_one_grad(384, 640)
    advance(0, 1)
    advance(1, 0)
    advance(3, 5)
    advance(2, 3)
    sum_lat.stage(6)
    advance(0, 2)
    dbessel = ds_t[0:8, :]
    da, db, _ = parts(den[...])
    ones = jnp.ones((8, LANES), bf16)
    through = (nt(ones, da) + nt(ones, db))[0:1]
    ux, uy, uz = geo[0:1], geo[1:2], geo[2:3]
    inverse = geo[3:4]
    envelope = geo[4:5]
    denv = geo[16:17] + through / envelope
    dlength = jnp.sum(dbessel * geo[8:16], axis=0, keepdims=True) + denv * geo[5:6]
    g = [dy[m : m + 1, :] for m in range(8)]
    dux = root3 * g[0] + root15 * (uy * g[3] + uz * g[6] + ux * g[7])
    duy = root3 * g[1] + root15 * (ux * g[3] + uz * g[4] - uy * g[7])
    duz = root3 * g[2] + root15 * (uy * g[4] + ux * g[6]) + (3.0 * root5) * uz * g[5]
    along = dlength - (ux * dux + uy * duy + uz * duz) * inverse
    near = jnp.concatenate(
        [
            dux * inverse + ux * along,
            duy * inverse + uy * along,
            duz * inverse + uz * along,
            jnp.zeros((5, ROWS), f32),
        ],
        axis=0,
    )
    summed = None
    for t in range(TILES):
        term = near[:, t * LANES : (t + 1) * LANES]
        summed = term if summed is None else summed + term
    centre = halves(summed)
    na, nb, nc = parts(near)
    spread = nt(na, hot[...]) + nt(nb, hot[...]) + nt(nc, hot[...])
    sides[0] = spread[:, :LANES]
    sides[1, :, 0:PLANE] = spread[:, LANES:]
    link_force.start(sides.at[0], sides.at[1])
    advance(0, 3)
    advance(1, 1)
    advance(2, 4)
    advance(3, 6)
    advance(0, 4)
    advance(0, 5)
    advance(1, 2)
    advance(1, 3)
    for step in range(6):
        for k in range(max(SUM_PIECES[:3])):
            for z, after in ((0, 6), (1, 4), (2, 5)):
                if k < SUM_PIECES[z] and after <= after + step - k < 7:
                    sum_first[z][k].stage(after + step - k)
    link_force.wait(sides.at[0], sides.at[1])
    forces_ref[...] = (
        centre - pltpu.roll(sides[0], PLANE, 1) - force_in[1] - force_in[0]
    )
    total = sum_vector.pass_on(3)
    normed = total * lax.rsqrt(jnp.sum(total[0:1] * total[0:1]) * (1.0 / FINAL) + epsilon)
    state = decay_rate * pack_ref[9:10] + (1.0 - decay_rate) * normed * normed
    vector_ref[0:1] = total[0:1]
    vector_ref[1:2] = state[0:1]
    vector_ref[2:3] = (pack_ref[8:9] - vector_rate * normed * lax.rsqrt(state + epsilon))[0:1]
    first_out[...] = first_units.get(me)
    late_out[...] = late_units.get(me)
    for group in sum((list(parts) for parts in sum_first), [sum_out, sum_lat, sum_vector]):
        group.finish()
    link_halo.finish(own_at, own_at)
    link_force.finish(sides.at[0], sides.at[1])


def run_network(devices, small, blocks, late):
    S = jax.ShapeDtypeStruct
    wide = pltpu.VMEM((ROWS, LATENT), bf16)
    slab = pltpu.VMEM((ROWS, LANES), f32)
    panels = lambda amount: pltpu.VMEM((amount * devices // PANEL * BLOCK_ROWS, WIDE), bf16)
    scratch = [
        panels(blocks.shape[0]),
        panels(late.shape[0]),
        pltpu.VMEM((3 * PLANE, ROWS), bf16),
        pltpu.VMEM((LANES, ROWS), bf16),
        pltpu.VMEM((ROWS, LANES), bf16),
        pltpu.VMEM((24, ROWS), f32),
        pltpu.VMEM((24, ROWS), f32),
        slab,
        pltpu.VMEM((256, ROWS), f32),
        pltpu.VMEM((128, ROWS), f32),
        pltpu.VMEM((192, ROWS), bf16),
        pltpu.VMEM((192, ROWS), bf16),
        pltpu.VMEM((9, CHANNELS, LANES), f32),
        pltpu.VMEM((9, CHANNELS, LANES), f32),
        pltpu.VMEM((11, CHANNELS, LANES), f32),
        pltpu.VMEM((192, ROWS), f32),
        pltpu.VMEM((128, ROWS), f32),
        pltpu.VMEM((8, ROWS), f32),
        pltpu.VMEM((11, CHANNELS, LANES), f32),
        pltpu.VMEM((256, ROWS), bf16),
        pltpu.VMEM((ROWS, 256), bf16),
        pltpu.VMEM((ROWS, LANES), bf16),
        slab,
        pltpu.VMEM((ROWS, LATENT), f32),
    ] + [wide] * 8 + [
        pltpu.VMEM((LATENT, LANES), bf16),
        pltpu.VMEM((2, 8, LANES), f32),
        pltpu.VMEM((2, 8, LANES), f32),
        pltpu.VMEM((2, 8, LANES), f32),
        pltpu.VMEM((Total.slots(devices), 8, LANES), f32),
        pltpu.VMEM((16, LANES), f32),
        pltpu.SemaphoreType.DMA((PIECES, Gather.amount(devices, 1))),
        pltpu.SemaphoreType.DMA((Gather.amount(devices, 1),)),
        pltpu.SemaphoreType.DMA((Gather.amount(devices, 2),)),
        pltpu.SemaphoreType.DMA((Gather.amount(devices, 4),)),
        pltpu.SemaphoreType.DMA((2, Reduce.amount(devices, 2))),
        pltpu.SemaphoreType.DMA((4 * max(SUM_PIECES), Reduce.amount(devices, 1))),
        pltpu.SemaphoreType.DMA((2, 4)),
        pltpu.SemaphoreType.DMA((2 * Total.slots(devices),)),
        pltpu.SemaphoreType.REGULAR((6, 7)),
    ]
    vmem = pl.BlockSpec(memory_space=pltpu.VMEM)
    return pl.pallas_call(
        network,
        out_shape=[
            S((1, LANES), f32),
            S((8, LANES), f32),
            S((8, LANES), f32),
            S(unit_shape(blocks.shape[0]), bf16),
            S(unit_shape(late.shape[0]), bf16),
        ],
        in_specs=[vmem] * (len(small) + 2),
        out_specs=[vmem] * 5,
        scratch_shapes=scratch,
        compiler_params=pltpu.CompilerParams(
            vmem_limit_bytes=63 << 20, collective_id=0, has_side_effects=True
        ),
        name="network",
    )(*small, blocks, late)


def shampoo(
    energy,
    force,
    vectors,
    grads,
    left,
    right,
    left_root,
    right_root,
    master,
    late_grads,
    late_left,
    late_right,
    late_left_root,
    late_right_root,
    late_master,
    energy_out,
    force_out,
    vector_out,
    state_out,
    moved_out,
    *outs,
):
    energy_out[...] = energy[:, :PLANE]
    force_out[...] = force[0:3, :PLANE]
    vector_out[...] = vectors[0:1]
    state_out[...] = vectors[1:2]
    moved_out[...] = vectors[2:3]

    todo = []
    for j in range(left.shape[0]):
        todo.append((grads, j, left, right, left_root, right_root, master) + outs[:4])
    for j in range(late_left.shape[0]):
        todo.append(
            (late_grads, j, late_left, late_right, late_left_root, late_right_root, late_master)
            + outs[4:]
        )
    size = 1.0 / (BLOCK_ROWS * BLOCK_COLS)
    held, scales, steps = [], [], []
    for panels, j, left, *_ in todo:
        per = panels.shape[1] // BLOCK_COLS
        at = pl.program_id(0) * left.shape[0] + j
        row = pl.multiple_of(at // per * BLOCK_ROWS, BLOCK_ROWS)
        col = pl.multiple_of(at % per * BLOCK_COLS, BLOCK_COLS)
        held.append(panels[pl.ds(row, BLOCK_ROWS), pl.ds(col, BLOCK_COLS)])
    for g, (_, j, *_, grad_out, left_out, right_out, master_out) in zip(held, todo):
        grad = g.astype(f32)
        grad_out[j] = grad
        scales.append(lax.rsqrt(jnp.sum(grad * grad, keepdims=True) * size + epsilon))
    turned = []
    for g, (_, j, left, right, left_root, *_) in zip(held, todo):
        turned.append(nn(left_root[j].astype(bf16), g))
    for g, s, (_, j, left, right, *_, grad_out, left_out, right_out, master_out) in zip(
        held, scales, todo
    ):
        square = (1.0 - decay_rate) * s * s
        left_out[j] = decay_rate * left[j] + square * nt(g, g)
        right_out[j] = decay_rate * right[j] + square * tn(g, g)
    for turn, s, (_, j, left, right, left_root, right_root, *_) in zip(turned, scales, todo):
        steps.append(nn((turn * s).astype(bf16), right_root[j].astype(bf16)))
    for step, (_, j, left, right, left_root, right_root, master, *_, master_out) in zip(steps, todo):
        slope = lax.rsqrt(jnp.sum(step * step, keepdims=True) * size + epsilon)
        master_out[j] = master[j] - (learn_rate * slope) * step


def run_shampoo(energy, force, vectors, first, late):
    S = jax.ShapeDtypeStruct
    steps = min(2, late[1].shape[0])

    def whole(x):
        return pl.BlockSpec(x.shape, lambda i: (0,) * len(x.shape))

    def share(x):
        return pl.BlockSpec((x.shape[0] // steps,) + x.shape[1:], lambda i: (i, 0, 0))

    small = [S((1, PLANE), f32), S((3, PLANE), f32)] + [S((1, FINAL), f32)] * 3
    grown = []
    for group in (first, late):
        left, right, _, _, master = group[1:]
        grown += [S(x.shape, f32) for x in (master, left, right, master)]
    return pl.pallas_call(
        shampoo,
        grid=(steps,),
        out_shape=small + grown,
        in_specs=[whole(energy), whole(force), whole(vectors)]
        + [whole(first[0])]
        + [share(x) for x in first[1:]]
        + [whole(late[0])]
        + [share(x) for x in late[1:]],
        out_specs=[whole(x) for x in small] + [share(x) for x in grown],
        compiler_params=pltpu.CompilerParams(vmem_limit_bytes=60 << 20),
        name="shampoo",
    )(energy, force, vectors, *first, *late)


def local(
    positions,
    species,
    neighbours,
    counts,
    species_scale,
    species_shift,
    energy_cot,
    blocks,
    left,
    right,
    left_root,
    right_root,
    late_blocks,
    late_left,
    late_right,
    late_left_root,
    late_right_root,
    out_vector,
    vector_state,
):
    devices = lax.axis_size("atoms")
    small = (
        neighbours.reshape(PLANE, SLOTS),
        positions,
        species[None],
        counts[None],
        energy_cot[None],
        species_scale[None],
        species_shift[None],
        out_vector[None],
        vector_state[None],
    )
    energy, force, vectors, first_units, late_units = run_network(
        devices, small, blocks, late_blocks
    )
    out = run_shampoo(
        energy,
        force,
        vectors,
        (first_units, left, right, left_root, right_root, blocks),
        (late_units, late_left, late_right, late_left_root, late_right_root, late_blocks),
    )
    energies, forces, vector_grad, new_state, new_vector = out[:5]
    return (
        energies.reshape(-1),
        forces,
        *out[5:],
        vector_grad.reshape(-1),
        new_state.reshape(-1),
        new_vector.reshape(-1),
    )


def solution(mesh):
    row = P("atoms")
    block = P("atoms", None, None)
    placed = (
        (P(None, "atoms"), row, row, row, P(), P(), row)
        + (block,) * 10
        + (P(), P())
    )
    return jax.shard_map(
        local,
        mesh=mesh,
        in_specs=placed,
        out_specs=(row, P(None, "atoms")) + (block,) * 8 + (P(), P(), P()),
        check_vma=False,
    )
```

```python
import functools
import math

import jax
import jax.numpy as jnp
from jax import lax
from jax.experimental import pallas as pl
from jax.experimental.pallas import tpu as pltpu
from jax.sharding import PartitionSpec as P

SIDE = 8
SLOTS = 26
SPECIES = 60
BESSEL = 8
CHANNELS = 64
LATENT = 1024
FINAL = 128
BLOCK_ROWS = 64
BLOCK_COLS = 128
PLANE = SIDE * SIDE

f32 = jnp.float32
bf16 = jnp.bfloat16
spacing = 1.6
cutoff_radius = 4.0
env_scale = 0.25
half_root = 0.7071067811865476
decay_rate = 0.5
learn_rate = 0.02
vector_rate = 0.03
epsilon = 1e-06

LANES = 128
ROWS = SLOTS * PLANE
TILES = ROWS // LANES
KINDS = 64

PANEL = 8
WIDE = PANEL * BLOCK_COLS
W_INPUT = (0, 128)
W_TWO = (128, 1024)
W_EMBED = (1152, 128)
W_ENV_ONE = (1280, 128)
W_LAT_ONE = (1408, 1024)
W_SCAL_ONE = (2432, 192)
W_OUT_ONE = (2624, 1024)
W_ENV_TWO = (3648, 128)
W_SCAL_TWO = (3776, 192)
W_FINAL = (3968, 128)
W_LAT_TWO = (0, 1024)
W_OUT_TWO = (1024, 1024)

MESH = pl.DeviceIdType.MESH


def nn(a, b):
    return lax.dot_general(a, b, (((1,), (0,)), ((), ())), preferred_element_type=f32)


def nt(a, b):
    return lax.dot_general(a, b, (((1,), (1,)), ((), ())), preferred_element_type=f32)


def tn(a, b):
    return lax.dot_general(a, b, (((0,), (0,)), ((), ())), preferred_element_type=f32)


def cols_panel(ref, where, n):
    return ref[where[0] : where[0] + where[1], panel(n, STRIP)]


def rows_panel(ref, where, n):
    return ref[pl.ds(pl.multiple_of(where[0] + n * STRIP, 64), STRIP), :]


def narrow(ref, where):
    pieces = []
    for j in range(LATENT // BLOCK_ROWS):
        row = where[0] + j // PANEL * BLOCK_ROWS
        col = j % PANEL * BLOCK_COLS
        pieces.append(ref[row : row + BLOCK_ROWS, col : col + BLOCK_COLS])
    return jnp.concatenate(pieces, axis=0)


def narrow_panel(ref, where, n):
    part = ref[pl.ds(pl.multiple_of(where[0] + n * BLOCK_ROWS, BLOCK_ROWS), BLOCK_ROWS), :]
    return jnp.concatenate([part[:, b * 128 : (b + 1) * 128] for b in range(PANEL)], axis=0)


def sigmoid(x):
    return 0.5 * jnp.tanh(0.5 * x) + 0.5


def halves(x):
    return x + pltpu.roll(x, PLANE, 1)


def lanes(t):
    if isinstance(t, int):
        return pl.ds(t * LANES, LANES)
    return pl.ds(pl.multiple_of(t * LANES, LANES), LANES)


def panel(n, width=256):
    return pl.ds(pl.multiple_of(n * width, width), width)


STRIP = 512
CHUNKS = 2
PIECES = 2
SUM_PIECES = (1, 1, 1, 1)
CHUNK = ROWS // CHUNKS


def loop_panels(body):
    def step(n):
        for c in range(CHUNKS):
            body(n, slice(c * CHUNK, (c + 1) * CHUNK))

    loop(LATENT // STRIP, step)


def beside(count, step, tile):
    share = TILES // count

    def body(i):
        step(i)
        for u in range(share):
            tile(i * share + u)

    loop(count, body)
    for t in range(share * count, TILES):
        tile(t)


def loop(count, body):
    def step(i, carry):
        body(i)
        return carry

    lax.fori_loop(0, count, step, 0)


def parts(x):
    a = x.astype(bf16)
    rest = x - a.astype(f32)
    b = rest.astype(bf16)
    c = (rest - b.astype(f32)).astype(bf16)
    return a, b, c


class Place:
    def __init__(self, devices):
        side = math.isqrt(devices // 8)
        self.devices = devices
        self.sizes = (4, side, side)
        me = lax.axis_index("atoms")
        core = me % 2
        chip = me // 2
        last = chip % side
        middle = chip // side % side
        self.me = me
        self.core = core
        self.pos = (
            chip // (side * side),
            last + core * (middle - last),
            middle + core * (last - middle),
        )
        self.half = (side * side, 1 + core * (side - 1), side + core * (1 - side))
        self.step = tuple(2 * h for h in self.half)
        self.sibling = me + 1 - 2 * core
        self.plain = (self.pos[0], middle, last)
        self.plain_step = (2 * side * side, 2 * side, 2)

    def owner(self, q):
        return q[0] * self.step[0] + q[1] * self.step[1] + q[2] * self.step[2] + self.core

    def near(self, dim, up):
        return self.me + self.step[dim] if up else self.me - self.step[dim]

    def has(self, dim, up):
        return self.pos[dim] < self.sizes[dim] - 1 if up else self.pos[dim] > 0

    def peers(self, dim):
        n, p = self.sizes[dim], self.plain[dim]
        return [(r, (p + r) % n, self.me + ((p + r) % n - p) * self.plain_step[dim]) for r in range(1, n)]


class Units:
    def __init__(self, ref, rows, cols, base=0, part=(0, 1)):
        self.ref, self.rows, self.cols = ref, rows, cols
        self.per = WIDE // cols
        self.base = base
        self.high = rows // part[1]
        self.off = part[0] * self.high

    def window(self, s):
        s = s + self.base
        if self.per == 1:
            row, col = s * self.rows, slice(None)
        else:
            row = s // self.per * self.rows
            col = pl.ds(pl.multiple_of(s % self.per * self.cols, self.cols), self.cols)
        return (pl.ds(pl.multiple_of(row + self.off, 16), self.high), col)

    def at(self, s):
        return self.ref.at[self.window(s)]

    def get(self, s):
        return self.ref[self.window(s)]

    def put(self, s, value):
        self.ref[self.window(s)] = value

    def stretch(self, count):
        return self.ref.at[pl.ds(0, count * self.high // self.per), slice(None)]


def remote(src, dst, send, recv, device):
    return pltpu.make_async_remote_copy(
        src_ref=src,
        dst_ref=dst,
        send_sem=send,
        recv_sem=recv,
        device_id=(device,),
        device_id_type=MESH,
    )


def signal(sem, device):
    pl.semaphore_signal(sem, inc=1, device_id=(device,), device_id_type=MESH)


def others(place, dim):
    n, p = place.sizes[dim], place.pos[dim]
    if n == 2:
        return [(1 - p, None)]
    found = []
    for distance in range(1, n):
        found.append((p - distance, p >= distance))
        found.append((p + distance, p < n - distance))
    return found


def gated(cond, body):
    if cond is None:
        body()
    else:
        pl.when(cond)(body)


def both(a, b):
    return b if a is None else (a if b is None else a & b)


class Gather:
    def __init__(self, place, units, lo, hi, sems, direct=False, eager=True):
        self.place, self.units, self.lo, self.hi, self.sems = place, units, lo, hi, sems
        self.direct, self.eager = direct, eager
        _, na, nb = place.sizes
        self.waits = []
        self.shared = 0
        self.first_owner = 2 * lo * na * nb
        at = 2 * (hi - lo) * na * nb
        self.shared_send, self.core_recv = at, at + 1
        at += 2
        self.base = []
        for dim in range(3):
            length = (hi - lo) * (1, na, na * nb)[dim]
            self.base.append((at, at + length))
            at += 2 * length
        self.core_base = at

    @staticmethod
    def amount(devices, share):
        side = math.isqrt(devices // 8)
        return 2 + share * (2 + 2 * side + 5 * side * side)

    def linear(self, q, dim):
        _, na, nb = self.place.sizes
        q0 = q[0] - self.lo
        return (q0, q0 * na + q[1], (q0 * na + q[1]) * nb + q[2])[dim]

    def emit(self, cond, q, sem, device, core=False, once=None):
        owner = self.place.owner(q)
        common = cond is None or once is not None
        if common:
            sem = self.shared_send
            self.shared += 1 if once is None else once

        def copy():
            piece = self.units.at(owner)
            recv = self.core_recv if core else owner - self.first_owner
            return remote(piece, piece, self.sems.at[sem], self.sems.at[recv], device)

        gated(cond, lambda: copy().start())
        if not common:
            self.waits.append(lambda: gated(cond, lambda: copy().wait_send()))

    def onward(self, cond, q):
        place, p = self.place, self.place.pos[0]
        for up in (True, False):
            away = (p >= q[0]) if up else (p <= q[0])
            self.emit(
                both(cond, away & place.has(0, up)),
                q,
                self.base[0][0 if up else 1] + self.linear(q, 0),
                place.near(0, up),
            )

    def sideways(self, cond, q, dims, via=None, once=None):
        place = self.place
        for dim in dims:
            if place.sizes[dim] == 2:
                if dim != via:
                    toward = place.me + (1 - 2 * place.pos[dim]) * place.step[dim]
                    self.emit(
                        cond, q, self.base[dim][0] + self.linear(q, dim), toward, False, once
                    )
                continue
            for up in (True, False):
                open_end = place.has(dim, up)
                if dim == via:
                    p = place.pos[dim]
                    open_end = open_end & ((q[dim] < p) if up else (q[dim] > p))
                self.emit(
                    both(cond, open_end),
                    q,
                    self.base[dim][0 if up else 1] + self.linear(q, dim),
                    place.near(dim, up),
                )
        self.emit(cond, q, self.core_base + self.linear(q, 2), place.sibling, True, once)

    def wait(self, cond, q):
        owner = self.place.owner(q)
        piece = self.units.at(owner)
        gated(
            cond,
            lambda: remote(
                piece,
                piece,
                self.sems.at[self.shared_send],
                self.sems.at[owner - self.first_owner],
                self.place.sibling,
            ).wait_recv(),
        )

    def own(self):
        place, p = self.place, self.place.pos
        if self.direct:
            for r in range(1, 4):
                self.emit(None, p, 0, place.me + ((p[0] + r) % 4 - p[0]) * place.step[0])
            self.sideways(None, p, (2, 1))
            return
        for q0 in range(self.lo, self.hi):
            q = (q0, p[1], p[2])
            self.onward(p[0] == q0, q)
            if self.eager:
                self.sideways(p[0] == q0, q, (2, 1), None, 1)

    def column(self):
        p = self.place.pos
        if self.direct:
            for r in range(1, 4):
                q = ((p[0] + r) % 4, p[1], p[2])
                self.wait(None, q)
                self.sideways(None, q, (2, 1))
            return
        for q0 in range(self.lo, self.hi):
            q = (q0, p[1], p[2])
            self.wait(p[0] != q0, q)
            self.onward(p[0] != q0, q)
            if self.eager:
                self.sideways(p[0] != q0, q, (2, 1), None, 0)
            else:
                self.sideways(None, q, (2, 1))

    def second(self):
        for q0 in range(self.lo, self.hi):
            for qa, there in others(self.place, 1):
                q = (q0, qa, self.place.pos[2])
                self.wait(there, q)
                self.sideways(there, q, (2, 1), 1)

    def third(self):
        for qb, there in others(self.place, 2):
            for q0 in range(self.lo, self.hi):
                for qa in range(self.place.sizes[1]):
                    q = (q0, qa, qb)
                    self.wait(there, q)
                    self.sideways(there, q, (2,), 2)

    def across(self):
        _, na, nb = self.place.sizes
        piece = self.units.stretch((self.hi - self.lo) * na * nb)
        remote(
            piece,
            piece,
            self.sems.at[self.shared_send],
            self.sems.at[self.core_recv],
            self.place.sibling,
        ).wait_recv()

    def finish(self):
        for wait in self.waits:
            wait()
        if self.shared:
            piece = self.units.stretch(self.shared)
            remote(
                piece,
                piece,
                self.sems.at[self.shared_send],
                self.sems.at[self.core_recv],
                self.place.sibling,
            ).wait_send()
        self.waits, self.shared = [], 0


def landing(n):
    return 1 if n == 2 else n + 1


class Reduce:
    def __init__(self, place, units, lo, hi, land, sems, ready):
        self.place, self.units, self.lo, self.hi, self.land = place, units, lo, hi, land
        n0, na, nb = place.sizes
        self.count = (hi - lo) * na * nb
        lines = ((1, n0), (hi - lo, na), ((hi - lo) * na, nb))
        z_at = self.count
        b_at = z_at + landing(n0)
        a_at = b_at + lines[2][0] * landing(nb)
        self.land_at = (z_at, a_at, b_at)
        self.sems, self.ready = sems, ready
        self.shared = 0
        at = 4
        self.recv_at, self.up_at, self.down_at = [], [], []
        for units_here, n in lines:
            self.recv_at.append(at)
            at += units_here * landing(n)
            self.up_at.append(at)
            at += units_here * n
            self.down_at.append(at)
            at += units_here * n
        self.waits = []

    @staticmethod
    def slots(devices, share):
        side = math.isqrt(devices // 8)
        return share * side * side + landing(4) + share * (1 + side) * landing(side)

    @staticmethod
    def amount(devices, share):
        side = math.isqrt(devices // 8)
        total = 4
        for units_here, n in ((1, 4), (share, side), (share * side, side)):
            total += units_here * (landing(n) + 2 * n)
        return total

    def stage(self, k):
        if k == 0:
            self.start()
        elif k == 1:
            self.pairs()
        elif k < 4:
            self.along(4 - k)
        else:
            self.hop(0, k - 3, [(None,) + self.place.pos[1:]])

    def unit(self, dim, q):
        na = self.place.sizes[1]
        return (0, q[0] - self.lo, (q[0] - self.lo) * na + q[1])[dim]

    def add(self, owner, slot):
        self.units.put(owner, self.units.get(owner) + self.land.get(slot))

    def start(self):
        place = self.place
        if self.ready is not None:
            signal(self.ready.at[0], place.sibling)
            for dim in range(3):
                for up in (True, False):
                    pl.when(place.has(dim, up))(
                        lambda dim=dim, up=up: signal(
                            self.ready.at[1 + 2 * dim + (1 if up else 0)], place.near(dim, up)
                        )
                    )
            pl.semaphore_wait(self.ready.at[0], 1)
        per = place.sizes[1] * place.sizes[2]

        def copy(j):
            owner = 2 * (self.lo * per + j) + 1 - place.core
            return remote(
                self.units.at(owner), self.land.at(j), self.sems.at[0], self.sems.at[1], place.sibling
            )

        loop(self.count, lambda j: copy(j).start())
        self.shared += self.count

    def allow(self, dim):
        if self.ready is None:
            return
        for up in (True, False):
            pl.when(self.place.has(dim, up))(
                lambda up=up: pl.semaphore_wait(self.ready.at[1 + 2 * dim + (0 if up else 1)], 1)
            )

    def push(self, cond, dim, q, sem, slot, device):
        owner = self.place.owner(q)
        target = self.unit(dim, q) * landing(self.place.sizes[dim]) + slot
        recv = self.recv_at[dim] + target
        if cond is None:
            self.shared += 1
            sem, recv = 0, 1 + dim

        def copy():
            return remote(
                self.units.at(owner),
                self.land.at(self.land_at[dim] + target),
                self.sems.at[sem],
                self.sems.at[recv],
                device,
            )

        gated(cond, lambda: copy().start())
        if cond is not None:
            self.waits.append(lambda: gated(cond, lambda: copy().wait_send()))

    def arrived(self, sem, count):
        piece = self.land.stretch(count)
        remote(
            piece, piece, self.sems.at[0], self.sems.at[sem], self.place.sibling
        ).wait_recv()

    def pull(self, dim, q, slot):
        target = self.unit(dim, q) * landing(self.place.sizes[dim]) + slot
        piece = self.land.at(self.land_at[dim] + target)
        remote(
            piece,
            piece,
            self.sems.at[0],
            self.sems.at[self.recv_at[dim] + target],
            self.place.sibling,
        ).wait_recv()
        self.add(self.place.owner(q), self.land_at[dim] + target)

    def first(self, dim, q):
        place = self.place
        n, p = place.sizes[dim], place.pos[dim]
        u = self.unit(dim, q)
        if n == 2:
            toward = place.me + (1 - 2 * p) * place.step[dim]
            self.push(None, dim, q, self.up_at[dim] + u * n, 0, toward)
            return
        for up in (True, False):
            away = (q[dim] > 0) if up else (q[dim] < n - 1)
            self.push(
                (p == (0 if up else n - 1)) & away,
                dim,
                q,
                (self.up_at if up else self.down_at)[dim] + u * n + q[dim],
                self.slot_up(q[dim], 0) if up else self.slot_down(n, q[dim], n - 1),
                place.near(dim, up),
            )

    @staticmethod
    def slot_up(q, p):
        return q - (p + 1)

    @staticmethod
    def slot_down(n, q, p):
        to = p - 1
        return q + (n - to if to > 0 else 0)

    def order(self, dim):
        place = self.place
        if place.sizes[dim] == 2:
            return [1 - place.pos[dim], place.pos[dim]]
        return list(range(place.sizes[dim]))

    def mine(self, dim, at):
        return at is self.place.pos[dim]

    def pairs(self):
        place = self.place
        self.allow(2)
        self.arrived(1, self.count)
        for qb in self.order(2):
            for qa in self.order(1):
                for q0 in range(self.lo, self.hi):
                    q = (q0, qa, qb)
                    j = (q0 - self.lo) * place.half[0] + qa * place.half[1] + qb * place.half[2]
                    self.add(place.owner(q), j)
                    if not self.mine(2, qb):
                        self.first(2, q)

    def along(self, dim):
        place = self.place
        n, p = place.sizes[dim], place.pos[dim]
        self.allow(dim - 1)
        if dim == 2:
            rows = [(q0, qa) for qa in self.order(1) for q0 in range(self.lo, self.hi)]
        else:
            rows = [(q0,) for q0 in range(self.lo, self.hi)]

        def whole(row, at):
            return row + (at,) + place.pos[dim + 1 :]

        if n == 2:
            self.arrived(1 + dim, len(rows))
            for row in rows:
                q = whole(row, p)
                self.add(place.owner(q), self.land_at[dim] + self.unit(dim, q))
                if not self.mine(dim - 1, row[dim - 1]):
                    self.first(dim - 1, whole(row, p))
        else:
            for k in range(1, n):
                self.hop(dim, k, [whole(row, None) for row in rows])
            for row in rows:
                self.first(dim - 1, whole(row, p))

    def hop(self, dim, k, rows):
        place = self.place
        n, p = place.sizes[dim], place.pos[dim]
        lo, hi = (self.lo, self.hi) if dim == 0 else (0, n)
        for up in (True, False):
            here = k if up else n - 1 - k
            cond = p == here
            span = range(max(lo, here), hi) if up else range(lo, min(hi, here + 1))
            if len(span) == 0:
                continue

            def receive(up=up, here=here, span=span):
                for row in rows:
                    for at in span:
                        slot = at - here if up else at + (n - here if here > 0 else 0)
                        q = row[:dim] + (at,) + row[dim + 1 :]
                        self.pull(dim, q, slot)
                        if at != here:
                            self.hop_copy(dim, q, up, here).start()

            pl.when(cond)(receive)
            for row in rows:
                for at in span:
                    if at != here:
                        q = row[:dim] + (at,) + row[dim + 1 :]
                        self.waits.append(
                            lambda cond=cond, q=q, up=up, here=here: pl.when(cond)(
                                lambda: self.hop_copy(dim, q, up, here).wait_send()
                            )
                        )

    def hop_copy(self, dim, q, up, here):
        place = self.place
        n = place.sizes[dim]
        u = self.unit(dim, q)
        slot = self.slot_up(q[dim], here) if up else self.slot_down(n, q[dim], here)
        target = u * landing(n) + slot
        return remote(
            self.units.at(place.owner(q)),
            self.land.at(self.land_at[dim] + target),
            self.sems.at[(self.up_at if up else self.down_at)[dim] + u * n + q[dim]],
            self.sems.at[self.recv_at[dim] + target],
            place.near(dim, up),
        )

    def finish(self):
        for wait in self.waits:
            wait()
        piece = self.land.stretch(self.shared)
        remote(
            piece, piece, self.sems.at[0], self.sems.at[1], self.place.sibling
        ).wait_send()
        self.waits, self.shared = [], 0


class Total:
    def __init__(self, place, land, sems):
        self.place, self.land, self.sems = place, land, sems
        self.sizes = (2,) + place.sizes[::-1]
        self.at = [sum(self.sizes[:k]) for k in range(4)]
        self.waits = []

    @staticmethod
    def slots(devices):
        return 6 + 2 * math.isqrt(devices // 8)

    def lines(self, k):
        place = self.place
        if k == 0:
            return place.core, [(1, 1 - place.core, place.sibling)]
        return place.plain[3 - k], place.peers(3 - k)

    def send(self, k, value):
        p, peers = self.lines(k)
        here = self.land.at[self.at[k] + p]
        self.land[self.at[k] + p] = value
        half = self.at[3] + self.sizes[3]
        for r, _, device in peers:

            def copy(r=r, device=device):
                sems = self.sems
                return remote(
                    here, here, sems.at[self.at[k] + r], sems.at[half + self.at[k] + p], device
                )

            copy().start()
            self.waits.append(lambda copy=copy: copy().wait_send())

    def take(self, k):
        _, peers = self.lines(k)
        half = self.at[3] + self.sizes[3]
        for r, at, device in peers:
            there = self.land.at[self.at[k] + at]
            remote(
                there, there, self.sems.at[0], self.sems.at[half + self.at[k] + at], device
            ).wait_recv()
        total = self.land[self.at[k]]
        for s in range(1, self.sizes[k]):
            total = total + self.land[self.at[k] + s]
        return total

    def pass_on(self, k):
        value = self.take(k)
        if k < 3:
            self.send(k + 1, value)
        return value

    def finish(self):
        for wait in self.waits:
            wait()
        self.waits = []


class Ring:
    def __init__(self, me, devices, land, sems):
        self.after = (me + 1) % devices
        self.before = (me + devices - 1) % devices
        self.land, self.sems = land, sems

    def copies(self, to_before, to_after):
        return (
            remote(to_before, self.land.at[1], self.sems.at[0], self.sems.at[1], self.before),
            remote(to_after, self.land.at[0], self.sems.at[2], self.sems.at[3], self.after),
        )

    def start(self, to_before, to_after):
        for copy in self.copies(to_before, to_after):
            copy.start()

    def wait(self, to_before, to_after):
        for copy in self.copies(to_before, to_after):
            copy.wait_recv()

    def finish(self, to_before, to_after):
        for copy in self.copies(to_before, to_after):
            copy.wait_send()


def unit_shape(amount):
    across = min(amount, PANEL)
    return amount // across * BLOCK_ROWS, across * BLOCK_COLS


def own_unit(units, me, blocks):
    across = units.cols // BLOCK_COLS
    rows = []
    for a in range(units.rows // BLOCK_ROWS):
        row = [blocks[a * across + b].astype(bf16) for b in range(across)]
        rows.append(jnp.concatenate(row, axis=1))
    units.put(me, jnp.concatenate(rows, axis=0))


def network(
    idx_ref,
    positions_ref,
    species_ref,
    counts_ref,
    cot_ref,
    scale_ref,
    shift_ref,
    weight_ref,
    state_ref,
    blocks_ref,
    late_in,
    energy_ref,
    forces_ref,
    vector_ref,
    first_out,
    late_out,
    first_w,
    late_w,
    hot,
    z_t,
    z_r,
    geo,
    yrow,
    env_b,
    ee_t,
    en2_t,
    s1_t,
    s2_t,
    gam,
    dlt,
    coef,
    ds_t,
    de_t,
    dy,
    dg,
    dw_t,
    dw_r,
    dpf,
    den,
    lat,
    hid,
    low0,
    act1,
    sl1,
    low1,
    act2,
    sl2,
    low2,
    stage,
    halo,
    force_in,
    sides,
    vector_in,
    pack_ref,
    low_gather,
    mid_gather,
    high_gather,
    late_gather,
    late_sems,
    first_sems,
    ring_sems,
    vector_sems,
    ready,
):
    s_r = dw_r
    fact = den

    wee_t = dw_t.at[:, 0:LATENT]
    we2_t = dw_t.at[0:128, 0:LATENT]
    devices = lax.axis_size("atoms")
    me = lax.axis_index("atoms")
    place = Place(devices)
    own_at = pack_ref.at[0:8]
    first_units = Units(first_w, *unit_shape(blocks_ref.shape[0]))
    late_units = Units(late_w, *unit_shape(late_in.shape[0]))
    top = place.sizes[0]
    middle = top // 2

    def pieces(k, count):
        return Units(first_w, first_units.rows, first_units.cols, part=(k, count))

    def free(ref, units, k=0, count=1):
        slots = Reduce.slots(devices, 1)
        return Units(ref, units.rows // count, units.cols, base=k * slots)

    gather_low = [Gather(place, pieces(k, PIECES), 0, 1, low_gather.at[k]) for k in range(PIECES)]
    gather_mid = Gather(place, first_units, 1, middle, mid_gather)
    gather_high = Gather(place, first_units, middle, top, high_gather)
    gather_late = Gather(place, late_units, 0, top, late_gather, True)
    sum_out = Reduce(
        place, late_units, middle, top, free(low2, late_units), late_sems.at[0], ready.at[0]
    )
    sum_lat = Reduce(
        place, late_units, 0, middle, free(sl2, late_units), late_sems.at[1], ready.at[1]
    )
    sum_first = [
        [
            Reduce(
                place,
                pieces(k, SUM_PIECES[z]),
                z,
                z + 1,
                free(ref, first_units, k, SUM_PIECES[z]),
                first_sems.at[PIECES * z + k],
                ready.at[2 + z] if k == 0 else None,
            )
            for k in range(SUM_PIECES[z])
        ]
        for z, ref in enumerate((hid, low0, low2, act2))
    ]

    def advance(z, stage):
        for part in sum_first[z]:
            part.stage(stage)
    link_halo = Ring(me, devices, halo, ring_sems.at[0])
    link_force = Ring(me, devices, force_in, ring_sems.at[1])
    sum_vector = Total(place, vector_in, vector_sems)

    barrier = pltpu.get_barrier_semaphore()
    partners = [place.sibling, link_halo.before, link_halo.after]
    for dim in range(3):
        partners += [device for _, _, device in place.peers(dim)]
    for device in partners:
        signal(barrier, device)
    for part in (slice(0, PLANE), slice(PLANE, LANES)):
        pack_ref[0:3, part] = positions_ref[...]
        pack_ref[3:4, part] = species_ref[...].astype(f32)
        pack_ref[4:5, part] = counts_ref[...].astype(f32)
        pack_ref[5:6, part] = cot_ref[...]
    pack_ref[6:16] = jnp.zeros((10, LANES), f32)
    pack_ref[6:7, 0:SPECIES] = scale_ref[...]
    pack_ref[7:8, 0:SPECIES] = shift_ref[...]
    pack_ref[8:9] = weight_ref[...]
    pack_ref[9:10] = state_ref[...]
    own_unit(first_units, me, blocks_ref)
    own_unit(late_units, me, late_in)
    pl.semaphore_wait(barrier, len(partners))
    link_halo.start(own_at, own_at)
    for part in gather_low:
        part.own()
    gather_high.own()

    ids = lax.broadcasted_iota(jnp.int32, (3 * PLANE, LANES), 0)

    whole = PLANE * devices
    coef[0, :, 0:SLOTS] = idx_ref[...].astype(f32)
    listed = coef[0].T[: SLOTS + 6].astype(jnp.int32) - (me - 1) * PLANE
    listed = jnp.where(
        listed < 0, listed + whole, jnp.where(listed >= whole, listed - whole, listed)
    )
    for t in range(TILES):
        near = jnp.concatenate([listed[2 * t : 2 * t + 1], listed[2 * t + 1 : 2 * t + 2]], axis=1)
        hot[:, t * LANES : (t + 1) * LANES] = jnp.where(ids == near, 1.0, 0.0).astype(bf16)

    link_halo.wait(own_at, own_at)
    own = pack_ref[0:8]
    lane = lax.broadcasted_iota(jnp.int32, (8, LANES), 1)
    row = lax.broadcasted_iota(jnp.int32, (8, LANES), 0)
    edge = spacing * devices
    x_row = row == 0
    before = halo[0] - jnp.where(x_row, jnp.where(me == 0, edge, 0.0), 0.0)
    after = halo[1] + jnp.where(x_row, jnp.where(me == devices - 1, edge, 0.0), 0.0)
    rank_y = ((lane & (PLANE - 1)) >> 3).astype(f32)
    rank_z = (lane & (SIDE - 1)).astype(f32)
    table = jnp.concatenate([jnp.where(lane < PLANE, before, own), after], axis=1)
    ranks = jnp.where(row == 4, rank_y, rank_z)
    table = jnp.where(
        jnp.concatenate([row, row], axis=1) < 4, table, jnp.concatenate([ranks, ranks], axis=1)
    )[:, : 3 * PLANE]
    ga, gb, gc = parts(table)
    got = nn(ga, hot[...]) + nn(gb, hot[...]) + nn(gc, hot[...])
    mine = jnp.concatenate([own] * TILES, axis=1)
    lane = lax.broadcasted_iota(jnp.int32, (1, ROWS), 1)
    slot = lane >> 6
    atom = lane & (PLANE - 1)
    for part in gather_low:
        part.column()
    for part in gather_low:
        part.second()
    gather_mid.own()
    gather_mid.column()

    def wrapped(step):
        return jnp.where(step > 1.5, -8.0, jnp.where(step < -1.5, 8.0, 0.0)) * spacing

    disp = [
        got[0:1] - mine[0:1],
        got[1:2] - mine[1:2] + wrapped(got[4:5] - (atom >> 3).astype(f32)),
        got[2:3] - mine[2:3] + wrapped(got[5:6] - (atom & (SIDE - 1)).astype(f32)),
    ]
    length = jnp.sqrt(disp[0] * disp[0] + disp[1] * disp[1] + disp[2] * disp[2])
    inverse = 1.0 / length
    unit = [disp[0] * inverse, disp[1] * inverse, disp[2] * inverse]
    angle = length * (math.pi / cutoff_radius)
    sin_k = [jnp.sin(angle)]
    cos_k = [jnp.cos(angle)]
    sin_k.append(2.0 * cos_k[0] * sin_k[0])
    cos_k.append(2.0 * cos_k[0] * cos_k[0] - 1.0)
    for k in range(2, BESSEL):
        sin_k.append(2.0 * cos_k[0] * sin_k[k - 1] - sin_k[k - 2])
        cos_k.append(2.0 * cos_k[0] * cos_k[k - 1] - cos_k[k - 2])
    sines = jnp.concatenate(sin_k, axis=0)
    cosines = jnp.concatenate(cos_k, axis=0)
    bessel = (math.sqrt(2.0 / cutoff_radius) * inverse) * sines
    scaled = length * (1.0 / cutoff_radius)
    t2 = scaled * scaled
    t4 = t2 * t2
    t5 = t4 * scaled
    t6 = t4 * t2
    envelope = 1.0 - 28.0 * t6 + 48.0 * (t6 * scaled) - 21.0 * (t4 * t4)
    denvelope = (-168.0 * t5 + 336.0 * t6 - 168.0 * (t6 * scaled)) * (1.0 / cutoff_radius)
    live = jnp.where(slot.astype(f32) < mine[4:5], 1.0, 0.0)

    kind = lax.broadcasted_iota(jnp.int32, (KINDS, LANES), 0).astype(f32)
    is_kind = kind == own[3:4]
    by_kind = own.T
    scale = jnp.sum(jnp.where(is_kind, by_kind[:KINDS, 6:7], 0.0), axis=0, keepdims=True)
    shift = jnp.sum(jnp.where(is_kind, by_kind[:KINDS, 7:8], 0.0), axis=0, keepdims=True)
    cot = jnp.concatenate([own[5:6] * scale] * TILES, axis=1) * live
    weight = cot * envelope

    root3 = math.sqrt(3.0)
    root15 = math.sqrt(15.0)
    root5 = math.sqrt(5.0)
    ux, uy, uz = unit
    yrow[0:8] = jnp.concatenate(
        [
            root3 * ux,
            root3 * uy,
            root3 * uz,
            root15 * ux * uy,
            root15 * uy * uz,
            0.5 * root5 * (3.0 * uz * uz - 1.0),
            root15 * ux * uz,
            0.5 * root15 * (ux * ux - uy * uy),
        ],
        axis=0,
    )
    yrow[8:16] = yrow[0:8] * (live * env_scale)
    yrow[16:17] = live * env_scale
    geo[0:8] = jnp.concatenate([ux, uy, uz, inverse, envelope, denvelope, live, cot], axis=0)
    geo[8:16] = math.sqrt(2.0 / cutoff_radius) * (
        (math.pi / cutoff_radius)
        * lax.broadcasted_iota(jnp.int32, (BESSEL, ROWS), 0).astype(f32)
        * cosines
        + (math.pi / cutoff_radius) * cosines
        - sines * inverse
    ) * inverse


    def one_hots(t):
        row = lax.broadcasted_iota(jnp.int32, (LANES, LANES), 0).astype(f32)
        here = jnp.where(row == own[3:4] + float(BESSEL), 1.0, 0.0)
        there = jnp.where(row == kinds_near[t] + float(BESSEL + SPECIES), 1.0, 0.0)
        return here + there

    kinds_near = [got[3:4, t * LANES : (t + 1) * LANES] for t in range(TILES)]
    gather_mid.second()
    for part in gather_low:
        part.third()
    gather_high.column()
    for t in range(TILES):
        at = slice(t * LANES, (t + 1) * LANES)
        column = jnp.concatenate([bessel[:, at], one_hots(t)[BESSEL:]], axis=0)
        z_t[:, at] = column.astype(bf16)
        z_r[at, :] = column.T.astype(bf16)
        env_b[at, :] = jnp.broadcast_to(envelope[:, at], (LANES, LANES)).T
        fact[at, :] = jnp.broadcast_to(weight[:, at], (LANES, LANES)).T
    for part in gather_low:
        part.across()


    def twice(x):
        return jnp.concatenate([x] * (STRIP // LANES), axis=1)

    def in_body(n, r):
        pre = nn(z_r[r], cols_panel(first_w, W_INPUT, n))
        hid[r, panel(n, STRIP)] = (pre * sigmoid(pre)).astype(bf16)

    loop_panels(in_body)
    gather_mid.third()
    gather_high.second()
    gather_late.own()
    gather_mid.across()

    def two_body(n, r):
        zero = nn(hid[r], cols_panel(first_w, W_TWO, n)) * twice(env_b[r])
        lat[r, panel(n, STRIP)] = zero
        low0[r, panel(n, STRIP)] = zero.astype(bf16)

    loop_panels(two_body)
    gather_high.third()

    def transposed_product(out, weights, right, width=256):
        at = 0
        while at < ROWS:
            end = min(at + width, ROWS)
            out[:, at:end] = nt(weights, right[at:end, :])
            at = end

    wee_t[0:128, :] = narrow(first_w, W_EMBED).T
    wee_t[128:256, :] = narrow(first_w, W_ENV_ONE).T
    transposed_product(ee_t, wee_t[...], low0)
    gather_late.column()

    def environment(out, v0_ref, v0_at, v1_at):
        for m in range(9):
            total = None
            begin = v0_at if m == 0 else v1_at
            y = yrow[16:17, :] if m == 0 else yrow[7 + m : 8 + m, :]
            for t in range(TILES):
                at = slice(t * LANES, (t + 1) * LANES)
                term = v0_ref[begin : begin + CHANNELS, at] * y[:, at]
                total = term if total is None else total + term
            out[m] = halves(total)

    def put_scalars(t, s_t, rows):
        s_t[:, lanes(t)] = jnp.concatenate(rows, axis=0).astype(bf16)
        filled = jnp.concatenate(rows + [jnp.zeros_like(rows[0])], axis=0)
        flipped = filled.T.astype(bf16)
        s_r[lanes(t), :] = flipped

    def weighted(y, first, count, source, offset):
        total = None
        for m in range(count):
            term = y[first + m : first + m + 1] * source[offset + m]
            total = term if total is None else total + term
        return total

    environment(gam, ee_t, 128, 192)

    def scalars_one(t):
        e0 = ee_t[0:64, lanes(t)]
        e1 = ee_t[64:128, lanes(t)]
        y = yrow[0:8, lanes(t)]
        put_scalars(
            t,
            s1_t,
            [e0 * gam[0], e1 * weighted(y, 0, 3, gam, 1), e1 * weighted(y, 3, 5, gam, 4)],
        )

    beside(6, lambda i: None, scalars_one)
    gather_high.across()

    def pre_one(n, r):
        pre = nn(low0[r], cols_panel(first_w, W_LAT_ONE, n)) + nn(
            s_r[r, : 3 * CHANNELS], cols_panel(first_w, W_SCAL_ONE, n)
        )
        sig = sigmoid(pre)
        act = pre * sig
        act1[r, panel(n, STRIP)] = act.astype(bf16)
        sl1[r, panel(n, STRIP)] = (sig + act * (1.0 - sig)).astype(bf16)

    loop_panels(pre_one)
    gather_late.second()

    def out_one(n, r):
        new = (lat[r, panel(n, STRIP)] + nn(act1[r], cols_panel(first_w, W_OUT_ONE, n))) * half_root
        lat[r, panel(n, STRIP)] = new
        low1[r, panel(n, STRIP)] = new.astype(bf16)

    loop_panels(out_one)
    gather_late.third()
    we2_t[...] = narrow(first_w, W_ENV_TWO).T
    transposed_product(en2_t, we2_t[...], low1)
    environment(dlt, en2_t, 0, 64)

    g0 = gam[0]
    coef[0] = g0 * dlt[0]
    for m in range(3):
        a, b = 1 + (m + 1) % 3, 1 + (m + 2) % 3
        coef[1 + m] = g0 * dlt[1 + m] + (gam[a] * dlt[b] - gam[b] * dlt[a])
    coef[9] = gam[1] * dlt[1] + gam[2] * dlt[2] + gam[3] * dlt[3]
    second = None
    for m in range(4, 9):
        coef[m] = g0 * dlt[m]
        term = gam[m] * dlt[m]
        second = term if second is None else second + term
    coef[10] = second

    def scalars_two(t):
        e0 = ee_t[0:64, lanes(t)]
        e1 = ee_t[64:128, lanes(t)]
        y = yrow[0:8, lanes(t)]
        put_scalars(
            t,
            s2_t,
            [
                e0 * coef[0],
                e1 * weighted(y, 0, 3, coef, 1) + e0 * coef[9],
                e1 * weighted(y, 3, 5, coef, 4) + e0 * coef[10],
            ],
        )

    beside(6, lambda i: None, scalars_two)
    gather_late.across()

    for part in gather_low + [gather_mid, gather_high, gather_late]:
        part.finish()
    def pre_two(n, r):
        pre = nn(low1[r], cols_panel(late_w, W_LAT_TWO, n)) + nn(
            s_r[r, : 3 * CHANNELS], cols_panel(first_w, W_SCAL_TWO, n)
        )
        sig = sigmoid(pre)
        act = pre * sig
        act2[r, panel(n, STRIP)] = act.astype(bf16)
        sl2[r, panel(n, STRIP)] = (sig + act * (1.0 - sig)).astype(bf16)

    loop_panels(pre_two)

    def out_two(n, r):
        new = (lat[r, panel(n, STRIP)] + nn(act2[r], cols_panel(late_w, W_OUT_TWO, n))) * half_root
        low2[r, panel(n, STRIP)] = new.astype(bf16)

    loop_panels(out_two)

    vec = jnp.broadcast_to(pack_ref[8:9], (8, LANES))
    stage[...] = narrow(first_w, W_FINAL)

    def read_out(i):
        r = pl.ds(pl.multiple_of(i * 416, 16), 416)
        pre = nn(low2[r, :], stage[...])
        sig = sigmoid(pre)
        final_act = pre * sig
        dpf[r, :] = (fact[r, :] * vec[0:1] * (sig + final_act * (1.0 - sig))).astype(bf16)
        fact[r, :] = final_act

    loop(4, read_out)
    fa, fb, _ = parts(fact[...])
    va, vb, _ = parts(vec)
    value = (nt(va, fa) + (nt(va, fb) + nt(vb, fa)))[0:1]
    geo_live = geo[6:7]
    geo_env = geo[4:5]
    geo_cot = geo[7:8]
    edge_energy = geo_live * geo_env * value
    summed = None
    for t in range(TILES):
        term = edge_energy[:, t * LANES : (t + 1) * LANES]
        summed = term if summed is None else summed + term
    energy_ref[...] = scale * halves(summed) + shift
    all_weights = jnp.broadcast_to(geo_cot * geo_env, (8, ROWS))
    wa, wb, _ = parts(all_weights)
    sum_vector.send(0, nn(wa, fa) + (nn(wa, fb) + nn(wb, fa)))
    geo[16:17] = geo_cot * value

    def big_step(out, where, left, right):
        def step(i):
            grad = tn(left[:, panel(i, STRIP)], right[...])
            out[pl.ds(pl.multiple_of(where[0] + i * STRIP, 64), STRIP), :] = grad.astype(bf16)

        return step

    def big_grad(out, where, left, right):
        loop(LATENT // STRIP, big_step(out, where, left, right))

    def wide_step(out, where, left, right):
        def step(n):
            out[where[0] : where[0] + where[1], panel(n)] = nn(
                left[...], right[:, panel(n)]
            ).astype(bf16)

        return step

    def wide_grad(out, where, left, right):
        loop(4, wide_step(out, where, left, right))

    def narrow_grad(left, right, put):
        def step(n):
            put(n, nn(left, right[:, panel(n)]).T.astype(bf16))

        loop(4, step)

    def put_narrow(where, n, grad):
        row = pl.multiple_of(where[0] + n // 2 * BLOCK_ROWS, BLOCK_ROWS)
        col = pl.multiple_of(n % 2 * 512, 512)
        first_w[pl.ds(row, BLOCK_ROWS), pl.ds(col, 512)] = jnp.concatenate(
            [grad[b * BLOCK_ROWS : (b + 1) * BLOCK_ROWS] for b in range(4)], axis=1
        )

    def put_stage(n, grad):
        stage[panel(n), :] = grad

    def back_final(n, r):
        grad = nt(dpf[r], narrow_panel(first_w, W_FINAL, n)) * half_root
        lat[r, panel(n, STRIP)] = grad
        low2[r, panel(n, STRIP)] = grad.astype(bf16)

    def back_out_two(n, r):
        grad = nt(low2[r], rows_panel(late_w, W_OUT_TWO, n))
        sl2[r, panel(n, STRIP)] = (grad * sl2[r, panel(n, STRIP)].astype(f32)).astype(bf16)

    def tensors_two(t):
        e0 = ee_t[0:64, lanes(t)]
        e1 = ee_t[64:128, lanes(t)]
        y = yrow[0:8, lanes(t)]
        r0 = ds_t[0:64, lanes(t)]
        r1 = ds_t[64:128, lanes(t)]
        r2 = ds_t[128:192, lanes(t)]
        de_t[0:64, lanes(t)] = r0 * coef[0] + r1 * coef[9] + r2 * coef[10]
        de_t[64:128, lanes(t)] = r1 * weighted(y, 0, 3, coef, 1) + r2 * weighted(y, 3, 5, coef, 4)
        p1 = r1 * e1
        p2 = r2 * e1
        rows = []
        for m in range(8):
            p = p1 if m < 3 else p2
            rows.append(jnp.sum(p * coef[1 + m], axis=0, keepdims=True))
            dg[1 + m] += p * y[m : m + 1]
        dy[:, lanes(t)] = jnp.concatenate(rows, axis=0)
        dg[0] += r0 * e0
        dg[9] += r1 * e0
        dg[10] += r2 * e0

    def environment_back(t, grads, source, v1_at, at):
        y4 = yrow[8:16, lanes(t)]
        l4 = yrow[16:17, lanes(t)]
        v1 = source[v1_at : v1_at + 64, lanes(t)]
        low = l4 * grads[0]
        high = weighted(y4, 0, 8, grads, 1)
        both = jnp.concatenate([low, high], axis=0)
        dw_t[at : at + 128, lanes(t)] = both.astype(bf16)
        dw_r[lanes(t), at : at + 128] = both.T.astype(bf16)
        v1 = v1 * l4
        rows = [jnp.sum(v1 * grads[1 + m], axis=0, keepdims=True) for m in range(8)]
        dy[:, lanes(t)] += jnp.concatenate(rows, axis=0)

    def back_lat_two(n, r):
        grad = (
            lat[r, panel(n, STRIP)]
            + nt(sl2[r], rows_panel(late_w, W_LAT_TWO, n))
            + nt(dw_r[r, 128:256], narrow_panel(first_w, W_ENV_TWO, n))
        ) * half_root
        lat[r, panel(n, STRIP)] = grad
        act2[r, panel(n, STRIP)] = grad.astype(bf16)

    def back_out_one(n, r):
        grad = nt(act2[r], rows_panel(first_w, W_OUT_ONE, n))
        sl1[r, panel(n, STRIP)] = (grad * sl1[r, panel(n, STRIP)].astype(f32)).astype(bf16)

    def tensors_one(t):
        e0 = ee_t[0:64, lanes(t)]
        e1 = ee_t[64:128, lanes(t)]
        y = yrow[0:8, lanes(t)]
        r0 = ds_t[0:64, lanes(t)]
        r1 = ds_t[64:128, lanes(t)]
        r2 = ds_t[128:192, lanes(t)]
        low = de_t[0:64, lanes(t)] + r0 * gam[0]
        high = (
            de_t[64:128, lanes(t)]
            + r1 * weighted(y, 0, 3, gam, 1)
            + r2 * weighted(y, 3, 5, gam, 4)
        )
        both = jnp.concatenate([low, high], axis=0)
        dw_t[0:128, lanes(t)] = both.astype(bf16)
        dw_r[lanes(t), 0:128] = both.T.astype(bf16)
        p1 = r1 * e1
        p2 = r2 * e1
        rows = []
        for m in range(8):
            p = p1 if m < 3 else p2
            rows.append(jnp.sum(p * gam[1 + m], axis=0, keepdims=True))
            coef[1 + m] += p * y[m : m + 1]
        dy[:, lanes(t)] += jnp.concatenate(rows, axis=0)
        coef[0] += r0 * e0

    def back_lat_one(n, r):
        both = jnp.concatenate(
            [narrow_panel(first_w, W_EMBED, n), narrow_panel(first_w, W_ENV_ONE, n)], axis=1
        )
        grad = (
            lat[r, panel(n, STRIP)]
            + nt(sl1[r], rows_panel(first_w, W_LAT_ONE, n))
            + nt(dw_r[r], both)
        )
        low1[r, panel(n, STRIP)] = (grad * twice(env_b[r])).astype(bf16)
        part = grad * low0[r, panel(n, STRIP)].astype(f32)
        for b in range(STRIP // LANES):
            den[r] += part[:, b * LANES : (b + 1) * LANES]

    def back_two(n, r):
        grad = nt(low1[r], rows_panel(first_w, W_TWO, n))
        pre = nn(z_r[r], cols_panel(first_w, W_INPUT, n))
        sig = sigmoid(pre)
        act1[r, panel(n, STRIP)] = (grad * (sig + pre * sig * (1.0 - sig))).astype(bf16)

    def lat_one_grad(low, high):
        grad = tn(low0[:, low:high], sl1[...])
        first_w[W_LAT_ONE[0] + low : W_LAT_ONE[0] + high, :] = grad.astype(bf16)

    narrow_grad(dpf[...].T, low2, put_stage)
    loop_panels(back_final)
    loop(4, lambda n: put_narrow(W_FINAL, n, stage[panel(n), :]))
    loop_panels(back_out_two)
    transposed_product(ds_t, first_w[W_SCAL_TWO[0] : W_SCAL_TWO[0] + W_SCAL_TWO[1], :], sl2)
    dg[...] = jnp.zeros_like(dg)
    beside(2, big_step(late_w, W_OUT_TWO, act2, low2), tensors_two)
    sum_vector.pass_on(0)
    sum_out.stage(0)
    total = [halves(dg[m]) for m in range(11)]
    g0 = gam[0]
    d0 = dlt[0]
    new_g0 = total[0] * d0
    for m in range(1, 9):
        new_g0 = new_g0 + total[m] * dlt[m]
    dlt_grads = [total[0] * g0]
    gam_grads = [new_g0]
    for m in range(3):
        a, b = 1 + (m + 1) % 3, 1 + (m + 2) % 3
        dlt_grads.append(
            total[1 + m] * g0 + total[9] * gam[1 + m] + (total[a] * gam[b] - total[b] * gam[a])
        )
        gam_grads.append(total[9] * dlt[1 + m] + (dlt[a] * total[b] - dlt[b] * total[a]))
    for m in range(4, 9):
        dlt_grads.append(total[m] * g0 + total[10] * gam[m])
        gam_grads.append(total[10] * dlt[m])
    for m in range(9):
        dlt[m] = dlt_grads[m]
        dg[m] = gam_grads[m]
    beside(
        4,
        wide_step(first_w, W_SCAL_TWO, s2_t, sl2),
        lambda t: environment_back(t, dlt, en2_t, 64, 128),
    )
    sum_out.stage(1)
    loop_panels(back_lat_two)
    sum_out.stage(2)
    big_grad(late_w, W_LAT_TWO, low1, sl2)
    sum_vector.pass_on(1)
    sum_out.stage(3)
    sum_lat.stage(0)
    loop_panels(back_out_one)
    sum_out.stage(4)
    sum_lat.stage(1)
    transposed_product(ds_t, first_w[W_SCAL_ONE[0] : W_SCAL_ONE[0] + W_SCAL_ONE[1], :], sl1)
    narrow_grad(dw_t[128:256, :], low1, functools.partial(put_narrow, W_ENV_TWO))
    for m in range(9):
        coef[m] = jnp.zeros((CHANNELS, LANES), f32)
    beside(2, big_step(first_w, W_OUT_ONE, act1, act2), tensors_one)
    sum_vector.pass_on(2)
    sum_out.stage(5)
    sum_lat.stage(2)
    advance(3, 0)
    for m in range(9):
        dg[m] = dg[m] + halves(coef[m])
    beside(
        4,
        wide_step(first_w, W_SCAL_ONE, s1_t, sl1),
        lambda t: environment_back(t, dg, ee_t, 192, 128),
    )
    advance(3, 1)
    sum_out.stage(6)
    sum_lat.stage(3)
    den[...] = jnp.zeros_like(den)
    loop_panels(back_lat_one)
    lat_one_grad(640, 1024)
    sum_lat.stage(4)
    advance(3, 2)
    advance(2, 0)
    loop_panels(back_two)
    sum_lat.stage(5)
    advance(3, 3)
    advance(2, 1)
    big_grad(first_w, W_TWO, hid, low1)
    transposed_product(ds_t.at[0:64], first_w[0:64, :], act1)
    wide_grad(first_w, W_INPUT, z_t, act1)
    advance(0, 0)
    advance(2, 2)
    narrow_grad(dw_t[0:128, :], low0, functools.partial(put_narrow, W_EMBED))
    narrow_grad(dw_t[128:256, :], low0, functools.partial(put_narrow, W_ENV_ONE))
    advance(3, 4)
    advance(0, 1)
    lat_one_grad(0, 384)
    lat_one_grad(384, 640)
    advance(1, 0)
    advance(3, 5)
    advance(2, 3)
    sum_lat.stage(6)
    advance(0, 2)
    dbessel = ds_t[0:8, :]
    da, db, _ = parts(den[...])
    ones = jnp.ones((8, LANES), bf16)
    through = (nt(ones, da) + nt(ones, db))[0:1]
    ux, uy, uz = geo[0:1], geo[1:2], geo[2:3]
    inverse = geo[3:4]
    envelope = geo[4:5]
    denv = geo[16:17] + through / envelope
    dlength = jnp.sum(dbessel * geo[8:16], axis=0, keepdims=True) + denv * geo[5:6]
    g = [dy[m : m + 1, :] for m in range(8)]
    dux = root3 * g[0] + root15 * (uy * g[3] + uz * g[6] + ux * g[7])
    duy = root3 * g[1] + root15 * (ux * g[3] + uz * g[4] - uy * g[7])
    duz = root3 * g[2] + root15 * (uy * g[4] + ux * g[6]) + (3.0 * root5) * uz * g[5]
    along = dlength - (ux * dux + uy * duy + uz * duz) * inverse
    near = jnp.concatenate(
        [
            dux * inverse + ux * along,
            duy * inverse + uy * along,
            duz * inverse + uz * along,
            jnp.zeros((5, ROWS), f32),
        ],
        axis=0,
    )
    summed = None
    for t in range(TILES):
        term = near[:, t * LANES : (t + 1) * LANES]
        summed = term if summed is None else summed + term
    centre = halves(summed)
    na, nb, nc = parts(near)
    spread = nt(na, hot[...]) + nt(nb, hot[...]) + nt(nc, hot[...])
    sides[0] = spread[:, :LANES]
    sides[1, :, 0:PLANE] = spread[:, LANES:]
    link_force.start(sides.at[0], sides.at[1])
    advance(1, 1)
    advance(2, 4)
    advance(0, 3)
    advance(3, 6)
    advance(0, 4)
    for step in range(6):
        for k in range(max(SUM_PIECES[:3])):
            for z, after in ((0, 5), (1, 2), (2, 5)):
                if k < SUM_PIECES[z] and after <= after + step - k < 7:
                    sum_first[z][k].stage(after + step - k)
    link_force.wait(sides.at[0], sides.at[1])
    forces_ref[...] = (
        centre - pltpu.roll(sides[0], PLANE, 1) - force_in[1] - force_in[0]
    )
    total = sum_vector.pass_on(3)
    normed = total * lax.rsqrt(jnp.sum(total[0:1] * total[0:1]) * (1.0 / FINAL) + epsilon)
    state = decay_rate * pack_ref[9:10] + (1.0 - decay_rate) * normed * normed
    vector_ref[0:1] = total[0:1]
    vector_ref[1:2] = state[0:1]
    vector_ref[2:3] = (pack_ref[8:9] - vector_rate * normed * lax.rsqrt(state + epsilon))[0:1]
    first_out[...] = first_units.get(me)
    late_out[...] = late_units.get(me)
    for group in sum((list(parts) for parts in sum_first), [sum_out, sum_lat, sum_vector]):
        group.finish()
    link_halo.finish(own_at, own_at)
    link_force.finish(sides.at[0], sides.at[1])


def run_network(devices, small, blocks, late):
    S = jax.ShapeDtypeStruct
    wide = pltpu.VMEM((ROWS, LATENT), bf16)
    slab = pltpu.VMEM((ROWS, LANES), f32)
    panels = lambda amount: pltpu.VMEM((amount * devices // PANEL * BLOCK_ROWS, WIDE), bf16)
    scratch = [
        panels(blocks.shape[0]),
        panels(late.shape[0]),
        pltpu.VMEM((3 * PLANE, ROWS), bf16),
        pltpu.VMEM((LANES, ROWS), bf16),
        pltpu.VMEM((ROWS, LANES), bf16),
        pltpu.VMEM((24, ROWS), f32),
        pltpu.VMEM((24, ROWS), f32),
        slab,
        pltpu.VMEM((256, ROWS), f32),
        pltpu.VMEM((128, ROWS), f32),
        pltpu.VMEM((192, ROWS), bf16),
        pltpu.VMEM((192, ROWS), bf16),
        pltpu.VMEM((9, CHANNELS, LANES), f32),
        pltpu.VMEM((9, CHANNELS, LANES), f32),
        pltpu.VMEM((11, CHANNELS, LANES), f32),
        pltpu.VMEM((192, ROWS), f32),
        pltpu.VMEM((128, ROWS), f32),
        pltpu.VMEM((8, ROWS), f32),
        pltpu.VMEM((11, CHANNELS, LANES), f32),
        pltpu.VMEM((256, ROWS), bf16),
        pltpu.VMEM((ROWS, 256), bf16),
        pltpu.VMEM((ROWS, LANES), bf16),
        slab,
        pltpu.VMEM((ROWS, LATENT), f32),
    ] + [wide] * 8 + [
        pltpu.VMEM((LATENT, LANES), bf16),
        pltpu.VMEM((2, 8, LANES), f32),
        pltpu.VMEM((2, 8, LANES), f32),
        pltpu.VMEM((2, 8, LANES), f32),
        pltpu.VMEM((Total.slots(devices), 8, LANES), f32),
        pltpu.VMEM((16, LANES), f32),
        pltpu.SemaphoreType.DMA((PIECES, Gather.amount(devices, 1))),
        pltpu.SemaphoreType.DMA((Gather.amount(devices, 1),)),
        pltpu.SemaphoreType.DMA((Gather.amount(devices, 2),)),
        pltpu.SemaphoreType.DMA((Gather.amount(devices, 4),)),
        pltpu.SemaphoreType.DMA((2, Reduce.amount(devices, 2))),
        pltpu.SemaphoreType.DMA((4 * PIECES, Reduce.amount(devices, 1))),
        pltpu.SemaphoreType.DMA((2, 4)),
        pltpu.SemaphoreType.DMA((2 * Total.slots(devices),)),
        pltpu.SemaphoreType.REGULAR((6, 7)),
    ]
    vmem = pl.BlockSpec(memory_space=pltpu.VMEM)
    return pl.pallas_call(
        network,
        out_shape=[
            S((1, LANES), f32),
            S((8, LANES), f32),
            S((8, LANES), f32),
            S(unit_shape(blocks.shape[0]), bf16),
            S(unit_shape(late.shape[0]), bf16),
        ],
        in_specs=[vmem] * (len(small) + 2),
        out_specs=[vmem] * 5,
        scratch_shapes=scratch,
        compiler_params=pltpu.CompilerParams(
            vmem_limit_bytes=63 << 20, collective_id=0, has_side_effects=True
        ),
        name="network",
    )(*small, blocks, late)


def shampoo(
    energy,
    force,
    vectors,
    grads,
    left,
    right,
    left_root,
    right_root,
    master,
    late_grads,
    late_left,
    late_right,
    late_left_root,
    late_right_root,
    late_master,
    energy_out,
    force_out,
    vector_out,
    state_out,
    moved_out,
    *outs,
):
    energy_out[...] = energy[:, :PLANE]
    force_out[...] = force[0:3, :PLANE]
    vector_out[...] = vectors[0:1]
    state_out[...] = vectors[1:2]
    moved_out[...] = vectors[2:3]

    todo = []
    for j in range(left.shape[0]):
        todo.append((grads, j, left, right, left_root, right_root, master) + outs[:4])
    for j in range(late_left.shape[0]):
        todo.append(
            (late_grads, j, late_left, late_right, late_left_root, late_right_root, late_master)
            + outs[4:]
        )
    size = 1.0 / (BLOCK_ROWS * BLOCK_COLS)
    held, scales, steps = [], [], []
    for panels, j, left, *_ in todo:
        per = panels.shape[1] // BLOCK_COLS
        at = pl.program_id(0) * left.shape[0] + j
        row = pl.multiple_of(at // per * BLOCK_ROWS, BLOCK_ROWS)
        col = pl.multiple_of(at % per * BLOCK_COLS, BLOCK_COLS)
        held.append(panels[pl.ds(row, BLOCK_ROWS), pl.ds(col, BLOCK_COLS)])
    for g, (_, j, *_, grad_out, left_out, right_out, master_out) in zip(held, todo):
        grad = g.astype(f32)
        grad_out[j] = grad
        scales.append(lax.rsqrt(jnp.sum(grad * grad, keepdims=True) * size + epsilon))
    turned = []
    for g, (_, j, left, right, left_root, *_) in zip(held, todo):
        turned.append(nn(left_root[j].astype(bf16), g))
    for g, s, (_, j, left, right, *_, grad_out, left_out, right_out, master_out) in zip(
        held, scales, todo
    ):
        square = (1.0 - decay_rate) * s * s
        left_out[j] = decay_rate * left[j] + square * nt(g, g)
        right_out[j] = decay_rate * right[j] + square * tn(g, g)
    for turn, s, (_, j, left, right, left_root, right_root, *_) in zip(turned, scales, todo):
        steps.append(nn((turn * s).astype(bf16), right_root[j].astype(bf16)))
    for step, (_, j, left, right, left_root, right_root, master, *_, master_out) in zip(steps, todo):
        slope = lax.rsqrt(jnp.sum(step * step, keepdims=True) * size + epsilon)
        master_out[j] = master[j] - (learn_rate * slope) * step


def run_shampoo(energy, force, vectors, first, late):
    S = jax.ShapeDtypeStruct
    steps = min(2, late[1].shape[0])

    def whole(x):
        return pl.BlockSpec(x.shape, lambda i: (0,) * len(x.shape))

    def share(x):
        return pl.BlockSpec((x.shape[0] // steps,) + x.shape[1:], lambda i: (i, 0, 0))

    small = [S((1, PLANE), f32), S((3, PLANE), f32)] + [S((1, FINAL), f32)] * 3
    grown = []
    for group in (first, late):
        left, right, _, _, master = group[1:]
        grown += [S(x.shape, f32) for x in (master, left, right, master)]
    return pl.pallas_call(
        shampoo,
        grid=(steps,),
        out_shape=small + grown,
        in_specs=[whole(energy), whole(force), whole(vectors)]
        + [whole(first[0])]
        + [share(x) for x in first[1:]]
        + [whole(late[0])]
        + [share(x) for x in late[1:]],
        out_specs=[whole(x) for x in small] + [share(x) for x in grown],
        compiler_params=pltpu.CompilerParams(vmem_limit_bytes=60 << 20),
        name="shampoo",
    )(energy, force, vectors, *first, *late)


def local(
    positions,
    species,
    neighbours,
    counts,
    species_scale,
    species_shift,
    energy_cot,
    blocks,
    left,
    right,
    left_root,
    right_root,
    late_blocks,
    late_left,
    late_right,
    late_left_root,
    late_right_root,
    out_vector,
    vector_state,
):
    devices = lax.axis_size("atoms")
    small = (
        neighbours.reshape(PLANE, SLOTS),
        positions,
        species[None],
        counts[None],
        energy_cot[None],
        species_scale[None],
        species_shift[None],
        out_vector[None],
        vector_state[None],
    )
    energy, force, vectors, first_units, late_units = run_network(
        devices, small, blocks, late_blocks
    )
    out = run_shampoo(
        energy,
        force,
        vectors,
        (first_units, left, right, left_root, right_root, blocks),
        (late_units, late_left, late_right, late_left_root, late_right_root, late_blocks),
    )
    energies, forces, vector_grad, new_state, new_vector = out[:5]
    return (
        energies.reshape(-1),
        forces,
        *out[5:],
        vector_grad.reshape(-1),
        new_state.reshape(-1),
        new_vector.reshape(-1),
    )


def solution(mesh):
    row = P("atoms")
    block = P("atoms", None, None)
    placed = (
        (P(None, "atoms"), row, row, row, P(), P(), row)
        + (block,) * 10
        + (P(), P())
    )
    return jax.shard_map(
        local,
        mesh=mesh,
        in_specs=placed,
        out_specs=(row, P(None, "atoms")) + (block,) * 8 + (P(), P(), P()),
        check_vma=False,
    )
```
